32 devices in a mesh: parts: 2 (over y), dp: 16 (over z, x, core).
Axes of the slice: x: 2, y: 2, z: 4, core: 2. Of those that a mesh axis runs over, the one named last changes fastest.
Arguments:
- acts: bfloat16 [4096, 8192], P(('parts', 'dp')), parts along dimension 0, may hold values from -6 to 6
- cotan: bfloat16 [4096, 8192], P(('parts', 'dp')), parts along dimension 0, may hold values from -6 to 6
- token_task_index: int32 [4096, 1], P(('parts', 'dp')), parts along dimension 0, may hold values from 0 to 15; in each aligned block of 128 rows (0 to 127, 128 to 255, ...) at most 16 rows name the same one
- task_slot_lookup: int32 [32], P('parts'), parts along dimension 0, may hold values from 0 to 15, each once
- pool_down_factors: bfloat16 [32, 64, 8192], P(('parts', 'dp')), parts along dimension 0, may hold values from -0.0625 to 0.0625
- pool_up_factors: bfloat16 [32, 64, 8192], P(('parts', 'dp')), parts along dimension 0, may hold values from -0.75 to 0.75
Outputs:
- grad_acts: bfloat16 [4096, 8192], P(('parts', 'dp')), parts along dimension 0
- grad_down: float32 [32, 64, 8192], P(('parts', 'dp')), parts along dimension 0
- grad_up: float32 [32, 64, 8192], P(('parts', 'dp')), parts along dimension 0
The draws below stay inside these ranges and needn't reach their ends.
There are 2 independent parts, one for each index of `parts`. The reference program is written for one: setup_inputs(seed, part) draws one part's arguments, and reference() takes and returns one part's arrays. A program takes and returns all parts, laid end to end along the dimension named above; each array names one. Nothing has to cross between parts.
Inputs may be any that keep to these rules, and one draw needn't show every extreme that they name: `token_task_index`: among the 128 tokens of one device (aligned blocks) no task is named by more than 16 tokens; some task is named by exactly 16. `task_slot_lookup`: each slot appears once.
All inputs are finite; a program needn't handle non-finite values.
Results may differ from the reference program's by a relative error of at most 0.0049.
Values may be sent and summed in bfloat16 or wider, within the bound.
No kernel may reach another device: no remote copies, remote signals or barrier semaphores. Data moves between devices by JAX's collectives and lax.ppermute only.
A program may use at most 128 MiB of HBM per device.

```python
import math
import jax
import jax.numpy as jnp
import numpy as np
from jax import lax

MODEL_WIDTH = 8192
ADAPTER_RANK = 64
TOK_DEV = 128
ADAPTER_POOL = 16
CAP = 16
TOKENS = 2048
N_DP = 16


def shard_levels(key, shape, cuts, low, largest):
    factor_of = 1.0
    for dim, blocks in cuts:
        steps = jax.random.uniform(jax.random.fold_in(jax.random.fold_in(key, 6), dim), (blocks,), jnp.float32, low / len(cuts), largest / len(cuts))
        factor_of = factor_of * jnp.repeat(jnp.exp(steps), shape[dim] // blocks).reshape((-1,) + (1,) * (len(shape) - 1 - dim))
    return factor_of


def assign_block(own_key, own, number, rows, number_of, top, reach, skew):
    order = jax.random.permutation(own_key, number_of)
    packed, common = portions_of(number_of, rows * top, reach, skew, True), portions_of(number_of, rows * top, reach, skew, False)
    places = jnp.arange(number_of)

    def named(sizes, turn):
        used = int((sizes > 0).sum())
        fixed = max(1, used // 4)
        passed = fixed + (places - fixed + turn * (used - fixed)) % max(1, number_of - fixed)
        return jnp.zeros((number_of,), jnp.int32).at[order[jnp.where(places < fixed, places, passed)]].set(jnp.asarray(sizes, jnp.int32))

    sizes = jnp.where(number % 4 == 0, named(packed, number // 4), named(common, number - number // 4 - 1))
    mixed = jax.random.permutation(jax.random.fold_in(own, 3), number_of)
    giver, receiver = mixed[0:number_of // 2 * 2:2], mixed[1:number_of // 2 * 2:2]
    room = jnp.minimum(sizes[giver] - 1, reach - sizes[receiver]) // 2
    room = jnp.where((giver == order[0]) | (receiver == order[0]) | (sizes[receiver] == 0), 0, jnp.maximum(room, 0))
    passed = jax.random.randint(jax.random.fold_in(own, 4), (number_of // 2,), 0, 1 << 20) % (room + 1)
    sizes = sizes.at[giver].add(-passed).at[receiver].add(passed)
    labels = jnp.searchsorted(jnp.cumsum(sizes), jnp.arange(rows * top), side="right").astype(jnp.int32)
    grid = labels.reshape(top, rows).T
    grid = grid[jax.random.permutation(jax.random.fold_in(own, 1), rows)]
    turn = jax.random.randint(jax.random.fold_in(own, 2), (rows, 1), 0, top)
    return jnp.take_along_axis(grid, (jnp.arange(top)[None, :] + turn) % top, axis=1)


def portions_of(amount, total, bound, slope, full):
    loads = [(1 << 20) // math.isqrt(rank ** slope) + 1 for rank in range(1, amount + 1)]
    largest = bound if full else min(bound, max(-(-total // amount), total * loads[0] // sum(loads)))
    least = 1 if total - largest >= amount - 1 else 0
    given, surplus = [largest] + [least] * (amount - 1), total - largest - least * (amount - 1)
    while surplus > 0:
        movable = [i for i in range(1, amount) if given[i] < largest] or [i for i in range(1, amount) if given[i] < bound]
        mass, remaining = sum([loads[i] for i in movable]), surplus
        for i in movable:
            extra = min(bound - given[i], max(1, remaining * loads[i] // mass), surplus)
            given[i] = given[i] + extra
            surplus = surplus - extra
    return np.array(given)


def gaussian(own_key, extent, deviation, bound, pieces=(), held_as=jnp.bfloat16):
    drawn = jax.random.normal(own_key, extent, jnp.float32) * deviation
    if len(pieces) > 0:
        drawn = shard_levels(own_key, extent, pieces, -0.22, 0.18) * drawn
    return jnp.clip(drawn, min=-bound, max=bound).astype(held_as)


def setup_inputs(seed: int = 0, part: int = 0) -> dict:
    seeds = jax.random.split(jax.random.key(seed), 7)
    own_keys = jax.random.split(jax.random.fold_in(seeds[6], part), 7)
    acts = gaussian(own_keys[0], (TOKENS, MODEL_WIDTH), 1.0, 6.0, ((0, 16),))
    cotan = gaussian(own_keys[1], (TOKENS, MODEL_WIDTH), 1.0, 6.0, ((0, 16),))
    token_task_index_keys = jax.random.split(jax.random.fold_in(own_keys[2], 1), TOKENS // TOK_DEV)
    token_task_index_turns = jax.random.permutation(jax.random.fold_in(own_keys[2], 3), TOKENS // TOK_DEV)
    token_task_index = jax.vmap(lambda own, number: assign_block(jax.random.fold_in(own_keys[2], 2), own, number, TOK_DEV, ADAPTER_POOL, 1, CAP, 2))(token_task_index_keys, token_task_index_turns).reshape((TOKENS, 1))
    task_slot_lookup = jax.random.permutation(own_keys[3], ADAPTER_POOL).astype(jnp.int32)
    pool_down_factors = gaussian(own_keys[4], (ADAPTER_POOL, ADAPTER_RANK, MODEL_WIDTH), MODEL_WIDTH ** -0.5, 0.0625, ((0, 16),))
    pool_up_factors = gaussian(own_keys[5], (ADAPTER_POOL, ADAPTER_RANK, MODEL_WIDTH), ADAPTER_RANK ** -0.5, 0.75, ((0, 16),))
    return dict(acts=acts, cotan=cotan, token_task_index=token_task_index, task_slot_lookup=task_slot_lookup, pool_down_factors=pool_down_factors, pool_up_factors=pool_up_factors)


def reference(acts, cotan, token_task_index, task_slot_lookup, pool_down_factors, pool_up_factors):
    width = acts.shape[1]
    slot_tok = task_slot_lookup[token_task_index[:, 0]].astype(jnp.int32)
    order = jnp.argsort(slot_tok, stable=True).astype(jnp.int32)
    counts = lax.optimization_barrier(jnp.sum((slot_tok[:, None] == jnp.arange(ADAPTER_POOL, dtype=jnp.int32)[None, :]).astype(jnp.int32), axis=0))
    starts = (jnp.cumsum(counts) - counts).astype(jnp.int32)
    most = N_DP * CAP
    lanes = jnp.arange(most, dtype=jnp.int32)

    def per_slot(slot_index):
        count = counts[slot_index]
        valid = lanes < count
        where = jnp.clip(starts[slot_index] + lanes, 0, TOKENS - 1)
        rows = order[where]
        rows_x = jnp.where(valid[:, None], acts[rows], jnp.zeros((), acts.dtype))
        rows_g = jnp.where(valid[:, None], cotan[rows], jnp.zeros((), cotan.dtype))
        down_matrix = pool_down_factors[slot_index]
        up_matrix = pool_up_factors[slot_index]
        dims = (((1,), (1,)), ((), ()))
        hidden = lax.dot_general(rows_x, down_matrix, dims, preferred_element_type=jnp.float32).astype(jnp.bfloat16)
        inner = lax.dot_general(rows_g, up_matrix, dims, preferred_element_type=jnp.float32).astype(jnp.bfloat16)
        rows_dx = jnp.dot(inner, down_matrix, preferred_element_type=jnp.float32).astype(jnp.bfloat16)
        tdims = (((0,), (0,)), ((), ()))
        raw_up = lax.dot_general(hidden, rows_g, tdims, preferred_element_type=jnp.float32)
        raw_down = lax.dot_general(inner, rows_x, tdims, preferred_element_type=jnp.float32)
        target = jnp.where(valid, rows, TOKENS).astype(jnp.int32)
        return (rows_dx, target, raw_down, raw_up)
    rows_dx, target, raw_down, raw_up = lax.map(per_slot, jnp.arange(ADAPTER_POOL, dtype=jnp.int32))
    grad_acts = jnp.zeros((TOKENS, width), jnp.bfloat16).at[target.reshape(-1)].set(rows_dx.reshape(-1, width), mode='drop')
    total = jnp.sum(raw_down * raw_down) + jnp.sum(raw_up * raw_up)
    norm = jnp.sqrt(total + 1e-06)
    limit = jnp.sqrt(jnp.float32(2 * ADAPTER_RANK * MODEL_WIDTH * ADAPTER_POOL))
    factor = jnp.minimum(jnp.float32(1.0), limit / norm)
    return (grad_acts, raw_down * factor, raw_up * factor)
```

```python
import jax
import jax.numpy as jnp
from jax import lax
from jax.sharding import PartitionSpec as P

ROWS_OF = (((1,), (1,)), ((), ()))
OUTER = (((0,), (0,)), ((), ()))


def dot32(a, b, dims=(((1,), (0,)), ((), ()))):
    return lax.dot_general(a, b, dims, preferred_element_type=jnp.float32)


def route(token_task_index, task_slot_lookup, ndevices):
    pool = task_slot_lookup.shape[0]
    task_hot = (token_task_index == jnp.arange(pool, dtype=jnp.int32)[None, :]).astype(jnp.int32)
    owner = jnp.sum(task_hot * task_slot_lookup[None, :], axis=1)
    owner_hot = (owner[:, None] == jnp.arange(ndevices, dtype=jnp.int32)[None, :]).astype(jnp.int32)
    before = jnp.cumsum(owner_hot, axis=0) - owner_hot
    position = jnp.sum(before * owner_hot, axis=1)
    return owner, position


def clipped(raw_down, raw_up, ndevices):
    local_sq = jnp.sum(raw_down * raw_down) + jnp.sum(raw_up * raw_up)
    total = lax.psum(local_sq, "dp")
    norm = jnp.sqrt(total + 1e-06)
    limit = jnp.sqrt(jnp.float32(2 * raw_down.shape[0] * raw_down.shape[1] * ndevices))
    factor = jnp.minimum(jnp.float32(1.0), limit / norm)
    return (raw_down * factor)[None], (raw_up * factor)[None]


def move_tokens(acts, cotan, token_task_index, task_slot_lookup, pool_down_factors, pool_up_factors):
    ndevices = lax.axis_size("dp")
    tokens, width = acts.shape
    capacity = 2 * ((tokens + ndevices - 1) // ndevices)
    slots = ndevices * capacity
    owner, position = route(token_task_index, task_slot_lookup, ndevices)
    dest = owner * capacity + position
    placed = (jnp.arange(slots, dtype=jnp.int32)[:, None] == dest[None, :]).astype(jnp.bfloat16)

    def exchange(rows):
        rows = rows.reshape(ndevices, capacity, width)
        return lax.all_to_all(rows, "dp", split_axis=0, concat_axis=0, tiled=True).reshape(slots, width)

    down, up = pool_down_factors[0], pool_up_factors[0]
    rows_x = exchange(dot32(placed, acts).astype(jnp.bfloat16))
    rows_g = exchange(dot32(placed, cotan).astype(jnp.bfloat16))
    hidden = dot32(rows_x, down, ROWS_OF).astype(jnp.bfloat16)
    inner = dot32(rows_g, up, ROWS_OF).astype(jnp.bfloat16)
    returned = exchange(dot32(inner, down).astype(jnp.bfloat16))
    grad_acts = dot32(placed, returned, OUTER).astype(jnp.bfloat16)
    raw_up = dot32(hidden, rows_g, OUTER)
    raw_down = dot32(inner, rows_x, OUTER)
    return (grad_acts,) + clipped(raw_down, raw_up, ndevices)


def move_adapters(plane, acts, cotan, token_task_index, task_slot_lookup, pool_down_factors, pool_up_factors):
    ndevices = lax.axis_size("dp")
    tokens, width = acts.shape
    capacity = 2 * ((tokens + ndevices - 1) // ndevices)
    me = lax.axis_index("dp")
    z, column = me // plane, me % plane
    is_end = (z == 0) | (z == 3)
    bf16 = jnp.bfloat16

    def planes(pairs):
        return [(a * plane + c, b * plane + c) for a, b in pairs for c in range(plane)]

    swap = planes([(0, 1), (1, 0), (2, 3), (3, 2)])
    cross = planes([(1, 2), (2, 1)])
    outward = planes([(1, 0), (2, 3)])
    inward = planes([(0, 1), (3, 2)])

    def beside(m):
        return [(i, (i // plane) * plane + ((i % plane) ^ m)) for i in range(ndevices)]

    def send(array, pairs):
        return lax.ppermute(array, "dp", pairs)

    owner, position = route(token_task_index, task_slot_lookup, ndevices)
    owner_z, turn = owner // plane, (owner % plane) ^ column
    other_mid = jnp.where(z < 2, 2, 1)
    kind = jnp.where(owner_z == z, 0, jnp.where(owner_z == (z ^ 1), 1, jnp.where(owner_z == other_mid, 2, 3)))

    def places(wanted, row, rows):
        hot = jnp.arange(rows, dtype=jnp.int32)[:, None] == row[None, :]
        return (hot & wanted[None, :]).astype(bf16)

    block = plane * capacity
    place3 = places(kind == 3, turn * capacity + position, block)
    place2 = places(kind == 2, turn * capacity + position, block)
    place10 = places(kind < 2, turn * (2 * capacity) + kind * capacity + position, 2 * block)

    def in_plane(blocks):
        return [blocks[0]] + [send(blocks[m], beside(m)) for m in range(1, plane)]

    def packed(place, rows):
        out = dot32(place, rows).astype(bf16)
        return list(out.reshape(plane, -1, width))

    down, up = pool_down_factors[0], pool_up_factors[0]
    down_e, up_e = send(down, swap), send(up, swap)
    down_x, up_x = send(down, cross), send(up, cross)

    x3, g3 = in_plane(packed(place3, acts)), in_plane(packed(place3, cotan))
    x2, g2 = in_plane(packed(place2, acts)), in_plane(packed(place2, cotan))
    x3, g3 = jnp.concatenate(x3), jnp.concatenate(g3)
    x3t, g3t = send(x3, inward), send(g3, inward)
    x10, g10 = in_plane(packed(place10, acts)), in_plane(packed(place10, cotan))

    down_o, up_o = send(down_x, outward), send(up_x, outward)
    down_f, up_f = send(down_e, cross), send(up_e, cross)
    down_2, up_2 = jnp.where(is_end, down_o, down_x), jnp.where(is_end, up_o, up_x)

    x2, g2 = jnp.concatenate(x2), jnp.concatenate(g2)
    x3, g3 = jnp.concatenate([x3, x3t]), jnp.concatenate([g3, g3t])
    x0 = jnp.concatenate([b[:capacity] for b in x10])
    g0 = jnp.concatenate([b[:capacity] for b in g10])
    x1 = jnp.concatenate([b[capacity:] for b in x10])
    g1 = jnp.concatenate([b[capacity:] for b in g10])

    def group(x, g, d, u):
        hidden = dot32(x, d, ROWS_OF).astype(bf16)
        inner = dot32(g, u, ROWS_OF).astype(bf16)
        return dot32(inner, d).astype(bf16), dot32(hidden, g, OUTER), dot32(inner, x, OUTER)

    dx3, ru3, rd3 = group(x3, g3, down_f, up_f)
    dx2, ru2, rd2 = group(x2, g2, down_2, up_2)
    dx1, ru1, rd1 = group(x1, g1, down_e, up_e)
    dx0, ru0, rd0 = group(x0, g0, down, up)

    ru3, rd3 = send(ru3.astype(bf16), cross), send(rd3.astype(bf16), cross)
    ru2i, rd2i = send(ru2.astype(bf16), inward), send(rd2.astype(bf16), inward)
    ru2, rd2 = send((ru2 + ru2i).astype(bf16), cross), send((rd2 + rd2i).astype(bf16), cross)
    ru1, rd1 = send((ru1 + ru3).astype(bf16), swap), send((rd1 + rd3).astype(bf16), swap)
    raw_up = ru0 + ru2 + ru1
    raw_down = rd0 + rd2 + rd1

    dx3 = jnp.where(is_end, send(dx3[block:], outward), dx3[:block])
    back3 = in_plane(list(dx3.reshape(plane, capacity, width)))
    back2 = in_plane(list(dx2.reshape(plane, capacity, width)))
    dx10 = jnp.concatenate([dx0.reshape(plane, capacity, width), dx1.reshape(plane, capacity, width)], axis=1)
    back10 = in_plane(list(dx10))
    place = jnp.concatenate([place3, place2, place10])
    grad_acts = dot32(place, jnp.concatenate(back3 + back2 + back10), OUTER).astype(bf16)
    return (grad_acts,) + clipped(raw_down, raw_up, ndevices)


def solution(mesh):
    ndevices = mesh.shape["dp"]
    plane = 1
    while (2 * plane) ** 2 <= ndevices:
        plane *= 2

    def per_device(*arrays):
        if ndevices == 4 * plane:
            return move_adapters(plane, *arrays)
        return move_tokens(*arrays)

    rows, pools = P(("parts", "dp"), None), P(("parts", "dp"), None, None)
    return jax.shard_map(
        per_device,
        mesh=mesh,
        in_specs=(rows, rows, rows, P("parts"), pools, pools),
        out_specs=(rows, pools, pools),
        check_vma=False,
    )
```

```python
import functools

import jax
import jax.numpy as jnp
from jax import lax
from jax.experimental import pallas as pl
from jax.experimental.pallas import tpu as pltpu
from jax.sharding import PartitionSpec as P

BF16, F32 = jnp.bfloat16, jnp.float32
ROWS_OF = (((1,), (1,)), ((), ()))
OUTER = (((0,), (0,)), ((), ()))
INNER = (((1,), (0,)), ((), ()))
ANY = pl.BlockSpec(memory_space=pl.ANY)
VMEM_BYTES = 50 * 2**20


def dot32(a, b, dims=INNER):
    return lax.dot_general(a, b, dims, preferred_element_type=F32)


def route(token_task_index, task_slot_lookup, ndevices):
    pool = task_slot_lookup.shape[0]
    task_hot = (token_task_index == jnp.arange(pool, dtype=jnp.int32)[None, :]).astype(jnp.int32)
    owner = jnp.sum(task_hot * task_slot_lookup[None, :], axis=1)
    owner_hot = (owner[:, None] == jnp.arange(ndevices, dtype=jnp.int32)[None, :]).astype(jnp.int32)
    before = jnp.cumsum(owner_hot, axis=0) - owner_hot
    position = jnp.sum(before * owner_hot, axis=1)
    return owner, position


def clipped(raw_down, raw_up, ndevices):
    local_sq = jnp.sum(raw_down * raw_down) + jnp.sum(raw_up * raw_up)
    total = lax.psum(local_sq, "dp")
    norm = jnp.sqrt(total + 1e-06)
    limit = jnp.sqrt(jnp.float32(2 * raw_down.shape[0] * raw_down.shape[1] * ndevices))
    factor = jnp.minimum(jnp.float32(1.0), limit / norm)
    return (raw_down * factor)[None], (raw_up * factor)[None]


def move_tokens(acts, cotan, token_task_index, task_slot_lookup, pool_down_factors, pool_up_factors):
    ndevices = lax.axis_size("dp")
    tokens, width = acts.shape
    capacity = 2 * ((tokens + ndevices - 1) // ndevices)
    slots = ndevices * capacity
    owner, position = route(token_task_index, task_slot_lookup, ndevices)
    dest = owner * capacity + position
    placed = (jnp.arange(slots, dtype=jnp.int32)[:, None] == dest[None, :]).astype(BF16)

    def exchange(rows):
        rows = rows.reshape(ndevices, capacity, width)
        return lax.all_to_all(rows, "dp", split_axis=0, concat_axis=0, tiled=True).reshape(slots, width)

    down, up = pool_down_factors[0], pool_up_factors[0]
    rows_x = exchange(dot32(placed, acts).astype(BF16))
    rows_g = exchange(dot32(placed, cotan).astype(BF16))
    hidden = dot32(rows_x, down, ROWS_OF).astype(BF16)
    inner = dot32(rows_g, up, ROWS_OF).astype(BF16)
    returned = exchange(dot32(inner, down).astype(BF16))
    grad_acts = dot32(placed, returned, OUTER).astype(BF16)
    raw_up = dot32(hidden, rows_g, OUTER)
    raw_down = dot32(inner, rows_x, OUTER)
    return (grad_acts,) + clipped(raw_down, raw_up, ndevices)


def kernel_params(semantics=("arbitrary",)):
    return pltpu.CompilerParams(dimension_semantics=semantics, vmem_limit_bytes=VMEM_BYTES)


def cost(flops, nbytes):
    return pl.CostEstimate(flops=flops, bytes_accessed=nbytes, transcendentals=0)


def pack(place, acts, cotan, plane):
    rows, (tokens, width) = place.shape[0] // plane, acts.shape
    tile = min(width, 1024)

    def body(place_ref, x_ref, g_ref, *out_refs):
        for k, ref in enumerate((x_ref, g_ref)):
            moved = dot32(place_ref[...], ref[...]).astype(BF16)
            for m in range(plane):
                out_refs[m][k] = moved[m * rows:(m + 1) * rows]

    rows_spec = pl.BlockSpec((tokens, tile), lambda i: (0, i))
    return pl.pallas_call(
        body,
        grid=(width // tile,),
        in_specs=[pl.BlockSpec(place.shape, lambda i: (0, 0)), rows_spec, rows_spec],
        out_specs=[pl.BlockSpec((2, rows, tile), lambda i: (0, 0, i))] * plane,
        out_shape=[jax.ShapeDtypeStruct((2, rows, width), BF16)] * plane,
        compiler_params=kernel_params(),
        cost_estimate=cost(4 * place.shape[0] * tokens * width, 4 * (tokens + place.shape[0]) * width),
    )(place, acts, cotan)


def unpack(place, blocks, tokens):
    width = blocks[0].shape[1]
    tile = min(width, 1024)
    total = place.shape[0]

    def body(place_ref, *refs):
        rows = jnp.concatenate([ref[...] for ref in refs[:-1]], axis=0)
        refs[-1][...] = dot32(place_ref[...], rows, OUTER).astype(BF16)

    return pl.pallas_call(
        body,
        grid=(width // tile,),
        in_specs=[pl.BlockSpec(place.shape, lambda i: (0, 0))]
        + [pl.BlockSpec((b.shape[0], tile), lambda i: (0, i)) for b in blocks],
        out_specs=pl.BlockSpec((tokens, tile), lambda i: (0, i)),
        out_shape=jax.ShapeDtypeStruct((tokens, width), BF16),
        compiler_params=kernel_params(),
        cost_estimate=cost(2 * total * tokens * width, 2 * (tokens + total) * width),
    )(place, *blocks)


def far_groups(is_end, stage, mids, far, outer, crossed, capacity):
    plane = len(stage)
    _, rank, width = far.shape
    block = plane * capacity
    tile = min(width, 1024)
    tiles = width // tile

    def body(end_ref, *refs):
        stage_in, (mids_in, far_in, outer_in, crossed_in) = refs[:plane], refs[plane:plane + 4]
        sum3_ref, sum2_ref, dx_ref, inner3_ref, inner2_ref = refs[plane + 4:plane + 9]
        tokens, ends, far_w, near_w, hidden3, hidden2, sems = refs[plane + 9:]
        step = pl.program_id(0)

        def copies(i):
            cut = pl.ds(i * tile, tile)
            pairs = [(stage_in[m], tokens.at[m]) for m in range(plane)] + [(mids_in, ends), (far_in, far_w)]
            return [
                pltpu.make_async_copy(src.at[:, :, cut], dst.at[:, :, cut], sems.at[i, n])
                for n, (src, dst) in enumerate(pairs)
            ]

        def near_copy(src, i):
            cut = pl.ds(i * tile, tile)
            return pltpu.make_async_copy(src.at[:, :, cut], near_w.at[:, :, cut], sems.at[i, plane + 2])

        def rows3(k, cut):
            return jnp.concatenate([tokens[m, k, :capacity, cut] for m in range(plane)] + [ends[k, :, cut]], axis=0)

        def rows2(k, cut):
            return jnp.concatenate([tokens[m, k, capacity:, cut] for m in range(plane)], axis=0)

        @pl.when(step == 0)
        def _():
            for i in range(tiles):
                for c in copies(i):
                    c.start()

                @pl.when(end_ref[0] == 1)
                def _():
                    near_copy(outer_in, i).start()

                @pl.when(end_ref[0] != 1)
                def _():
                    near_copy(crossed_in, i).start()

            sums = [jnp.zeros((2 * block, rank), F32)] * 2 + [jnp.zeros((block, rank), F32)] * 2
            for i in range(tiles):
                for c in copies(i):
                    c.wait()
                near_copy(outer_in, i).wait()
                cut = pl.ds(i * tile, tile)
                for k in range(2):
                    sums[k] += dot32(rows3(k, cut), far_w[k, :, cut], ROWS_OF)
                    sums[2 + k] += dot32(rows2(k, cut), near_w[k, :, cut], ROWS_OF)
            hidden3[...] = sums[0].astype(BF16)
            inner3_ref[...] = sums[1].astype(BF16)
            hidden2[...] = sums[2].astype(BF16)
            inner2_ref[...] = sums[3].astype(BF16)

        cut = pl.ds(pl.multiple_of(step * tile, tile), tile)
        sum3_ref[0] = dot32(hidden3[...], rows3(1, cut), OUTER).astype(BF16)
        sum3_ref[1] = dot32(inner3_ref[...], rows3(0, cut), OUTER).astype(BF16)
        sum2_ref[0] = dot32(hidden2[...], rows2(1, cut), OUTER).astype(BF16)
        sum2_ref[1] = dot32(inner2_ref[...], rows2(0, cut), OUTER).astype(BF16)
        dx_ref[...] = dot32(inner3_ref[block:], far_w[0, :, cut]).astype(BF16)

    pair = jax.ShapeDtypeStruct((2, rank, width), BF16)
    pair_spec = pl.BlockSpec((2, rank, tile), lambda i: (0, 0, i))
    return pl.pallas_call(
        body,
        grid=(tiles,),
        in_specs=[pl.BlockSpec(memory_space=pltpu.SMEM)] + [ANY] * (plane + 4),
        out_specs=[
            pair_spec,
            pair_spec,
            pl.BlockSpec((block, tile), lambda i: (0, i)),
            pl.BlockSpec((2 * block, rank), lambda i: (0, 0)),
            pl.BlockSpec((block, rank), lambda i: (0, 0)),
        ],
        out_shape=[
            pair,
            pair,
            jax.ShapeDtypeStruct((block, width), BF16),
            jax.ShapeDtypeStruct((2 * block, rank), BF16),
            jax.ShapeDtypeStruct((block, rank), BF16),
        ],
        scratch_shapes=[
            pltpu.VMEM((plane, 2, 2 * capacity, width), BF16),
            pltpu.VMEM((2, block, width), BF16),
            pltpu.VMEM((2, rank, width), BF16),
            pltpu.VMEM((2, rank, width), BF16),
            pltpu.VMEM((2 * block, rank), BF16),
            pltpu.VMEM((block, rank), BF16),
            pltpu.SemaphoreType.DMA((tiles, plane + 3)),
        ],
        compiler_params=kernel_params(),
        cost_estimate=cost(26 * block * rank * width, 38 * block * width),
    )(is_end, *stage, mids, far, outer, crossed)


def near_groups(is_end, stage, pair, down, up, far, outer, crossed, inner3, inner2, capacity):
    plane = len(stage)
    _, rank, width = far.shape
    block = plane * capacity
    tile = min(width, 1024)
    tiles = width // tile

    def body(end_ref, *refs):
        stage_in, refs = refs[:plane], refs[plane:]
        pair_in, down_in, up_in, far_in, outer_in, crossed_in, inner3, inner2 = refs[:8]
        dx_refs, (sum1_ref, sum0_ref) = refs[8:8 + plane], refs[8 + plane:10 + plane]
        tokens, pair_w, own_w, dx_w, hidden1, inner1, hidden0, inner0, sems = refs[10 + plane:]
        step = pl.program_id(0)

        def copies(i):
            cut = pl.ds(i * tile, tile)
            pairs = [(stage_in[m].at[:, :, cut], tokens.at[m, :, :, cut]) for m in range(plane)] + [
                (pair_in.at[:, :, cut], pair_w.at[:, :, cut]),
                (down_in.at[:, cut], own_w.at[0, :, cut]),
                (up_in.at[:, cut], own_w.at[1, :, cut]),
                (far_in.at[0, :, cut], dx_w.at[0, :, cut]),
            ]
            return [pltpu.make_async_copy(src, dst, sems.at[i, n]) for n, (src, dst) in enumerate(pairs)]

        def near_copy(src, i):
            cut = pl.ds(i * tile, tile)
            return pltpu.make_async_copy(src.at[0, :, cut], dx_w.at[1, :, cut], sems.at[i, plane + 4])

        def rows1(k, cut):
            return jnp.concatenate([tokens[m, k, :capacity, cut] for m in range(plane)], axis=0)

        def rows0(k, cut):
            return jnp.concatenate([tokens[m, k, capacity:, cut] for m in range(plane)], axis=0)

        @pl.when(step == 0)
        def _():
            for i in range(tiles):
                for c in copies(i):
                    c.start()

                @pl.when(end_ref[0] == 1)
                def _():
                    near_copy(outer_in, i).start()

                @pl.when(end_ref[0] != 1)
                def _():
                    near_copy(crossed_in, i).start()

            sums = [jnp.zeros((block, rank), F32)] * 4
            for i in range(tiles):
                for c in copies(i):
                    c.wait()
                near_copy(outer_in, i).wait()
                cut = pl.ds(i * tile, tile)
                for k in range(2):
                    sums[k] += dot32(rows1(k, cut), pair_w[k, :, cut], ROWS_OF)
                    sums[2 + k] += dot32(rows0(k, cut), own_w[k, :, cut], ROWS_OF)
            for ref, value in zip((hidden1, inner1, hidden0, inner0), sums):
                ref[...] = value.astype(BF16)

        cut = pl.ds(pl.multiple_of(step * tile, tile), tile)
        sum1_ref[0] = dot32(hidden1[...], rows1(1, cut), OUTER)
        sum1_ref[1] = dot32(inner1[...], rows1(0, cut), OUTER)
        sum0_ref[0] = dot32(hidden0[...], rows0(1, cut), OUTER)
        sum0_ref[1] = dot32(inner0[...], rows0(0, cut), OUTER)
        moved = [
            dot32(inner3[:block], dx_w[0, :, cut]),
            dot32(inner2[...], dx_w[1, :, cut]),
            dot32(inner1[...], pair_w[0, :, cut]),
            dot32(inner0[...], own_w[0, :, cut]),
        ]
        for n, dx in enumerate(moved):
            dx = dx.astype(BF16)
            for m in range(plane):
                dx_refs[m][n * capacity:(n + 1) * capacity] = dx[m * capacity:(m + 1) * capacity]

    total = jax.ShapeDtypeStruct((2, rank, width), F32)
    total_spec = pl.BlockSpec((2, rank, tile), lambda i: (0, 0, i))
    whole = [pl.BlockSpec(a.shape, lambda i: (0, 0)) for a in (inner3, inner2)]
    return pl.pallas_call(
        body,
        grid=(tiles,),
        in_specs=[pl.BlockSpec(memory_space=pltpu.SMEM)] + [ANY] * (plane + 6) + whole,
        out_specs=[pl.BlockSpec((4 * capacity, tile), lambda i: (0, i))] * plane + [total_spec] * 2,
        out_shape=[jax.ShapeDtypeStruct((4 * capacity, width), BF16)] * plane + [total] * 2,
        scratch_shapes=[
            pltpu.VMEM((plane, 2, 2 * capacity, width), BF16),
            pltpu.VMEM((2, rank, width), BF16),
            pltpu.VMEM((2, rank, width), BF16),
            pltpu.VMEM((2, rank, width), BF16),
        ]
        + [pltpu.VMEM((block, rank), BF16)] * 4
        + [pltpu.SemaphoreType.DMA((tiles, plane + 5))],
        compiler_params=kernel_params(),
        cost_estimate=cost(24 * block * rank * width, 48 * block * width),
    )(is_end, *stage, pair, down, up, far, outer, crossed, inner3, inner2)


def move_adapters(plane, acts, cotan, token_task_index, task_slot_lookup, pool_down_factors, pool_up_factors):
    ndevices = lax.axis_size("dp")
    tokens, width = acts.shape
    capacity = 2 * ((tokens + ndevices - 1) // ndevices)
    me = lax.axis_index("dp")
    z, column = me // plane, me % plane
    is_end = (z == 0) | (z == 3)
    end_flag = is_end.astype(jnp.int32).reshape(1)

    def planes(pairs):
        return [(a * plane + c, b * plane + c) for a, b in pairs for c in range(plane)]

    swap = planes([(0, 1), (1, 0), (2, 3), (3, 2)])
    cross = planes([(1, 2), (2, 1)])
    outward = planes([(1, 0), (2, 3)])
    inward = planes([(0, 1), (3, 2)])

    def send(array, pairs):
        return lax.ppermute(array, "dp", pairs)

    def in_plane(blocks, among=(0, 1, 2, 3)):
        moved = [blocks[0]]
        for m in range(1, plane):
            pairs = [(i, (i // plane) * plane + ((i % plane) ^ m)) for i in range(ndevices) if i // plane in among]
            moved.append(send(blocks[m], pairs))
        return moved

    down, up = pool_down_factors[0], pool_up_factors[0]
    own = jnp.concatenate([pool_down_factors, pool_up_factors])
    pair = send(own, swap)
    crossed = send(own, cross)

    owner, position = route(token_task_index, task_slot_lookup, ndevices)
    owner_z, turn = owner // plane, (owner % plane) ^ column
    other_mid = jnp.where(z < 2, 2, 1)
    kind = jnp.where(owner_z == z, 0, jnp.where(owner_z == (z ^ 1), 1, jnp.where(owner_z == other_mid, 2, 3)))

    def places(wanted, row, rows):
        hot = jnp.arange(rows, dtype=jnp.int32)[:, None] == row[None, :]
        return (hot & wanted[None, :]).astype(BF16)

    half = 2 * capacity
    place_a = places(kind >= 2, turn * half + (3 - kind) * capacity + position, plane * half)
    place_b = places(kind < 2, turn * half + (1 - kind) * capacity + position, plane * half)
    place_back = places(kind >= 0, turn * 2 * half + (3 - kind) * capacity + position, 2 * plane * half)
    place_ends = places(kind == 3, turn * capacity + position, plane * capacity)

    stage_a = in_plane(pack(place_a, acts, cotan, plane))
    ends = send(jnp.concatenate([b[:, :capacity] for b in stage_a], axis=1), inward)
    packed_b, _ = lax.optimization_barrier((pack(place_b, acts, cotan, plane), stage_a))
    stage_b = in_plane(packed_b)
    outer = send(crossed, outward)
    far = send(pair, cross)

    sum3, sum2, dx_ends, inner3, inner2 = far_groups(end_flag, stage_a, ends, far, outer, crossed, capacity)
    sum3 = send(sum3, cross)
    sum2_in = send(sum2, inward)
    dx_ends = send(dx_ends, outward)

    *dx, sum1, sum0 = near_groups(
        end_flag, stage_b, pair, down, up, far, outer, crossed, inner3, inner2, capacity
    )
    sum2 = send((sum2.astype(F32) + sum2_in.astype(F32)).astype(BF16), cross)
    sum1 = send((sum1 + sum3.astype(F32)).astype(BF16), swap)

    back = in_plane(dx)
    back_ends = in_plane([dx_ends[m * capacity:(m + 1) * capacity] for m in range(plane)], (0, 3))
    grad_acts = unpack(jnp.concatenate([place_back, place_ends]), back + back_ends, tokens)
    raw_up, raw_down = (sum0[k] + sum2[k].astype(F32) + sum1[k].astype(F32) for k in range(2))
    return (grad_acts,) + clipped(raw_down, raw_up, ndevices)


def solution(mesh):
    ndevices = mesh.shape["dp"]
    plane = 1
    while (2 * plane) ** 2 <= ndevices:
        plane *= 2

    def per_device(*arrays):
        if ndevices == 4 * plane:
            return move_adapters(plane, *arrays)
        return move_tokens(*arrays)

    rows, pools = P(("parts", "dp"), None), P(("parts", "dp"), None, None)
    return jax.shard_map(
        per_device,
        mesh=mesh,
        in_specs=(rows, rows, rows, P("parts"), pools, pools),
        out_specs=(rows, pools, pools),
        check_vma=False,
    )
```

```python
import functools

import jax
import jax.numpy as jnp
from jax import lax
from jax.experimental import pallas as pl
from jax.experimental.pallas import tpu as pltpu
from jax.sharding import PartitionSpec as P

BF16, F32 = jnp.bfloat16, jnp.float32
ROWS_OF = (((1,), (1,)), ((), ()))
OUTER = (((0,), (0,)), ((), ()))
INNER = (((1,), (0,)), ((), ()))
ANY = pl.BlockSpec(memory_space=pl.ANY)
VMEM_BYTES = 50 * 2**20


def dot32(a, b, dims=INNER):
    return lax.dot_general(a, b, dims, preferred_element_type=F32)


def route(token_task_index, task_slot_lookup, ndevices):
    pool = task_slot_lookup.shape[0]
    task_hot = (token_task_index == jnp.arange(pool, dtype=jnp.int32)[None, :]).astype(jnp.int32)
    owner = jnp.sum(task_hot * task_slot_lookup[None, :], axis=1)
    owner_hot = (owner[:, None] == jnp.arange(ndevices, dtype=jnp.int32)[None, :]).astype(jnp.int32)
    before = jnp.cumsum(owner_hot, axis=0) - owner_hot
    position = jnp.sum(before * owner_hot, axis=1)
    return owner, position


def clipped(raw_down, raw_up, ndevices):
    local_sq = jnp.sum(raw_down * raw_down) + jnp.sum(raw_up * raw_up)
    shares = jnp.broadcast_to(local_sq, (ndevices, 8, 128))
    total = jnp.sum(lax.all_to_all(shares, "dp", split_axis=0, concat_axis=0, tiled=True)[:, 0, 0])
    norm = jnp.sqrt(total + 1e-06)
    limit = jnp.sqrt(jnp.float32(2 * raw_down.shape[0] * raw_down.shape[1] * ndevices))
    factor = jnp.minimum(jnp.float32(1.0), limit / norm)
    return (raw_down * factor)[None], (raw_up * factor)[None]


def move_tokens(acts, cotan, token_task_index, task_slot_lookup, pool_down_factors, pool_up_factors):
    ndevices = lax.axis_size("dp")
    tokens, width = acts.shape
    capacity = 2 * ((tokens + ndevices - 1) // ndevices)
    slots = ndevices * capacity
    owner, position = route(token_task_index, task_slot_lookup, ndevices)
    dest = owner * capacity + position
    placed = (jnp.arange(slots, dtype=jnp.int32)[:, None] == dest[None, :]).astype(BF16)

    def exchange(rows):
        rows = rows.reshape(ndevices, capacity, width)
        return lax.all_to_all(rows, "dp", split_axis=0, concat_axis=0, tiled=True).reshape(slots, width)

    down, up = pool_down_factors[0], pool_up_factors[0]
    rows_x = exchange(dot32(placed, acts).astype(BF16))
    rows_g = exchange(dot32(placed, cotan).astype(BF16))
    hidden = dot32(rows_x, down, ROWS_OF).astype(BF16)
    inner = dot32(rows_g, up, ROWS_OF).astype(BF16)
    returned = exchange(dot32(inner, down).astype(BF16))
    grad_acts = dot32(placed, returned, OUTER).astype(BF16)
    raw_up = dot32(hidden, rows_g, OUTER)
    raw_down = dot32(inner, rows_x, OUTER)
    return (grad_acts,) + clipped(raw_down, raw_up, ndevices)


def kernel_params(semantics=("arbitrary",)):
    return pltpu.CompilerParams(dimension_semantics=semantics, vmem_limit_bytes=VMEM_BYTES)


def cost(flops, nbytes):
    return pl.CostEstimate(flops=flops, bytes_accessed=nbytes, transcendentals=0)


def pack(place, acts, cotan, plane, parts):
    tokens, width = acts.shape
    tile = min(width, 1024)
    cuts, start = [], 0
    for rows in parts:
        for _ in range(plane):
            cuts.append((start, rows))
            start += rows

    def body(place_ref, x_ref, g_ref, *out_refs):
        for k, ref in enumerate((x_ref, g_ref)):
            moved = dot32(place_ref[...], ref[...]).astype(BF16)
            for out_ref, (first, rows) in zip(out_refs, cuts):
                out_ref[k] = moved[first:first + rows]

    rows_spec = pl.BlockSpec((tokens, tile), lambda i: (0, i))
    packed = pl.pallas_call(
        body,
        grid=(width // tile,),
        in_specs=[pl.BlockSpec(place.shape, lambda i: (0, 0)), rows_spec, rows_spec],
        out_specs=[pl.BlockSpec((2, rows, tile), lambda i: (0, 0, i)) for _, rows in cuts],
        out_shape=[jax.ShapeDtypeStruct((2, rows, width), BF16) for _, rows in cuts],
        compiler_params=kernel_params(),
        cost_estimate=cost(4 * place.shape[0] * tokens * width, 4 * (tokens + place.shape[0]) * width),
    )(place, acts, cotan)
    return [packed[n * plane:(n + 1) * plane] for n in range(len(parts))]


def unpack(place, blocks, tokens):
    width = blocks[0].shape[1]
    tile = min(width, 1024)
    total = place.shape[0]

    def body(place_ref, *refs):
        rows = jnp.concatenate([ref[...] for ref in refs[:-1]], axis=0)
        refs[-1][...] = dot32(place_ref[...], rows, OUTER).astype(BF16)

    return pl.pallas_call(
        body,
        grid=(width // tile,),
        in_specs=[pl.BlockSpec(place.shape, lambda i: (0, 0))]
        + [pl.BlockSpec((b.shape[0], tile), lambda i: (0, i)) for b in blocks],
        out_specs=pl.BlockSpec((tokens, tile), lambda i: (0, i)),
        out_shape=jax.ShapeDtypeStruct((tokens, width), BF16),
        compiler_params=kernel_params(),
        cost_estimate=cost(2 * total * tokens * width, 2 * (tokens + total) * width),
    )(place, *blocks)


def far_groups(is_end, stage3, stage2, ends, far, outer, crossed, capacity):
    plane = len(stage3)
    _, rank, width = far.shape
    block = plane * capacity
    tile = min(width, 1024)
    tiles = width // tile

    def body(end_ref, *refs):
        stage_in, refs = refs[:2 * plane], refs[2 * plane:]
        ends_in, far_in, outer_in, crossed_in = refs[:4]
        sum3_ref, sum2_ref, dx_ref, inner3_ref, inner2_ref = refs[4:9]
        tokens, ends_t, far_w, near_w, hidden3, hidden2, sems = refs[9:]
        step = pl.program_id(0)

        def copies(i):
            cut = pl.ds(i * tile, tile)
            pairs = [(stage_in[m], tokens.at[m]) for m in range(2 * plane)] + [(ends_in, ends_t), (far_in, far_w)]
            return [
                pltpu.make_async_copy(src.at[:, :, cut], dst.at[:, :, cut], sems.at[i, n])
                for n, (src, dst) in enumerate(pairs)
            ]

        def near_copy(src, i):
            cut = pl.ds(i * tile, tile)
            return pltpu.make_async_copy(src.at[:, :, cut], near_w.at[:, :, cut], sems.at[i, 2 * plane + 2])

        def rows3(k, cut):
            return jnp.concatenate([tokens[m, k, :, cut] for m in range(plane)] + [ends_t[k, :, cut]], axis=0)

        def rows2(k, cut):
            return jnp.concatenate([tokens[m, k, :, cut] for m in range(plane, 2 * plane)], axis=0)

        @pl.when(step == 0)
        def _():
            for i in range(tiles):
                for c in copies(i):
                    c.start()

                @pl.when(end_ref[0] == 1)
                def _():
                    near_copy(outer_in, i).start()

                @pl.when(end_ref[0] != 1)
                def _():
                    near_copy(crossed_in, i).start()

            sums = [jnp.zeros((2 * block, rank), F32)] * 2 + [jnp.zeros((block, rank), F32)] * 2
            for i in range(tiles):
                for c in copies(i):
                    c.wait()
                near_copy(outer_in, i).wait()
                cut = pl.ds(i * tile, tile)
                for k in range(2):
                    sums[k] += dot32(rows3(k, cut), far_w[k, :, cut], ROWS_OF)
                    sums[2 + k] += dot32(rows2(k, cut), near_w[k, :, cut], ROWS_OF)
            hidden3[...] = sums[0].astype(BF16)
            inner3_ref[...] = sums[1].astype(BF16)
            hidden2[...] = sums[2].astype(BF16)
            inner2_ref[...] = sums[3].astype(BF16)

        cut = pl.ds(pl.multiple_of(step * tile, tile), tile)
        sum3_ref[0] = dot32(hidden3[...], rows3(1, cut), OUTER).astype(BF16)
        sum3_ref[1] = dot32(inner3_ref[...], rows3(0, cut), OUTER).astype(BF16)
        sum2_ref[0] = dot32(hidden2[...], rows2(1, cut), OUTER).astype(BF16)
        sum2_ref[1] = dot32(inner2_ref[...], rows2(0, cut), OUTER).astype(BF16)
        dx_ref[...] = dot32(inner3_ref[block:], far_w[0, :, cut]).astype(BF16)

    pair = jax.ShapeDtypeStruct((2, rank, width), BF16)
    pair_spec = pl.BlockSpec((2, rank, tile), lambda i: (0, 0, i))
    return pl.pallas_call(
        body,
        grid=(tiles,),
        in_specs=[pl.BlockSpec(memory_space=pltpu.SMEM)] + [ANY] * (2 * plane + 4),
        out_specs=[
            pair_spec,
            pair_spec,
            pl.BlockSpec((block, tile), lambda i: (0, i)),
            pl.BlockSpec((2 * block, rank), lambda i: (0, 0)),
            pl.BlockSpec((block, rank), lambda i: (0, 0)),
        ],
        out_shape=[
            pair,
            pair,
            jax.ShapeDtypeStruct((block, width), BF16),
            jax.ShapeDtypeStruct((2 * block, rank), BF16),
            jax.ShapeDtypeStruct((block, rank), BF16),
        ],
        scratch_shapes=[
            pltpu.VMEM((2 * plane, 2, capacity, width), BF16),
            pltpu.VMEM((2, block, width), BF16),
            pltpu.VMEM((2, rank, width), BF16),
            pltpu.VMEM((2, rank, width), BF16),
            pltpu.VMEM((2 * block, rank), BF16),
            pltpu.VMEM((block, rank), BF16),
            pltpu.SemaphoreType.DMA((tiles, 2 * plane + 3)),
        ],
        compiler_params=kernel_params(),
        cost_estimate=cost(26 * block * rank * width, 38 * block * width),
    )(is_end, *stage3, *stage2, ends, far, outer, crossed)


def near_groups(stage, pair, down, up, capacity):
    plane = len(stage)
    _, rank, width = pair.shape
    block = plane * capacity
    tile = min(width, 1024)
    tiles = width // tile

    def body(*refs):
        stage_in, refs = refs[:plane], refs[plane:]
        pair_in, down_in, up_in = refs[:3]
        dx_refs, (sum1_ref, sum0_ref) = refs[3:3 + plane], refs[3 + plane:5 + plane]
        tokens, pair_w, own_w, hidden1, inner1, hidden0, inner0, sems = refs[5 + plane:]
        step = pl.program_id(0)

        def copies(i):
            cut = pl.ds(i * tile, tile)
            pairs = [(stage_in[m].at[:, :, cut], tokens.at[m, :, :, cut]) for m in range(plane)] + [
                (pair_in.at[:, :, cut], pair_w.at[:, :, cut]),
                (down_in.at[:, cut], own_w.at[0, :, cut]),
                (up_in.at[:, cut], own_w.at[1, :, cut]),
            ]
            return [pltpu.make_async_copy(src, dst, sems.at[i, n]) for n, (src, dst) in enumerate(pairs)]

        def rows1(k, cut):
            return jnp.concatenate([tokens[m, k, :capacity, cut] for m in range(plane)], axis=0)

        def rows0(k, cut):
            return jnp.concatenate([tokens[m, k, capacity:, cut] for m in range(plane)], axis=0)

        @pl.when(step == 0)
        def _():
            for i in range(tiles):
                for c in copies(i):
                    c.start()
            sums = [jnp.zeros((block, rank), F32)] * 4
            for i in range(tiles):
                for c in copies(i):
                    c.wait()
                cut = pl.ds(i * tile, tile)
                for k in range(2):
                    sums[k] += dot32(rows1(k, cut), pair_w[k, :, cut], ROWS_OF)
                    sums[2 + k] += dot32(rows0(k, cut), own_w[k, :, cut], ROWS_OF)
            for ref, value in zip((hidden1, inner1, hidden0, inner0), sums):
                ref[...] = value.astype(BF16)

        cut = pl.ds(pl.multiple_of(step * tile, tile), tile)
        sum1_ref[0] = dot32(hidden1[...], rows1(1, cut), OUTER)
        sum1_ref[1] = dot32(inner1[...], rows1(0, cut), OUTER)
        sum0_ref[0] = dot32(hidden0[...], rows0(1, cut), OUTER)
        sum0_ref[1] = dot32(inner0[...], rows0(0, cut), OUTER)
        for n, (inner, w) in enumerate(((inner1, pair_w), (inner0, own_w))):
            dx = dot32(inner[...], w[0, :, cut]).astype(BF16)
            for m in range(plane):
                dx_refs[m][n * capacity:(n + 1) * capacity] = dx[m * capacity:(m + 1) * capacity]

    total = jax.ShapeDtypeStruct((2, rank, width), F32)
    total_spec = pl.BlockSpec((2, rank, tile), lambda i: (0, 0, i))
    return pl.pallas_call(
        body,
        grid=(tiles,),
        in_specs=[ANY] * (plane + 3),
        out_specs=[pl.BlockSpec((2 * capacity, tile), lambda i: (0, i))] * plane + [total_spec] * 2,
        out_shape=[jax.ShapeDtypeStruct((2 * capacity, width), BF16)] * plane + [total] * 2,
        scratch_shapes=[
            pltpu.VMEM((plane, 2, 2 * capacity, width), BF16),
            pltpu.VMEM((2, rank, width), BF16),
            pltpu.VMEM((2, rank, width), BF16),
        ]
        + [pltpu.VMEM((block, rank), BF16)] * 4
        + [pltpu.SemaphoreType.DMA((tiles, plane + 3))],
        compiler_params=kernel_params(),
        cost_estimate=cost(20 * block * rank * width, 36 * block * width),
    )(*stage, pair, down, up)


def far_inputs(is_end, dx_ends, far, outer, crossed, inner3, inner2, capacity):
    block = inner2.shape[0]
    plane = block // capacity
    _, rank, width = far.shape
    tile = min(width, 1024)

    def body(end_ref, ends_ref, far_ref, outer_ref, crossed_ref, inner3_ref, inner2_ref, *dx_refs):
        end = end_ref[0] == 1
        near = jnp.where(end, outer_ref[0], crossed_ref[0])
        dx3 = dot32(inner3_ref[:block], far_ref[0]).astype(BF16)
        dx3 = jnp.where(end, ends_ref[...], dx3)
        dx2 = dot32(inner2_ref[...], near).astype(BF16)
        for m in range(plane):
            dx_refs[m][:capacity] = dx3[m * capacity:(m + 1) * capacity]
            dx_refs[m][capacity:] = dx2[m * capacity:(m + 1) * capacity]

    down_spec = pl.BlockSpec((1, rank, tile), lambda i: (0, 0, i))
    return pl.pallas_call(
        body,
        grid=(width // tile,),
        in_specs=[pl.BlockSpec(memory_space=pltpu.SMEM), pl.BlockSpec((block, tile), lambda i: (0, i))]
        + [down_spec] * 3
        + [pl.BlockSpec(a.shape, lambda i: (0, 0)) for a in (inner3, inner2)],
        out_specs=[pl.BlockSpec((2 * capacity, tile), lambda i: (0, i))] * plane,
        out_shape=[jax.ShapeDtypeStruct((2 * capacity, width), BF16)] * plane,
        compiler_params=kernel_params(),
        cost_estimate=cost(4 * block * rank * width, 12 * block * width),
    )(is_end, dx_ends, far, outer, crossed, inner3, inner2)


def move_adapters(plane, acts, cotan, token_task_index, task_slot_lookup, pool_down_factors, pool_up_factors):
    ndevices = lax.axis_size("dp")
    tokens, width = acts.shape
    capacity = 2 * ((tokens + ndevices - 1) // ndevices)
    me = lax.axis_index("dp")
    z, column = me // plane, me % plane
    is_end = (z == 0) | (z == 3)
    end_flag = is_end.astype(jnp.int32).reshape(1)

    def planes(pairs):
        return [(a * plane + c, b * plane + c) for a, b in pairs for c in range(plane)]

    swap = planes([(0, 1), (1, 0), (2, 3), (3, 2)])
    cross = planes([(1, 2), (2, 1)])
    outward = planes([(1, 0), (2, 3)])
    inward = planes([(0, 1), (3, 2)])

    def send(array, pairs):
        return lax.ppermute(array, "dp", pairs)

    def in_plane(blocks):
        moved = [blocks[0]]
        for m in range(1, plane):
            moved.append(send(blocks[m], [(i, (i // plane) * plane + ((i % plane) ^ m)) for i in range(ndevices)]))
        return moved

    down, up = pool_down_factors[0], pool_up_factors[0]
    own = jnp.concatenate([pool_down_factors, pool_up_factors])
    pair = send(own, swap)
    crossed = send(own, cross)

    owner, position = route(token_task_index, task_slot_lookup, ndevices)
    owner_z, turn = owner // plane, (owner % plane) ^ column
    other_mid = jnp.where(z < 2, 2, 1)
    kind = jnp.where(owner_z == z, 0, jnp.where(owner_z == (z ^ 1), 1, jnp.where(owner_z == other_mid, 2, 3)))

    def places(wanted, row, rows):
        hot = jnp.arange(rows, dtype=jnp.int32)[:, None] == row[None, :]
        return (hot & wanted[None, :]).astype(BF16)

    def after(arrays, *others):
        return lax.optimization_barrier((arrays, others))[0]

    half, block = 2 * capacity, plane * capacity
    place3 = places(kind == 3, turn * capacity + position, block)
    place2 = places(kind == 2, turn * capacity + position, block)
    place10 = places(kind < 2, turn * half + (1 - kind) * capacity + position, 2 * block)
    place_back = places(
        kind >= 0,
        jnp.where(kind >= 2, turn * half + (3 - kind) * capacity, 2 * block + turn * half + (1 - kind) * capacity)
        + position,
        4 * block,
    )

    (packed3,) = pack(place3, acts, cotan, plane, (capacity,))
    packed2, packed10 = pack(
        jnp.concatenate([place2, place10]), after(acts, packed3), cotan, plane, (capacity, half)
    )
    stage3 = in_plane(packed3)
    ends = send(after(jnp.concatenate(stage3, axis=1), packed2, packed10), inward)
    stage2 = in_plane(after(packed2, stage3))
    outer = send(crossed, outward)
    far = send(pair, cross)
    stage10 = in_plane(after(packed10, stage2))

    ends = after(ends, stage10[1])
    sum3, sum2, dx_ends, inner3, inner2 = far_groups(
        end_flag, stage3, stage2, ends, far, outer, crossed, capacity
    )
    sum3 = send(sum3, cross)
    sum2_in = send(sum2, inward)
    dx_ends = send(dx_ends, outward)

    *dx10, sum1, sum0 = near_groups(stage10, pair, down, up, capacity)
    back10 = in_plane(dx10)
    sum2 = send((sum2.astype(F32) + sum2_in.astype(F32)).astype(BF16), cross)
    sum1 = send((sum1 + sum3.astype(F32)).astype(BF16), swap)

    back32 = in_plane(far_inputs(end_flag, dx_ends, far, outer, crossed, inner3, inner2, capacity))
    grad_acts = unpack(place_back, back32 + back10, tokens)
    raw_up, raw_down = (sum0[k] + sum2[k].astype(F32) + sum1[k].astype(F32) for k in range(2))
    return (grad_acts,) + clipped(raw_down, raw_up, ndevices)


def solution(mesh):
    ndevices = mesh.shape["dp"]
    plane = 1
    while (2 * plane) ** 2 <= ndevices:
        plane *= 2

    def per_device(*arrays):
        if ndevices == 4 * plane:
            return move_adapters(plane, *arrays)
        return move_tokens(*arrays)

    rows, pools = P(("parts", "dp"), None), P(("parts", "dp"), None, None)
    return jax.shard_map(
        per_device,
        mesh=mesh,
        in_specs=(rows, rows, rows, P("parts"), pools, pools),
        out_specs=(rows, pools, pools),
        check_vma=False,
    )
```

```python
import functools

import jax
import jax.numpy as jnp
from jax import lax
from jax.experimental import pallas as pl
from jax.experimental.pallas import tpu as pltpu
from jax.sharding import PartitionSpec as P

BF16, F32 = jnp.bfloat16, jnp.float32
ROWS_OF = (((1,), (1,)), ((), ()))
OUTER = (((0,), (0,)), ((), ()))
INNER = (((1,), (0,)), ((), ()))
ANY = pl.BlockSpec(memory_space=pl.ANY)
VMEM_BYTES = 28 * 2**20
NO_COST = pl.CostEstimate(flops=1, bytes_accessed=1, transcendentals=0)


def dot32(a, b, dims=INNER):
    return lax.dot_general(a, b, dims, preferred_element_type=F32)


def route(token_task_index, task_slot_lookup, ndevices):
    pool = task_slot_lookup.shape[0]
    task_hot = (token_task_index == jnp.arange(pool, dtype=jnp.int32)[None, :]).astype(jnp.int32)
    owner = jnp.sum(task_hot * task_slot_lookup[None, :], axis=1)
    owner_hot = (owner[:, None] == jnp.arange(ndevices, dtype=jnp.int32)[None, :]).astype(jnp.int32)
    before = jnp.cumsum(owner_hot, axis=0) - owner_hot
    position = jnp.sum(before * owner_hot, axis=1)
    return owner, position


def clipped(raw_down, raw_up, ndevices):
    local_sq = jnp.sum(raw_down * raw_down) + jnp.sum(raw_up * raw_up)
    shares = jnp.broadcast_to(local_sq, (ndevices, 8, 128))
    total = jnp.sum(lax.all_to_all(shares, "dp", split_axis=0, concat_axis=0, tiled=True)[:, 0, 0])
    norm = jnp.sqrt(total + 1e-06)
    limit = jnp.sqrt(jnp.float32(2 * raw_down.shape[0] * raw_down.shape[1] * ndevices))
    factor = jnp.minimum(jnp.float32(1.0), limit / norm)
    return (raw_down * factor)[None], (raw_up * factor)[None]


def move_tokens(acts, cotan, token_task_index, task_slot_lookup, pool_down_factors, pool_up_factors):
    ndevices = lax.axis_size("dp")
    tokens, width = acts.shape
    capacity = 2 * ((tokens + ndevices - 1) // ndevices)
    slots = ndevices * capacity
    owner, position = route(token_task_index, task_slot_lookup, ndevices)
    dest = owner * capacity + position
    placed = (jnp.arange(slots, dtype=jnp.int32)[:, None] == dest[None, :]).astype(BF16)

    def exchange(rows):
        rows = rows.reshape(ndevices, capacity, width)
        return lax.all_to_all(rows, "dp", split_axis=0, concat_axis=0, tiled=True).reshape(slots, width)

    down, up = pool_down_factors[0], pool_up_factors[0]
    rows_x = exchange(dot32(placed, acts).astype(BF16))
    rows_g = exchange(dot32(placed, cotan).astype(BF16))
    hidden = dot32(rows_x, down, ROWS_OF).astype(BF16)
    inner = dot32(rows_g, up, ROWS_OF).astype(BF16)
    returned = exchange(dot32(inner, down).astype(BF16))
    grad_acts = dot32(placed, returned, OUTER).astype(BF16)
    raw_up = dot32(hidden, rows_g, OUTER)
    raw_down = dot32(inner, rows_x, OUTER)
    return (grad_acts,) + clipped(raw_down, raw_up, ndevices)


def kernel_params(semantics=("arbitrary",)):
    return pltpu.CompilerParams(dimension_semantics=semantics, vmem_limit_bytes=VMEM_BYTES)


def pack(place, acts, cotan, plane, parts):
    tokens, width = acts.shape
    tile = min(width, 1024)
    cuts, start = [], 0
    for rows in parts:
        for _ in range(plane):
            cuts.append((start, rows))
            start += rows

    def body(place_ref, x_ref, g_ref, *out_refs):
        for k, ref in enumerate((x_ref, g_ref)):
            moved = dot32(place_ref[...], ref[...]).astype(BF16)
            for out_ref, (first, rows) in zip(out_refs, cuts):
                out_ref[k] = moved[first:first + rows]

    rows_spec = pl.BlockSpec((tokens, tile), lambda i: (0, i))
    packed = pl.pallas_call(
        body,
        grid=(width // tile,),
        in_specs=[pl.BlockSpec(place.shape, lambda i: (0, 0)), rows_spec, rows_spec],
        out_specs=[pl.BlockSpec((2, rows, tile), lambda i: (0, 0, i)) for _, rows in cuts],
        out_shape=[jax.ShapeDtypeStruct((2, rows, width), BF16) for _, rows in cuts],
        compiler_params=kernel_params(),
        cost_estimate=NO_COST,
    )(place, acts, cotan)
    return [packed[n * plane:(n + 1) * plane] for n in range(len(parts))]


def unpack(place, blocks, tokens):
    width = blocks[0].shape[1]
    tile = min(width, 1024)

    def body(place_ref, *refs):
        rows = jnp.concatenate([ref[...].reshape(-1, tile) for ref in refs[:-1]], axis=0)
        refs[-1][...] = dot32(place_ref[...], rows, OUTER).astype(BF16)

    return pl.pallas_call(
        body,
        grid=(width // tile,),
        in_specs=[pl.BlockSpec(place.shape, lambda i: (0, 0))]
        + [
            pl.BlockSpec((b.shape[0], tile), lambda i: (0, i))
            if b.ndim == 2
            else pl.BlockSpec((1, b.shape[1], tile), lambda i: (0, 0, i))
            for b in blocks
        ],
        out_specs=pl.BlockSpec((tokens, tile), lambda i: (0, i)),
        out_shape=jax.ShapeDtypeStruct((tokens, width), BF16),
        compiler_params=kernel_params(),
        cost_estimate=NO_COST,
    )(place, *blocks)


def far_sums(k, is_end, stage3, stage2, ends, far, outer, crossed, capacity):
    plane = len(stage3)
    _, rank, width = far.shape
    block = plane * capacity
    tile = min(width, 2048)
    tiles = width // tile
    last = k + 1

    def body(end_ref, *refs):
        stage3_in, stage2_in, refs = refs[:plane], refs[plane:2 * plane], refs[2 * plane:]
        ends_in, far_in, outer_in, crossed_in, sum3_ref, sum2_ref = refs[:6]
        outs, (rows3, rows2, far_w, near_w, left3, left2, sems) = refs[6:-7], refs[-7:]
        step = pl.program_id(0)

        def copies(i):
            cut = pl.ds(i * tile, tile)
            pairs = [(ends_in.at[:, :, cut], rows3.at[:, block:, cut]), (far_in.at[:last, :, cut], far_w.at[:, :, cut])]
            for m in range(plane):
                place = pl.ds(m * capacity, capacity)
                pairs.append((stage3_in[m].at[:, :, cut], rows3.at[:, place, cut]))
                pairs.append((stage2_in[m].at[:, :capacity, cut], rows2.at[:, place, cut]))
            return [pltpu.make_async_copy(src, dst, sems.at[i, n]) for n, (src, dst) in enumerate(pairs)]

        def near_copy(src, i):
            cut = pl.ds(i * tile, tile)
            return pltpu.make_async_copy(src.at[k, :, cut], near_w.at[:, cut], sems.at[i, 2 * plane + 2])

        @pl.when(step == 0)
        def _():
            for i in range(tiles):
                for c in copies(i):
                    c.start()

                @pl.when(end_ref[0] == 1)
                def _():
                    near_copy(outer_in, i).start()

                @pl.when(end_ref[0] != 1)
                def _():
                    near_copy(crossed_in, i).start()

            sum3, sum2 = jnp.zeros((2 * block, rank), F32), jnp.zeros((block, rank), F32)
            for i in range(tiles):
                for c in copies(i):
                    c.wait()
                near_copy(outer_in, i).wait()
                cut = pl.ds(i * tile, tile)
                sum3 += dot32(rows3[k, :, cut], far_w[k, :, cut], ROWS_OF)
                sum2 += dot32(rows2[k, :, cut], near_w[:, cut], ROWS_OF)
            left3[...] = sum3.astype(BF16)
            left2[...] = sum2.astype(BF16)
            if k == 1:
                outs[1][...] = left3[...]
                outs[2][...] = left2[...]

        cut = pl.ds(pl.multiple_of(step * tile, tile), tile)
        sum3_ref[...] = dot32(left3[...], rows3[1 - k, :, cut], OUTER).astype(BF16)
        sum2_ref[...] = dot32(left2[...], rows2[1 - k, :, cut], OUTER).astype(BF16)
        if k == 1:
            outs[0][...] = dot32(left3[block:], far_w[0, :, cut]).astype(BF16)

    def small(rows):
        return pl.BlockSpec((rows, rank), lambda i: (0, 0)), jax.ShapeDtypeStruct((rows, rank), BF16)

    def wide(rows):
        return pl.BlockSpec((rows, tile), lambda i: (0, i)), jax.ShapeDtypeStruct((rows, width), BF16)

    outs = [wide(rank), wide(rank)] + ([wide(block), small(2 * block), small(block)] if k == 1 else [])
    return pl.pallas_call(
        body,
        grid=(tiles,),
        in_specs=[pl.BlockSpec(memory_space=pltpu.SMEM)] + [ANY] * (2 * plane + 4),
        out_specs=[o[0] for o in outs],
        out_shape=[o[1] for o in outs],
        scratch_shapes=[
            pltpu.VMEM((2, 2 * block, width), BF16),
            pltpu.VMEM((2, block, width), BF16),
            pltpu.VMEM((last, rank, width), BF16),
            pltpu.VMEM((rank, width), BF16),
            pltpu.VMEM((2 * block, rank), BF16),
            pltpu.VMEM((block, rank), BF16),
            pltpu.SemaphoreType.DMA((tiles, 2 * plane + 3)),
        ],
        compiler_params=kernel_params(),
        cost_estimate=NO_COST,
    )(is_end, *stage3, *stage2, ends, far, outer, crossed)


def near_groups(is_end, stage, pair, down, up, dx_ends, far, outer, crossed, inner3, inner2, capacity):
    plane = len(stage)
    _, rank, width = pair.shape
    block = plane * capacity
    tile = min(width, 2048)
    tiles = width // tile

    def body(end_ref, *refs):
        stage_in, refs = refs[:plane], refs[plane:]
        pair_in, down_in, up_in, ends_in, far_in, outer_in, crossed_in, inner3, inner2 = refs[:9]
        dx_refs, sum_refs = [refs[9], refs[10], refs[11].at[0], refs[11].at[1]], refs[12:16]
        rows1, rows0, pair_w, own_w, far_w, near_w, ends, hidden1, inner1, hidden0, inner0, sems = refs[16:]
        step = pl.program_id(0)

        def copies(i):
            cut = pl.ds(i * tile, tile)
            pairs = [
                (pair_in.at[:, :, cut], pair_w.at[:, :, cut]),
                (down_in.at[:, cut], own_w.at[0, :, cut]),
                (up_in.at[:, cut], own_w.at[1, :, cut]),
                (far_in.at[0, :, cut], far_w.at[:, cut]),
                (ends_in.at[:, cut], ends.at[:, cut]),
            ]
            for m in range(plane):
                place = pl.ds(m * capacity, capacity)
                pairs.append((stage_in[m].at[:, capacity:2 * capacity, cut], rows1.at[:, place, cut]))
                pairs.append((stage_in[m].at[:, 2 * capacity:, cut], rows0.at[:, place, cut]))
            return [pltpu.make_async_copy(src, dst, sems.at[i, n]) for n, (src, dst) in enumerate(pairs)]

        def near_copy(src, i):
            cut = pl.ds(i * tile, tile)
            return pltpu.make_async_copy(src.at[0, :, cut], near_w.at[:, cut], sems.at[i, 2 * plane + 5])

        @pl.when(step == 0)
        def _():
            for i in range(tiles):
                for c in copies(i):
                    c.start()

                @pl.when(end_ref[0] == 1)
                def _():
                    near_copy(outer_in, i).start()

                @pl.when(end_ref[0] != 1)
                def _():
                    near_copy(crossed_in, i).start()

            sums = [jnp.zeros((block, rank), F32)] * 4
            for i in range(tiles):
                for c in copies(i):
                    c.wait()
                near_copy(outer_in, i).wait()
                cut = pl.ds(i * tile, tile)
                for k in range(2):
                    sums[k] += dot32(rows1[k, :, cut], pair_w[k, :, cut], ROWS_OF)
                    sums[2 + k] += dot32(rows0[k, :, cut], own_w[k, :, cut], ROWS_OF)
            for ref, value in zip((hidden1, inner1, hidden0, inner0), sums):
                ref[...] = value.astype(BF16)

        cut = pl.ds(pl.multiple_of(step * tile, tile), tile)
        sum_refs[0][...] = dot32(hidden1[...], rows1[1, :, cut], OUTER)
        sum_refs[1][...] = dot32(inner1[...], rows1[0, :, cut], OUTER)
        sum_refs[2][...] = dot32(hidden0[...], rows0[1, :, cut], OUTER)
        sum_refs[3][...] = dot32(inner0[...], rows0[0, :, cut], OUTER)
        moved = [
            jnp.where(end_ref[0] == 1, ends[:, cut], dot32(inner3[:block], far_w[:, cut]).astype(BF16)),
            dot32(inner2[...], near_w[:, cut]).astype(BF16),
            dot32(inner1[...], pair_w[0, :, cut]).astype(BF16),
            dot32(inner0[...], own_w[0, :, cut]).astype(BF16),
        ]
        for n, dx in enumerate(moved):
            for m in range(plane):
                dx_refs[m][n * capacity:(n + 1) * capacity] = dx[m * capacity:(m + 1) * capacity]

    return pl.pallas_call(
        body,
        grid=(tiles,),
        in_specs=[pl.BlockSpec(memory_space=pltpu.SMEM)]
        + [ANY] * (plane + 7)
        + [pl.BlockSpec(a.shape, lambda i: (0, 0)) for a in (inner3, inner2)],
        out_specs=[pl.BlockSpec((4 * capacity, tile), lambda i: (0, i))] * 2
        + [pl.BlockSpec((2, 4 * capacity, tile), lambda i: (0, 0, i))]
        + [pl.BlockSpec((rank, tile), lambda i: (0, i))] * 4,
        out_shape=[jax.ShapeDtypeStruct((4 * capacity, width), BF16)] * 2
        + [jax.ShapeDtypeStruct((2, 4 * capacity, width), BF16)]
        + [jax.ShapeDtypeStruct((rank, width), F32)] * 4,
        scratch_shapes=[
            pltpu.VMEM((2, block, width), BF16),
            pltpu.VMEM((2, block, width), BF16),
            pltpu.VMEM((2, rank, width), BF16),
            pltpu.VMEM((2, rank, width), BF16),
            pltpu.VMEM((rank, width), BF16),
            pltpu.VMEM((rank, width), BF16),
            pltpu.VMEM((block, width), BF16),
        ]
        + [pltpu.VMEM((block, rank), BF16)] * 4
        + [pltpu.SemaphoreType.DMA((tiles, 2 * plane + 6))],
        compiler_params=kernel_params(),
        cost_estimate=NO_COST,
    )(is_end, *stage, pair, down, up, dx_ends, far, outer, crossed, inner3, inner2)


def move_adapters(plane, acts, cotan, token_task_index, task_slot_lookup, pool_down_factors, pool_up_factors):
    ndevices = lax.axis_size("dp")
    tokens, width = acts.shape
    capacity = 2 * ((tokens + ndevices - 1) // ndevices)
    me = lax.axis_index("dp")
    z, column = me // plane, me % plane
    is_end = (z == 0) | (z == 3)
    end_flag = is_end.astype(jnp.int32).reshape(1)

    def planes(pairs):
        return [(a * plane + c, b * plane + c) for a, b in pairs for c in range(plane)]

    swap = planes([(0, 1), (1, 0), (2, 3), (3, 2)])
    cross = planes([(1, 2), (2, 1)])
    outward = planes([(1, 0), (2, 3)])
    inward = planes([(0, 1), (3, 2)])

    def send(array, pairs):
        return lax.ppermute(array, "dp", pairs)

    def after(arrays, *others):
        return lax.optimization_barrier((arrays, others))[0]

    def beside(m):
        return [(i, (i // plane) * plane + ((i % plane) ^ m)) for i in range(ndevices)]

    def in_plane(blocks):
        return [blocks[0]] + [send(blocks[m], beside(m)) for m in range(1, plane)]

    down, up = pool_down_factors[0], pool_up_factors[0]
    own = jnp.concatenate([pool_down_factors, pool_up_factors])
    pair = send(own, swap)
    crossed = send(own, cross)

    owner, position = route(token_task_index, task_slot_lookup, ndevices)
    owner_z, turn = owner // plane, (owner % plane) ^ column
    other_mid = jnp.where(z < 2, 2, 1)
    kind = jnp.where(owner_z == z, 0, jnp.where(owner_z == (z ^ 1), 1, jnp.where(owner_z == other_mid, 2, 3)))

    def places(wanted, row, rows):
        hot = jnp.arange(rows, dtype=jnp.int32)[:, None] == row[None, :]
        return (hot & wanted[None, :]).astype(BF16)

    def after(arrays, *others):
        return lax.optimization_barrier((arrays, others))[0]

    block = plane * capacity
    place3 = places(kind == 3, turn * capacity + position, block)
    place_rest = places(kind < 3, (turn * 3 + 2 - kind) * capacity + position, 3 * block)
    place_back = places(kind >= 0, (turn * 4 + 3 - kind) * capacity + position, 4 * block)

    packed3, packed = pack(jnp.concatenate([place3, place_rest]), acts, cotan, plane, (capacity, 3 * capacity))
    stage3 = in_plane(packed3)
    ends = send(jnp.concatenate(stage3, axis=1), inward)
    stage = in_plane(after(packed, stage3))
    outer = send(crossed, outward)
    far = send(pair, cross)

    far_args = (end_flag, stage3, after(stage, ends), ends, far, outer, crossed, capacity)
    up3, up2 = far_sums(0, *far_args)
    up3, up2_in = send(up3, cross), send(up2, inward)
    down3, down2, dx_ends, inner3, inner2 = far_sums(1, after(end_flag, up2), *far_args[1:])
    down3, down2_in = send(down3, cross), send(down2, inward)
    dx_ends = send(dx_ends, outward)

    dx_own, dx_beside, dx_across, up1, down1, up0, down0 = near_groups(
        end_flag, stage, pair, down, up, dx_ends, far, outer, crossed, inner3, inner2, capacity
    )

    def add(a, b):
        return (a.astype(F32) + b.astype(F32)).astype(BF16)

    up2, up1 = send(add(up2, up2_in), cross), send(add(up1, up3), swap)
    down2, down1 = send(add(down2, down2_in), cross), send(add(down1, down3), swap)

    dx_across = send(dx_across, beside(2))
    back = [dx_own, send(dx_beside, beside(1)), dx_across, send(dx_across[1], beside(1))]
    grad_acts = unpack(place_back, back, tokens)
    raw_up = up0 + up2.astype(F32) + up1.astype(F32)
    raw_down = down0 + down2.astype(F32) + down1.astype(F32)
    return (grad_acts,) + clipped(raw_down, raw_up, ndevices)


def solution(mesh):
    plane = 4
    by_planes = mesh.shape["dp"] == 4 * plane

    def per_device(*arrays):
        if by_planes:
            return move_adapters(plane, *arrays)
        return move_tokens(*arrays)

    rows, pools = P(("parts", "dp"), None), P(("parts", "dp"), None, None)
    return jax.shard_map(
        per_device,
        mesh=mesh,
        in_specs=(rows, rows, rows, P("parts"), pools, pools),
        out_specs=(rows, pools, pools),
        check_vma=False,
    )
```

```python
import jax
import jax.numpy as jnp
from jax import lax
from jax.experimental import pallas as pl
from jax.experimental.pallas import tpu as pltpu
from jax.sharding import PartitionSpec as P

BF16, F32 = jnp.bfloat16, jnp.float32
ROWS_OF = (((1,), (1,)), ((), ()))
OUTER = (((0,), (0,)), ((), ()))
INNER = (((1,), (0,)), ((), ()))
HBM = pl.BlockSpec(memory_space=pltpu.HBM)
WHOLE = pl.BlockSpec(memory_space=pltpu.VMEM)
VMEM_BYTES = 20 * 2**20


def dot32(a, b, dims=INNER):
    return lax.dot_general(a, b, dims, preferred_element_type=F32)


def route(token_task_index, task_slot_lookup, ndevices):
    pool = task_slot_lookup.shape[0]
    task_hot = (token_task_index == jnp.arange(pool, dtype=jnp.int32)[None, :]).astype(jnp.int32)
    owner = jnp.sum(task_hot * task_slot_lookup[None, :], axis=1)
    owner_hot = (owner[:, None] == jnp.arange(ndevices, dtype=jnp.int32)[None, :]).astype(jnp.int32)
    before = jnp.cumsum(owner_hot, axis=0) - owner_hot
    position = jnp.sum(before * owner_hot, axis=1)
    return owner, position


def clipped(raw_down, raw_up, ndevices, add_up):
    local_sq = jnp.sum(raw_down * raw_down) + jnp.sum(raw_up * raw_up)
    total = add_up(local_sq)
    norm = jnp.sqrt(total + 1e-06)
    limit = jnp.sqrt(jnp.float32(2 * raw_down.shape[0] * raw_down.shape[1] * ndevices))
    factor = jnp.minimum(jnp.float32(1.0), limit / norm)
    return (raw_down * factor)[None], (raw_up * factor)[None]


def move_tokens(acts, cotan, token_task_index, task_slot_lookup, pool_down_factors, pool_up_factors):
    ndevices = lax.axis_size("dp")
    tokens, width = acts.shape
    capacity = 2 * ((tokens + ndevices - 1) // ndevices)
    slots = ndevices * capacity
    owner, position = route(token_task_index, task_slot_lookup, ndevices)
    dest = owner * capacity + position
    placed = (jnp.arange(slots, dtype=jnp.int32)[:, None] == dest[None, :]).astype(BF16)

    def exchange(rows):
        rows = rows.reshape(ndevices, capacity, width)
        return lax.all_to_all(rows, "dp", split_axis=0, concat_axis=0, tiled=True).reshape(slots, width)

    down, up = pool_down_factors[0], pool_up_factors[0]
    rows_x = exchange(dot32(placed, acts).astype(BF16))
    rows_g = exchange(dot32(placed, cotan).astype(BF16))
    hidden = dot32(rows_x, down, ROWS_OF).astype(BF16)
    inner = dot32(rows_g, up, ROWS_OF).astype(BF16)
    returned = exchange(dot32(inner, down).astype(BF16))
    grad_acts = dot32(placed, returned, OUTER).astype(BF16)
    raw_up = dot32(hidden, rows_g, OUTER)
    raw_down = dot32(inner, rows_x, OUTER)
    return (grad_acts,) + clipped(raw_down, raw_up, ndevices, lambda term: lax.psum(term, "dp"))


def in_hbm(*arrays):
    return [pltpu.with_memory_space_constraint(a, pltpu.HBM) for a in arrays]


def in_vmem(*arrays):
    return [pltpu.with_memory_space_constraint(a, pltpu.VMEM) for a in arrays]


def kernel_params(semantics=("arbitrary",)):
    return pltpu.CompilerParams(dimension_semantics=semantics, vmem_limit_bytes=VMEM_BYTES)


def pack(place, acts, cotan, shapes):
    tokens, width = acts.shape
    tile = min(width, 1024)
    tiles = width // tile

    def body(place_ref, x_in, g_in, *refs):
        out_refs, (rows, sems) = refs[:-2], refs[-2:]
        step = pl.program_id(0)

        def copies(i):
            cut = pl.ds(pl.multiple_of(i * tile, tile), tile)
            return [pltpu.make_async_copy(r.at[:, cut], rows.at[k, :, cut], sems.at[k, i]) for k, r in enumerate((x_in, g_in))]

        @pl.when(step == 0)
        def _():
            for i in range(tiles):
                for c in copies(i):
                    c.start()

        for c in copies(step):
            c.wait()
        cut = pl.ds(pl.multiple_of(step * tile, tile), tile)
        for k in range(2):
            moved = dot32(place_ref[...], rows[k, :, cut]).astype(BF16)
            first = 0
            for out_ref, (columns, size) in zip(out_refs, shapes):
                for c in range(columns):
                    out_ref[c, k] = moved[first:first + size]
                    first += size

    return pl.pallas_call(
        body,
        grid=(tiles,),
        in_specs=[pl.BlockSpec(place.shape, lambda i: (0, 0)), HBM, HBM],
        out_specs=[pl.BlockSpec((c, 2, size, tile), lambda i: (0, 0, 0, i)) for c, size in shapes],
        out_shape=[jax.ShapeDtypeStruct((c, 2, size, width), BF16) for c, size in shapes],
        scratch_shapes=[pltpu.VMEM((2, tokens, width), BF16), pltpu.SemaphoreType.DMA((2, tiles))],
        compiler_params=kernel_params(),
    )(place, *in_hbm(acts, cotan))


def unpack(place, blocks, tokens):
    width = blocks[0].shape[1]
    tile = min(width, 2048)

    def body(place_ref, *refs):
        rows = jnp.concatenate([ref[...].reshape(-1, tile) for ref in refs[:-1]], axis=0)
        refs[-1][...] = dot32(place_ref[...], rows).astype(BF16)

    return pl.pallas_call(
        body,
        grid=(width // tile,),
        in_specs=[pl.BlockSpec(place.shape, lambda i: (0, 0))]
        + [
            pl.BlockSpec((b.shape[0], tile), lambda i: (0, i))
            if b.ndim == 2
            else pl.BlockSpec((1, b.shape[1], tile), lambda i: (0, 0, i))
            for b in blocks
        ],
        out_specs=pl.BlockSpec((tokens, tile), lambda i: (0, i)),
        out_shape=jax.ShapeDtypeStruct((tokens, width), BF16),
        compiler_params=kernel_params(),
    )(place, *blocks)


def far_groups(is_end, stage3, stage2, ends, far, outer, crossed, capacity, first2):
    plane = len(stage3)
    _, rank, width = far.shape
    block = plane * capacity
    tile = min(width, 2048)
    tiles = width // tile

    def body(end_ref, *refs):
        stage3_in, stage2_in, refs = refs[:plane], refs[plane:2 * plane], refs[2 * plane:]
        ends_in, far_in, outer_in, crossed_in = refs[:4]
        sum3_refs, sum2_refs, swap_ref, inner2_ref, dx_ref = refs[4:6], refs[6:8], *refs[8:11]
        left3, left2 = refs[11:]
        step = pl.program_id(0)

        def rows3(k, cut):
            return jnp.concatenate([r[0, k, :capacity, cut] for r in stage3_in] + [ends_in[k, :, cut]], axis=0)

        def rows2(k, cut):
            return jnp.concatenate([r[0, k, first:first + capacity, cut] for r, first in zip(stage2_in, first2)], axis=0)

        @pl.when(step == 0)
        def _():
            sums3, sums2 = [jnp.zeros((2 * block, rank), F32)] * 2, [jnp.zeros((block, rank), F32)] * 2
            for i in range(tiles):
                cut = pl.ds(i * tile, tile)
                for k in range(2):
                    near = jnp.where(end_ref[0] == 1, outer_in[k, :, cut], crossed_in[k, :, cut])
                    sums3[k] += dot32(rows3(k, cut), far_in[k, :, cut], ROWS_OF)
                    sums2[k] += dot32(rows2(k, cut), near, ROWS_OF)
            for k in range(2):
                left3[k] = sums3[k].astype(BF16)
                left2[k] = sums2[k].astype(BF16)
            inner2_ref[...] = left2[1]

        cut = pl.ds(pl.multiple_of(step * tile, tile), tile)
        for k in range(2):
            sum3_refs[k][...] = dot32(left3[k], rows3(1 - k, cut), OUTER).astype(BF16)
            sum2_refs[k][...] = dot32(left2[k], rows2(1 - k, cut), OUTER).astype(BF16)
        dx = dot32(left3[1], far_in[0, :, cut]).astype(BF16)
        dx_ref[...] = dx[:block]
        swap_ref[...] = jnp.where(end_ref[0] == 1, sum2_refs[1][...], dx[block:])

    def wide(rows):
        return pl.BlockSpec((rows, tile), lambda i: (0, i)), jax.ShapeDtypeStruct((rows, width), BF16)

    outs = [wide(rank)] * 4 + [wide(block)]
    outs += [(pl.BlockSpec((block, rank), lambda i: (0, 0)), jax.ShapeDtypeStruct((block, rank), BF16)), wide(block)]
    return pl.pallas_call(
        body,
        grid=(tiles,),
        in_specs=[pl.BlockSpec(memory_space=pltpu.SMEM)] + [WHOLE] * (2 * plane + 4),
        out_specs=[o[0] for o in outs],
        out_shape=[o[1] for o in outs],
        scratch_shapes=[pltpu.VMEM((2, 2 * block, rank), BF16), pltpu.VMEM((2, block, rank), BF16)],
        compiler_params=kernel_params(),
    )(is_end, *in_vmem(*stage3, *stage2, ends, far, outer, crossed))


def near_groups(is_end, stage, pair, down, up, outer, crossed, inner2, dx3, swapped, capacity, first1):
    plane = len(stage)
    _, rank, width = pair.shape
    block = plane * capacity
    tile = min(width, 2048)
    tiles = width // tile

    def body(end_ref, *refs):
        stage_in, refs = refs[:plane], refs[plane:]
        pair_in, down_in, up_in, outer_in, crossed_in, inner2, dx3, swapped = refs[:8]
        dx_refs, sum_refs = [refs[8], refs[9], refs[10].at[0], refs[10].at[1]], refs[11:15]
        hidden1, inner1, hidden0, inner0 = refs[15:]
        step = pl.program_id(0)
        own_in = (down_in, up_in)

        def rows(kind, k, cut):
            return jnp.concatenate(
                [r[0, k, pl.ds(first + (1 - kind) * capacity, capacity), cut] for r, first in zip(stage_in, first1)],
                axis=0,
            )

        @pl.when(step == 0)
        def _():
            sums = [jnp.zeros((block, rank), F32)] * 4
            for i in range(tiles):
                cut = pl.ds(i * tile, tile)
                for k in range(2):
                    sums[k] += dot32(rows(1, k, cut), pair_in[k, :, cut], ROWS_OF)
                    sums[2 + k] += dot32(rows(0, k, cut), own_in[k][:, cut], ROWS_OF)
            for ref, value in zip((hidden1, inner1, hidden0, inner0), sums):
                ref[...] = value.astype(BF16)

        cut = pl.ds(pl.multiple_of(step * tile, tile), tile)
        sum_refs[0][...] = dot32(hidden1[...], rows(1, 1, cut), OUTER)
        sum_refs[1][...] = dot32(inner1[...], rows(1, 0, cut), OUTER)
        sum_refs[2][...] = dot32(hidden0[...], rows(0, 1, cut), OUTER)
        sum_refs[3][...] = dot32(inner0[...], rows(0, 0, cut), OUTER)
        near = jnp.where(end_ref[0] == 1, outer_in[0, :, cut], crossed_in[0, :, cut])
        moved = [
            jnp.where(end_ref[0] == 1, swapped[...], dx3[...]),
            dot32(inner2[...], near).astype(BF16),
            dot32(inner1[...], pair_in[0, :, cut]).astype(BF16),
            dot32(inner0[...], down_in[:, cut]).astype(BF16),
        ]
        for n, dx in enumerate(moved):
            for m in range(plane):
                dx_refs[m][n * capacity:(n + 1) * capacity] = dx[m * capacity:(m + 1) * capacity]

    return pl.pallas_call(
        body,
        grid=(tiles,),
        in_specs=[pl.BlockSpec(memory_space=pltpu.SMEM)]
        + [WHOLE] * (plane + 5)
        + [pl.BlockSpec(inner2.shape, lambda i: (0, 0))]
        + [pl.BlockSpec((block, tile), lambda i: (0, i))] * 2,
        out_specs=[pl.BlockSpec((4 * capacity, tile), lambda i: (0, i))] * 2
        + [pl.BlockSpec((2, 4 * capacity, tile), lambda i: (0, 0, i))]
        + [pl.BlockSpec((rank, tile), lambda i: (0, i))] * 4,
        out_shape=[jax.ShapeDtypeStruct((4 * capacity, width), BF16)] * 2
        + [jax.ShapeDtypeStruct((2, 4 * capacity, width), BF16)]
        + [jax.ShapeDtypeStruct((rank, width), F32)] * 4,
        scratch_shapes=[pltpu.VMEM((block, rank), BF16)] * 4,
        compiler_params=kernel_params(),
    )(is_end, *in_vmem(*stage, pair, down, up, outer, crossed), inner2, dx3, swapped)


def move_adapters(plane, acts, cotan, token_task_index, task_slot_lookup, pool_down_factors, pool_up_factors):
    ndevices = lax.axis_size("dp")
    tokens, width = acts.shape
    capacity = 2 * ((tokens + ndevices - 1) // ndevices)
    me = lax.axis_index("dp")
    z, column = me // plane, me % plane
    is_end = (z == 0) | (z == 3)
    end_flag = is_end.astype(jnp.int32).reshape(1)

    def planes(pairs):
        return [(a * plane + c, b * plane + c) for a, b in pairs for c in range(plane)]

    swap = planes([(0, 1), (1, 0), (2, 3), (3, 2)])
    cross = planes([(1, 2), (2, 1)])
    outward = planes([(1, 0), (2, 3)])
    inward = planes([(0, 1), (3, 2)])

    def send(array, pairs):
        return lax.ppermute(array, "dp", pairs)

    def after(arrays, *others):
        return lax.optimization_barrier((arrays, others))[0]

    def beside(m):
        return [(i, (i // plane) * plane + ((i % plane) ^ m)) for i in range(ndevices)]

    def add_up(term):
        around = [beside(m) for m in range(1, plane)]
        along = [[(i, (i // plane ^ m) * plane + i % plane) for i in range(ndevices)] for m in range(1, 4)]
        term = jnp.broadcast_to(term, (8, 128))
        term = term + sum(send(term, pairs) for pairs in around)
        term = after(term, dx_across)
        return (term + sum(after([send(term, pairs) for pairs in along], grad_acts)))[0, 0]

    down, up = pool_down_factors[0], pool_up_factors[0]
    own = jnp.concatenate([pool_down_factors, pool_up_factors])
    pair = send(own, swap)
    crossed = send(own, cross)

    owner, position = route(token_task_index, task_slot_lookup, ndevices)
    owner_z, turn = owner // plane, (owner % plane) ^ column
    other_mid = jnp.where(z < 2, 2, 1)
    kind = jnp.where(owner_z == z, 0, jnp.where(owner_z == (z ^ 1), 1, jnp.where(owner_z == other_mid, 2, 3)))

    def places(wanted, row, rows):
        hot = jnp.arange(rows, dtype=jnp.int32)[:, None] == row[None, :]
        return (hot & wanted[None, :]).astype(BF16)

    def after(arrays, *others):
        return lax.optimization_barrier((arrays, others))[0]

    block = plane * capacity
    mine = (3 - kind) * capacity + position
    row = jnp.where(kind == 2, 10 * capacity, 12 * capacity) + (turn - 2) * jnp.where(kind == 2, capacity, 2 * capacity)
    row += jnp.where(kind == 2, 0, (1 - kind) * capacity) + position
    row = jnp.where(kind == 3, (6 + turn) * capacity + position, row)
    row = jnp.where(turn < 2, turn * block + mine, row)
    place = places(kind >= 0, row, 4 * block)
    place_back = places(kind >= 0, turn * block + mine, 4 * block)
    own_rows, beside_rows, across3, across2, across10 = pack(
        place, acts, cotan, [(1, 4 * capacity)] * 2 + [(2, capacity)] * 2 + [(2, 2 * capacity)]
    )

    def over_x(blocks):
        moved = send(blocks, beside(2))
        return moved, send(moved[1:], beside(1))

    beside_rows = send(beside_rows, beside(1))
    across3 = over_x(across3)
    stage3 = (own_rows, beside_rows) + across3
    ends = jnp.concatenate([r[0, :, :capacity] for r in stage3], axis=1)
    ends = send(ends, inward)
    across2 = over_x(after(across2, across3[0]))
    across10 = over_x(after(across10, across2[0]))
    stage2 = (own_rows, beside_rows) + across2
    stage10 = (own_rows, beside_rows) + across10
    outer = send(crossed, outward)
    far = send(pair, cross)

    up3, down3, up2, down2, swapped, inner2, dx3 = far_groups(
        end_flag, stage3, stage2, ends, far, outer, crossed, capacity, (capacity, capacity, 0, 0)
    )
    down3, swapped = send(down3, cross), send(swapped, swap)
    up3, up2_in = send(up3, cross), send(up2, inward)

    swapped, down3 = lax.optimization_barrier((swapped, down3))
    dx_own, dx_beside, dx_across, up1, down1, up0, down0 = near_groups(
        end_flag, stage10, pair, down, up, outer, crossed, inner2, dx3, swapped, capacity,
        (2 * capacity, 2 * capacity, 0, 0),
    )

    def add(a, b):
        return (a.astype(F32) + b.astype(F32)).astype(BF16)

    up2_in, up3 = after((up2_in, up3), dx_own)
    down2, down1 = send(add(down2, swapped), cross), send(add(down1, down3), swap)
    up2, up1 = send(add(up2, up2_in), cross), send(add(up1, up3), swap)

    dx_across = send(dx_across, beside(2))
    back = [dx_own, send(dx_beside, beside(1)), dx_across, send(dx_across[1], beside(1))]
    grad_acts = unpack(place_back.T, back, tokens)
    raw_up = up0 + up2.astype(F32) + up1.astype(F32)
    raw_down = down0 + down2.astype(F32) + down1.astype(F32)
    return (grad_acts,) + clipped(raw_down, raw_up, ndevices, add_up)


def solution(mesh):
    plane = 4
    by_planes = mesh.shape["dp"] == 4 * plane

    def per_device(*arrays):
        if by_planes:
            return move_adapters(plane, *arrays)
        return move_tokens(*arrays)

    rows, pools = P(("parts", "dp"), None), P(("parts", "dp"), None, None)
    return jax.shard_map(
        per_device,
        mesh=mesh,
        in_specs=(rows, rows, rows, P("parts"), pools, pools),
        out_specs=(rows, pools, pools),
        check_vma=False,
    )
```

```python
import jax
import jax.numpy as jnp
from jax import lax
from jax.experimental import pallas as pl
from jax.experimental.pallas import tpu as pltpu
from jax.sharding import PartitionSpec as P

BF16, F32 = jnp.bfloat16, jnp.float32
ROWS_OF = (((1,), (1,)), ((), ()))
OUTER = (((0,), (0,)), ((), ()))
INNER = (((1,), (0,)), ((), ()))
HBM = pl.BlockSpec(memory_space=pltpu.HBM)
WHOLE = pl.BlockSpec(memory_space=pltpu.VMEM)
VMEM_BYTES = 20 * 2**20


def dot32(a, b, dims=INNER):
    return lax.dot_general(a, b, dims, preferred_element_type=F32)


def route(token_task_index, task_slot_lookup, ndevices):
    pool = task_slot_lookup.shape[0]
    task_hot = (token_task_index == jnp.arange(pool, dtype=jnp.int32)[None, :]).astype(jnp.int32)
    owner = jnp.sum(task_hot * task_slot_lookup[None, :], axis=1)
    owner_hot = (owner[:, None] == jnp.arange(ndevices, dtype=jnp.int32)[None, :]).astype(jnp.int32)
    before = jnp.cumsum(owner_hot, axis=0) - owner_hot
    position = jnp.sum(before * owner_hot, axis=1)
    return owner, position


def clipped(raw_down, raw_up, ndevices, add_up):
    local_sq = jnp.sum(raw_down * raw_down) + jnp.sum(raw_up * raw_up)
    total = add_up(local_sq)
    norm = jnp.sqrt(total + 1e-06)
    limit = jnp.sqrt(jnp.float32(2 * raw_down.shape[0] * raw_down.shape[1] * ndevices))
    factor = jnp.minimum(jnp.float32(1.0), limit / norm)
    return (raw_down * factor)[None], (raw_up * factor)[None]


def move_tokens(acts, cotan, token_task_index, task_slot_lookup, pool_down_factors, pool_up_factors):
    ndevices = lax.axis_size("dp")
    tokens, width = acts.shape
    capacity = 2 * ((tokens + ndevices - 1) // ndevices)
    slots = ndevices * capacity
    owner, position = route(token_task_index, task_slot_lookup, ndevices)
    dest = owner * capacity + position
    placed = (jnp.arange(slots, dtype=jnp.int32)[:, None] == dest[None, :]).astype(BF16)

    def exchange(rows):
        rows = rows.reshape(ndevices, capacity, width)
        return lax.all_to_all(rows, "dp", split_axis=0, concat_axis=0, tiled=True).reshape(slots, width)

    down, up = pool_down_factors[0], pool_up_factors[0]
    rows_x = exchange(dot32(placed, acts).astype(BF16))
    rows_g = exchange(dot32(placed, cotan).astype(BF16))
    hidden = dot32(rows_x, down, ROWS_OF).astype(BF16)
    inner = dot32(rows_g, up, ROWS_OF).astype(BF16)
    returned = exchange(dot32(inner, down).astype(BF16))
    grad_acts = dot32(placed, returned, OUTER).astype(BF16)
    raw_up = dot32(hidden, rows_g, OUTER)
    raw_down = dot32(inner, rows_x, OUTER)
    return (grad_acts,) + clipped(raw_down, raw_up, ndevices, lambda term: lax.psum(term, "dp"))


def in_hbm(*arrays):
    return [pltpu.with_memory_space_constraint(a, pltpu.HBM) for a in arrays]


def in_vmem(*arrays):
    return [pltpu.with_memory_space_constraint(a, pltpu.VMEM) for a in arrays]


def kernel_params(semantics=("arbitrary",)):
    return pltpu.CompilerParams(dimension_semantics=semantics, vmem_limit_bytes=VMEM_BYTES)


def pack(place, acts, cotan, shapes):
    tokens, width = acts.shape
    tile = min(width, 1024)
    tiles = width // tile

    def body(place_ref, x_in, g_in, *refs):
        out_refs, (rows, sems) = refs[:-2], refs[-2:]
        step = pl.program_id(0)

        def copies(i):
            cut = pl.ds(pl.multiple_of(i * tile, tile), tile)
            return [pltpu.make_async_copy(r.at[:, cut], rows.at[k, :, cut], sems.at[k, i]) for k, r in enumerate((x_in, g_in))]

        @pl.when(step == 0)
        def _():
            for i in range(tiles):
                for c in copies(i):
                    c.start()

        for c in copies(step):
            c.wait()
        cut = pl.ds(pl.multiple_of(step * tile, tile), tile)
        for k in range(2):
            moved = dot32(place_ref[...], rows[k, :, cut]).astype(BF16)
            first = 0
            for out_ref, (columns, size) in zip(out_refs, shapes):
                for c in range(columns):
                    out_ref[c, k] = moved[first:first + size]
                    first += size

    return pl.pallas_call(
        body,
        grid=(tiles,),
        in_specs=[pl.BlockSpec(place.shape, lambda i: (0, 0)), HBM, HBM],
        out_specs=[pl.BlockSpec((c, 2, size, tile), lambda i: (0, 0, 0, i)) for c, size in shapes],
        out_shape=[jax.ShapeDtypeStruct((c, 2, size, width), BF16) for c, size in shapes],
        scratch_shapes=[pltpu.VMEM((2, tokens, width), BF16), pltpu.SemaphoreType.DMA((2, tiles))],
        compiler_params=kernel_params(),
    )(place, *in_hbm(acts, cotan))


def unpack(place, blocks, tokens):
    width = blocks[0].shape[1]
    tile = min(width, 2048)

    def body(place_ref, *refs):
        rows = jnp.concatenate([ref[...].reshape(-1, tile) for ref in refs[:-1]], axis=0)
        refs[-1][...] = dot32(place_ref[...], rows).astype(BF16)

    return pl.pallas_call(
        body,
        grid=(width // tile,),
        in_specs=[pl.BlockSpec(place.shape, lambda i: (0, 0))]
        + [
            pl.BlockSpec((b.shape[0], tile), lambda i: (0, i))
            if b.ndim == 2
            else pl.BlockSpec((1, b.shape[1], tile), lambda i: (0, 0, i))
            for b in blocks
        ],
        out_specs=pl.BlockSpec((tokens, tile), lambda i: (0, i)),
        out_shape=jax.ShapeDtypeStruct((tokens, width), BF16),
        compiler_params=kernel_params(),
    )(place, *blocks)


def corner(rows, first_rows, columns, first_columns):
    upper = lax.broadcasted_iota(jnp.int32, (rows, columns), 0) < first_rows
    return upper == (lax.broadcasted_iota(jnp.int32, (rows, columns), 1) < first_columns)


def stack(down, up):
    _, rank, width = down.shape
    pieces = 4
    part = rank // pieces

    def body(*refs):
        out, sems = refs[2:]
        copies = [
            pltpu.make_async_copy(refs[k].at[0, pl.ds(n * part, part)], out.at[k, pl.ds(n * part, part)], sems.at[k, n])
            for k in range(2)
            for n in range(pieces)
        ]
        for c in copies:
            c.start()
        for c in copies:
            c.wait()

    return pl.pallas_call(
        body,
        in_specs=[HBM, HBM],
        out_specs=pl.BlockSpec(memory_space=pl.ANY),
        out_shape=jax.ShapeDtypeStruct((2, rank, width), BF16),
        scratch_shapes=[pltpu.SemaphoreType.DMA((2, pieces))],
    )(*in_hbm(down, up))


def far_groups(is_end, stage3, stage2, ends, far, outer, crossed, capacity, first2):
    plane = len(stage3)
    _, rank, width = far.shape
    block = plane * capacity
    tile = min(width, 2048)
    tiles = width // tile

    tall = 3 * block

    def body(end_ref, *refs):
        stage_in, refs = refs[:2 * plane], refs[2 * plane:]
        ends_in, far_in, outer_in, crossed_in = refs[:4]
        sum3_refs, sum2_refs, swap_ref, inner2_ref, dx_ref = refs[4:6], refs[6:8], *refs[8:11]
        held, left, sems = refs[11:]
        step = pl.program_id(0)
        is_mine = corner(tall, 2 * block, 2 * rank, rank)

        def copies(i):
            cut = pl.ds(i * tile, tile)
            firsts = (0,) * plane + first2
            return [
                pltpu.make_async_copy(
                    r.at[0, :, pl.ds(first, capacity), cut], held.at[:, pl.ds(n * capacity, capacity), cut], sems.at[i, n]
                )
                for n, (r, first) in enumerate(zip(stage_in, firsts))
            ]

        def rows(k, cut):
            return jnp.concatenate([held[k, :block, cut], ends_in[k, :, cut], held[k, block:, cut]], axis=0)

        @pl.when(step == 0)
        def _():
            for i in range(tiles):
                for c in copies(i):
                    c.start()
            sums = [jnp.zeros((tall, 2 * rank), F32)] * 2
            for i in range(tiles):
                for c in copies(i):
                    c.wait()
                cut = pl.ds(i * tile, tile)
                for k in range(2):
                    near = jnp.where(end_ref[0] == 1, outer_in[k, :, cut], crossed_in[k, :, cut])
                    both = jnp.concatenate([far_in[k, :, cut], near], axis=0)
                    sums[k] += dot32(rows(k, cut), both, ROWS_OF)
            for k in range(2):
                left[k] = jnp.where(is_mine, sums[k], 0.0).astype(BF16)
            inner2_ref[...] = left[1, 2 * block:, rank:]

        cut = pl.ds(pl.multiple_of(step * tile, tile), tile)
        for k in range(2):
            both = dot32(left[k], rows(1 - k, cut), OUTER).astype(BF16)
            sum3_refs[k][...] = both[:rank]
            sum2_refs[k][...] = both[rank:]
        dx = dot32(left[1, :2 * block, :rank], far_in[0, :, cut]).astype(BF16)
        dx_ref[...] = dx[:block]
        swap_ref[...] = jnp.where(end_ref[0] == 1, both[rank:], dx[block:])

    def wide(rows):
        return pl.BlockSpec((rows, tile), lambda i: (0, i)), jax.ShapeDtypeStruct((rows, width), BF16)

    outs = [wide(rank)] * 4 + [wide(block)]
    outs += [(pl.BlockSpec((block, rank), lambda i: (0, 0)), jax.ShapeDtypeStruct((block, rank), BF16)), wide(block)]
    return pl.pallas_call(
        body,
        grid=(tiles,),
        in_specs=[pl.BlockSpec(memory_space=pltpu.SMEM)] + [HBM] * (2 * plane) + [WHOLE] * 4,
        out_specs=[o[0] for o in outs],
        out_shape=[o[1] for o in outs],
        scratch_shapes=[
            pltpu.VMEM((2, 2 * block, width), BF16),
            pltpu.VMEM((2, tall, 2 * rank), BF16),
            pltpu.SemaphoreType.DMA((tiles, 2 * plane)),
        ],
        compiler_params=kernel_params(),
    )(is_end, *in_hbm(*stage3, *stage2), *in_vmem(ends, far, outer, crossed))


def near_groups(is_end, stage, pair, down, up, outer, crossed, inner2, dx3, swapped, capacity, first1):
    plane = len(stage)
    _, rank, width = pair.shape
    block = plane * capacity
    tile = min(width, 2048)
    tiles = width // tile

    def body(end_ref, *refs):
        stage_in, refs = refs[:plane], refs[plane:]
        pair_in, down_in, up_in, outer_in, crossed_in, inner2, dx3, swapped = refs[:8]
        dx_refs, sum_refs = [refs[8], refs[9], refs[10].at[0], refs[10].at[1]], refs[11:15]
        left, inners = refs[15:]
        step = pl.program_id(0)
        own_in = (down_in, up_in)
        is_mine = corner(2 * block, block, 2 * rank, rank)

        def rows(k, cut):
            return jnp.concatenate(
                [
                    r[0, k, pl.ds(first + n * capacity, capacity), cut]
                    for n in range(2)
                    for r, first in zip(stage_in, first1)
                ],
                axis=0,
            )

        @pl.when(step == 0)
        def _():
            sums = [jnp.zeros((2 * block, 2 * rank), F32)] * 2
            for i in range(tiles):
                cut = pl.ds(i * tile, tile)
                for k in range(2):
                    both = jnp.concatenate([pair_in[k, :, cut], own_in[k][:, cut]], axis=0)
                    sums[k] += dot32(rows(k, cut), both, ROWS_OF)
            for k in range(2):
                left[k] = jnp.where(is_mine, sums[k], 0.0).astype(BF16)
            first = jnp.concatenate([inner2[...], jnp.zeros((block, 2 * rank), BF16)], axis=1)
            inners[...] = jnp.concatenate([first, jnp.concatenate([jnp.zeros((2 * block, rank), BF16), left[1]], axis=1)])

        cut = pl.ds(pl.multiple_of(step * tile, tile), tile)
        for k in range(2):
            both = dot32(left[k], rows(1 - k, cut), OUTER)
            sum_refs[k][...] = both[:rank]
            sum_refs[2 + k][...] = both[rank:]
        near = jnp.where(end_ref[0] == 1, outer_in[0, :, cut], crossed_in[0, :, cut])
        downs = jnp.concatenate([near, pair_in[0, :, cut], down_in[:, cut]], axis=0)
        dx = dot32(inners[...], downs).astype(BF16)
        moved = [jnp.where(end_ref[0] == 1, swapped[...], dx3[...])] + [dx[n * block:(n + 1) * block] for n in range(3)]
        for n, dx in enumerate(moved):
            for m in range(plane):
                dx_refs[m][n * capacity:(n + 1) * capacity] = dx[m * capacity:(m + 1) * capacity]

    return pl.pallas_call(
        body,
        grid=(tiles,),
        in_specs=[pl.BlockSpec(memory_space=pltpu.SMEM)]
        + [WHOLE] * (plane + 5)
        + [pl.BlockSpec(inner2.shape, lambda i: (0, 0))]
        + [pl.BlockSpec((block, tile), lambda i: (0, i))] * 2,
        out_specs=[pl.BlockSpec((4 * capacity, tile), lambda i: (0, i))] * 2
        + [pl.BlockSpec((2, 4 * capacity, tile), lambda i: (0, 0, i))]
        + [pl.BlockSpec((rank, tile), lambda i: (0, i))] * 4,
        out_shape=[jax.ShapeDtypeStruct((4 * capacity, width), BF16)] * 2
        + [jax.ShapeDtypeStruct((2, 4 * capacity, width), BF16)]
        + [jax.ShapeDtypeStruct((rank, width), F32)] * 4,
        scratch_shapes=[pltpu.VMEM((2, 2 * block, 2 * rank), BF16), pltpu.VMEM((3 * block, 3 * rank), BF16)],
        compiler_params=kernel_params(),
    )(is_end, *in_vmem(*stage, pair, down, up, outer, crossed), inner2, dx3, swapped)


def move_adapters(plane, acts, cotan, token_task_index, task_slot_lookup, pool_down_factors, pool_up_factors):
    ndevices = lax.axis_size("dp")
    tokens, width = acts.shape
    capacity = 2 * ((tokens + ndevices - 1) // ndevices)
    me = lax.axis_index("dp")
    z, column = me // plane, me % plane
    is_end = (z == 0) | (z == 3)
    end_flag = is_end.astype(jnp.int32).reshape(1)

    def planes(pairs):
        return [(a * plane + c, b * plane + c) for a, b in pairs for c in range(plane)]

    swap = planes([(0, 1), (1, 0), (2, 3), (3, 2)])
    cross = planes([(1, 2), (2, 1)])
    outward = planes([(1, 0), (2, 3)])
    inward = planes([(0, 1), (3, 2)])

    def send(array, pairs):
        return lax.ppermute(array, "dp", pairs)

    def after(arrays, *others):
        return lax.optimization_barrier((arrays, others))[0]

    def beside(m):
        return [(i, (i // plane) * plane + ((i % plane) ^ m)) for i in range(ndevices)]

    def add_up(term):
        around = [beside(m) for m in range(1, plane)]
        along = [[(i, (i // plane ^ m) * plane + i % plane) for i in range(ndevices)] for m in range(1, 4)]
        term = jnp.broadcast_to(term, (8, 128))
        term = term + sum(send(term, pairs) for pairs in around)
        term = after(term, dx_across)
        return (term + sum(after([send(term, pairs) for pairs in along], grad_acts)))[0, 0]

    down, up = pool_down_factors[0], pool_up_factors[0]
    own = stack(pool_down_factors, pool_up_factors)
    pair = send(own, swap)

    owner, position = route(after(token_task_index, own), task_slot_lookup, ndevices)
    owner_z, turn = owner // plane, (owner % plane) ^ column
    other_mid = jnp.where(z < 2, 2, 1)
    kind = jnp.where(owner_z == z, 0, jnp.where(owner_z == (z ^ 1), 1, jnp.where(owner_z == other_mid, 2, 3)))

    def places(wanted, row, rows):
        hot = jnp.arange(rows, dtype=jnp.int32)[:, None] == row[None, :]
        return (hot & wanted[None, :]).astype(BF16)

    def after(arrays, *others):
        return lax.optimization_barrier((arrays, others))[0]

    block = plane * capacity
    mine = (3 - kind) * capacity + position
    row = jnp.where(kind == 2, 10 * capacity, 12 * capacity) + (turn - 2) * jnp.where(kind == 2, capacity, 2 * capacity)
    row += jnp.where(kind == 2, 0, (1 - kind) * capacity) + position
    row = jnp.where(kind == 3, (6 + turn) * capacity + position, row)
    row = jnp.where(turn < 2, turn * block + mine, row)
    place = places(kind >= 0, row, 4 * block)
    place_back = places(kind >= 0, turn * block + mine, 4 * block)
    crossed = send(own, cross)
    own_rows, beside_rows, across3, across2, across10 = pack(
        place, acts, cotan, [(1, 4 * capacity)] * 2 + [(2, capacity)] * 2 + [(2, 2 * capacity)]
    )

    def over_x(blocks):
        moved = send(blocks, beside(2))
        return moved, send(moved[1:], beside(1))

    beside_rows = send(beside_rows, beside(1))
    across3 = over_x(across3)
    stage3 = (own_rows, beside_rows) + across3
    ends = jnp.concatenate([r[0, :, :capacity] for r in stage3], axis=1)
    ends = send(ends, inward)
    across2 = over_x(after(across2, across3[0]))
    across10 = over_x(after(across10, across2[0]))
    stage2 = (own_rows, beside_rows) + across2
    stage10 = (own_rows, beside_rows) + across10
    outer = send(crossed, outward)
    far = send(pair, cross)

    up3, down3, up2, down2, swapped, inner2, dx3 = far_groups(
        end_flag, stage3, stage2, ends, far, outer, crossed, capacity, (capacity, capacity, 0, 0)
    )
    down3, swapped = send(down3, cross), send(swapped, swap)
    up3, up2_in = send(up3, cross), send(up2, inward)

    swapped, down3 = lax.optimization_barrier((swapped, down3))
    dx_own, dx_beside, dx_across, up1, down1, up0, down0 = near_groups(
        end_flag, stage10, pair, down, up, outer, crossed, inner2, dx3, swapped, capacity,
        (2 * capacity, 2 * capacity, 0, 0),
    )

    def add(a, b):
        return (a.astype(F32) + b.astype(F32)).astype(BF16)

    down2, down1 = add(down2, swapped), add(down1, down3)
    up2_in, up3 = after((up2_in, up3), down2, down1)
    down2, down1 = send(down2, cross), send(down1, swap)
    up2, up1 = send(add(up2, up2_in), cross), send(add(up1, up3), swap)

    dx_across = send(dx_across, beside(2))
    back = [dx_own, send(dx_beside, beside(1)), dx_across, send(dx_across[1], beside(1))]
    grad_acts = unpack(place_back.T, back, tokens)
    raw_up = up0 + up2.astype(F32) + up1.astype(F32)
    raw_down = down0 + down2.astype(F32) + down1.astype(F32)
    return (grad_acts,) + clipped(raw_down, raw_up, ndevices, add_up)


def solution(mesh):
    plane = 4
    by_planes = mesh.shape["dp"] == 4 * plane

    def per_device(*arrays):
        if by_planes:
            return move_adapters(plane, *arrays)
        return move_tokens(*arrays)

    rows, pools = P(("parts", "dp"), None), P(("parts", "dp"), None, None)
    return jax.shard_map(
        per_device,
        mesh=mesh,
        in_specs=(rows, rows, rows, P("parts"), pools, pools),
        out_specs=(rows, pools, pools),
        check_vma=False,
    )
```

```python
import jax
import jax.numpy as jnp
from jax import lax
from jax.experimental import pallas as pl
from jax.experimental.pallas import tpu as pltpu
from jax.sharding import PartitionSpec as P

BF16, F32 = jnp.bfloat16, jnp.float32
ROWS_OF = (((1,), (1,)), ((), ()))
OUTER = (((0,), (0,)), ((), ()))
INNER = (((1,), (0,)), ((), ()))
HBM = pl.BlockSpec(memory_space=pltpu.HBM)
WHOLE = pl.BlockSpec(memory_space=pltpu.VMEM)
VMEM_BYTES = 20 * 2**20


def dot32(a, b, dims=INNER):
    return lax.dot_general(a, b, dims, preferred_element_type=F32)


def route(token_task_index, task_slot_lookup, ndevices):
    pool = task_slot_lookup.shape[0]
    task_hot = (token_task_index == jnp.arange(pool, dtype=jnp.int32)[None, :]).astype(jnp.int32)
    owner = jnp.sum(task_hot * task_slot_lookup[None, :], axis=1)
    owner_hot = (owner[:, None] == jnp.arange(ndevices, dtype=jnp.int32)[None, :]).astype(jnp.int32)
    before = jnp.cumsum(owner_hot, axis=0) - owner_hot
    position = jnp.sum(before * owner_hot, axis=1)
    return owner, position


def clipped(raw_down, raw_up, ndevices, add_up):
    local_sq = jnp.sum(raw_down * raw_down) + jnp.sum(raw_up * raw_up)
    total = add_up(local_sq)
    norm = jnp.sqrt(total + 1e-06)
    limit = jnp.sqrt(jnp.float32(2 * raw_down.shape[0] * raw_down.shape[1] * ndevices))
    factor = jnp.minimum(jnp.float32(1.0), limit / norm)
    return (raw_down * factor)[None], (raw_up * factor)[None]


def move_tokens(acts, cotan, token_task_index, task_slot_lookup, pool_down_factors, pool_up_factors):
    ndevices = lax.axis_size("dp")
    tokens, width = acts.shape
    capacity = 2 * ((tokens + ndevices - 1) // ndevices)
    slots = ndevices * capacity
    owner, position = route(token_task_index, task_slot_lookup, ndevices)
    dest = owner * capacity + position
    placed = (jnp.arange(slots, dtype=jnp.int32)[:, None] == dest[None, :]).astype(BF16)

    def exchange(rows):
        rows = rows.reshape(ndevices, capacity, width)
        return lax.all_to_all(rows, "dp", split_axis=0, concat_axis=0, tiled=True).reshape(slots, width)

    down, up = pool_down_factors[0], pool_up_factors[0]
    rows_x = exchange(dot32(placed, acts).astype(BF16))
    rows_g = exchange(dot32(placed, cotan).astype(BF16))
    hidden = dot32(rows_x, down, ROWS_OF).astype(BF16)
    inner = dot32(rows_g, up, ROWS_OF).astype(BF16)
    returned = exchange(dot32(inner, down).astype(BF16))
    grad_acts = dot32(placed, returned, OUTER).astype(BF16)
    raw_up = dot32(hidden, rows_g, OUTER)
    raw_down = dot32(inner, rows_x, OUTER)
    return (grad_acts,) + clipped(raw_down, raw_up, ndevices, lambda term: lax.psum(term, "dp"))


def in_hbm(*arrays):
    return [pltpu.with_memory_space_constraint(a, pltpu.HBM) for a in arrays]


def in_vmem(*arrays):
    return [pltpu.with_memory_space_constraint(a, pltpu.VMEM) for a in arrays]


def kernel_params(semantics=("arbitrary",)):
    return pltpu.CompilerParams(dimension_semantics=semantics, vmem_limit_bytes=VMEM_BYTES)


def pack(place, acts, cotan, shapes):
    tokens, width = acts.shape
    tile = min(width, 1024)
    tiles = width // tile

    def body(place_ref, x_in, g_in, *refs):
        out_refs, (rows, sems) = refs[:-2], refs[-2:]
        step = pl.program_id(0)

        def copies(i):
            cut = pl.ds(pl.multiple_of(i * tile, tile), tile)
            return [pltpu.make_async_copy(r.at[:, cut], rows.at[k, :, cut], sems.at[k, i]) for k, r in enumerate((x_in, g_in))]

        @pl.when(step == 0)
        def _():
            for i in range(tiles):
                for c in copies(i):
                    c.start()

        for c in copies(step):
            c.wait()
        cut = pl.ds(pl.multiple_of(step * tile, tile), tile)
        for k in range(2):
            moved = dot32(place_ref[...], rows[k, :, cut]).astype(BF16)
            first = 0
            for out_ref, (columns, size) in zip(out_refs, shapes):
                for c in range(columns):
                    out_ref[c, k] = moved[first:first + size]
                    first += size

    return pl.pallas_call(
        body,
        grid=(tiles,),
        in_specs=[pl.BlockSpec(place.shape, lambda i: (0, 0)), HBM, HBM],
        out_specs=[pl.BlockSpec((c, 2, size, tile), lambda i: (0, 0, 0, i)) for c, size in shapes],
        out_shape=[jax.ShapeDtypeStruct((c, 2, size, width), BF16) for c, size in shapes],
        scratch_shapes=[pltpu.VMEM((2, tokens, width), BF16), pltpu.SemaphoreType.DMA((2, tiles))],
        compiler_params=kernel_params(),
    )(place, *in_hbm(acts, cotan))


def unpack(place, blocks, tokens):
    width = blocks[0].shape[1]
    tile = min(width, 2048)

    def body(place_ref, *refs):
        rows = jnp.concatenate([ref[...].reshape(-1, tile) for ref in refs[:-1]], axis=0)
        refs[-1][...] = dot32(place_ref[...], rows).astype(BF16)

    return pl.pallas_call(
        body,
        grid=(width // tile,),
        in_specs=[pl.BlockSpec(place.shape, lambda i: (0, 0))]
        + [
            pl.BlockSpec((b.shape[0], tile), lambda i: (0, i))
            if b.ndim == 2
            else pl.BlockSpec((1, b.shape[1], tile), lambda i: (0, 0, i))
            for b in blocks
        ],
        out_specs=pl.BlockSpec((tokens, tile), lambda i: (0, i)),
        out_shape=jax.ShapeDtypeStruct((tokens, width), BF16),
        compiler_params=kernel_params(),
    )(place, *blocks)


def corner(rows, first_rows, columns, first_columns):
    upper = lax.broadcasted_iota(jnp.int32, (rows, columns), 0) < first_rows
    return upper == (lax.broadcasted_iota(jnp.int32, (rows, columns), 1) < first_columns)


def held_copies(source, held, sems, tile):
    return [
        pltpu.make_async_copy(source.at[:, :, pl.ds(i * tile, tile)], held.at[:, :, pl.ds(i * tile, tile)], sems.at[i])
        for i in range(held.shape[2] // tile)
    ]


def far_end(mine, handed, far):
    _, block, width = mine.shape
    rank = far.shape[1]
    tile = min(width, 2048)
    tiles = width // tile

    def body(mine_in, handed_in, far_in, up_ref, down_ref, dx_ref, handed_dx_ref, held, left, sems):
        step = pl.program_id(0)

        def rows(k, cut):
            return jnp.concatenate([held[k, :, cut], handed_in[k, :, cut]], axis=0)

        @pl.when(step == 0)
        def _():
            copies = held_copies(mine_in, held, sems, tile)
            for c in copies:
                c.start()
            sums = [jnp.zeros((rank, 2 * block), F32)] * 2
            for i, c in enumerate(copies):
                c.wait()
                cut = pl.ds(i * tile, tile)
                for k in range(2):
                    sums[k] += dot32(far_in[k, :, cut], rows(k, cut), ROWS_OF)
            for k in range(2):
                left[k] = sums[k].astype(BF16)

        cut = pl.ds(pl.multiple_of(step * tile, tile), tile)
        up_ref[...] = dot32(left[0], rows(1, cut)).astype(BF16)
        down_ref[...] = dot32(left[1], rows(0, cut)).astype(BF16)
        dx = dot32(left[1], far_in[0, :, cut], OUTER).astype(BF16)
        dx_ref[...] = dx[:block]
        handed_dx_ref[...] = dx[block:]

    def wide(rows):
        return pl.BlockSpec((rows, tile), lambda i: (0, i))

    sizes = (rank, rank, block, block)
    return pl.pallas_call(
        body,
        grid=(tiles,),
        in_specs=[HBM] + [WHOLE] * 2,
        out_specs=[wide(n) for n in sizes],
        out_shape=[jax.ShapeDtypeStruct((n, width), BF16) for n in sizes],
        scratch_shapes=[
            pltpu.VMEM((2, block, width), BF16),
            pltpu.VMEM((2, rank, 2 * block), BF16),
            pltpu.SemaphoreType.DMA((tiles,)),
        ],
        compiler_params=kernel_params(),
    )(*in_hbm(mine), *in_vmem(handed, far))


def far_mid(is_end, mine, outer, crossed, handed_dx):
    _, block, width = mine.shape
    rank = outer.shape[1]
    tile = min(width, 2048)
    tiles = width // tile

    def body(end_ref, mine_in, outer_in, crossed_in, handed_ref, up_ref, down_ref, swap_ref, inner_ref, held, left, sems):
        step = pl.program_id(0)

        @pl.when(step == 0)
        def _():
            copies = held_copies(mine_in, held, sems, tile)
            for c in copies:
                c.start()
            sums = [jnp.zeros((rank, block), F32)] * 2
            for i, c in enumerate(copies):
                c.wait()
                cut = pl.ds(i * tile, tile)
                for k in range(2):
                    factors = jnp.where(end_ref[0] == 1, outer_in[k, :, cut], crossed_in[k, :, cut])
                    sums[k] += dot32(factors, held[k, :, cut], ROWS_OF)
            for k in range(2):
                left[k] = sums[k].astype(BF16)
            inner_ref[...] = sums[1].T.astype(BF16)

        cut = pl.ds(pl.multiple_of(step * tile, tile), tile)
        up_ref[...] = dot32(left[0], held[1, :, cut]).astype(BF16)
        down = dot32(left[1], held[0, :, cut]).astype(BF16)
        down_ref[...] = down
        swap_ref[...] = jnp.where(end_ref[0] == 1, down, handed_ref[...])

    wide = pl.BlockSpec((rank, tile), lambda i: (0, i))
    return pl.pallas_call(
        body,
        grid=(tiles,),
        in_specs=[pl.BlockSpec(memory_space=pltpu.SMEM), HBM, WHOLE, WHOLE, pl.BlockSpec((block, tile), lambda i: (0, i))],
        out_specs=[wide] * 3 + [pl.BlockSpec((block, rank), lambda i: (0, 0))],
        out_shape=[jax.ShapeDtypeStruct((rank, width), BF16)] * 3 + [jax.ShapeDtypeStruct((block, rank), BF16)],
        scratch_shapes=[
            pltpu.VMEM((2, block, width), BF16),
            pltpu.VMEM((2, rank, block), BF16),
            pltpu.SemaphoreType.DMA((tiles,)),
        ],
        compiler_params=kernel_params(),
    )(is_end, *in_hbm(mine), *in_vmem(outer, crossed), handed_dx)


def near_groups(is_end, stage, pair, down, up, outer, crossed, inner2, dx3, swapped, capacity, first1):
    plane = len(stage)
    rank, width = down.shape
    block = plane * capacity
    tile = min(width, 2048)
    tiles = width // tile

    def body(end_ref, *refs):
        stage_in, refs = refs[:plane], refs[plane:]
        pair_in, down_in, up_in, outer_in, crossed_in, inner2, dx3, swapped = refs[:8]
        dx_refs, sum_refs = [refs[8], refs[9], refs[10].at[0], refs[10].at[1]], refs[11:15]
        left, inners = refs[15:]
        step = pl.program_id(0)
        own_in = (down_in, up_in)
        is_mine = corner(2 * block, block, 2 * rank, rank)

        def rows(k, cut):
            return jnp.concatenate(
                [
                    r[0, k, pl.ds(first + n * capacity, capacity), cut]
                    for n in range(2)
                    for r, first in zip(stage_in, first1)
                ],
                axis=0,
            )

        @pl.when(step == 0)
        def _():
            sums = [jnp.zeros((2 * block, 2 * rank), F32)] * 2
            for i in range(tiles):
                cut = pl.ds(i * tile, tile)
                for k in range(2):
                    both = jnp.concatenate([pair_in[k, :, cut], own_in[k][:, cut]], axis=0)
                    sums[k] += dot32(rows(k, cut), both, ROWS_OF)
            for k in range(2):
                left[k] = jnp.where(is_mine, sums[k], 0.0).astype(BF16)
            first = jnp.concatenate([inner2[...], jnp.zeros((block, 2 * rank), BF16)], axis=1)
            inners[...] = jnp.concatenate([first, jnp.concatenate([jnp.zeros((2 * block, rank), BF16), left[1]], axis=1)])

        cut = pl.ds(pl.multiple_of(step * tile, tile), tile)
        for k in range(2):
            both = dot32(left[k], rows(1 - k, cut), OUTER)
            sum_refs[k][...] = both[:rank]
            sum_refs[2 + k][...] = both[rank:]
        near = jnp.where(end_ref[0] == 1, outer_in[0, :, cut], crossed_in[0, :, cut])
        downs = jnp.concatenate([near, pair_in[0, :, cut], down_in[:, cut]], axis=0)
        dx = dot32(inners[...], downs).astype(BF16)
        moved = [jnp.where(end_ref[0] == 1, swapped[...], dx3[...])] + [dx[n * block:(n + 1) * block] for n in range(3)]
        for n, dx in enumerate(moved):
            for m in range(plane):
                dx_refs[m][n * capacity:(n + 1) * capacity] = dx[m * capacity:(m + 1) * capacity]

    return pl.pallas_call(
        body,
        grid=(tiles,),
        in_specs=[pl.BlockSpec(memory_space=pltpu.SMEM)]
        + [WHOLE] * (plane + 5)
        + [pl.BlockSpec(inner2.shape, lambda i: (0, 0))]
        + [pl.BlockSpec((block, tile), lambda i: (0, i))] * 2,
        out_specs=[pl.BlockSpec((4 * capacity, tile), lambda i: (0, i))] * 2
        + [pl.BlockSpec((2, 4 * capacity, tile), lambda i: (0, 0, i))]
        + [pl.BlockSpec((rank, tile), lambda i: (0, i))] * 4,
        out_shape=[jax.ShapeDtypeStruct((4 * capacity, width), BF16)] * 2
        + [jax.ShapeDtypeStruct((2, 4 * capacity, width), BF16)]
        + [jax.ShapeDtypeStruct((rank, width), F32)] * 4,
        scratch_shapes=[pltpu.VMEM((2, 2 * block, 2 * rank), BF16), pltpu.VMEM((3 * block, 3 * rank), BF16)],
        compiler_params=kernel_params(),
    )(is_end, *in_vmem(*stage, pair, down, up, outer, crossed), inner2, dx3, swapped)


def move_adapters(plane, acts, cotan, token_task_index, task_slot_lookup, pool_down_factors, pool_up_factors):
    ndevices = lax.axis_size("dp")
    tokens, width = acts.shape
    capacity = 2 * ((tokens + ndevices - 1) // ndevices)
    me = lax.axis_index("dp")
    z, column = me // plane, me % plane
    is_end = (z == 0) | (z == 3)
    end_flag = is_end.astype(jnp.int32).reshape(1)

    def planes(pairs):
        return [(a * plane + c, b * plane + c) for a, b in pairs for c in range(plane)]

    swap = planes([(0, 1), (1, 0), (2, 3), (3, 2)])
    cross = planes([(1, 2), (2, 1)])
    outward = planes([(1, 0), (2, 3)])
    inward = planes([(0, 1), (3, 2)])

    def send(array, pairs):
        return lax.ppermute(array, "dp", pairs)

    def after(arrays, *others):
        return lax.optimization_barrier((arrays, others))[0]

    def beside(m):
        return [(i, (i // plane) * plane + ((i % plane) ^ m)) for i in range(ndevices)]

    def add_up(term):
        around = [beside(m) for m in range(1, plane)]
        along = [[(i, (i // plane ^ m) * plane + i % plane) for i in range(ndevices)] for m in range(1, 4)]
        term = jnp.broadcast_to(term, (8, 128))
        term = term + sum(send(term, pairs) for pairs in around)
        term = after(term, dx_across)
        return (term + sum(after([send(term, pairs) for pairs in along], grad_acts)))[0, 0]

    down, up = pool_down_factors[0], pool_up_factors[0]
    own = jnp.concatenate([pool_down_factors, pool_up_factors])
    pair = send(own, swap)
    crossed = send(own, cross)

    owner, position = route(token_task_index, task_slot_lookup, ndevices)
    owner_z, turn = owner // plane, (owner % plane) ^ column
    other_mid = jnp.where(z < 2, 2, 1)
    kind = jnp.where(owner_z == z, 0, jnp.where(owner_z == (z ^ 1), 1, jnp.where(owner_z == other_mid, 2, 3)))

    def places(wanted, row, rows):
        hot = jnp.arange(rows, dtype=jnp.int32)[:, None] == row[None, :]
        return (hot & wanted[None, :]).astype(BF16)

    def after(arrays, *others):
        return lax.optimization_barrier((arrays, others))[0]

    block = plane * capacity
    mine = (3 - kind) * capacity + position
    row = jnp.where(kind == 2, 10 * capacity, 12 * capacity) + (turn - 2) * jnp.where(kind == 2, capacity, 2 * capacity)
    row += jnp.where(kind == 2, 0, (1 - kind) * capacity) + position
    row = jnp.where(kind == 3, (6 + turn) * capacity + position, row)
    row = jnp.where(turn < 2, turn * block + mine, row)
    place = places(kind >= 0, row, 4 * block)
    place_back = places(kind >= 0, turn * block + mine, 4 * block)
    own_rows, beside_rows, across3, across2, across10 = pack(
        place, acts, cotan, [(1, 4 * capacity)] * 2 + [(2, capacity)] * 2 + [(2, 2 * capacity)]
    )

    def over_x(blocks):
        moved = send(blocks, beside(2))
        return moved, send(moved[1:], beside(1))

    beside_rows = send(beside_rows, beside(1))
    across3 = over_x(across3)
    stage3 = (own_rows, beside_rows) + across3
    rows3 = jnp.concatenate([r[0, :, :capacity] for r in stage3], axis=1)
    handed = send(rows3, inward)
    across2 = over_x(after(across2, across3[0]))
    across10 = over_x(after(across10, across2[0]))
    rows2 = [r[0, :, capacity:2 * capacity] for r in (own_rows, beside_rows)] + [r[0] for r in across2]
    rows2 = jnp.concatenate(rows2, axis=1)
    stage10 = (own_rows, beside_rows) + across10
    outer = send(crossed, outward)
    far = send(pair, cross)

    up3, down3, dx3, handed_dx = far_end(rows3, handed, far)
    down3, up3 = send(down3, cross), send(up3, cross)
    up2, down2, swapped, inner2 = far_mid(end_flag, rows2, outer, crossed, handed_dx)
    swapped, up2_in = send(swapped, swap), send(up2, inward)

    swapped, down3 = lax.optimization_barrier((swapped, down3))
    dx_own, dx_beside, dx_across, up1, down1, up0, down0 = near_groups(
        end_flag, stage10, pair, down, up, outer, crossed, inner2, dx3, swapped, capacity,
        (2 * capacity, 2 * capacity, 0, 0),
    )

    def add(a, b):
        return (a.astype(F32) + b.astype(F32)).astype(BF16)

    down2, down1 = add(down2, swapped), add(down1, down3)
    up2_in, up3 = after((up2_in, up3), down2, down1)
    down2, down1 = send(down2, cross), send(down1, swap)
    up2, up1 = send(add(up2, up2_in), cross), send(add(up1, up3), swap)

    dx_across = send(dx_across, beside(2))
    back = [dx_own, send(dx_beside, beside(1)), dx_across, send(dx_across[1], beside(1))]
    grad_acts = unpack(place_back.T, back, tokens)
    raw_up = up0 + up2.astype(F32) + up1.astype(F32)
    raw_down = down0 + down2.astype(F32) + down1.astype(F32)
    return (grad_acts,) + clipped(raw_down, raw_up, ndevices, add_up)


def solution(mesh):
    plane = 4
    by_planes = mesh.shape["dp"] == 4 * plane

    def per_device(*arrays):
        if by_planes:
            return move_adapters(plane, *arrays)
        return move_tokens(*arrays)

    rows, pools = P(("parts", "dp"), None), P(("parts", "dp"), None, None)
    return jax.shard_map(
        per_device,
        mesh=mesh,
        in_specs=(rows, rows, rows, P("parts"), pools, pools),
        out_specs=(rows, pools, pools),
        check_vma=False,
    )
```

```python
import jax
import jax.numpy as jnp
from jax import lax
from jax.experimental import pallas as pl
from jax.experimental.pallas import tpu as pltpu
from jax.sharding import PartitionSpec as P

BF16, F32 = jnp.bfloat16, jnp.float32
ROWS_OF = (((1,), (1,)), ((), ()))
OUTER = (((0,), (0,)), ((), ()))
INNER = (((1,), (0,)), ((), ()))
HBM = pl.BlockSpec(memory_space=pltpu.HBM)
WHOLE = pl.BlockSpec(memory_space=pltpu.VMEM)
VMEM_BYTES = 20 * 2**20


def dot32(a, b, dims=INNER):
    return lax.dot_general(a, b, dims, preferred_element_type=F32)


def route(token_task_index, task_slot_lookup, ndevices):
    pool = task_slot_lookup.shape[0]
    task_hot = (token_task_index == jnp.arange(pool, dtype=jnp.int32)[None, :]).astype(jnp.int32)
    owner = jnp.sum(task_hot * task_slot_lookup[None, :], axis=1)
    owner_hot = (owner[:, None] == jnp.arange(ndevices, dtype=jnp.int32)[None, :]).astype(jnp.int32)
    before = jnp.cumsum(owner_hot, axis=0) - owner_hot
    position = jnp.sum(before * owner_hot, axis=1)
    return owner, position


def clipped(raw_down, raw_up, ndevices, add_up):
    local_sq = jnp.sum(raw_down * raw_down) + jnp.sum(raw_up * raw_up)
    total = add_up(local_sq)
    norm = jnp.sqrt(total + 1e-06)
    limit = jnp.sqrt(jnp.float32(2 * raw_down.shape[0] * raw_down.shape[1] * ndevices))
    factor = jnp.minimum(jnp.float32(1.0), limit / norm)
    return (raw_down * factor)[None], (raw_up * factor)[None]


def move_tokens(acts, cotan, token_task_index, task_slot_lookup, pool_down_factors, pool_up_factors):
    ndevices = lax.axis_size("dp")
    tokens, width = acts.shape
    capacity = 2 * ((tokens + ndevices - 1) // ndevices)
    slots = ndevices * capacity
    owner, position = route(token_task_index, task_slot_lookup, ndevices)
    dest = owner * capacity + position
    placed = (jnp.arange(slots, dtype=jnp.int32)[:, None] == dest[None, :]).astype(BF16)

    def exchange(rows):
        rows = rows.reshape(ndevices, capacity, width)
        return lax.all_to_all(rows, "dp", split_axis=0, concat_axis=0, tiled=True).reshape(slots, width)

    down, up = pool_down_factors[0], pool_up_factors[0]
    rows_x = exchange(dot32(placed, acts).astype(BF16))
    rows_g = exchange(dot32(placed, cotan).astype(BF16))
    hidden = dot32(rows_x, down, ROWS_OF).astype(BF16)
    inner = dot32(rows_g, up, ROWS_OF).astype(BF16)
    returned = exchange(dot32(inner, down).astype(BF16))
    grad_acts = dot32(placed, returned, OUTER).astype(BF16)
    raw_up = dot32(hidden, rows_g, OUTER)
    raw_down = dot32(inner, rows_x, OUTER)
    return (grad_acts,) + clipped(raw_down, raw_up, ndevices, lambda term: lax.psum(term, "dp"))


def in_hbm(*arrays):
    return [pltpu.with_memory_space_constraint(a, pltpu.HBM) for a in arrays]


def in_vmem(*arrays):
    return [pltpu.with_memory_space_constraint(a, pltpu.VMEM) for a in arrays]


def kernel_params(semantics=("arbitrary",)):
    return pltpu.CompilerParams(dimension_semantics=semantics, vmem_limit_bytes=VMEM_BYTES)


def pack(place, acts, cotan, shapes):
    tokens, width = acts.shape
    tile = min(width, 1024)
    tiles = width // tile

    def body(place_ref, x_in, g_in, *refs):
        out_refs, (rows, sems) = refs[:-2], refs[-2:]
        step = pl.program_id(0)

        def copies(i):
            cut = pl.ds(pl.multiple_of(i * tile, tile), tile)
            return [pltpu.make_async_copy(r.at[:, cut], rows.at[k, :, cut], sems.at[k, i]) for k, r in enumerate((x_in, g_in))]

        @pl.when(step == 0)
        def _():
            for i in range(tiles):
                for c in copies(i):
                    c.start()

        for c in copies(step):
            c.wait()
        cut = pl.ds(pl.multiple_of(step * tile, tile), tile)
        for k in range(2):
            moved = dot32(place_ref[...], rows[k, :, cut]).astype(BF16)
            first = 0
            for out_ref, (columns, size) in zip(out_refs, shapes):
                for c in range(columns):
                    out_ref[c, k] = moved[first:first + size]
                    first += size

    return pl.pallas_call(
        body,
        grid=(tiles,),
        in_specs=[pl.BlockSpec(place.shape, lambda i: (0, 0)), HBM, HBM],
        out_specs=[pl.BlockSpec((c, 2, size, tile), lambda i: (0, 0, 0, i)) for c, size in shapes],
        out_shape=[jax.ShapeDtypeStruct((c, 2, size, width), BF16) for c, size in shapes],
        scratch_shapes=[pltpu.VMEM((2, tokens, width), BF16), pltpu.SemaphoreType.DMA((2, tiles))],
        compiler_params=kernel_params(),
    )(place, *in_hbm(acts, cotan))


def unpack(place, blocks, tokens):
    width = blocks[0].shape[1]
    tile = min(width, 2048)

    def body(place_ref, *refs):
        rows = jnp.concatenate([ref[...] for ref in refs[:-1]], axis=0)
        refs[-1][...] = dot32(place_ref[...], rows).astype(BF16)

    return pl.pallas_call(
        body,
        grid=(width // tile,),
        in_specs=[pl.BlockSpec(place.shape, lambda i: (0, 0))]
        + [pl.BlockSpec((b.shape[0], tile), lambda i: (0, i)) for b in blocks],
        out_specs=pl.BlockSpec((tokens, tile), lambda i: (0, i)),
        out_shape=jax.ShapeDtypeStruct((tokens, width), BF16),
        compiler_params=kernel_params(),
    )(place, *in_hbm(blocks[0]), *blocks[1:])


def corner(rows, first_rows, columns, first_columns):
    upper = lax.broadcasted_iota(jnp.int32, (rows, columns), 0) < first_rows
    return upper == (lax.broadcasted_iota(jnp.int32, (rows, columns), 1) < first_columns)


def far_group(is_end, rows, factors, handed=None):
    _, block, width = rows[0].shape
    rank = factors[0].shape[1]
    tile = min(width, 2048)
    tiles = width // tile
    total = block if handed is None else 2 * block

    def body(end_ref, *refs):
        rows_in, refs = refs[:len(rows)], refs[len(rows):]
        factors_in, refs = refs[:len(factors)], refs[len(factors):]
        handed_in, refs = (None, refs) if handed is None else (refs[0], refs[1:])
        (up_ref, down_ref, dx_ref), (held, left, sems) = refs[:3], refs[-3:]
        step = pl.program_id(0)
        at_end = end_ref[0] == 1

        def copy(source, i):
            cut = pl.ds(i * tile, tile)
            return pltpu.make_async_copy(source.at[:, :, cut], held.at[:, :, cut], sems.at[i])

        def tokens(k, cut):
            own = held[k, :, cut]
            return own if handed is None else jnp.concatenate([own, handed_in[k, :, cut]], axis=0)

        def factor(k, cut):
            first = factors_in[0][k, :, cut]
            return first if len(factors) == 1 else jnp.where(at_end, factors_in[1][k, :, cut], first)

        @pl.when(step == 0)
        def _():
            for n, source in enumerate(rows_in):
                chosen = at_end == (n == 1) if len(rows) == 2 else step == 0

                @pl.when(chosen)
                def _(source=source):
                    for i in range(tiles):
                        copy(source, i).start()

            sums = [jnp.zeros((rank, total), F32)] * 2
            for i in range(tiles):
                copy(rows_in[0], i).wait()
                cut = pl.ds(i * tile, tile)
                for k in range(2):
                    sums[k] += dot32(factor(k, cut), tokens(k, cut), ROWS_OF)
            for k in range(2):
                left[k] = sums[k].astype(BF16)

        cut = pl.ds(pl.multiple_of(step * tile, tile), tile)
        up_ref[...] = dot32(left[0], tokens(1, cut)).astype(BF16)
        down = dot32(left[1], tokens(0, cut)).astype(BF16)
        down_ref[...] = down
        dx = dot32(left[1], factor(0, cut), OUTER).astype(BF16)
        dx_ref[...] = dx[:block]
        if handed is not None:
            refs[3][...] = jnp.where(at_end, down, dx[block:])

    outs = 3 if handed is None else 4
    more = () if handed is None else (handed,)
    return pl.pallas_call(
        body,
        grid=(tiles,),
        in_specs=[pl.BlockSpec(memory_space=pltpu.SMEM)] + [HBM] * len(rows) + [WHOLE] * (len(factors) + len(more)),
        out_specs=[pl.BlockSpec((rank, tile), lambda i: (0, i))] * outs,
        out_shape=[jax.ShapeDtypeStruct((rank, width), BF16)] * outs,
        scratch_shapes=[
            pltpu.VMEM((2, block, width), BF16),
            pltpu.VMEM((2, rank, total), BF16),
            pltpu.SemaphoreType.DMA((tiles,)),
        ],
        compiler_params=kernel_params(),
    )(is_end, *in_hbm(*rows), *in_vmem(*factors, *more))


def near_groups(is_end, stage, pair, down, up, dx_late, dx_early, swapped, capacity, first1):
    plane = len(stage)
    rank, width = down.shape
    block = plane * capacity
    tile = min(width, 2048)
    tiles = width // tile

    def body(end_ref, *refs):
        stage_in, refs = refs[:plane], refs[plane:]
        pair_in, down_in, up_in, late_ref, early_ref, swapped_ref = refs[:6]
        dx_refs, sum_refs = refs[6:10], refs[10:14]
        (left,) = refs[14:]
        step = pl.program_id(0)
        own_in = (down_in, up_in)
        is_mine = corner(2 * block, block, 2 * rank, rank)

        def rows(k, cut):
            return jnp.concatenate(
                [
                    r[0, k, pl.ds(first + n * capacity, capacity), cut]
                    for n in range(2)
                    for r, first in zip(stage_in, first1)
                ],
                axis=0,
            )

        @pl.when(step == 0)
        def _():
            sums = [jnp.zeros((2 * block, 2 * rank), F32)] * 2
            for i in range(tiles):
                cut = pl.ds(i * tile, tile)
                for k in range(2):
                    both = jnp.concatenate([pair_in[k, :, cut], own_in[k][:, cut]], axis=0)
                    sums[k] += dot32(rows(k, cut), both, ROWS_OF)
            for k in range(2):
                left[k] = jnp.where(is_mine, sums[k], 0.0).astype(BF16)

        cut = pl.ds(pl.multiple_of(step * tile, tile), tile)
        for k in range(2):
            both = dot32(left[k], rows(1 - k, cut), OUTER)
            sum_refs[k][...] = both[:rank]
            sum_refs[2 + k][...] = both[rank:]
        downs = jnp.concatenate([pair_in[0, :, cut], down_in[:, cut]], axis=0)
        dx = dot32(left[1], downs).astype(BF16)
        at_end, late = end_ref[0] == 1, late_ref[...]
        moved = [jnp.where(at_end, swapped_ref[...], late), jnp.where(at_end, late, early_ref[...]), dx[:block], dx[block:]]
        for n, dx in enumerate(moved):
            for m in range(plane):
                dx_refs[m][n * capacity:(n + 1) * capacity] = dx[m * capacity:(m + 1) * capacity]

    return pl.pallas_call(
        body,
        grid=(tiles,),
        in_specs=[pl.BlockSpec(memory_space=pltpu.SMEM)]
        + [WHOLE] * (plane + 3)
        + [pl.BlockSpec((block, tile), lambda i: (0, i))] * 3,
        out_specs=[pl.BlockSpec((4 * capacity, tile), lambda i: (0, i))] * plane
        + [pl.BlockSpec((rank, tile), lambda i: (0, i))] * 4,
        out_shape=[jax.ShapeDtypeStruct((4 * capacity, width), BF16)] * plane
        + [jax.ShapeDtypeStruct((rank, width), F32)] * 4,
        scratch_shapes=[pltpu.VMEM((2, 2 * block, 2 * rank), BF16)],
        compiler_params=kernel_params(),
    )(is_end, *in_vmem(*stage, pair, down, up), dx_late, dx_early, swapped)


def move_adapters(plane, acts, cotan, token_task_index, task_slot_lookup, pool_down_factors, pool_up_factors):
    ndevices = lax.axis_size("dp")
    tokens, width = acts.shape
    capacity = 2 * ((tokens + ndevices - 1) // ndevices)
    me = lax.axis_index("dp")
    z, column = me // plane, me % plane
    is_end = (z == 0) | (z == 3)
    end_flag = is_end.astype(jnp.int32).reshape(1)

    def planes(pairs):
        return [(a * plane + c, b * plane + c) for a, b in pairs for c in range(plane)]

    swap = planes([(0, 1), (1, 0), (2, 3), (3, 2)])
    cross = planes([(1, 2), (2, 1)])
    outward = planes([(1, 0), (2, 3)])
    inward = planes([(0, 1), (3, 2)])

    def send(array, pairs):
        return lax.ppermute(array, "dp", pairs)

    def after(arrays, *others):
        return lax.optimization_barrier((arrays, others))[0]

    def beside(m):
        return [(i, (i // plane) * plane + ((i % plane) ^ m)) for i in range(ndevices)]

    def add_up(term):
        around = [beside(m) for m in range(1, plane)]
        along = [[(i, (i // plane ^ m) * plane + i % plane) for i in range(ndevices)] for m in range(1, 4)]
        term = jnp.broadcast_to(term, (8, 128))
        term = term + sum(send(term, pairs) for pairs in around)
        term = after(term, dx_across[1])
        return (term + sum(after([send(term, pairs) for pairs in along], grad_acts)))[0, 0]

    down, up = pool_down_factors[0], pool_up_factors[0]
    own = jnp.concatenate([pool_down_factors, pool_up_factors])
    pair = send(own, swap)
    crossed = send(own, cross)

    owner, position = route(token_task_index, task_slot_lookup, ndevices)
    owner_z, turn = owner // plane, (owner % plane) ^ column
    other_mid = jnp.where(z < 2, 2, 1)
    kind = jnp.where(owner_z == z, 0, jnp.where(owner_z == (z ^ 1), 1, jnp.where(owner_z == other_mid, 2, 3)))

    def places(wanted, row, rows):
        hot = jnp.arange(rows, dtype=jnp.int32)[:, None] == row[None, :]
        return (hot & wanted[None, :]).astype(BF16)

    def after(arrays, *others):
        return lax.optimization_barrier((arrays, others))[0]

    block = plane * capacity
    mine = (3 - kind) * capacity + position
    row = jnp.where(kind == 2, 10 * capacity, 12 * capacity) + (turn - 2) * jnp.where(kind == 2, capacity, 2 * capacity)
    row += jnp.where(kind == 2, 0, (1 - kind) * capacity) + position
    row = jnp.where(kind == 3, (6 + turn) * capacity + position, row)
    row = jnp.where(turn < 2, turn * block + mine, row)
    place = places(kind >= 0, row, 4 * block)
    place_back = places(kind >= 0, turn * block + mine, 4 * block)
    own_rows, beside_rows, across3, across2, across10 = pack(
        place, acts, cotan, [(1, 4 * capacity)] * 2 + [(2, capacity)] * 2 + [(2, 2 * capacity)]
    )

    def over_x(blocks):
        moved = send(blocks, beside(2))
        return moved, send(moved[1:], beside(1))

    beside_rows = send(beside_rows, beside(1))
    across3 = over_x(across3)
    stage3 = (own_rows, beside_rows) + across3
    rows3 = jnp.concatenate([r[0, :, :capacity] for r in stage3], axis=1)
    handed = send(rows3, inward)
    across2 = over_x(after(across2, across3[0]))
    across10 = over_x(after(across10, across2[0]))
    rows2 = [r[0, :, capacity:2 * capacity] for r in (own_rows, beside_rows)] + [r[0] for r in across2]
    rows2 = jnp.concatenate(rows2, axis=1)
    stage10 = (own_rows, beside_rows) + across10
    outer = send(crossed, outward)
    far = send(pair, cross)

    up2, down2, dx_early = far_group(end_flag, (rows2,), (crossed,))
    rows3, rows2 = after((rows3, rows2), dx_early)
    up3, down3, dx_late, swapped = far_group(end_flag, (rows3, rows2), (far, outer), handed)
    up2_in = send(up3, inward)
    down3, swapped, up3 = send(down3, cross), send(swapped, swap), send(up3, cross)

    swapped, down3 = lax.optimization_barrier((swapped, down3))
    dx_own, dx_beside, *dx_across, up1, down1, up0, down0 = near_groups(
        end_flag, stage10, pair, down, up, dx_late, dx_early, swapped, capacity,
        (2 * capacity, 2 * capacity, 0, 0),
    )

    def add(a, b):
        return (a.astype(F32) + b.astype(F32)).astype(BF16)

    down2, down1 = add(down2, swapped), add(down1, down3)
    dx_across = [send(block, beside(2)) for block in dx_across]
    up2_in, up3 = after((up2_in, up3), down2, down1, dx_across[0])
    down2, down1 = send(down2, cross), send(down1, swap)
    up2, up1 = send(add(up2, up2_in), cross), send(add(up1, up3), swap)

    back = [dx_own, send(dx_beside, beside(1)), dx_across[0], send(dx_across[1], beside(1))]
    grad_acts = unpack(place_back.T, back, tokens)
    raw_up = up0 + up2.astype(F32) + up1.astype(F32)
    raw_down = down0 + down2.astype(F32) + down1.astype(F32)
    return (grad_acts,) + clipped(raw_down, raw_up, ndevices, add_up)


def solution(mesh):
    plane = 4
    by_planes = mesh.shape["dp"] == 4 * plane

    def per_device(*arrays):
        if by_planes:
            return move_adapters(plane, *arrays)
        return move_tokens(*arrays)

    rows, pools = P(("parts", "dp"), None), P(("parts", "dp"), None, None)
    return jax.shard_map(
        per_device,
        mesh=mesh,
        in_specs=(rows, rows, rows, P("parts"), pools, pools),
        out_specs=(rows, pools, pools),
        check_vma=False,
    )
```

```python
import jax
import jax.numpy as jnp
from jax import lax
from jax.experimental import pallas as pl
from jax.experimental.pallas import tpu as pltpu
from jax.sharding import PartitionSpec as P

BF16, F32 = jnp.bfloat16, jnp.float32
ROWS_OF = (((1,), (1,)), ((), ()))
OUTER = (((0,), (0,)), ((), ()))
INNER = (((1,), (0,)), ((), ()))
HBM = pl.BlockSpec(memory_space=pltpu.HBM)
WHOLE = pl.BlockSpec(memory_space=pltpu.VMEM)
VMEM_BYTES = 20 * 2**20


def dot32(a, b, dims=INNER):
    return lax.dot_general(a, b, dims, preferred_element_type=F32)


def route(token_task_index, task_slot_lookup, ndevices):
    pool = task_slot_lookup.shape[0]
    task_hot = (token_task_index == jnp.arange(pool, dtype=jnp.int32)[None, :]).astype(jnp.int32)
    owner = jnp.sum(task_hot * task_slot_lookup[None, :], axis=1)
    owner_hot = (owner[:, None] == jnp.arange(ndevices, dtype=jnp.int32)[None, :]).astype(jnp.int32)
    before = jnp.cumsum(owner_hot, axis=0) - owner_hot
    position = jnp.sum(before * owner_hot, axis=1)
    return owner, position


def clipped(raw_down, raw_up, ndevices, add_up):
    local_sq = jnp.sum(raw_down * raw_down) + jnp.sum(raw_up * raw_up)
    total = add_up(local_sq)
    norm = jnp.sqrt(total + 1e-06)
    limit = jnp.sqrt(jnp.float32(2 * raw_down.shape[0] * raw_down.shape[1] * ndevices))
    factor = jnp.minimum(jnp.float32(1.0), limit / norm)
    return (raw_down * factor)[None], (raw_up * factor)[None]


def move_tokens(acts, cotan, token_task_index, task_slot_lookup, pool_down_factors, pool_up_factors):
    ndevices = lax.axis_size("dp")
    tokens, width = acts.shape
    capacity = 2 * ((tokens + ndevices - 1) // ndevices)
    slots = ndevices * capacity
    owner, position = route(token_task_index, task_slot_lookup, ndevices)
    dest = owner * capacity + position
    placed = (jnp.arange(slots, dtype=jnp.int32)[:, None] == dest[None, :]).astype(BF16)

    def exchange(rows):
        rows = rows.reshape(ndevices, capacity, width)
        return lax.all_to_all(rows, "dp", split_axis=0, concat_axis=0, tiled=True).reshape(slots, width)

    down, up = pool_down_factors[0], pool_up_factors[0]
    rows_x = exchange(dot32(placed, acts).astype(BF16))
    rows_g = exchange(dot32(placed, cotan).astype(BF16))
    hidden = dot32(rows_x, down, ROWS_OF).astype(BF16)
    inner = dot32(rows_g, up, ROWS_OF).astype(BF16)
    returned = exchange(dot32(inner, down).astype(BF16))
    grad_acts = dot32(placed, returned, OUTER).astype(BF16)
    raw_up = dot32(hidden, rows_g, OUTER)
    raw_down = dot32(inner, rows_x, OUTER)
    return (grad_acts,) + clipped(raw_down, raw_up, ndevices, lambda term: lax.psum(term, "dp"))


def in_hbm(*arrays):
    return [pltpu.with_memory_space_constraint(a, pltpu.HBM) for a in arrays]


def in_vmem(*arrays):
    return [pltpu.with_memory_space_constraint(a, pltpu.VMEM) for a in arrays]


def kernel_params(semantics=("arbitrary",)):
    return pltpu.CompilerParams(dimension_semantics=semantics, vmem_limit_bytes=VMEM_BYTES)


def pack(place, acts, cotan, shapes):
    tokens, width = acts.shape
    tile = min(width, 1024)
    tiles = width // tile

    def body(place_ref, x_in, g_in, *refs):
        out_refs, (rows, sems) = refs[:-2], refs[-2:]
        step = pl.program_id(0)

        def copies(i):
            cut = pl.ds(pl.multiple_of(i * tile, tile), tile)
            return [pltpu.make_async_copy(r.at[:, cut], rows.at[k, :, cut], sems.at[k, i]) for k, r in enumerate((x_in, g_in))]

        @pl.when(step == 0)
        def _():
            for i in range(tiles):
                for c in copies(i):
                    c.start()

        for c in copies(step):
            c.wait()
        cut = pl.ds(pl.multiple_of(step * tile, tile), tile)
        for k in range(2):
            moved = dot32(place_ref[...], rows[k, :, cut]).astype(BF16)
            first = 0
            for out_ref, (columns, size) in zip(out_refs, shapes):
                for c in range(columns):
                    out_ref[c, k] = moved[first:first + size]
                    first += size

    return pl.pallas_call(
        body,
        grid=(tiles,),
        in_specs=[pl.BlockSpec(place.shape, lambda i: (0, 0)), HBM, HBM],
        out_specs=[pl.BlockSpec((c, 2, size, tile), lambda i: (0, 0, 0, i)) for c, size in shapes],
        out_shape=[jax.ShapeDtypeStruct((c, 2, size, width), BF16) for c, size in shapes],
        scratch_shapes=[pltpu.VMEM((2, tokens, width), BF16), pltpu.SemaphoreType.DMA((2, tiles))],
        compiler_params=kernel_params(),
    )(place, *in_hbm(acts, cotan))


def unpack(place, blocks, tokens):
    width = blocks[0].shape[1]
    tile = min(width, 2048)

    def body(place_ref, *refs):
        rows = jnp.concatenate([ref[...] for ref in refs[:-1]], axis=0)
        refs[-1][...] = dot32(place_ref[...], rows).astype(BF16)

    return pl.pallas_call(
        body,
        grid=(width // tile,),
        in_specs=[pl.BlockSpec(place.shape, lambda i: (0, 0))]
        + [pl.BlockSpec((b.shape[0], tile), lambda i: (0, i)) for b in blocks],
        out_specs=pl.BlockSpec((tokens, tile), lambda i: (0, i)),
        out_shape=jax.ShapeDtypeStruct((tokens, width), BF16),
        compiler_params=kernel_params(),
    )(place, *in_hbm(blocks[0]), *blocks[1:])


def corner(rows, first_rows, columns, first_columns):
    upper = lax.broadcasted_iota(jnp.int32, (rows, columns), 0) < first_rows
    return upper == (lax.broadcasted_iota(jnp.int32, (rows, columns), 1) < first_columns)


def far_group(is_end, rows, factors, handed=None, terms=(0, 1)):
    _, block, width = rows[0].shape
    rank = factors[0].shape[1]
    tile = min(width, 2048)
    tiles = width // tile
    total = block if handed is None else 2 * block

    def body(end_ref, *refs):
        rows_in, refs = refs[:len(rows)], refs[len(rows):]
        factors_in, refs = refs[:len(factors)], refs[len(factors):]
        handed_in, refs = (None, refs) if handed is None else (refs[0], refs[1:])
        outs, (held, left, sems) = list(refs[:-3]), refs[-3:]
        step = pl.program_id(0)
        at_end = end_ref[0] == 1

        def copy(source, i):
            cut = pl.ds(i * tile, tile)
            return pltpu.make_async_copy(source.at[:, :, cut], held.at[:, :, cut], sems.at[i])

        def tokens(k, cut):
            own = held[k, :, cut]
            return own if handed is None else jnp.concatenate([own, handed_in[k, :, cut]], axis=0)

        def factor(k, cut):
            first = factors_in[0][k, :, cut]
            return first if len(factors) == 1 else jnp.where(at_end, factors_in[1][k, :, cut], first)

        @pl.when(step == 0)
        def _():
            for n, source in enumerate(rows_in):
                chosen = at_end == (n == 1) if len(rows) == 2 else step == 0

                @pl.when(chosen)
                def _(source=source):
                    for i in range(tiles):
                        copy(source, i).start()

            sums = {k: jnp.zeros((rank, total), F32) for k in terms}
            for i in range(tiles):
                copy(rows_in[0], i).wait()
                cut = pl.ds(i * tile, tile)
                for k in terms:
                    sums[k] += dot32(factor(k, cut), tokens(k, cut), ROWS_OF)
            for k in terms:
                left[k] = sums[k].astype(BF16)

        cut = pl.ds(pl.multiple_of(step * tile, tile), tile)
        for out, k in zip(outs, terms):
            out[...] = dot32(left[k], tokens(1 - k, cut)).astype(BF16)
        if 1 in terms:
            dx = dot32(left[1], factor(0, cut), OUTER).astype(BF16)
            outs[len(terms)][...] = dx[:block]
            if handed is not None:
                outs[-1][...] = jnp.where(at_end, outs[len(terms) - 1][...], dx[block:])

    outs = len(terms) + (0 if 1 not in terms else 1 if handed is None else 2)
    more = () if handed is None else (handed,)
    return pl.pallas_call(
        body,
        grid=(tiles,),
        in_specs=[pl.BlockSpec(memory_space=pltpu.SMEM)] + [HBM] * len(rows) + [WHOLE] * (len(factors) + len(more)),
        out_specs=[pl.BlockSpec((rank, tile), lambda i: (0, i))] * outs,
        out_shape=[jax.ShapeDtypeStruct((rank, width), BF16)] * outs,
        scratch_shapes=[
            pltpu.VMEM((2, block, width), BF16),
            pltpu.VMEM((2, rank, total), BF16),
            pltpu.SemaphoreType.DMA((tiles,)),
        ],
        compiler_params=kernel_params(),
    )(is_end, *in_hbm(*rows), *in_vmem(*factors, *more))


def near_groups(is_end, stage, pair, down, up, dx_late, dx_early, swapped, capacity, first1):
    plane = len(stage)
    rank, width = down.shape
    block = plane * capacity
    tile = min(width, 2048)
    tiles = width // tile

    def body(end_ref, *refs):
        stage_in, refs = refs[:plane], refs[plane:]
        pair_in, down_in, up_in, late_ref, early_ref, swapped_ref = refs[:6]
        dx_refs, sum_refs = refs[6:10], refs[10:14]
        (left,) = refs[14:]
        step = pl.program_id(0)
        own_in = (down_in, up_in)
        is_mine = corner(2 * block, block, 2 * rank, rank)

        def rows(k, cut):
            return jnp.concatenate(
                [
                    r[0, k, pl.ds(first + n * capacity, capacity), cut]
                    for n in range(2)
                    for r, first in zip(stage_in, first1)
                ],
                axis=0,
            )

        @pl.when(step == 0)
        def _():
            sums = [jnp.zeros((2 * block, 2 * rank), F32)] * 2
            for i in range(tiles):
                cut = pl.ds(i * tile, tile)
                for k in range(2):
                    both = jnp.concatenate([pair_in[k, :, cut], own_in[k][:, cut]], axis=0)
                    sums[k] += dot32(rows(k, cut), both, ROWS_OF)
            for k in range(2):
                left[k] = jnp.where(is_mine, sums[k], 0.0).astype(BF16)

        cut = pl.ds(pl.multiple_of(step * tile, tile), tile)
        for k in range(2):
            both = dot32(left[k], rows(1 - k, cut), OUTER)
            sum_refs[k][...] = both[:rank]
            sum_refs[2 + k][...] = both[rank:]
        downs = jnp.concatenate([pair_in[0, :, cut], down_in[:, cut]], axis=0)
        dx = dot32(left[1], downs).astype(BF16)
        at_end, late = end_ref[0] == 1, late_ref[...]
        moved = [jnp.where(at_end, swapped_ref[...], late), jnp.where(at_end, late, early_ref[...]), dx[:block], dx[block:]]
        for n, dx in enumerate(moved):
            for m in range(plane):
                dx_refs[m][n * capacity:(n + 1) * capacity] = dx[m * capacity:(m + 1) * capacity]

    return pl.pallas_call(
        body,
        grid=(tiles,),
        in_specs=[pl.BlockSpec(memory_space=pltpu.SMEM)]
        + [WHOLE] * (plane + 3)
        + [pl.BlockSpec((block, tile), lambda i: (0, i))] * 3,
        out_specs=[pl.BlockSpec((4 * capacity, tile), lambda i: (0, i))] * plane
        + [pl.BlockSpec((rank, tile), lambda i: (0, i))] * 4,
        out_shape=[jax.ShapeDtypeStruct((4 * capacity, width), BF16)] * plane
        + [jax.ShapeDtypeStruct((rank, width), F32)] * 4,
        scratch_shapes=[pltpu.VMEM((2, 2 * block, 2 * rank), BF16)],
        compiler_params=kernel_params(),
    )(is_end, *in_vmem(*stage, pair, down, up), dx_late, dx_early, swapped)


def move_adapters(plane, acts, cotan, token_task_index, task_slot_lookup, pool_down_factors, pool_up_factors):
    ndevices = lax.axis_size("dp")
    tokens, width = acts.shape
    capacity = 2 * ((tokens + ndevices - 1) // ndevices)
    me = lax.axis_index("dp")
    z, column = me // plane, me % plane
    is_end = (z == 0) | (z == 3)
    end_flag = is_end.astype(jnp.int32).reshape(1)

    def planes(pairs):
        return [(a * plane + c, b * plane + c) for a, b in pairs for c in range(plane)]

    swap = planes([(0, 1), (1, 0), (2, 3), (3, 2)])
    cross = planes([(1, 2), (2, 1)])
    outward = planes([(1, 0), (2, 3)])
    inward = planes([(0, 1), (3, 2)])

    def send(array, pairs):
        return lax.ppermute(array, "dp", pairs)

    def after(arrays, *others):
        return lax.optimization_barrier((arrays, others))[0]

    def beside(m):
        return [(i, (i // plane) * plane + ((i % plane) ^ m)) for i in range(ndevices)]

    def add_up(term):
        around = [beside(m) for m in range(1, plane)]
        along = [[(i, (i // plane ^ m) * plane + i % plane) for i in range(ndevices)] for m in range(1, 4)]
        term = jnp.broadcast_to(term, (8, 128))
        term = term + sum(send(term, pairs) for pairs in around)
        term = after(term, dx_across[1])
        return (term + sum(after([send(term, pairs) for pairs in along], grad_acts)))[0, 0]

    down, up = pool_down_factors[0], pool_up_factors[0]
    own = jnp.concatenate([pool_down_factors, pool_up_factors])
    pair = send(own, swap)
    crossed = send(own, cross)

    owner, position = route(token_task_index, task_slot_lookup, ndevices)
    owner_z, turn = owner // plane, (owner % plane) ^ column
    other_mid = jnp.where(z < 2, 2, 1)
    kind = jnp.where(owner_z == z, 0, jnp.where(owner_z == (z ^ 1), 1, jnp.where(owner_z == other_mid, 2, 3)))

    def places(wanted, row, rows):
        hot = jnp.arange(rows, dtype=jnp.int32)[:, None] == row[None, :]
        return (hot & wanted[None, :]).astype(BF16)

    def after(arrays, *others):
        return lax.optimization_barrier((arrays, others))[0]

    block = plane * capacity
    mine = (3 - kind) * capacity + position
    row = jnp.where(kind == 2, 10 * capacity, 12 * capacity) + (turn - 2) * jnp.where(kind == 2, capacity, 2 * capacity)
    row += jnp.where(kind == 2, 0, (1 - kind) * capacity) + position
    row = jnp.where(kind == 3, (6 + turn) * capacity + position, row)
    row = jnp.where(turn < 2, turn * block + mine, row)
    place = places(kind >= 0, row, 4 * block)
    place_back = places(kind >= 0, turn * block + mine, 4 * block)
    own_rows, beside_rows, across3, across2, across10 = pack(
        place, acts, cotan, [(1, 4 * capacity)] * 2 + [(2, capacity)] * 2 + [(2, 2 * capacity)]
    )

    def over_x(blocks):
        moved = send(blocks, beside(2))
        return moved, send(moved[1:], beside(1))

    beside_rows = send(beside_rows, beside(1))
    across3 = over_x(across3)
    stage3 = (own_rows, beside_rows) + across3
    rows3 = jnp.concatenate([r[0, :, :capacity] for r in stage3], axis=1)
    handed = send(rows3, inward)
    across2 = over_x(after(across2, across3[0]))
    across10 = over_x(after(across10, across2[0]))
    rows2 = [r[0, :, capacity:2 * capacity] for r in (own_rows, beside_rows)] + [r[0] for r in across2]
    rows2 = jnp.concatenate(rows2, axis=1)
    stage10 = (own_rows, beside_rows) + across10
    outer = send(crossed, outward)
    far = send(pair, cross)

    up2, down2, dx_early = far_group(end_flag, (rows2,), (crossed,))
    rows3, rows2 = after((rows3, rows2), dx_early)
    down3, dx_late, swapped = far_group(end_flag, (rows3, rows2), (far, outer), handed, (1,))
    (up3,) = far_group(after(end_flag, dx_late), (rows3, rows2), (far, outer), handed, (0,))
    down3, swapped = send(down3, cross), send(swapped, swap)
    up3, up2_in = send(up3, cross), send(up3, inward)

    swapped, down3 = lax.optimization_barrier((swapped, down3))
    dx_own, dx_beside, *dx_across, up1, down1, up0, down0 = near_groups(
        end_flag, stage10, pair, down, up, dx_late, dx_early, swapped, capacity,
        (2 * capacity, 2 * capacity, 0, 0),
    )

    def add(a, b):
        return (a.astype(F32) + b.astype(F32)).astype(BF16)

    down2, down1 = add(down2, swapped), add(down1, down3)
    dx_across = [send(block, beside(2)) for block in dx_across]
    up2_in, up3 = after((up2_in, up3), down2, down1, dx_across[0])
    down2, down1 = send(down2, cross), send(down1, swap)
    up2, up1 = send(add(up2, up2_in), cross), send(add(up1, up3), swap)

    back = [dx_own, send(dx_beside, beside(1)), dx_across[0], send(dx_across[1], beside(1))]
    grad_acts = unpack(place_back.T, back, tokens)
    raw_up = up0 + up2.astype(F32) + up1.astype(F32)
    raw_down = down0 + down2.astype(F32) + down1.astype(F32)
    return (grad_acts,) + clipped(raw_down, raw_up, ndevices, add_up)


def solution(mesh):
    plane = 4
    by_planes = mesh.shape["dp"] == 4 * plane

    def per_device(*arrays):
        if by_planes:
            return move_adapters(plane, *arrays)
        return move_tokens(*arrays)

    rows, pools = P(("parts", "dp"), None), P(("parts", "dp"), None, None)
    return jax.shard_map(
        per_device,
        mesh=mesh,
        in_specs=(rows, rows, rows, P("parts"), pools, pools),
        out_specs=(rows, pools, pools),
        check_vma=False,
    )
```

```python
import jax
import jax.numpy as jnp
from jax import lax
from jax.experimental import pallas as pl
from jax.experimental.pallas import tpu as pltpu
from jax.sharding import PartitionSpec as P

BF16, F32 = jnp.bfloat16, jnp.float32
ROWS_OF = (((1,), (1,)), ((), ()))
OUTER = (((0,), (0,)), ((), ()))
INNER = (((1,), (0,)), ((), ()))
HBM = pl.BlockSpec(memory_space=pltpu.HBM)
WHOLE = pl.BlockSpec(memory_space=pltpu.VMEM)
VMEM_BYTES = 20 * 2**20


def dot32(a, b, dims=INNER):
    return lax.dot_general(a, b, dims, preferred_element_type=F32)


def route(token_task_index, task_slot_lookup, ndevices):
    pool = task_slot_lookup.shape[0]
    task_hot = (token_task_index == jnp.arange(pool, dtype=jnp.int32)[None, :]).astype(jnp.int32)
    owner = jnp.sum(task_hot * task_slot_lookup[None, :], axis=1)
    owner_hot = (owner[:, None] == jnp.arange(ndevices, dtype=jnp.int32)[None, :]).astype(jnp.int32)
    before = jnp.cumsum(owner_hot, axis=0) - owner_hot
    position = jnp.sum(before * owner_hot, axis=1)
    return owner, position


def clipped(raw_down, raw_up, ndevices, add_up):
    local_sq = jnp.sum(raw_down * raw_down) + jnp.sum(raw_up * raw_up)
    total = add_up(local_sq)
    norm = jnp.sqrt(total + 1e-06)
    limit = jnp.sqrt(jnp.float32(2 * raw_down.shape[0] * raw_down.shape[1] * ndevices))
    factor = jnp.minimum(jnp.float32(1.0), limit / norm)
    return (raw_down * factor)[None], (raw_up * factor)[None]


def move_tokens(acts, cotan, token_task_index, task_slot_lookup, pool_down_factors, pool_up_factors):
    ndevices = lax.axis_size("dp")
    tokens, width = acts.shape
    capacity = 2 * ((tokens + ndevices - 1) // ndevices)
    slots = ndevices * capacity
    owner, position = route(token_task_index, task_slot_lookup, ndevices)
    dest = owner * capacity + position
    placed = (jnp.arange(slots, dtype=jnp.int32)[:, None] == dest[None, :]).astype(BF16)

    def exchange(rows):
        rows = rows.reshape(ndevices, capacity, width)
        return lax.all_to_all(rows, "dp", split_axis=0, concat_axis=0, tiled=True).reshape(slots, width)

    down, up = pool_down_factors[0], pool_up_factors[0]
    rows_x = exchange(dot32(placed, acts).astype(BF16))
    rows_g = exchange(dot32(placed, cotan).astype(BF16))
    hidden = dot32(rows_x, down, ROWS_OF).astype(BF16)
    inner = dot32(rows_g, up, ROWS_OF).astype(BF16)
    returned = exchange(dot32(inner, down).astype(BF16))
    grad_acts = dot32(placed, returned, OUTER).astype(BF16)
    raw_up = dot32(hidden, rows_g, OUTER)
    raw_down = dot32(inner, rows_x, OUTER)
    return (grad_acts,) + clipped(raw_down, raw_up, ndevices, lambda term: lax.psum(term, "dp"))


def in_hbm(*arrays):
    return [pltpu.with_memory_space_constraint(a, pltpu.HBM) for a in arrays]


def in_vmem(*arrays):
    return [pltpu.with_memory_space_constraint(a, pltpu.VMEM) for a in arrays]


def kernel_params(semantics=("arbitrary",)):
    return pltpu.CompilerParams(dimension_semantics=semantics, vmem_limit_bytes=VMEM_BYTES)


def pack(place, acts, cotan, shapes):
    tokens, width = acts.shape
    tile = min(width, 1024)
    tiles = width // tile

    def body(place_ref, x_in, g_in, *refs):
        out_refs, (rows, sems) = refs[:-2], refs[-2:]
        step = pl.program_id(0)

        def copies(i):
            cut = pl.ds(pl.multiple_of(i * tile, tile), tile)
            return [pltpu.make_async_copy(r.at[:, cut], rows.at[k, :, cut], sems.at[k, i]) for k, r in enumerate((x_in, g_in))]

        @pl.when(step == 0)
        def _():
            for i in range(tiles):
                for c in copies(i):
                    c.start()

        for c in copies(step):
            c.wait()
        cut = pl.ds(pl.multiple_of(step * tile, tile), tile)
        for k in range(2):
            moved = dot32(place_ref[...], rows[k, :, cut]).astype(BF16)
            first = 0
            for out_ref, (columns, size) in zip(out_refs, shapes):
                for c in range(columns):
                    out_ref[c, k] = moved[first:first + size]
                    first += size

    return pl.pallas_call(
        body,
        grid=(tiles,),
        in_specs=[pl.BlockSpec(place.shape, lambda i: (0, 0)), HBM, HBM],
        out_specs=[pl.BlockSpec((c, 2, size, tile), lambda i: (0, 0, 0, i)) for c, size in shapes],
        out_shape=[jax.ShapeDtypeStruct((c, 2, size, width), BF16) for c, size in shapes],
        scratch_shapes=[pltpu.VMEM((2, tokens, width), BF16), pltpu.SemaphoreType.DMA((2, tiles))],
        compiler_params=kernel_params(),
    )(place, *in_hbm(acts, cotan))


def unpack(place, blocks, tokens):
    width = blocks[0].shape[1]
    tile = min(width, 2048)

    def body(place_ref, *refs):
        rows = jnp.concatenate([ref[...] for ref in refs[:-1]], axis=0)
        refs[-1][...] = dot32(place_ref[...], rows).astype(BF16)

    return pl.pallas_call(
        body,
        grid=(width // tile,),
        in_specs=[pl.BlockSpec(place.shape, lambda i: (0, 0))]
        + [pl.BlockSpec((b.shape[0], tile), lambda i: (0, i)) for b in blocks],
        out_specs=pl.BlockSpec((tokens, tile), lambda i: (0, i)),
        out_shape=jax.ShapeDtypeStruct((tokens, width), BF16),
        compiler_params=kernel_params(),
    )(place, *in_hbm(blocks[0]), *blocks[1:])


def corner(rows, first_rows, columns, first_columns):
    upper = lax.broadcasted_iota(jnp.int32, (rows, columns), 0) < first_rows
    return upper == (lax.broadcasted_iota(jnp.int32, (rows, columns), 1) < first_columns)


def far_group(is_end, rows, factors, handed=None):
    _, block, width = rows[0].shape
    rank = factors[0].shape[1]
    tile = min(width, 2048)
    tiles = width // tile
    total = block if handed is None else 2 * block

    def body(end_ref, *refs):
        rows_in, refs = refs[:len(rows)], refs[len(rows):]
        factors_in, refs = refs[:len(factors)], refs[len(factors):]
        handed_in, refs = (None, refs) if handed is None else (refs[0], refs[1:])
        (up_ref, down_ref, dx_ref), (held, left, inner, sems) = refs[:3], refs[-4:]
        step = pl.program_id(0)
        at_end = end_ref[0] == 1

        def copy(source, i):
            cut = pl.ds(i * tile, tile)
            return pltpu.make_async_copy(source.at[:, :, cut], held.at[:, :, cut], sems.at[i])

        def tokens(k, cut):
            own = held[k, :, cut]
            return own if handed is None else jnp.concatenate([own, handed_in[k, :, cut]], axis=0)

        def factor(k, cut):
            first = factors_in[0][k, :, cut]
            return first if len(factors) == 1 else jnp.where(at_end, factors_in[1][k, :, cut], first)

        @pl.when(step == 0)
        def _():
            for n, source in enumerate(rows_in):
                chosen = at_end == (n == 1) if len(rows) == 2 else step == 0

                @pl.when(chosen)
                def _(source=source):
                    for i in range(tiles):
                        copy(source, i).start()

            sums = [jnp.zeros((total, rank), F32)] * 2
            for i in range(tiles):
                copy(rows_in[0], i).wait()
                cut = pl.ds(i * tile, tile)
                for k in range(2):
                    sums[k] += dot32(tokens(k, cut), factor(k, cut), ROWS_OF)
            for k in range(2):
                left[k] = sums[k].T.astype(BF16)
            inner[...] = sums[1].astype(BF16)

        cut = pl.ds(pl.multiple_of(step * tile, tile), tile)
        up_ref[...] = dot32(left[0], tokens(1, cut)).astype(BF16)
        down = dot32(left[1], tokens(0, cut)).astype(BF16)
        down_ref[...] = down
        dx = dot32(inner[...], factor(0, cut)).astype(BF16)
        dx_ref[...] = dx[:block]
        if handed is not None:
            refs[3][...] = jnp.where(at_end, down, dx[block:])

    sizes = (rank, rank, block) + (() if handed is None else (block,))
    more = () if handed is None else (handed,)
    return pl.pallas_call(
        body,
        grid=(tiles,),
        in_specs=[pl.BlockSpec(memory_space=pltpu.SMEM)] + [HBM] * len(rows) + [WHOLE] * (len(factors) + len(more)),
        out_specs=[pl.BlockSpec((n, tile), lambda i: (0, i)) for n in sizes],
        out_shape=[jax.ShapeDtypeStruct((n, width), BF16) for n in sizes],
        scratch_shapes=[
            pltpu.VMEM((2, block, width), BF16),
            pltpu.VMEM((2, rank, total), BF16),
            pltpu.VMEM((total, rank), BF16),
            pltpu.SemaphoreType.DMA((tiles,)),
        ],
        compiler_params=kernel_params(),
    )(is_end, *in_hbm(*rows), *in_vmem(*factors, *more))


def near_groups(is_end, stage, pair, down, up, dx_late, dx_early, swapped, capacity, first1):
    plane = len(stage)
    rank, width = down.shape
    block = plane * capacity
    tile = min(width, 2048)
    tiles = width // tile

    def body(end_ref, *refs):
        stage_in, refs = refs[:plane], refs[plane:]
        pair_in, down_in, up_in, late_ref, early_ref, swapped_ref = refs[:6]
        dx_refs, sum_refs = refs[6:10], refs[10:14]
        left, inner = refs[14:]
        step = pl.program_id(0)
        own_in = (down_in, up_in)
        is_mine = corner(2 * block, block, 2 * rank, rank)

        def rows(k, cut):
            return jnp.concatenate(
                [
                    r[0, k, pl.ds(first + n * capacity, capacity), cut]
                    for n in range(2)
                    for r, first in zip(stage_in, first1)
                ],
                axis=0,
            )

        @pl.when(step == 0)
        def _():
            sums = [jnp.zeros((2 * block, 2 * rank), F32)] * 2
            for i in range(tiles):
                cut = pl.ds(i * tile, tile)
                for k in range(2):
                    both = jnp.concatenate([pair_in[k, :, cut], own_in[k][:, cut]], axis=0)
                    sums[k] += dot32(rows(k, cut), both, ROWS_OF)
            for k in range(2):
                masked = jnp.where(is_mine, sums[k], 0.0)
                left[k] = masked.T.astype(BF16)
            inner[...] = masked.astype(BF16)

        cut = pl.ds(pl.multiple_of(step * tile, tile), tile)
        for k in range(2):
            both = dot32(left[k], rows(1 - k, cut))
            sum_refs[k][...] = both[:rank]
            sum_refs[2 + k][...] = both[rank:]
        downs = jnp.concatenate([pair_in[0, :, cut], down_in[:, cut]], axis=0)
        dx = dot32(inner[...], downs).astype(BF16)
        at_end, late = end_ref[0] == 1, late_ref[...]
        moved = [jnp.where(at_end, swapped_ref[...], late), jnp.where(at_end, late, early_ref[...]), dx[:block], dx[block:]]
        for n, dx in enumerate(moved):
            for m in range(plane):
                dx_refs[m][n * capacity:(n + 1) * capacity] = dx[m * capacity:(m + 1) * capacity]

    return pl.pallas_call(
        body,
        grid=(tiles,),
        in_specs=[pl.BlockSpec(memory_space=pltpu.SMEM)]
        + [WHOLE] * (plane + 3)
        + [pl.BlockSpec((block, tile), lambda i: (0, i))] * 3,
        out_specs=[pl.BlockSpec((4 * capacity, tile), lambda i: (0, i))] * plane
        + [pl.BlockSpec((rank, tile), lambda i: (0, i))] * 4,
        out_shape=[jax.ShapeDtypeStruct((4 * capacity, width), BF16)] * plane
        + [jax.ShapeDtypeStruct((rank, width), F32)] * 4,
        scratch_shapes=[pltpu.VMEM((2, 2 * rank, 2 * block), BF16), pltpu.VMEM((2 * block, 2 * rank), BF16)],
        compiler_params=kernel_params(),
    )(is_end, *in_vmem(*stage, pair, down, up), dx_late, dx_early, swapped)


def move_adapters(plane, acts, cotan, token_task_index, task_slot_lookup, pool_down_factors, pool_up_factors):
    ndevices = lax.axis_size("dp")
    tokens, width = acts.shape
    capacity = 2 * ((tokens + ndevices - 1) // ndevices)
    me = lax.axis_index("dp")
    z, column = me // plane, me % plane
    is_end = (z == 0) | (z == 3)
    end_flag = is_end.astype(jnp.int32).reshape(1)

    def planes(pairs):
        return [(a * plane + c, b * plane + c) for a, b in pairs for c in range(plane)]

    swap = planes([(0, 1), (1, 0), (2, 3), (3, 2)])
    cross = planes([(1, 2), (2, 1)])
    outward = planes([(1, 0), (2, 3)])
    inward = planes([(0, 1), (3, 2)])

    def send(array, pairs):
        return lax.ppermute(array, "dp", pairs)

    def after(arrays, *others):
        return lax.optimization_barrier((arrays, others))[0]

    def beside(m):
        return [(i, (i // plane) * plane + ((i % plane) ^ m)) for i in range(ndevices)]

    def add_up(term):
        around = [beside(m) for m in range(1, plane)]
        along = [[(i, (i // plane ^ m) * plane + i % plane) for i in range(ndevices)] for m in range(1, 4)]
        term = jnp.broadcast_to(term, (8, 128))
        term = term + sum(send(term, pairs) for pairs in around)
        term = after(term, dx_across[1])
        return (term + sum(after([send(term, pairs) for pairs in along], grad_acts)))[0, 0]

    down, up = pool_down_factors[0], pool_up_factors[0]
    own = jnp.concatenate([pool_down_factors, pool_up_factors])
    pair = send(own, swap)
    crossed = send(own, cross)

    owner, position = route(token_task_index, task_slot_lookup, ndevices)
    owner_z, turn = owner // plane, (owner % plane) ^ column
    other_mid = jnp.where(z < 2, 2, 1)
    kind = jnp.where(owner_z == z, 0, jnp.where(owner_z == (z ^ 1), 1, jnp.where(owner_z == other_mid, 2, 3)))

    def places(wanted, row, rows):
        hot = jnp.arange(rows, dtype=jnp.int32)[:, None] == row[None, :]
        return (hot & wanted[None, :]).astype(BF16)

    def after(arrays, *others):
        return lax.optimization_barrier((arrays, others))[0]

    block = plane * capacity
    mine = (3 - kind) * capacity + position
    row = jnp.where(kind == 2, 10 * capacity, 12 * capacity) + (turn - 2) * jnp.where(kind == 2, capacity, 2 * capacity)
    row += jnp.where(kind == 2, 0, (1 - kind) * capacity) + position
    row = jnp.where(kind == 3, (6 + turn) * capacity + position, row)
    row = jnp.where(turn < 2, turn * block + mine, row)
    place = places(kind >= 0, row, 4 * block)
    place_back = places(kind >= 0, turn * block + mine, 4 * block)
    own_rows, beside_rows, across3, across2, across10 = pack(
        place, acts, cotan, [(1, 4 * capacity)] * 2 + [(2, capacity)] * 2 + [(2, 2 * capacity)]
    )

    def over_x(blocks):
        moved = send(blocks, beside(2))
        return moved, send(moved[1:], beside(1))

    beside_rows = send(beside_rows, beside(1))
    across3 = over_x(across3)
    stage3 = (own_rows, beside_rows) + across3
    rows3 = jnp.concatenate([r[0, :, :capacity] for r in stage3], axis=1)
    handed = send(rows3, inward)
    across2 = over_x(after(across2, across3[0]))
    across10 = over_x(after(across10, across2[0]))
    rows2 = [r[0, :, capacity:2 * capacity] for r in (own_rows, beside_rows)] + [r[0] for r in across2]
    rows2 = jnp.concatenate(rows2, axis=1)
    stage10 = (own_rows, beside_rows) + across10
    outer = send(crossed, outward)
    far = send(pair, cross)

    up2, down2, dx_early = far_group(end_flag, (rows2,), (crossed,))
    rows3, rows2 = after((rows3, rows2), dx_early)
    up3, down3, dx_late, swapped = far_group(end_flag, (rows3, rows2), (far, outer), handed)
    up2_in = send(up3, inward)
    down3, swapped, up3 = send(down3, cross), send(swapped, swap), send(up3, cross)

    swapped, down3 = lax.optimization_barrier((swapped, down3))
    dx_own, dx_beside, *dx_across, up1, down1, up0, down0 = near_groups(
        end_flag, stage10, pair, down, up, dx_late, dx_early, swapped, capacity,
        (2 * capacity, 2 * capacity, 0, 0),
    )

    def add(a, b):
        return (a.astype(F32) + b.astype(F32)).astype(BF16)

    down2, down1 = add(down2, swapped), add(down1, down3)
    dx_across = [send(block, beside(2)) for block in dx_across]
    up2_in, up3 = after((up2_in, up3), down2, down1, dx_across[0])
    down2, down1 = send(down2, cross), send(down1, swap)
    up2, up1 = send(add(up2, up2_in), cross), send(add(up1, up3), swap)

    back = [dx_own, send(dx_beside, beside(1)), dx_across[0], send(dx_across[1], beside(1))]
    grad_acts = unpack(place_back.T, back, tokens)
    raw_up = up0 + up2.astype(F32) + up1.astype(F32)
    raw_down = down0 + down2.astype(F32) + down1.astype(F32)
    return (grad_acts,) + clipped(raw_down, raw_up, ndevices, add_up)


def solution(mesh):
    plane = 4
    by_planes = mesh.shape["dp"] == 4 * plane

    def per_device(*arrays):
        if by_planes:
            return move_adapters(plane, *arrays)
        return move_tokens(*arrays)

    rows, pools = P(("parts", "dp"), None), P(("parts", "dp"), None, None)
    return jax.shard_map(
        per_device,
        mesh=mesh,
        in_specs=(rows, rows, rows, P("parts"), pools, pools),
        out_specs=(rows, pools, pools),
        check_vma=False,
    )
```

```python
import jax
import jax.numpy as jnp
from jax import lax
from jax.experimental import pallas as pl
from jax.experimental.pallas import tpu as pltpu
from jax.sharding import PartitionSpec as P

BF16, F32 = jnp.bfloat16, jnp.float32
ROWS_OF = (((1,), (1,)), ((), ()))
OUTER = (((0,), (0,)), ((), ()))
INNER = (((1,), (0,)), ((), ()))
HBM = pl.BlockSpec(memory_space=pltpu.HBM)
WHOLE = pl.BlockSpec(memory_space=pltpu.VMEM)
VMEM_BYTES = 20 * 2**20


def dot32(a, b, dims=INNER):
    return lax.dot_general(a, b, dims, preferred_element_type=F32)


def route(token_task_index, task_slot_lookup, ndevices):
    pool = task_slot_lookup.shape[0]
    task_hot = (token_task_index == jnp.arange(pool, dtype=jnp.int32)[None, :]).astype(jnp.int32)
    owner = jnp.sum(task_hot * task_slot_lookup[None, :], axis=1)
    owner_hot = (owner[:, None] == jnp.arange(ndevices, dtype=jnp.int32)[None, :]).astype(jnp.int32)
    before = jnp.cumsum(owner_hot, axis=0) - owner_hot
    position = jnp.sum(before * owner_hot, axis=1)
    return owner, position


def clipped(raw_down, raw_up, ndevices, add_up):
    local_sq = jnp.sum(raw_down * raw_down) + jnp.sum(raw_up * raw_up)
    total = add_up(local_sq)
    norm = jnp.sqrt(total + 1e-06)
    limit = jnp.sqrt(jnp.float32(2 * raw_down.shape[0] * raw_down.shape[1] * ndevices))
    factor = jnp.minimum(jnp.float32(1.0), limit / norm)
    return (raw_down * factor)[None], (raw_up * factor)[None]


def move_tokens(acts, cotan, token_task_index, task_slot_lookup, pool_down_factors, pool_up_factors):
    ndevices = lax.axis_size("dp")
    tokens, width = acts.shape
    capacity = 2 * ((tokens + ndevices - 1) // ndevices)
    slots = ndevices * capacity
    owner, position = route(token_task_index, task_slot_lookup, ndevices)
    dest = owner * capacity + position
    placed = (jnp.arange(slots, dtype=jnp.int32)[:, None] == dest[None, :]).astype(BF16)

    def exchange(rows):
        rows = rows.reshape(ndevices, capacity, width)
        return lax.all_to_all(rows, "dp", split_axis=0, concat_axis=0, tiled=True).reshape(slots, width)

    down, up = pool_down_factors[0], pool_up_factors[0]
    rows_x = exchange(dot32(placed, acts).astype(BF16))
    rows_g = exchange(dot32(placed, cotan).astype(BF16))
    hidden = dot32(rows_x, down, ROWS_OF).astype(BF16)
    inner = dot32(rows_g, up, ROWS_OF).astype(BF16)
    returned = exchange(dot32(inner, down).astype(BF16))
    grad_acts = dot32(placed, returned, OUTER).astype(BF16)
    raw_up = dot32(hidden, rows_g, OUTER)
    raw_down = dot32(inner, rows_x, OUTER)
    return (grad_acts,) + clipped(raw_down, raw_up, ndevices, lambda term: lax.psum(term, "dp"))


def in_hbm(*arrays):
    return [pltpu.with_memory_space_constraint(a, pltpu.HBM) for a in arrays]


def in_vmem(*arrays):
    return [pltpu.with_memory_space_constraint(a, pltpu.VMEM) for a in arrays]


def kernel_params(semantics=("arbitrary",)):
    return pltpu.CompilerParams(dimension_semantics=semantics, vmem_limit_bytes=VMEM_BYTES)


def pack(place, acts, cotan, shapes):
    tokens, width = acts.shape
    tile = min(width, 1024)
    tiles = width // tile

    def body(place_ref, x_in, g_in, *refs):
        out_refs, (rows, sems) = refs[:-2], refs[-2:]
        step = pl.program_id(0)

        def copies(i):
            cut = pl.ds(pl.multiple_of(i * tile, tile), tile)
            return [pltpu.make_async_copy(r.at[:, cut], rows.at[k, :, cut], sems.at[k, i]) for k, r in enumerate((x_in, g_in))]

        @pl.when(step == 0)
        def _():
            for i in range(tiles):
                for c in copies(i):
                    c.start()

        for c in copies(step):
            c.wait()
        cut = pl.ds(pl.multiple_of(step * tile, tile), tile)
        for k in range(2):
            moved = dot32(place_ref[...], rows[k, :, cut]).astype(BF16)
            first = 0
            for out_ref, (columns, size) in zip(out_refs, shapes):
                for c in range(columns):
                    out_ref[c, k] = moved[first:first + size]
                    first += size

    return pl.pallas_call(
        body,
        grid=(tiles,),
        in_specs=[pl.BlockSpec(place.shape, lambda i: (0, 0)), HBM, HBM],
        out_specs=[pl.BlockSpec((c, 2, size, tile), lambda i: (0, 0, 0, i)) for c, size in shapes],
        out_shape=[jax.ShapeDtypeStruct((c, 2, size, width), BF16) for c, size in shapes],
        scratch_shapes=[pltpu.VMEM((2, tokens, width), BF16), pltpu.SemaphoreType.DMA((2, tiles))],
        compiler_params=kernel_params(),
    )(place, *in_hbm(acts, cotan))


def unpack(place, blocks, tokens, half, into=None):
    width = blocks[0].shape[1]
    tile = min(width // 2, 2048)
    first = half * (width // 2 // tile)
    rest = () if into is None else (into,)

    def body(place_ref, *refs):
        rows = jnp.concatenate([ref[...] for ref in refs[:len(blocks)]], axis=0)
        refs[-1][...] = dot32(place_ref[...], rows).astype(BF16)

    return pl.pallas_call(
        body,
        grid=(width // 2 // tile,),
        in_specs=[pl.BlockSpec(place.shape, lambda i: (0, 0))]
        + [pl.BlockSpec((b.shape[0], tile), lambda i: (0, i + first)) for b in blocks]
        + [pl.BlockSpec(memory_space=pl.ANY)] * len(rest),
        out_specs=pl.BlockSpec((tokens, tile), lambda i: (0, i + first)),
        out_shape=jax.ShapeDtypeStruct((tokens, width), BF16),
        input_output_aliases={1 + len(blocks): 0} if rest else {},
        compiler_params=kernel_params(),
    )(place, *in_hbm(blocks[0]), *blocks[1:], *rest)


def corner(rows, first_rows, columns, first_columns):
    upper = lax.broadcasted_iota(jnp.int32, (rows, columns), 0) < first_rows
    return upper == (lax.broadcasted_iota(jnp.int32, (rows, columns), 1) < first_columns)


def far_group(is_end, rows, factors, handed=None):
    _, block, width = rows[0].shape
    rank = factors[0].shape[1]
    tile = min(width, 2048)
    tiles = width // tile
    total = block if handed is None else 2 * block

    def body(end_ref, *refs):
        rows_in, refs = refs[:len(rows)], refs[len(rows):]
        factors_in, refs = refs[:len(factors)], refs[len(factors):]
        handed_in, refs = (None, refs) if handed is None else (refs[0], refs[1:])
        (up_ref, down_ref, dx_ref), (held, left, inner, sems) = refs[:3], refs[-4:]
        step = pl.program_id(0)
        at_end = end_ref[0] == 1

        def copy(source, i):
            cut = pl.ds(i * tile, tile)
            return pltpu.make_async_copy(source.at[:, :, cut], held.at[:, :, cut], sems.at[i])

        def tokens(k, cut):
            own = held[k, :, cut]
            return own if handed is None else jnp.concatenate([own, handed_in[k, :, cut]], axis=0)

        def factor(k, cut):
            first = factors_in[0][k, :, cut]
            return first if len(factors) == 1 else jnp.where(at_end, factors_in[1][k, :, cut], first)

        @pl.when(step == 0)
        def _():
            for n, source in enumerate(rows_in):
                chosen = at_end == (n == 1) if len(rows) == 2 else step == 0

                @pl.when(chosen)
                def _(source=source):
                    for i in range(tiles):
                        copy(source, i).start()

            sums = jnp.zeros((2 * total, 2 * rank), F32)
            for i in range(tiles):
                copy(rows_in[0], i).wait()
                cut = pl.ds(i * tile, tile)
                both = [jnp.concatenate([piece(k, cut) for k in range(2)], axis=0) for piece in (tokens, factor)]
                sums += dot32(*both, ROWS_OF)
            left[0] = sums[:total, :rank].T.astype(BF16)
            inner[...] = sums[total:, rank:].astype(BF16)
            left[1] = sums[total:, rank:].T.astype(BF16)

        cut = pl.ds(pl.multiple_of(step * tile, tile), tile)
        up_ref[...] = dot32(left[0], tokens(1, cut)).astype(BF16)
        down = dot32(left[1], tokens(0, cut)).astype(BF16)
        down_ref[...] = down
        dx = dot32(inner[...], factor(0, cut)).astype(BF16)
        dx_ref[...] = dx[:block]
        if handed is not None:
            refs[3][...] = jnp.where(at_end, down, dx[block:])

    sizes = (rank, rank, block) + (() if handed is None else (block,))
    more = () if handed is None else (handed,)
    return pl.pallas_call(
        body,
        grid=(tiles,),
        in_specs=[pl.BlockSpec(memory_space=pltpu.SMEM)] + [HBM] * len(rows) + [WHOLE] * (len(factors) + len(more)),
        out_specs=[pl.BlockSpec((n, tile), lambda i: (0, i)) for n in sizes],
        out_shape=[jax.ShapeDtypeStruct((n, width), BF16) for n in sizes],
        scratch_shapes=[
            pltpu.VMEM((2, block, width), BF16),
            pltpu.VMEM((2, rank, total), BF16),
            pltpu.VMEM((total, rank), BF16),
            pltpu.SemaphoreType.DMA((tiles,)),
        ],
        compiler_params=kernel_params(),
    )(is_end, *in_hbm(*rows), *in_vmem(*factors, *more))


def near_groups(is_end, stage, pair, down, up, dx_late, dx_early, swapped, capacity, first1):
    plane = len(stage)
    rank, width = down.shape
    block = plane * capacity
    tile = min(width, 2048)
    tiles = width // tile

    def body(end_ref, *refs):
        stage_in, refs = refs[:plane], refs[plane:]
        pair_in, down_in, up_in, late_ref, early_ref, swapped_ref = refs[:6]
        dx_refs, sum_refs = refs[6:10], refs[10:14]
        left, inner = refs[14:]
        step = pl.program_id(0)
        own_in = (down_in, up_in)
        is_mine = corner(2 * block, block, 2 * rank, rank)

        def rows(k, cut):
            return jnp.concatenate(
                [
                    r[0, k, pl.ds(first + n * capacity, capacity), cut]
                    for n in range(2)
                    for r, first in zip(stage_in, first1)
                ],
                axis=0,
            )

        @pl.when(step == 0)
        def _():
            sums = [jnp.zeros((2 * block, 2 * rank), F32)] * 2
            for i in range(tiles):
                cut = pl.ds(i * tile, tile)
                for k in range(2):
                    both = jnp.concatenate([pair_in[k, :, cut], own_in[k][:, cut]], axis=0)
                    sums[k] += dot32(rows(k, cut), both, ROWS_OF)
            for k in range(2):
                masked = jnp.where(is_mine, sums[k], 0.0)
                left[k] = masked.T.astype(BF16)
            inner[...] = masked.astype(BF16)

        cut = pl.ds(pl.multiple_of(step * tile, tile), tile)
        for k in range(2):
            both = dot32(left[k], rows(1 - k, cut))
            sum_refs[k][...] = both[:rank]
            sum_refs[2 + k][...] = both[rank:]
        downs = jnp.concatenate([pair_in[0, :, cut], down_in[:, cut]], axis=0)
        dx = dot32(inner[...], downs).astype(BF16)
        at_end, late = end_ref[0] == 1, late_ref[...]
        moved = [jnp.where(at_end, swapped_ref[...], late), jnp.where(at_end, late, early_ref[...]), dx[:block], dx[block:]]
        for n, dx in enumerate(moved):
            for m in range(plane):
                dx_refs[m][n * capacity:(n + 1) * capacity] = dx[m * capacity:(m + 1) * capacity]

    return pl.pallas_call(
        body,
        grid=(tiles,),
        in_specs=[pl.BlockSpec(memory_space=pltpu.SMEM)]
        + [WHOLE] * (plane + 3)
        + [pl.BlockSpec((block, tile), lambda i: (0, i))] * 3,
        out_specs=[pl.BlockSpec((4 * capacity, tile), lambda i: (0, i))] * plane
        + [pl.BlockSpec((rank, tile), lambda i: (0, i))] * 4,
        out_shape=[jax.ShapeDtypeStruct((4 * capacity, width), BF16)] * plane
        + [jax.ShapeDtypeStruct((rank, width), F32)] * 4,
        scratch_shapes=[pltpu.VMEM((2, 2 * rank, 2 * block), BF16), pltpu.VMEM((2 * block, 2 * rank), BF16)],
        compiler_params=kernel_params(),
    )(is_end, *in_vmem(*stage, pair, down, up), dx_late, dx_early, swapped)


def move_adapters(plane, acts, cotan, token_task_index, task_slot_lookup, pool_down_factors, pool_up_factors):
    ndevices = lax.axis_size("dp")
    tokens, width = acts.shape
    capacity = 2 * ((tokens + ndevices - 1) // ndevices)
    me = lax.axis_index("dp")
    z, column = me // plane, me % plane
    is_end = (z == 0) | (z == 3)
    end_flag = is_end.astype(jnp.int32).reshape(1)

    def planes(pairs):
        return [(a * plane + c, b * plane + c) for a, b in pairs for c in range(plane)]

    swap = planes([(0, 1), (1, 0), (2, 3), (3, 2)])
    cross = planes([(1, 2), (2, 1)])
    outward = planes([(1, 0), (2, 3)])
    inward = planes([(0, 1), (3, 2)])

    def send(array, pairs):
        return lax.ppermute(array, "dp", pairs)

    def after(arrays, *others):
        return lax.optimization_barrier((arrays, others))[0]

    def beside(m):
        return [(i, (i // plane) * plane + ((i % plane) ^ m)) for i in range(ndevices)]

    def add_up(term):
        around = [beside(m) for m in range(1, plane)]
        along = [[(i, (i // plane ^ m) * plane + i % plane) for i in range(ndevices)] for m in range(1, 4)]
        term = jnp.broadcast_to(term, (8, 128))
        term = term + sum(after([send(term, pairs) for pairs in around], half_acts))
        return (term + sum(after([send(term, pairs) for pairs in along], grad_acts)))[0, 0]

    down, up = pool_down_factors[0], pool_up_factors[0]
    own = jnp.concatenate([pool_down_factors, pool_up_factors])
    pair = send(own, swap)
    crossed = send(own, cross)

    owner, position = route(token_task_index, task_slot_lookup, ndevices)
    owner_z, turn = owner // plane, (owner % plane) ^ column
    other_mid = jnp.where(z < 2, 2, 1)
    kind = jnp.where(owner_z == z, 0, jnp.where(owner_z == (z ^ 1), 1, jnp.where(owner_z == other_mid, 2, 3)))

    def places(wanted, row, rows):
        hot = jnp.arange(rows, dtype=jnp.int32)[:, None] == row[None, :]
        return (hot & wanted[None, :]).astype(BF16)

    def after(arrays, *others):
        return lax.optimization_barrier((arrays, others))[0]

    block = plane * capacity
    mine = (3 - kind) * capacity + position
    row = jnp.where(kind == 2, 10 * capacity, 12 * capacity) + (turn - 2) * jnp.where(kind == 2, capacity, 2 * capacity)
    row += jnp.where(kind == 2, 0, (1 - kind) * capacity) + position
    row = jnp.where(kind == 3, (6 + turn) * capacity + position, row)
    row = jnp.where(turn < 2, turn * block + mine, row)
    place = places(kind >= 0, row, 4 * block)
    place_back = places(kind >= 0, turn * block + mine, 4 * block)
    own_rows, beside_rows, across3, across2, across10 = pack(
        place, acts, cotan, [(1, 4 * capacity)] * 2 + [(2, capacity)] * 2 + [(2, 2 * capacity)]
    )

    def over_x(blocks):
        moved = send(blocks, beside(2))
        return moved, send(moved[1:], beside(1))

    beside_rows = send(beside_rows, beside(1))
    across3 = over_x(across3)
    stage3 = (own_rows, beside_rows) + across3
    rows3 = jnp.concatenate([r[0, :, :capacity] for r in stage3], axis=1)
    handed = send(rows3, inward)
    across2 = over_x(after(across2, across3[0]))
    across10 = over_x(after(across10, across3[0]))
    rows2 = [r[0, :, capacity:2 * capacity] for r in (own_rows, beside_rows)] + [r[0] for r in across2]
    rows2 = jnp.concatenate(rows2, axis=1)
    stage10 = (own_rows, beside_rows) + across10
    outer = send(crossed, outward)
    far = send(pair, cross)

    up2, down2, dx_early = far_group(end_flag, (rows2,), (crossed,))
    rows3, rows2 = after((rows3, rows2), dx_early)
    up3, down3, dx_late, swapped = far_group(end_flag, (rows3, rows2), (far, outer), handed)
    down3, swapped = send(down3, cross), send(swapped, swap)
    up3, up2_in = send(up3, cross), send(up3, inward)

    down3, swapped = lax.optimization_barrier((down3, swapped))
    dx_own, dx_beside, *dx_across, up1, down1, up0, down0 = near_groups(
        end_flag, stage10, pair, down, up, dx_late, dx_early, swapped, capacity,
        (2 * capacity, 2 * capacity, 0, 0),
    )

    def add(a, b):
        return (a.astype(F32) + b.astype(F32)).astype(BF16)

    down2, down1 = add(down2, swapped), add(down1, down3)
    dx_across = [send(block, beside(2)) for block in dx_across]
    up3, up2_in = after((up3, up2_in), down2, down1, dx_across[0])
    down2, down1 = send(down2, cross), send(down1, swap)
    up2, up1 = send(add(up2, up2_in), cross), send(add(up1, up3), swap)

    back = [dx_own, send(dx_beside, beside(1)), dx_across[0], send(dx_across[1], beside(1))]
    half_acts = unpack(place_back.T, back, tokens, 0)
    grad_acts = unpack(place_back.T, back, tokens, 1, half_acts)
    raw_up = up0 + up2.astype(F32) + up1.astype(F32)
    raw_down = down0 + down2.astype(F32) + down1.astype(F32)
    return (grad_acts,) + clipped(raw_down, raw_up, ndevices, add_up)


def solution(mesh):
    plane = 4
    by_planes = mesh.shape["dp"] == 4 * plane

    def per_device(*arrays):
        if by_planes:
            return move_adapters(plane, *arrays)
        return move_tokens(*arrays)

    rows, pools = P(("parts", "dp"), None), P(("parts", "dp"), None, None)
    return jax.shard_map(
        per_device,
        mesh=mesh,
        in_specs=(rows, rows, rows, P("parts"), pools, pools),
        out_specs=(rows, pools, pools),
        check_vma=False,
    )
```

```python
import jax
import jax.numpy as jnp
from jax import lax
from jax.experimental import pallas as pl
from jax.experimental.pallas import tpu as pltpu
from jax.sharding import PartitionSpec as P

BF16, F32 = jnp.bfloat16, jnp.float32
ROWS_OF = (((1,), (1,)), ((), ()))
OUTER = (((0,), (0,)), ((), ()))
INNER = (((1,), (0,)), ((), ()))
HBM = pl.BlockSpec(memory_space=pltpu.HBM)
WHOLE = pl.BlockSpec(memory_space=pltpu.VMEM)
VMEM_BYTES = 20 * 2**20


def dot32(a, b, dims=INNER):
    return lax.dot_general(a, b, dims, preferred_element_type=F32)


def route(token_task_index, task_slot_lookup, ndevices):
    pool = task_slot_lookup.shape[0]
    task_hot = (token_task_index == jnp.arange(pool, dtype=jnp.int32)[None, :]).astype(jnp.int32)
    owner = jnp.sum(task_hot * task_slot_lookup[None, :], axis=1)
    owner_hot = (owner[:, None] == jnp.arange(ndevices, dtype=jnp.int32)[None, :]).astype(jnp.int32)
    before = jnp.cumsum(owner_hot, axis=0) - owner_hot
    position = jnp.sum(before * owner_hot, axis=1)
    return owner, position


def clipped(raw_down, raw_up, ndevices, add_up):
    local_sq = jnp.sum(raw_down * raw_down) + jnp.sum(raw_up * raw_up)
    total = add_up(local_sq)
    norm = jnp.sqrt(total + 1e-06)
    limit = jnp.sqrt(jnp.float32(2 * raw_down.shape[0] * raw_down.shape[1] * ndevices))
    factor = jnp.minimum(jnp.float32(1.0), limit / norm)
    return (raw_down * factor)[None], (raw_up * factor)[None]


def move_tokens(acts, cotan, token_task_index, task_slot_lookup, pool_down_factors, pool_up_factors):
    ndevices = lax.axis_size("dp")
    tokens, width = acts.shape
    capacity = 2 * ((tokens + ndevices - 1) // ndevices)
    slots = ndevices * capacity
    owner, position = route(token_task_index, task_slot_lookup, ndevices)
    dest = owner * capacity + position
    placed = (jnp.arange(slots, dtype=jnp.int32)[:, None] == dest[None, :]).astype(BF16)

    def exchange(rows):
        rows = rows.reshape(ndevices, capacity, width)
        return lax.all_to_all(rows, "dp", split_axis=0, concat_axis=0, tiled=True).reshape(slots, width)

    down, up = pool_down_factors[0], pool_up_factors[0]
    rows_x = exchange(dot32(placed, acts).astype(BF16))
    rows_g = exchange(dot32(placed, cotan).astype(BF16))
    hidden = dot32(rows_x, down, ROWS_OF).astype(BF16)
    inner = dot32(rows_g, up, ROWS_OF).astype(BF16)
    returned = exchange(dot32(inner, down).astype(BF16))
    grad_acts = dot32(placed, returned, OUTER).astype(BF16)
    raw_up = dot32(hidden, rows_g, OUTER)
    raw_down = dot32(inner, rows_x, OUTER)
    return (grad_acts,) + clipped(raw_down, raw_up, ndevices, lambda term: lax.psum(term, "dp"))


def in_hbm(*arrays):
    return [pltpu.with_memory_space_constraint(a, pltpu.HBM) for a in arrays]


def in_vmem(*arrays):
    return [pltpu.with_memory_space_constraint(a, pltpu.VMEM) for a in arrays]


def kernel_params(semantics=("arbitrary",)):
    return pltpu.CompilerParams(dimension_semantics=semantics, vmem_limit_bytes=VMEM_BYTES)


def pack(place, acts, cotan, shapes):
    tokens, width = acts.shape
    tile = min(width, 1024)
    tiles = width // tile

    def body(place_ref, x_in, g_in, *refs):
        out_refs, (rows, sems) = refs[:-2], refs[-2:]
        step = pl.program_id(0)

        def copies(i):
            cut = pl.ds(pl.multiple_of(i * tile, tile), tile)
            return [pltpu.make_async_copy(r.at[:, cut], rows.at[k, :, cut], sems.at[k, i]) for k, r in enumerate((x_in, g_in))]

        @pl.when(step == 0)
        def _():
            for i in range(tiles):
                for c in copies(i):
                    c.start()

        for c in copies(step):
            c.wait()
        cut = pl.ds(pl.multiple_of(step * tile, tile), tile)
        for k in range(2):
            moved = dot32(place_ref[...], rows[k, :, cut]).astype(BF16)
            first = 0
            for out_ref, (columns, size) in zip(out_refs, shapes):
                for c in range(columns):
                    out_ref[c, k] = moved[first:first + size]
                    first += size

    return pl.pallas_call(
        body,
        grid=(tiles,),
        in_specs=[pl.BlockSpec(place.shape, lambda i: (0, 0)), HBM, HBM],
        out_specs=[pl.BlockSpec((c, 2, size, tile), lambda i: (0, 0, 0, i)) for c, size in shapes],
        out_shape=[jax.ShapeDtypeStruct((c, 2, size, width), BF16) for c, size in shapes],
        scratch_shapes=[pltpu.VMEM((2, tokens, width), BF16), pltpu.SemaphoreType.DMA((2, tiles))],
        compiler_params=kernel_params(),
    )(place, *in_hbm(acts, cotan))


def unpack(place, blocks, tokens, half, into=None):
    width = blocks[0].shape[1]
    tile = min(width // 2, 2048)
    first = half * (width // 2 // tile)
    rest = () if into is None else (into,)

    def body(place_ref, *refs):
        rows = jnp.concatenate([ref[...] for ref in refs[:len(blocks)]], axis=0)
        refs[-1][...] = dot32(place_ref[...], rows).astype(BF16)

    return pl.pallas_call(
        body,
        grid=(width // 2 // tile,),
        in_specs=[pl.BlockSpec(place.shape, lambda i: (0, 0))]
        + [pl.BlockSpec((b.shape[0], tile), lambda i: (0, i + first)) for b in blocks]
        + [pl.BlockSpec(memory_space=pl.ANY)] * len(rest),
        out_specs=pl.BlockSpec((tokens, tile), lambda i: (0, i + first)),
        out_shape=jax.ShapeDtypeStruct((tokens, width), BF16),
        input_output_aliases={1 + len(blocks): 0} if rest else {},
        compiler_params=kernel_params(),
    )(place, *in_hbm(blocks[0]), *blocks[1:], *rest)


def corner(rows, first_rows, columns, first_columns):
    upper = lax.broadcasted_iota(jnp.int32, (rows, columns), 0) < first_rows
    return upper == (lax.broadcasted_iota(jnp.int32, (rows, columns), 1) < first_columns)


def stack(down, up):
    _, rank, width = down.shape

    def body(down_in, up_in, out, sems):
        copies = [pltpu.make_async_copy(r.at[0], out.at[k], sems.at[k]) for k, r in enumerate((down_in, up_in))]
        for c in copies:
            c.start()
        for c in copies:
            c.wait()

    return pl.pallas_call(
        body,
        in_specs=[HBM, HBM],
        out_specs=WHOLE,
        out_shape=pltpu.VMEM((2, rank, width), BF16),
        scratch_shapes=[pltpu.SemaphoreType.DMA((2,))],
        compiler_params=pltpu.CompilerParams(vmem_limit_bytes=VMEM_BYTES),
    )(*in_hbm(down, up))


def far_group(is_end, rows, factors, handed=None):
    _, block, width = rows[0].shape
    rank = factors[0].shape[1]
    tile = min(width, 2048)
    tiles = width // tile
    total = block if handed is None else 2 * block

    def body(end_ref, *refs):
        rows_in, refs = refs[:len(rows)], refs[len(rows):]
        factors_in, refs = refs[:len(factors)], refs[len(factors):]
        handed_in, refs = (None, refs) if handed is None else (refs[0], refs[1:])
        (up_ref, down_ref, dx_ref), (held, left, inner, sems) = refs[:3], refs[-4:]
        step = pl.program_id(0)
        at_end = end_ref[0] == 1

        def copy(source, i):
            cut = pl.ds(i * tile, tile)
            return pltpu.make_async_copy(source.at[:, :, cut], held.at[:, :, cut], sems.at[i])

        def tokens(k, cut):
            own = held[k, :, cut]
            return own if handed is None else jnp.concatenate([own, handed_in[k, :, cut]], axis=0)

        def factor(k, cut):
            first = factors_in[0][k, :, cut]
            return first if len(factors) == 1 else jnp.where(at_end, factors_in[1][k, :, cut], first)

        @pl.when(step == 0)
        def _():
            for n, source in enumerate(rows_in):
                chosen = at_end == (n == 1) if len(rows) == 2 else step == 0

                @pl.when(chosen)
                def _(source=source):
                    for i in range(tiles):
                        copy(source, i).start()

            sums = [jnp.zeros((total, rank), F32)] * 2
            for i in range(tiles):
                copy(rows_in[0], i).wait()
                cut = pl.ds(i * tile, tile)
                for k in range(2):
                    sums[k] += dot32(tokens(k, cut), factor(k, cut), ROWS_OF)
            for k in range(2):
                left[k] = sums[k].T.astype(BF16)
            inner[...] = sums[1].astype(BF16)

        cut = pl.ds(pl.multiple_of(step * tile, tile), tile)
        up_ref[...] = dot32(left[0], tokens(1, cut)).astype(BF16)
        down = dot32(left[1], tokens(0, cut)).astype(BF16)
        down_ref[...] = down
        dx = dot32(inner[...], factor(0, cut)).astype(BF16)
        dx_ref[...] = dx[:block]
        if handed is not None:
            refs[3][...] = jnp.where(at_end, down, dx[block:])

    sizes = (rank, rank, block) + (() if handed is None else (block,))
    more = () if handed is None else (handed,)
    return pl.pallas_call(
        body,
        grid=(tiles,),
        in_specs=[pl.BlockSpec(memory_space=pltpu.SMEM)] + [HBM] * len(rows) + [WHOLE] * (len(factors) + len(more)),
        out_specs=[pl.BlockSpec((n, tile), lambda i: (0, i)) for n in sizes],
        out_shape=[jax.ShapeDtypeStruct((n, width), BF16) for n in sizes],
        scratch_shapes=[
            pltpu.VMEM((2, block, width), BF16),
            pltpu.VMEM((2, rank, total), BF16),
            pltpu.VMEM((total, rank), BF16),
            pltpu.SemaphoreType.DMA((tiles,)),
        ],
        compiler_params=kernel_params(),
    )(is_end, *in_hbm(*rows), *in_vmem(*factors, *more))


def near_groups(is_end, stage, pair, down, up, dx_late, dx_early, swapped, capacity, first1):
    plane = len(stage)
    rank, width = down.shape
    block = plane * capacity
    tile = min(width, 2048)
    tiles = width // tile

    def body(end_ref, *refs):
        stage_in, refs = refs[:plane], refs[plane:]
        pair_in, down_in, up_in, late_ref, early_ref, swapped_ref = refs[:6]
        dx_refs, sum_refs = refs[6:10], refs[10:14]
        left, inner = refs[14:]
        step = pl.program_id(0)
        own_in = (down_in, up_in)
        is_mine = corner(2 * block, block, 2 * rank, rank)

        def rows(k, cut):
            return jnp.concatenate(
                [
                    r[0, k, pl.ds(first + n * capacity, capacity), cut]
                    for n in range(2)
                    for r, first in zip(stage_in, first1)
                ],
                axis=0,
            )

        @pl.when(step == 0)
        def _():
            sums = [jnp.zeros((2 * block, 2 * rank), F32)] * 2
            for i in range(tiles):
                cut = pl.ds(i * tile, tile)
                for k in range(2):
                    both = jnp.concatenate([pair_in[k, :, cut], own_in[k][:, cut]], axis=0)
                    sums[k] += dot32(rows(k, cut), both, ROWS_OF)
            for k in range(2):
                masked = jnp.where(is_mine, sums[k], 0.0)
                left[k] = masked.T.astype(BF16)
            inner[...] = masked.astype(BF16)

        cut = pl.ds(pl.multiple_of(step * tile, tile), tile)
        for k in range(2):
            both = dot32(left[k], rows(1 - k, cut))
            sum_refs[k][...] = both[:rank]
            sum_refs[2 + k][...] = both[rank:]
        downs = jnp.concatenate([pair_in[0, :, cut], down_in[:, cut]], axis=0)
        dx = dot32(inner[...], downs).astype(BF16)
        at_end, late = end_ref[0] == 1, late_ref[...]
        moved = [jnp.where(at_end, swapped_ref[...], late), jnp.where(at_end, late, early_ref[...]), dx[:block], dx[block:]]
        for n, dx in enumerate(moved):
            for m in range(plane):
                dx_refs[m][n * capacity:(n + 1) * capacity] = dx[m * capacity:(m + 1) * capacity]

    return pl.pallas_call(
        body,
        grid=(tiles,),
        in_specs=[pl.BlockSpec(memory_space=pltpu.SMEM)]
        + [WHOLE] * (plane + 3)
        + [pl.BlockSpec((block, tile), lambda i: (0, i))] * 3,
        out_specs=[pl.BlockSpec((4 * capacity, tile), lambda i: (0, i))] * plane
        + [pl.BlockSpec((rank, tile), lambda i: (0, i))] * 4,
        out_shape=[jax.ShapeDtypeStruct((4 * capacity, width), BF16)] * plane
        + [jax.ShapeDtypeStruct((rank, width), F32)] * 4,
        scratch_shapes=[pltpu.VMEM((2, 2 * rank, 2 * block), BF16), pltpu.VMEM((2 * block, 2 * rank), BF16)],
        compiler_params=kernel_params(),
    )(is_end, *in_vmem(*stage, pair, down, up), dx_late, dx_early, swapped)


def move_adapters(plane, acts, cotan, token_task_index, task_slot_lookup, pool_down_factors, pool_up_factors):
    ndevices = lax.axis_size("dp")
    tokens, width = acts.shape
    capacity = 2 * ((tokens + ndevices - 1) // ndevices)
    me = lax.axis_index("dp")
    z, column = me // plane, me % plane
    is_end = (z == 0) | (z == 3)
    end_flag = is_end.astype(jnp.int32).reshape(1)

    def planes(pairs):
        return [(a * plane + c, b * plane + c) for a, b in pairs for c in range(plane)]

    swap = planes([(0, 1), (1, 0), (2, 3), (3, 2)])
    cross = planes([(1, 2), (2, 1)])
    outward = planes([(1, 0), (2, 3)])
    inward = planes([(0, 1), (3, 2)])

    def send(array, pairs):
        return lax.ppermute(array, "dp", pairs)

    def after(arrays, *others):
        return lax.optimization_barrier((arrays, others))[0]

    def beside(m):
        return [(i, (i // plane) * plane + ((i % plane) ^ m)) for i in range(ndevices)]

    def add_up(term):
        around = [beside(m) for m in range(1, plane)]
        along = [[(i, (i // plane ^ m) * plane + i % plane) for i in range(ndevices)] for m in range(1, 4)]
        term = jnp.broadcast_to(term, (8, 128))
        term = term + sum(after([send(term, pairs) for pairs in around], half_acts))
        return (term + sum(after([send(term, pairs) for pairs in along], grad_acts)))[0, 0]

    down, up = pool_down_factors[0], pool_up_factors[0]
    own = stack(pool_down_factors, pool_up_factors)
    pair = send(own, swap)
    crossed = send(own, cross)

    owner, position = route(token_task_index, task_slot_lookup, ndevices)
    owner_z, turn = owner // plane, (owner % plane) ^ column
    other_mid = jnp.where(z < 2, 2, 1)
    kind = jnp.where(owner_z == z, 0, jnp.where(owner_z == (z ^ 1), 1, jnp.where(owner_z == other_mid, 2, 3)))

    def places(wanted, row, rows):
        hot = jnp.arange(rows, dtype=jnp.int32)[:, None] == row[None, :]
        return (hot & wanted[None, :]).astype(BF16)

    def after(arrays, *others):
        return lax.optimization_barrier((arrays, others))[0]

    block = plane * capacity
    mine = (3 - kind) * capacity + position
    row = jnp.where(kind == 2, 10 * capacity, 12 * capacity) + (turn - 2) * jnp.where(kind == 2, capacity, 2 * capacity)
    row += jnp.where(kind == 2, 0, (1 - kind) * capacity) + position
    row = jnp.where(kind == 3, (6 + turn) * capacity + position, row)
    row = jnp.where(turn < 2, turn * block + mine, row)
    place = places(kind >= 0, row, 4 * block)
    place_back = places(kind >= 0, turn * block + mine, 4 * block)
    own_rows, beside_rows, across3, across2, across10 = pack(
        place, acts, cotan, [(1, 4 * capacity)] * 2 + [(2, capacity)] * 2 + [(2, 2 * capacity)]
    )

    def over_x(blocks):
        moved = send(blocks, beside(2))
        return moved, send(moved[1:], beside(1))

    beside_rows = send(beside_rows, beside(1))
    across3 = over_x(across3)
    stage3 = (own_rows, beside_rows) + across3
    rows3 = jnp.concatenate([r[0, :, :capacity] for r in stage3], axis=1)
    handed = send(rows3, inward)
    across2 = over_x(after(across2, across3[0]))
    across10 = over_x(after(across10, across3[0]))
    rows2 = [r[0, :, capacity:2 * capacity] for r in (own_rows, beside_rows)] + [r[0] for r in across2]
    rows2 = jnp.concatenate(rows2, axis=1)
    stage10 = (own_rows, beside_rows) + across10
    outer = send(crossed, outward)
    far = send(pair, cross)

    up2, down2, dx_early = far_group(end_flag, (rows2,), (crossed,))
    rows3, rows2 = after((rows3, rows2), dx_early)
    up3, down3, dx_late, swapped = far_group(end_flag, (rows3, rows2), (far, outer), handed)
    down3, swapped = send(down3, cross), send(swapped, swap)
    up3, up2_in = send(up3, cross), send(up3, inward)

    down3, swapped = lax.optimization_barrier((down3, swapped))
    dx_own, dx_beside, *dx_across, up1, down1, up0, down0 = near_groups(
        end_flag, stage10, pair, down, up, dx_late, dx_early, swapped, capacity,
        (2 * capacity, 2 * capacity, 0, 0),
    )

    def add(a, b):
        return (a.astype(F32) + b.astype(F32)).astype(BF16)

    down2, down1 = add(down2, swapped), add(down1, down3)
    dx_across[0] = send(dx_across[0], beside(2))
    dx_across[1] = send(after(dx_across[1], dx_across[0]), beside(2))
    up3, up2_in = after((up3, up2_in), down2, down1, dx_across[0])
    down2, down1 = send(down2, cross), send(down1, swap)
    up2, up1 = send(add(up2, up2_in), cross), send(add(up1, up3), swap)

    back = [dx_own, send(dx_beside, beside(1)), dx_across[0], send(dx_across[1], beside(1))]
    half_acts = unpack(place_back.T, back, tokens, 0)
    grad_acts = unpack(place_back.T, back, tokens, 1, half_acts)
    raw_up = up0 + up2.astype(F32) + up1.astype(F32)
    raw_down = down0 + down2.astype(F32) + down1.astype(F32)
    return (grad_acts,) + clipped(raw_down, raw_up, ndevices, add_up)


def solution(mesh):
    plane = 4
    by_planes = mesh.shape["dp"] == 4 * plane

    def per_device(*arrays):
        if by_planes:
            return move_adapters(plane, *arrays)
        return move_tokens(*arrays)

    rows, pools = P(("parts", "dp"), None), P(("parts", "dp"), None, None)
    return jax.shard_map(
        per_device,
        mesh=mesh,
        in_specs=(rows, rows, rows, P("parts"), pools, pools),
        out_specs=(rows, pools, pools),
        check_vma=False,
    )
```

```python
import jax
import jax.numpy as jnp
from jax import lax
from jax.experimental import pallas as pl
from jax.experimental.pallas import tpu as pltpu
from jax.sharding import PartitionSpec as P

BF16, F32 = jnp.bfloat16, jnp.float32
ROWS_OF = (((1,), (1,)), ((), ()))
OUTER = (((0,), (0,)), ((), ()))
INNER = (((1,), (0,)), ((), ()))
HBM = pl.BlockSpec(memory_space=pltpu.HBM)
WHOLE = pl.BlockSpec(memory_space=pltpu.VMEM)
VMEM_BYTES = 20 * 2**20


def dot32(a, b, dims=INNER):
    return lax.dot_general(a, b, dims, preferred_element_type=F32)


def route(token_task_index, task_slot_lookup, ndevices):
    pool = task_slot_lookup.shape[0]
    task_hot = (token_task_index == jnp.arange(pool, dtype=jnp.int32)[None, :]).astype(jnp.int32)
    owner = jnp.sum(task_hot * task_slot_lookup[None, :], axis=1)
    owner_hot = (owner[:, None] == jnp.arange(ndevices, dtype=jnp.int32)[None, :]).astype(jnp.int32)
    before = jnp.cumsum(owner_hot, axis=0) - owner_hot
    position = jnp.sum(before * owner_hot, axis=1)
    return owner, position


def clipped(raw_down, raw_up, ndevices, add_up):
    local_sq = jnp.sum(raw_down * raw_down) + jnp.sum(raw_up * raw_up)
    total = add_up(local_sq)
    norm = jnp.sqrt(total + 1e-06)
    limit = jnp.sqrt(jnp.float32(2 * raw_down.shape[0] * raw_down.shape[1] * ndevices))
    factor = jnp.minimum(jnp.float32(1.0), limit / norm)
    return (raw_down * factor)[None], (raw_up * factor)[None]


def move_tokens(acts, cotan, token_task_index, task_slot_lookup, pool_down_factors, pool_up_factors):
    ndevices = lax.axis_size("dp")
    tokens, width = acts.shape
    capacity = 2 * ((tokens + ndevices - 1) // ndevices)
    slots = ndevices * capacity
    owner, position = route(token_task_index, task_slot_lookup, ndevices)
    dest = owner * capacity + position
    placed = (jnp.arange(slots, dtype=jnp.int32)[:, None] == dest[None, :]).astype(BF16)

    def exchange(rows):
        rows = rows.reshape(ndevices, capacity, width)
        return lax.all_to_all(rows, "dp", split_axis=0, concat_axis=0, tiled=True).reshape(slots, width)

    down, up = pool_down_factors[0], pool_up_factors[0]
    rows_x = exchange(dot32(placed, acts).astype(BF16))
    rows_g = exchange(dot32(placed, cotan).astype(BF16))
    hidden = dot32(rows_x, down, ROWS_OF).astype(BF16)
    inner = dot32(rows_g, up, ROWS_OF).astype(BF16)
    returned = exchange(dot32(inner, down).astype(BF16))
    grad_acts = dot32(placed, returned, OUTER).astype(BF16)
    raw_up = dot32(hidden, rows_g, OUTER)
    raw_down = dot32(inner, rows_x, OUTER)
    return (grad_acts,) + clipped(raw_down, raw_up, ndevices, lambda term: lax.psum(term, "dp"))


def in_hbm(*arrays):
    return [pltpu.with_memory_space_constraint(a, pltpu.HBM) for a in arrays]


def in_vmem(*arrays):
    return [pltpu.with_memory_space_constraint(a, pltpu.VMEM) for a in arrays]


def kernel_params(semantics=("arbitrary",)):
    return pltpu.CompilerParams(dimension_semantics=semantics, vmem_limit_bytes=VMEM_BYTES)


def pack(place, acts, cotan, shapes):
    tokens, width = acts.shape
    tile = min(width, 1024)
    tiles = width // tile

    def body(place_ref, x_in, g_in, *refs):
        out_refs, (rows, sems) = refs[:-2], refs[-2:]
        step = pl.program_id(0)

        def copies(i):
            cut = pl.ds(pl.multiple_of(i * tile, tile), tile)
            return [pltpu.make_async_copy(r.at[:, cut], rows.at[k, :, cut], sems.at[k, i]) for k, r in enumerate((x_in, g_in))]

        @pl.when(step == 0)
        def _():
            for i in range(tiles):
                for c in copies(i):
                    c.start()

        for c in copies(step):
            c.wait()
        cut = pl.ds(pl.multiple_of(step * tile, tile), tile)
        for k in range(2):
            moved = dot32(place_ref[...], rows[k, :, cut]).astype(BF16)
            first = 0
            for out_ref, (columns, size) in zip(out_refs, shapes):
                for c in range(columns):
                    out_ref[c, k] = moved[first:first + size]
                    first += size

    return pl.pallas_call(
        body,
        grid=(tiles,),
        in_specs=[pl.BlockSpec(place.shape, lambda i: (0, 0)), HBM, HBM],
        out_specs=[pl.BlockSpec((c, 2, size, tile), lambda i: (0, 0, 0, i)) for c, size in shapes],
        out_shape=[jax.ShapeDtypeStruct((c, 2, size, width), BF16) for c, size in shapes],
        scratch_shapes=[pltpu.VMEM((2, tokens, width), BF16), pltpu.SemaphoreType.DMA((2, tiles))],
        compiler_params=kernel_params(),
    )(place, *in_hbm(acts, cotan))


def unpack(place, blocks, tokens, half, into=None):
    width = blocks[0].shape[1]
    tile = min(width // 2, 2048)
    first = half * (width // 2 // tile)
    rest = () if into is None else (into,)

    def body(place_ref, *refs):
        rows = jnp.concatenate([ref[...] for ref in refs[:len(blocks)]], axis=0)
        refs[-1][...] = dot32(place_ref[...], rows).astype(BF16)

    return pl.pallas_call(
        body,
        grid=(width // 2 // tile,),
        in_specs=[pl.BlockSpec(place.shape, lambda i: (0, 0))]
        + [pl.BlockSpec((b.shape[0], tile), lambda i: (0, i + first)) for b in blocks]
        + [pl.BlockSpec(memory_space=pl.ANY)] * len(rest),
        out_specs=pl.BlockSpec((tokens, tile), lambda i: (0, i + first)),
        out_shape=jax.ShapeDtypeStruct((tokens, width), BF16),
        input_output_aliases={1 + len(blocks): 0} if rest else {},
        compiler_params=kernel_params(),
    )(place, *in_hbm(blocks[0]), *blocks[1:], *rest)


def corner(rows, first_rows, columns, first_columns):
    upper = lax.broadcasted_iota(jnp.int32, (rows, columns), 0) < first_rows
    return upper == (lax.broadcasted_iota(jnp.int32, (rows, columns), 1) < first_columns)


def stack(down, up):
    _, rank, width = down.shape
    pieces = 4
    part = width // pieces

    def body(down_in, up_in, out, sems):
        copies = [
            pltpu.make_async_copy(r.at[0, :, pl.ds(i * part, part)], out.at[k, :, pl.ds(i * part, part)], sems.at[k, i])
            for k, r in enumerate((down_in, up_in))
            for i in range(pieces)
        ]
        for c in copies:
            c.start()
        for c in copies:
            c.wait()

    return pl.pallas_call(
        body,
        in_specs=[HBM, HBM],
        out_specs=WHOLE,
        out_shape=pltpu.VMEM((2, rank, width), BF16),
        scratch_shapes=[pltpu.SemaphoreType.DMA((2, pieces))],
        compiler_params=pltpu.CompilerParams(vmem_limit_bytes=VMEM_BYTES),
    )(*in_hbm(down, up))


def far_group(flags, rows, factors, handed=None):
    _, block, width = rows[0].shape
    rank = factors[0].shape[1]
    tile = min(width, 2048)
    tiles = width // tile
    total = block if handed is None else 2 * block

    def body(flags_ref, *refs):
        rows_in, refs = refs[:len(rows)], refs[len(rows):]
        factors_in, refs = refs[:len(factors)], refs[len(factors):]
        handed_in, refs = (None, refs) if handed is None else (refs[0], refs[1:])
        (up_ref, down_ref, dx_ref), (held, left, inner, sems) = refs[:3], refs[-4:]
        step = pl.program_id(0)
        at_end, below = flags_ref[0] == 1, flags_ref[1] == 1

        def copy(source, i):
            cut = pl.ds(i * tile, tile)
            return pltpu.make_async_copy(source.at[:, :, cut], held.at[:, :, cut], sems.at[i])

        def tokens(k, cut):
            own = held[k, :, cut]
            return own if handed is None else jnp.concatenate([own, handed_in[k, :, cut]], axis=0)

        def factor(k, cut):
            return jnp.where(below, factors_in[1][k, :, cut], factors_in[0][k, :, cut])

        @pl.when(step == 0)
        def _():
            for n, source in enumerate(rows_in):
                chosen = at_end == (n == 1) if len(rows) == 2 else step == 0

                @pl.when(chosen)
                def _(source=source):
                    for i in range(tiles):
                        copy(source, i).start()

            sums = [jnp.zeros((total, rank), F32)] * 2
            for i in range(tiles):
                copy(rows_in[0], i).wait()
                cut = pl.ds(i * tile, tile)
                for k in range(2):
                    sums[k] += dot32(tokens(k, cut), factor(k, cut), ROWS_OF)
            for k in range(2):
                left[k] = sums[k].T.astype(BF16)
            inner[...] = sums[1].astype(BF16)

        cut = pl.ds(pl.multiple_of(step * tile, tile), tile)
        up_ref[...] = dot32(left[0], tokens(1, cut)).astype(BF16)
        down = dot32(left[1], tokens(0, cut)).astype(BF16)
        down_ref[...] = down
        dx = dot32(inner[...], factor(0, cut)).astype(BF16)
        dx_ref[...] = dx[:block]
        if handed is not None:
            refs[3][...] = jnp.where(at_end, down, dx[block:])

    sizes = (rank, rank, block) + (() if handed is None else (block,))
    more = () if handed is None else (handed,)
    return pl.pallas_call(
        body,
        grid=(tiles,),
        in_specs=[pl.BlockSpec(memory_space=pltpu.SMEM)] + [HBM] * len(rows) + [WHOLE] * (len(factors) + len(more)),
        out_specs=[pl.BlockSpec((n, tile), lambda i: (0, i)) for n in sizes],
        out_shape=[jax.ShapeDtypeStruct((n, width), BF16) for n in sizes],
        scratch_shapes=[
            pltpu.VMEM((2, block, width), BF16),
            pltpu.VMEM((2, rank, total), BF16),
            pltpu.VMEM((total, rank), BF16),
            pltpu.SemaphoreType.DMA((tiles,)),
        ],
        compiler_params=kernel_params(),
    )(flags, *in_hbm(*rows), *in_vmem(*factors, *more))


def near_groups(flags, stage, pairs, down, up, dx_late, dx_early, swapped, capacity, first1):
    plane = len(stage)
    rank, width = down.shape
    block = plane * capacity
    tile = min(width, 2048)
    tiles = width // tile

    def body(flags_ref, *refs):
        stage_in, refs = refs[:plane], refs[plane:]
        pairs_in, (down_in, up_in, late_ref, early_ref, swapped_ref) = refs[:2], refs[2:7]
        dx_refs, sum_refs = refs[7:11], refs[11:15]
        left, inner = refs[15:]
        step = pl.program_id(0)
        own_in = (down_in, up_in)

        def pair(k, cut):
            return jnp.where(flags_ref[2] == 1, pairs_in[1][k, :, cut], pairs_in[0][k, :, cut])

        is_mine = corner(2 * block, block, 2 * rank, rank)

        def rows(k, cut):
            return jnp.concatenate(
                [
                    r[0, k, pl.ds(first + n * capacity, capacity), cut]
                    for n in range(2)
                    for r, first in zip(stage_in, first1)
                ],
                axis=0,
            )

        @pl.when(step == 0)
        def _():
            sums = [jnp.zeros((2 * block, 2 * rank), F32)] * 2
            for i in range(tiles):
                cut = pl.ds(i * tile, tile)
                for k in range(2):
                    both = jnp.concatenate([pair(k, cut), own_in[k][:, cut]], axis=0)
                    sums[k] += dot32(rows(k, cut), both, ROWS_OF)
            for k in range(2):
                masked = jnp.where(is_mine, sums[k], 0.0)
                left[k] = masked.T.astype(BF16)
            inner[...] = masked.astype(BF16)

        cut = pl.ds(pl.multiple_of(step * tile, tile), tile)
        for k in range(2):
            both = dot32(left[k], rows(1 - k, cut))
            sum_refs[k][...] = both[:rank]
            sum_refs[2 + k][...] = both[rank:]
        downs = jnp.concatenate([pair(0, cut), down_in[:, cut]], axis=0)
        dx = dot32(inner[...], downs).astype(BF16)
        at_end, late = flags_ref[0] == 1, late_ref[...]
        moved = [jnp.where(at_end, swapped_ref[...], late), jnp.where(at_end, late, early_ref[...]), dx[:block], dx[block:]]
        for n, dx in enumerate(moved):
            for m in range(plane):
                dx_refs[m][n * capacity:(n + 1) * capacity] = dx[m * capacity:(m + 1) * capacity]

    return pl.pallas_call(
        body,
        grid=(tiles,),
        in_specs=[pl.BlockSpec(memory_space=pltpu.SMEM)]
        + [WHOLE] * (plane + 4)
        + [pl.BlockSpec((block, tile), lambda i: (0, i))] * 3,
        out_specs=[pl.BlockSpec((4 * capacity, tile), lambda i: (0, i))] * plane
        + [pl.BlockSpec((rank, tile), lambda i: (0, i))] * 4,
        out_shape=[jax.ShapeDtypeStruct((4 * capacity, width), BF16)] * plane
        + [jax.ShapeDtypeStruct((rank, width), F32)] * 4,
        scratch_shapes=[pltpu.VMEM((2, 2 * rank, 2 * block), BF16), pltpu.VMEM((2 * block, 2 * rank), BF16)],
        compiler_params=kernel_params(),
    )(flags, *in_vmem(*stage, *pairs, down, up), dx_late, dx_early, swapped)


def move_adapters(plane, acts, cotan, token_task_index, task_slot_lookup, pool_down_factors, pool_up_factors):
    ndevices = lax.axis_size("dp")
    tokens, width = acts.shape
    capacity = 2 * ((tokens + ndevices - 1) // ndevices)
    me = lax.axis_index("dp")
    z, column = me // plane, me % plane
    is_end = (z == 0) | (z == 3)
    flags = jnp.stack([is_end, z < 2, z % 2 == 0]).astype(jnp.int32)

    def planes(pairs):
        return [(a * plane + c, b * plane + c) for a, b in pairs for c in range(plane)]

    swap = planes([(0, 1), (1, 0), (2, 3), (3, 2)])
    cross = planes([(1, 2), (2, 1)])
    inward = planes([(0, 1), (3, 2)])

    def send(array, pairs):
        return lax.ppermute(array, "dp", pairs)

    def after(arrays, *others):
        return lax.optimization_barrier((arrays, others))[0]

    def beside(m):
        return [(i, (i // plane) * plane + ((i % plane) ^ m)) for i in range(ndevices)]

    def add_up(term):
        around = [beside(m) for m in range(1, plane)]
        along = [[(i, (i // plane ^ m) * plane + i % plane) for i in range(ndevices)] for m in range(1, 4)]
        term = jnp.broadcast_to(term, (8, 128))
        term = term + sum(after([send(term, pairs) for pairs in around], half_acts))
        return (term + sum(after([send(term, pairs) for pairs in along], grad_acts)))[0, 0]

    down, up = pool_down_factors[0], pool_up_factors[0]
    own = stack(pool_down_factors, pool_up_factors)
    from_left = send(own, planes([(0, 1), (1, 2), (2, 3)]))
    from_right = send(own, planes([(3, 2), (2, 1), (1, 0)]))

    owner, position = route(token_task_index, task_slot_lookup, ndevices)
    owner_z, turn = owner // plane, (owner % plane) ^ column
    other_mid = jnp.where(z < 2, 2, 1)
    kind = jnp.where(owner_z == z, 0, jnp.where(owner_z == (z ^ 1), 1, jnp.where(owner_z == other_mid, 2, 3)))

    def places(wanted, row, rows):
        hot = jnp.arange(rows, dtype=jnp.int32)[:, None] == row[None, :]
        return (hot & wanted[None, :]).astype(BF16)

    def after(arrays, *others):
        return lax.optimization_barrier((arrays, others))[0]

    block = plane * capacity
    mine = (3 - kind) * capacity + position
    row = jnp.where(kind == 2, 10 * capacity, 12 * capacity) + (turn - 2) * jnp.where(kind == 2, capacity, 2 * capacity)
    row += jnp.where(kind == 2, 0, (1 - kind) * capacity) + position
    row = jnp.where(kind == 3, (6 + turn) * capacity + position, row)
    row = jnp.where(turn < 2, turn * block + mine, row)
    place = places(kind >= 0, row, 4 * block)
    place_back = places(kind >= 0, turn * block + mine, 4 * block)
    own_rows, beside_rows, across3, across2, across10 = pack(
        place, acts, cotan, [(1, 4 * capacity)] * 2 + [(2, capacity)] * 2 + [(2, 2 * capacity)]
    )

    def over_x(blocks):
        moved = send(blocks, beside(2))
        return moved, send(moved[1:], beside(1))

    beside_rows = send(beside_rows, beside(1))
    across3 = over_x(across3)
    stage3 = (own_rows, beside_rows) + across3
    rows3 = jnp.concatenate([r[0, :, :capacity] for r in stage3], axis=1)
    handed = send(rows3, inward)
    across2 = over_x(after(across2, across3[0]))
    across10 = over_x(after(across10, across3[0]))
    rows2 = [r[0, :, capacity:2 * capacity] for r in (own_rows, beside_rows)] + [r[0] for r in across2]
    rows2 = jnp.concatenate(rows2, axis=1)
    stage10 = (own_rows, beside_rows) + across10
    far_left = send(from_left, planes([(1, 2), (2, 3)]))
    far_right = send(from_right, planes([(2, 1), (1, 0)]))

    up2, down2, dx_early = far_group(flags, (rows2,), (from_left, from_right))
    rows3, rows2 = after((rows3, rows2), dx_early)
    up3, down3, dx_late, swapped = far_group(flags, (rows3, rows2), (far_left, far_right), handed)
    up2_in = send(up3, inward)
    down3, swapped, up3 = send(down3, cross), send(swapped, swap), send(up3, cross)

    swapped, down3 = lax.optimization_barrier((swapped, down3))
    dx_own, dx_beside, *dx_across, up1, down1, up0, down0 = near_groups(
        flags, stage10, (from_left, from_right), down, up, dx_late, dx_early, swapped, capacity,
        (2 * capacity, 2 * capacity, 0, 0),
    )

    def add(a, b):
        return (a.astype(F32) + b.astype(F32)).astype(BF16)

    down2, down1 = add(down2, swapped), add(down1, down3)
    dx_across[0] = send(dx_across[0], beside(2))
    dx_across[1] = send(after(dx_across[1], dx_across[0]), beside(2))
    up2_in, up3 = after((up2_in, up3), down2, down1, dx_across[0])
    down2, down1 = send(down2, cross), send(down1, swap)
    up2, up1 = send(add(up2, up2_in), cross), send(add(up1, up3), swap)

    back = [dx_own, send(dx_beside, beside(1)), dx_across[0], send(dx_across[1], beside(1))]
    half_acts = unpack(place_back.T, back, tokens, 0)
    grad_acts = unpack(place_back.T, back, tokens, 1, half_acts)
    raw_up = up0 + up2.astype(F32) + up1.astype(F32)
    raw_down = down0 + down2.astype(F32) + down1.astype(F32)
    return (grad_acts,) + clipped(raw_down, raw_up, ndevices, add_up)


def solution(mesh):
    plane = 4
    by_planes = mesh.shape["dp"] == 4 * plane

    def per_device(*arrays):
        if by_planes:
            return move_adapters(plane, *arrays)
        return move_tokens(*arrays)

    rows, pools = P(("parts", "dp"), None), P(("parts", "dp"), None, None)
    return jax.shard_map(
        per_device,
        mesh=mesh,
        in_specs=(rows, rows, rows, P("parts"), pools, pools),
        out_specs=(rows, pools, pools),
        check_vma=False,
    )
```

```python
import jax
import jax.numpy as jnp
from jax import lax
from jax.experimental import pallas as pl
from jax.experimental.pallas import tpu as pltpu
from jax.sharding import PartitionSpec as P

BF16, F32 = jnp.bfloat16, jnp.float32
ROWS_OF = (((1,), (1,)), ((), ()))
OUTER = (((0,), (0,)), ((), ()))
INNER = (((1,), (0,)), ((), ()))
HBM = pl.BlockSpec(memory_space=pltpu.HBM)
WHOLE = pl.BlockSpec(memory_space=pltpu.VMEM)
VMEM_BYTES = 20 * 2**20


def dot32(a, b, dims=INNER):
    return lax.dot_general(a, b, dims, preferred_element_type=F32)


def route(token_task_index, task_slot_lookup, ndevices):
    pool = task_slot_lookup.shape[0]
    task_hot = (token_task_index == jnp.arange(pool, dtype=jnp.int32)[None, :]).astype(jnp.int32)
    owner = jnp.sum(task_hot * task_slot_lookup[None, :], axis=1)
    owner_hot = (owner[:, None] == jnp.arange(ndevices, dtype=jnp.int32)[None, :]).astype(jnp.int32)
    before = jnp.cumsum(owner_hot, axis=0) - owner_hot
    position = jnp.sum(before * owner_hot, axis=1)
    return owner, position


def clipped(raw_down, raw_up, ndevices):
    local_sq = jnp.sum(raw_down * raw_down) + jnp.sum(raw_up * raw_up)
    total = lax.psum(local_sq, "dp")
    norm = jnp.sqrt(total + 1e-06)
    limit = jnp.sqrt(jnp.float32(2 * raw_down.shape[0] * raw_down.shape[1] * ndevices))
    factor = jnp.minimum(jnp.float32(1.0), limit / norm)
    return (raw_down * factor)[None], (raw_up * factor)[None]


def move_tokens(acts, cotan, token_task_index, task_slot_lookup, pool_down_factors, pool_up_factors):
    ndevices = lax.axis_size("dp")
    tokens, width = acts.shape
    capacity = 2 * ((tokens + ndevices - 1) // ndevices)
    slots = ndevices * capacity
    owner, position = route(token_task_index, task_slot_lookup, ndevices)
    dest = owner * capacity + position
    placed = (jnp.arange(slots, dtype=jnp.int32)[:, None] == dest[None, :]).astype(BF16)

    def exchange(rows):
        rows = rows.reshape(ndevices, capacity, width)
        return lax.all_to_all(rows, "dp", split_axis=0, concat_axis=0, tiled=True).reshape(slots, width)

    down, up = pool_down_factors[0], pool_up_factors[0]
    rows_x = exchange(dot32(placed, acts).astype(BF16))
    rows_g = exchange(dot32(placed, cotan).astype(BF16))
    hidden = dot32(rows_x, down, ROWS_OF).astype(BF16)
    inner = dot32(rows_g, up, ROWS_OF).astype(BF16)
    returned = exchange(dot32(inner, down).astype(BF16))
    grad_acts = dot32(placed, returned, OUTER).astype(BF16)
    raw_up = dot32(hidden, rows_g, OUTER)
    raw_down = dot32(inner, rows_x, OUTER)
    return (grad_acts,) + clipped(raw_down, raw_up, ndevices)


def in_hbm(*arrays):
    return [pltpu.with_memory_space_constraint(a, pltpu.HBM) for a in arrays]


def in_vmem(*arrays):
    return [pltpu.with_memory_space_constraint(a, pltpu.VMEM) for a in arrays]


def kernel_params(semantics=("arbitrary",)):
    return pltpu.CompilerParams(dimension_semantics=semantics, vmem_limit_bytes=VMEM_BYTES)


def pack(place, acts, cotan, shapes):
    tokens, width = acts.shape
    tile = min(width, 1024)
    tiles = width // tile

    def body(place_ref, x_in, g_in, *refs):
        out_refs, (rows, sems) = refs[:-2], refs[-2:]
        step = pl.program_id(0)

        def copies(i):
            cut = pl.ds(pl.multiple_of(i * tile, tile), tile)
            return [pltpu.make_async_copy(r.at[:, cut], rows.at[k, :, cut], sems.at[k, i]) for k, r in enumerate((x_in, g_in))]

        @pl.when(step == 0)
        def _():
            for i in range(tiles):
                for c in copies(i):
                    c.start()

        for c in copies(step):
            c.wait()
        cut = pl.ds(pl.multiple_of(step * tile, tile), tile)
        for k in range(2):
            moved = dot32(place_ref[...], rows[k, :, cut]).astype(BF16)
            first = 0
            for out_ref, (columns, size) in zip(out_refs, shapes):
                for c in range(columns):
                    out_ref[c, k] = moved[first:first + size]
                    first += size

    return pl.pallas_call(
        body,
        grid=(tiles,),
        in_specs=[pl.BlockSpec(place.shape, lambda i: (0, 0)), HBM, HBM],
        out_specs=[pl.BlockSpec((c, 2, size, tile), lambda i: (0, 0, 0, i)) for c, size in shapes],
        out_shape=[jax.ShapeDtypeStruct((c, 2, size, width), BF16) for c, size in shapes],
        scratch_shapes=[pltpu.VMEM((2, tokens, width), BF16), pltpu.SemaphoreType.DMA((2, tiles))],
        compiler_params=kernel_params(),
    )(place, *in_hbm(acts, cotan))


def unpack(place, blocks, tokens, half, into=None):
    width = blocks[0].shape[1]
    tile = min(width // 2, 2048)
    first = half * (width // 2 // tile)
    rest = () if into is None else (into,)

    def body(place_ref, *refs):
        rows = jnp.concatenate([ref[...] for ref in refs[:len(blocks)]], axis=0)
        refs[-1][...] = dot32(place_ref[...], rows).astype(BF16)

    return pl.pallas_call(
        body,
        grid=(width // 2 // tile,),
        in_specs=[pl.BlockSpec(place.shape, lambda i: (0, 0))]
        + [pl.BlockSpec((b.shape[0], tile), lambda i: (0, i + first)) for b in blocks]
        + [pl.BlockSpec(memory_space=pl.ANY)] * len(rest),
        out_specs=pl.BlockSpec((tokens, tile), lambda i: (0, i + first)),
        out_shape=jax.ShapeDtypeStruct((tokens, width), BF16),
        input_output_aliases={1 + len(blocks): 0} if rest else {},
        compiler_params=kernel_params(),
    )(place, *in_hbm(blocks[0]), *blocks[1:], *rest)


def final_sum(first, *others):
    rank, width = first.shape
    tile = min(width, 1024)

    def body(first_ref, *refs):
        other_refs, (total_ref, square_ref) = refs[:-2], refs[-2:]
        squares = jnp.zeros((8, 128), F32)
        for i in range(width // tile):
            cut = pl.ds(i * tile, tile)
            total = first_ref[:, cut]
            for ref in other_refs:
                total += ref[:, cut].astype(F32)
            total_ref[:, cut] = total
            total = total * total
            for r in range(0, rank, 8):
                for c in range(0, tile, 128):
                    squares += total[r:r + 8, c:c + 128]
        square_ref[...] = squares

    return pl.pallas_call(
        body,
        in_specs=[WHOLE] * (1 + len(others)),
        out_specs=[WHOLE] * 2,
        out_shape=[pltpu.VMEM((rank, width), F32), pltpu.VMEM((8, 128), F32)],
        compiler_params=pltpu.CompilerParams(vmem_limit_bytes=VMEM_BYTES),
    )(*in_vmem(first, *others))


def scaled(raws, parts, ndevices):
    rank, width = raws[0].shape
    tile = min(width, 1024)
    limit = float(2 * rank * width * ndevices) ** 0.5

    def body(*refs):
        raw_refs, part_refs, out_refs = refs[:len(raws)], refs[len(raws):-len(raws)], refs[-len(raws):]
        total = jnp.sum(sum(ref[...] for ref in part_refs), axis=(0, 1), keepdims=True)
        factor = jnp.minimum(jnp.float32(1.0), jnp.float32(limit) / jnp.sqrt(total + 1e-06))
        cut = pl.ds(pl.multiple_of(pl.program_id(0) * tile, tile), tile)
        for raw_ref, out_ref in zip(raw_refs, out_refs):
            out_ref[0] = raw_ref[:, cut] * factor

    return pl.pallas_call(
        body,
        grid=(width // tile,),
        in_specs=[WHOLE] * (len(raws) + len(parts)),
        out_specs=[pl.BlockSpec((1, rank, tile), lambda i: (0, 0, i))] * len(raws),
        out_shape=[jax.ShapeDtypeStruct((1, rank, width), F32)] * len(raws),
        compiler_params=kernel_params(),
    )(*in_vmem(*raws, *parts))


def corner(rows, first_rows, columns, first_columns):
    upper = lax.broadcasted_iota(jnp.int32, (rows, columns), 0) < first_rows
    return upper == (lax.broadcasted_iota(jnp.int32, (rows, columns), 1) < first_columns)


def far_group(is_end, rows, factors, handed=None):
    _, block, width = rows[0].shape
    rank = factors[0].shape[1]
    tile = min(width, 2048)
    tiles = width // tile
    total = block if handed is None else 2 * block

    def body(end_ref, *refs):
        rows_in, refs = refs[:len(rows)], refs[len(rows):]
        factors_in, refs = refs[:len(factors)], refs[len(factors):]
        handed_in, refs = (None, refs) if handed is None else (refs[0], refs[1:])
        (up_ref, down_ref, dx_ref), (held, left, sems) = refs[:3], refs[-3:]
        step = pl.program_id(0)
        at_end = end_ref[0] == 1

        def copy(source, i):
            cut = pl.ds(i * tile, tile)
            return pltpu.make_async_copy(source.at[:, :, cut], held.at[:, :, cut], sems.at[i])

        def tokens(k, cut):
            own = held[k, :, cut]
            return own if handed is None else jnp.concatenate([own, handed_in[k, :, cut]], axis=0)

        def factor(k, cut):
            first = factors_in[0][k, :, cut]
            return first if len(factors) == 1 else jnp.where(at_end, factors_in[1][k, :, cut], first)

        @pl.when(step == 0)
        def _():
            for n, source in enumerate(rows_in):
                chosen = at_end == (n == 1) if len(rows) == 2 else step == 0

                @pl.when(chosen)
                def _(source=source):
                    for i in range(tiles):
                        copy(source, i).start()

            sums = [jnp.zeros((rank, total), F32)] * 2
            for i in range(tiles):
                copy(rows_in[0], i).wait()
                cut = pl.ds(i * tile, tile)
                for k in range(2):
                    sums[k] += dot32(factor(k, cut), tokens(k, cut), ROWS_OF)
            for k in range(2):
                left[k] = sums[k].astype(BF16)

        cut = pl.ds(pl.multiple_of(step * tile, tile), tile)
        up_ref[...] = dot32(left[0], tokens(1, cut)).astype(BF16)
        down = dot32(left[1], tokens(0, cut)).astype(BF16)
        down_ref[...] = down
        dx = dot32(left[1], factor(0, cut), OUTER).astype(BF16)
        dx_ref[...] = dx[:block]
        if handed is not None:
            refs[3][...] = jnp.where(at_end, down, dx[block:])

    outs = 3 if handed is None else 4
    more = () if handed is None else (handed,)
    return pl.pallas_call(
        body,
        grid=(tiles,),
        in_specs=[pl.BlockSpec(memory_space=pltpu.SMEM)] + [HBM] * len(rows) + [WHOLE] * (len(factors) + len(more)),
        out_specs=[pl.BlockSpec((rank, tile), lambda i: (0, i))] * outs,
        out_shape=[jax.ShapeDtypeStruct((rank, width), BF16)] * outs,
        scratch_shapes=[
            pltpu.VMEM((2, block, width), BF16),
            pltpu.VMEM((2, rank, total), BF16),
            pltpu.SemaphoreType.DMA((tiles,)),
        ],
        compiler_params=kernel_params(),
    )(is_end, *in_hbm(*rows), *in_vmem(*factors, *more))


def near_groups(is_end, stage, pair, down, up, dx_late, dx_early, swapped, capacity, first1):
    plane = len(stage)
    rank, width = down.shape
    block = plane * capacity
    tile = min(width, 2048)
    tiles = width // tile

    def body(end_ref, *refs):
        stage_in, refs = refs[:plane], refs[plane:]
        pair_in, down_in, up_in, late_ref, early_ref, swapped_ref = refs[:6]
        dx_refs, sum_refs = refs[6:10], refs[10:14]
        (left,) = refs[14:]
        step = pl.program_id(0)
        own_in = (down_in, up_in)
        is_mine = corner(2 * block, block, 2 * rank, rank)

        def rows(k, cut):
            return jnp.concatenate(
                [
                    r[0, k, pl.ds(first + n * capacity, capacity), cut]
                    for n in range(2)
                    for r, first in zip(stage_in, first1)
                ],
                axis=0,
            )

        @pl.when(step == 0)
        def _():
            sums = [jnp.zeros((2 * block, 2 * rank), F32)] * 2
            for i in range(tiles):
                cut = pl.ds(i * tile, tile)
                for k in range(2):
                    both = jnp.concatenate([pair_in[k, :, cut], own_in[k][:, cut]], axis=0)
                    sums[k] += dot32(rows(k, cut), both, ROWS_OF)
            for k in range(2):
                left[k] = jnp.where(is_mine, sums[k], 0.0).astype(BF16)

        cut = pl.ds(pl.multiple_of(step * tile, tile), tile)
        for k in range(2):
            both = dot32(left[k], rows(1 - k, cut), OUTER)
            sum_refs[k][...] = both[:rank]
            sum_refs[2 + k][...] = both[rank:]
        downs = jnp.concatenate([pair_in[0, :, cut], down_in[:, cut]], axis=0)
        dx = dot32(left[1], downs).astype(BF16)
        at_end, late = end_ref[0] == 1, late_ref[...]
        moved = [jnp.where(at_end, swapped_ref[...], late), jnp.where(at_end, late, early_ref[...]), dx[:block], dx[block:]]
        for n, dx in enumerate(moved):
            for m in range(plane):
                dx_refs[m][n * capacity:(n + 1) * capacity] = dx[m * capacity:(m + 1) * capacity]

    return pl.pallas_call(
        body,
        grid=(tiles,),
        in_specs=[pl.BlockSpec(memory_space=pltpu.SMEM)]
        + [WHOLE] * (plane + 3)
        + [pl.BlockSpec((block, tile), lambda i: (0, i))] * 3,
        out_specs=[pl.BlockSpec((4 * capacity, tile), lambda i: (0, i))] * plane
        + [pl.BlockSpec((rank, tile), lambda i: (0, i))] * 4,
        out_shape=[jax.ShapeDtypeStruct((4 * capacity, width), BF16)] * plane
        + [jax.ShapeDtypeStruct((rank, width), F32)] * 4,
        scratch_shapes=[pltpu.VMEM((2, 2 * block, 2 * rank), BF16)],
        compiler_params=kernel_params(),
    )(is_end, *in_vmem(*stage, pair, down, up), dx_late, dx_early, swapped)


def move_adapters(plane, acts, cotan, token_task_index, task_slot_lookup, pool_down_factors, pool_up_factors):
    ndevices = lax.axis_size("dp")
    tokens, width = acts.shape
    capacity = 2 * ((tokens + ndevices - 1) // ndevices)
    me = lax.axis_index("dp")
    z, column = me // plane, me % plane
    is_end = (z == 0) | (z == 3)
    end_flag = is_end.astype(jnp.int32).reshape(1)

    def planes(pairs):
        return [(a * plane + c, b * plane + c) for a, b in pairs for c in range(plane)]

    swap = planes([(0, 1), (1, 0), (2, 3), (3, 2)])
    cross = planes([(1, 2), (2, 1)])
    outward = planes([(1, 0), (2, 3)])
    inward = planes([(0, 1), (3, 2)])

    def send(array, pairs):
        return lax.ppermute(array, "dp", pairs)

    def after(arrays, *others):
        return lax.optimization_barrier((arrays, others))[0]

    def beside(m):
        return [(i, (i // plane) * plane + ((i % plane) ^ m)) for i in range(ndevices)]

    down, up = pool_down_factors[0], pool_up_factors[0]
    own = jnp.concatenate([pool_down_factors, pool_up_factors])
    pair = send(own, swap)
    crossed = send(own, cross)

    owner, position = route(token_task_index, task_slot_lookup, ndevices)
    owner_z, turn = owner // plane, (owner % plane) ^ column
    other_mid = jnp.where(z < 2, 2, 1)
    kind = jnp.where(owner_z == z, 0, jnp.where(owner_z == (z ^ 1), 1, jnp.where(owner_z == other_mid, 2, 3)))

    def places(wanted, row, rows):
        hot = jnp.arange(rows, dtype=jnp.int32)[:, None] == row[None, :]
        return (hot & wanted[None, :]).astype(BF16)

    def after(arrays, *others):
        return lax.optimization_barrier((arrays, others))[0]

    block = plane * capacity
    mine = (3 - kind) * capacity + position
    row = jnp.where(kind == 2, 10 * capacity, 12 * capacity) + (turn - 2) * jnp.where(kind == 2, capacity, 2 * capacity)
    row += jnp.where(kind == 2, 0, (1 - kind) * capacity) + position
    row = jnp.where(kind == 3, (6 + turn) * capacity + position, row)
    row = jnp.where(turn < 2, turn * block + mine, row)
    place = places(kind >= 0, row, 4 * block)
    place_back = places(kind >= 0, turn * block + mine, 4 * block)
    own_rows, beside_rows, across3, across2, across10 = pack(
        place, acts, cotan, [(1, 4 * capacity)] * 2 + [(2, capacity)] * 2 + [(2, 2 * capacity)]
    )

    def over_x(blocks):
        moved = send(blocks, beside(2))
        return moved, send(moved[1:], beside(1))

    beside_rows = send(beside_rows, beside(1))
    across3 = over_x(across3)
    stage3 = (own_rows, beside_rows) + across3
    rows3 = jnp.concatenate([r[0, :, :capacity] for r in stage3], axis=1)
    handed = send(rows3, inward)
    across2 = over_x(after(across2, across3[0]))
    across10 = over_x(after(across10, across2[1]))
    rows2 = [r[0, :, capacity:2 * capacity] for r in (own_rows, beside_rows)] + [r[0] for r in across2]
    rows2 = jnp.concatenate(rows2, axis=1)
    stage10 = (own_rows, beside_rows) + across10
    outer = send(crossed, outward)
    far = send(pair, cross)

    up2, down2, dx_early = far_group(end_flag, (rows2,), (crossed,))
    rows3, rows2 = after((rows3, rows2), dx_early)
    up3, down3, dx_late, swapped = far_group(end_flag, (rows3, rows2), (far, outer), handed)
    up2_in = send(up3, inward)
    down3, swapped, up3 = send(down3, cross), send(swapped, swap), send(up3, cross)

    swapped, down3 = lax.optimization_barrier((swapped, down3))
    dx_own, dx_beside, *dx_across, up1, down1, up0, down0 = near_groups(
        end_flag, stage10, pair, down, up, dx_late, dx_early, swapped, capacity,
        (2 * capacity, 2 * capacity, 0, 0),
    )

    def add(a, b):
        return (a.astype(F32) + b.astype(F32)).astype(BF16)

    down2, down1 = add(down2, swapped), add(down1, down3)
    dx_across[0] = send(dx_across[0], beside(2))
    dx_across[1] = send(after(dx_across[1], dx_across[0]), beside(2))
    up2_in, up3 = after((up2_in, up3), down2, down1, dx_across[0])
    down2, down1 = send(down2, cross), send(down1, swap)
    up2, up1 = send(add(up2, up2_in), cross), send(add(up1, up3), swap)

    back = [dx_own, send(dx_beside, beside(1)), dx_across[0], send(dx_across[1], beside(1))]
    half_acts = unpack(place_back.T, back, tokens, 0)
    grad_acts = unpack(place_back.T, back, tokens, 1, half_acts)
    raw_down, down_squares = final_sum(down0, down2, down1)
    raw_up, up_squares = final_sum(up0, up2, up1)
    part = down_squares + up_squares
    part = part + sum(after([send(part, beside(m)) for m in range(1, plane)], half_acts))
    along = [[(i, (i // plane ^ m) * plane + i % plane) for i in range(ndevices)] for m in range(1, 4)]
    parts = after([send(part, pairs) for pairs in along], grad_acts)
    return (grad_acts, *scaled((raw_down, raw_up), (part, *parts), ndevices))


def solution(mesh):
    plane = 4
    by_planes = mesh.shape["dp"] == 4 * plane

    def per_device(*arrays):
        if by_planes:
            return move_adapters(plane, *arrays)
        return move_tokens(*arrays)

    rows, pools = P(("parts", "dp"), None), P(("parts", "dp"), None, None)
    return jax.shard_map(
        per_device,
        mesh=mesh,
        in_specs=(rows, rows, rows, P("parts"), pools, pools),
        out_specs=(rows, pools, pools),
        check_vma=False,
    )
```

```python
import jax
import jax.numpy as jnp
from jax import lax
from jax.experimental import pallas as pl
from jax.experimental.pallas import tpu as pltpu
from jax.sharding import PartitionSpec as P

BF16, F32 = jnp.bfloat16, jnp.float32
ROWS_OF = (((1,), (1,)), ((), ()))
OUTER = (((0,), (0,)), ((), ()))
INNER = (((1,), (0,)), ((), ()))
HBM = pl.BlockSpec(memory_space=pltpu.HBM)
WHOLE = pl.BlockSpec(memory_space=pltpu.VMEM)
VMEM_BYTES = 16 * 2**20


def dot32(a, b, dims=INNER):
    return lax.dot_general(a, b, dims, preferred_element_type=F32)


def route(token_task_index, task_slot_lookup, ndevices):
    pool = task_slot_lookup.shape[0]
    task_hot = (token_task_index == jnp.arange(pool, dtype=jnp.int32)[None, :]).astype(jnp.int32)
    owner = jnp.sum(task_hot * task_slot_lookup[None, :], axis=1)
    owner_hot = (owner[:, None] == jnp.arange(ndevices, dtype=jnp.int32)[None, :]).astype(jnp.int32)
    before = jnp.cumsum(owner_hot, axis=0) - owner_hot
    position = jnp.sum(before * owner_hot, axis=1)
    return owner, position


def clipped(raw_down, raw_up, ndevices):
    local_sq = jnp.sum(raw_down * raw_down) + jnp.sum(raw_up * raw_up)
    total = lax.psum(local_sq, "dp")
    norm = jnp.sqrt(total + 1e-06)
    limit = jnp.sqrt(jnp.float32(2 * raw_down.shape[0] * raw_down.shape[1] * ndevices))
    factor = jnp.minimum(jnp.float32(1.0), limit / norm)
    return (raw_down * factor)[None], (raw_up * factor)[None]


def move_tokens(acts, cotan, token_task_index, task_slot_lookup, pool_down_factors, pool_up_factors):
    ndevices = lax.axis_size("dp")
    tokens, width = acts.shape
    capacity = 2 * ((tokens + ndevices - 1) // ndevices)
    slots = ndevices * capacity
    owner, position = route(token_task_index, task_slot_lookup, ndevices)
    dest = owner * capacity + position
    placed = (jnp.arange(slots, dtype=jnp.int32)[:, None] == dest[None, :]).astype(BF16)

    def exchange(rows):
        rows = rows.reshape(ndevices, capacity, width)
        return lax.all_to_all(rows, "dp", split_axis=0, concat_axis=0, tiled=True).reshape(slots, width)

    down, up = pool_down_factors[0], pool_up_factors[0]
    rows_x = exchange(dot32(placed, acts).astype(BF16))
    rows_g = exchange(dot32(placed, cotan).astype(BF16))
    hidden = dot32(rows_x, down, ROWS_OF).astype(BF16)
    inner = dot32(rows_g, up, ROWS_OF).astype(BF16)
    returned = exchange(dot32(inner, down).astype(BF16))
    grad_acts = dot32(placed, returned, OUTER).astype(BF16)
    raw_up = dot32(hidden, rows_g, OUTER)
    raw_down = dot32(inner, rows_x, OUTER)
    return (grad_acts,) + clipped(raw_down, raw_up, ndevices)


def in_hbm(*arrays):
    return [pltpu.with_memory_space_constraint(a, pltpu.HBM) for a in arrays]


def in_vmem(*arrays):
    return [pltpu.with_memory_space_constraint(a, pltpu.VMEM) for a in arrays]


def kernel_params(semantics=("arbitrary",)):
    return pltpu.CompilerParams(dimension_semantics=semantics, vmem_limit_bytes=VMEM_BYTES)


def pack(place, acts, cotan, shapes):
    tokens, width = acts.shape
    tile = min(width, 1024)
    tiles = width // tile

    def body(place_ref, x_in, g_in, *refs):
        out_refs, (rows, sems) = refs[:-2], refs[-2:]
        step = pl.program_id(0)

        def copies(i):
            cut = pl.ds(pl.multiple_of(i * tile, tile), tile)
            return [pltpu.make_async_copy(r.at[:, cut], rows.at[k, :, cut], sems.at[k, i]) for k, r in enumerate((x_in, g_in))]

        @pl.when(step == 0)
        def _():
            for i in range(tiles):
                for c in copies(i):
                    c.start()

        for c in copies(step):
            c.wait()
        cut = pl.ds(pl.multiple_of(step * tile, tile), tile)
        for k in range(2):
            moved = dot32(place_ref[...], rows[k, :, cut]).astype(BF16)
            first = 0
            for out_ref, (columns, size) in zip(out_refs, shapes):
                for c in range(columns):
                    out_ref[c, k] = moved[first:first + size]
                    first += size

    return pl.pallas_call(
        body,
        grid=(tiles,),
        in_specs=[pl.BlockSpec(place.shape, lambda i: (0, 0)), HBM, HBM],
        out_specs=[pl.BlockSpec((c, 2, size, tile), lambda i: (0, 0, 0, i)) for c, size in shapes],
        out_shape=[jax.ShapeDtypeStruct((c, 2, size, width), BF16) for c, size in shapes],
        scratch_shapes=[pltpu.VMEM((2, tokens, width), BF16), pltpu.SemaphoreType.DMA((2, tiles))],
        compiler_params=kernel_params(),
    )(place, *in_hbm(acts, cotan))


def unpack(place, blocks, tokens, half, into=None):
    width = blocks[0].shape[1]
    tile = min(width // 2, 2048)
    first = half * (width // 2 // tile)
    rest = () if into is None else (into,)

    def body(place_ref, *refs):
        rows = jnp.concatenate([ref[...] for ref in refs[:len(blocks)]], axis=0)
        refs[-1][...] = dot32(place_ref[...], rows).astype(BF16)

    return pl.pallas_call(
        body,
        grid=(width // 2 // tile,),
        in_specs=[pl.BlockSpec(place.shape, lambda i: (0, 0))]
        + [pl.BlockSpec((b.shape[0], tile), lambda i: (0, i + first)) for b in blocks]
        + [pl.BlockSpec(memory_space=pl.ANY)] * len(rest),
        out_specs=pl.BlockSpec((tokens, tile), lambda i: (0, i + first)),
        out_shape=jax.ShapeDtypeStruct((tokens, width), BF16),
        input_output_aliases={1 + len(blocks): 0} if rest else {},
        compiler_params=kernel_params(),
    )(place, *in_hbm(blocks[0]), *blocks[1:], *rest)


def final_sum(first, *others):
    rank, width = first.shape
    tile = min(width, 1024)

    def body(first_ref, *refs):
        other_refs, (total_ref, square_ref) = refs[:-2], refs[-2:]
        squares = jnp.zeros((8, 128), F32)
        for i in range(width // tile):
            cut = pl.ds(i * tile, tile)
            total = first_ref[:, cut]
            for ref in other_refs:
                total += ref[:, cut].astype(F32)
            total_ref[:, cut] = total
            total = total * total
            for r in range(0, rank, 8):
                for c in range(0, tile, 128):
                    squares += total[r:r + 8, c:c + 128]
        square_ref[...] = squares

    return in_place(body, [((rank, width), F32), ((8, 128), F32)], first, *others)


def scaled(raws, parts, ndevices):
    rank, width = raws[0].shape
    tile = min(width, 1024)
    limit = float(2 * rank * width * ndevices) ** 0.5

    def body(*refs):
        raw_refs, part_refs = refs[:len(raws)], refs[len(raws):len(raws) + len(parts)]
        outs, (held, sems) = refs[len(raws) + len(parts):-2], refs[-2:]
        total = jnp.sum(sum(ref[...] for ref in part_refs), axis=(0, 1), keepdims=True)
        factor = jnp.minimum(jnp.float32(1.0), jnp.float32(limit) / jnp.sqrt(total + 1e-06))
        copies = []
        for i in range(width // tile):
            cut = pl.ds(i * tile, tile)
            for n, (raw_ref, out) in enumerate(zip(raw_refs, outs)):
                held[n, :, cut] = raw_ref[:, cut] * factor
                copies.append(pltpu.make_async_copy(held.at[n, :, cut], out.at[0, :, cut], sems.at[n, i]))
                copies[-1].start()
        for c in copies:
            c.wait()

    return pl.pallas_call(
        body,
        in_specs=[WHOLE] * (len(raws) + len(parts)),
        out_specs=[HBM] * len(raws),
        out_shape=[pltpu.HBM((1, rank, width), F32)] * len(raws),
        scratch_shapes=[
            pltpu.VMEM((len(raws), rank, width), F32),
            pltpu.SemaphoreType.DMA((len(raws), width // tile)),
        ],
        compiler_params=pltpu.CompilerParams(vmem_limit_bytes=VMEM_BYTES),
    )(*in_vmem(*raws, *parts))


def corner(rows, first_rows, columns, first_columns):
    upper = lax.broadcasted_iota(jnp.int32, (rows, columns), 0) < first_rows
    return upper == (lax.broadcasted_iota(jnp.int32, (rows, columns), 1) < first_columns)


def far_sums(tokens, factor, up_ref, down_ref, dx_refs):
    rank, width = up_ref.shape
    tile = min(width, 2048)
    cuts = [pl.ds(i * tile, tile) for i in range(width // tile)]
    hidden, inner = (sum(dot32(tokens(k, cut), factor(k, cut), ROWS_OF) for cut in cuts) for k in range(2))
    hidden_t, inner_t, inner = hidden.T.astype(BF16), inner.T.astype(BF16), inner.astype(BF16)
    for cut in cuts:
        up_ref[:, cut] = dot32(hidden_t, tokens(1, cut)).astype(BF16)
        down_ref[:, cut] = dot32(inner_t, tokens(0, cut)).astype(BF16)
        dx = dot32(inner, factor(0, cut)).astype(BF16)
        for n, ref in enumerate(dx_refs):
            rows = ref.shape[0]
            ref[:, cut] = dx[n * rows:(n + 1) * rows]


def in_place(body, out_shapes, *arrays, flags=None):
    first = [] if flags is None else [flags]
    return pl.pallas_call(
        body,
        in_specs=[pl.BlockSpec(memory_space=pltpu.SMEM)] * len(first) + [WHOLE] * len(arrays),
        out_specs=[WHOLE] * len(out_shapes),
        out_shape=[pltpu.VMEM(*shape) for shape in out_shapes],
        compiler_params=pltpu.CompilerParams(vmem_limit_bytes=VMEM_BYTES),
    )(*first, *in_vmem(*arrays))


def early_group(flags, rows3, rows2, crossed):
    _, block, width = rows2.shape
    rank = crossed.shape[1]

    def body(flags_ref, rows3_ref, rows2_ref, crossed_ref, up_ref, down_ref, dx_ref, late_ref):
        far_sums(
            lambda k, cut: rows2_ref[k, :, cut], lambda k, cut: crossed_ref[k, :, cut], up_ref, down_ref, (dx_ref,)
        )
        late_ref[...] = jnp.where(flags_ref[0] == 1, rows2_ref[...], rows3_ref[...])

    shapes = [((rank, width), BF16)] * 2 + [((block, width), BF16), ((2, block, width), BF16)]
    return in_place(body, shapes, rows3, rows2, crossed, flags=flags)


def late_group(flags, rows, handed, far, outer):
    _, block, width = rows.shape
    rank = far.shape[1]

    def body(flags_ref, rows_ref, handed_ref, outer_ref, far_ref, up_ref, down_ref, dx_ref, swap_ref):
        at_end = flags_ref[0] == 1
        far_sums(
            lambda k, cut: jnp.concatenate([rows_ref[k, :, cut], handed_ref[k, :, cut]], axis=0),
            lambda k, cut: jnp.where(at_end, outer_ref[k, :, cut], far_ref[k, :, cut]),
            up_ref,
            down_ref,
            (dx_ref, swap_ref),
        )

        @pl.when(at_end)
        def _():
            swap_ref[...] = down_ref[...]

    shapes = [((rank, width), BF16)] * 2 + [((block, width), BF16)] * 2
    return in_place(body, shapes, rows, handed, outer, far, flags=flags)


def near_groups(flags, stage, pair, down, up, dx_late, dx_early, swapped, capacity, first1):
    plane = len(stage)
    rank, width = down.shape
    block = plane * capacity
    tile = min(width, 2048)
    cuts = [pl.ds(i * tile, tile) for i in range(width // tile)]

    def body(flags_ref, *refs):
        stage_in, refs = refs[:plane], refs[plane:]
        pair_in, down_in, up_in, late_ref, early_ref, swapped_ref = refs[:6]
        dx_refs, sum_refs = refs[6:6 + plane], refs[6 + plane:]
        own_in = (down_in, up_in)
        at_end = flags_ref[0] == 1

        def rows(k, cut):
            return jnp.concatenate(
                [
                    r[0, k, pl.ds(first + n * capacity, capacity), cut]
                    for n in range(2)
                    for r, first in zip(stage_in, first1)
                ],
                axis=0,
            )

        def factors(k, cut):
            return jnp.concatenate([pair_in[k, :, cut], own_in[k][:, cut]], axis=0)

        is_mine = corner(2 * block, block, 2 * rank, rank)
        sums = [sum(dot32(rows(k, cut), factors(k, cut), ROWS_OF) for cut in cuts) for k in range(2)]
        sums = [jnp.where(is_mine, total, 0.0) for total in sums]
        left, inner = [total.T.astype(BF16) for total in sums], sums[1].astype(BF16)
        for cut in cuts:
            for k in range(2):
                both = dot32(left[k], rows(1 - k, cut))
                sum_refs[k][:, cut] = both[:rank]
                sum_refs[2 + k][:, cut] = both[rank:]
            dx = dot32(inner, factors(0, cut)).astype(BF16)
            late = late_ref[:, cut]
            moved = [jnp.where(at_end, swapped_ref[:, cut], late), jnp.where(at_end, late, early_ref[:, cut])]
            for n, dx in enumerate(moved + [dx[:block], dx[block:]]):
                for m in range(plane):
                    dx_refs[m][n * capacity:(n + 1) * capacity, cut] = dx[m * capacity:(m + 1) * capacity]

    shapes = [((4 * capacity, width), BF16)] * plane + [((rank, width), F32)] * 4
    return in_place(body, shapes, *stage, pair, down, up, dx_late, dx_early, swapped, flags=flags)


def move_adapters(plane, acts, cotan, token_task_index, task_slot_lookup, pool_down_factors, pool_up_factors):
    ndevices = lax.axis_size("dp")
    tokens, width = acts.shape
    capacity = 2 * ((tokens + ndevices - 1) // ndevices)
    me = lax.axis_index("dp")
    z, column = me // plane, me % plane
    is_end = (z == 0) | (z == 3)
    end_flag = is_end.astype(jnp.int32).reshape(1)

    def planes(pairs):
        return [(a * plane + c, b * plane + c) for a, b in pairs for c in range(plane)]

    swap = planes([(0, 1), (1, 0), (2, 3), (3, 2)])
    cross = planes([(1, 2), (2, 1)])
    outward = planes([(1, 0), (2, 3)])
    inward = planes([(0, 1), (3, 2)])

    def send(array, pairs):
        return lax.ppermute(array, "dp", pairs)

    def after(arrays, *others):
        return lax.optimization_barrier((arrays, others))[0]

    def beside(m):
        return [(i, (i // plane) * plane + ((i % plane) ^ m)) for i in range(ndevices)]

    down, up = pool_down_factors[0], pool_up_factors[0]
    own = jnp.concatenate([pool_down_factors, pool_up_factors])
    pair = send(own, swap)
    crossed = send(own, cross)

    owner, position = route(token_task_index, task_slot_lookup, ndevices)
    owner_z, turn = owner // plane, (owner % plane) ^ column
    other_mid = jnp.where(z < 2, 2, 1)
    kind = jnp.where(owner_z == z, 0, jnp.where(owner_z == (z ^ 1), 1, jnp.where(owner_z == other_mid, 2, 3)))

    def places(wanted, row, rows):
        hot = jnp.arange(rows, dtype=jnp.int32)[:, None] == row[None, :]
        return (hot & wanted[None, :]).astype(BF16)

    def after(arrays, *others):
        return lax.optimization_barrier((arrays, others))[0]

    block = plane * capacity
    mine = (3 - kind) * capacity + position
    row = jnp.where(kind == 2, 10 * capacity, 12 * capacity) + (turn - 2) * jnp.where(kind == 2, capacity, 2 * capacity)
    row += jnp.where(kind == 2, 0, (1 - kind) * capacity) + position
    row = jnp.where(kind == 3, (6 + turn) * capacity + position, row)
    row = jnp.where(turn < 2, turn * block + mine, row)
    place = places(kind >= 0, row, 4 * block)
    place_back = places(kind >= 0, turn * block + mine, 4 * block)
    own_rows, beside_rows, across3, across2, across10 = pack(
        place, acts, cotan, [(1, 4 * capacity)] * 2 + [(2, capacity)] * 2 + [(2, 2 * capacity)]
    )

    def over_x(blocks):
        moved = send(blocks, beside(2))
        return moved, send(moved[1:], beside(1))

    beside_rows = send(beside_rows, beside(1))
    across3 = over_x(across3)
    stage3 = (own_rows, beside_rows) + across3
    rows3 = jnp.concatenate([r[0, :, :capacity] for r in stage3], axis=1)
    handed = send(rows3, inward)
    across2 = over_x(after(across2, across3[0]))
    across10 = over_x(after(across10, across2[1]))
    rows2 = [r[0, :, capacity:2 * capacity] for r in (own_rows, beside_rows)] + [r[0] for r in across2]
    rows2 = jnp.concatenate(rows2, axis=1)
    stage10 = (own_rows, beside_rows) + across10
    outer = send(crossed, outward)
    far = send(pair, cross)

    up2, down2, dx_early, late_rows = early_group(end_flag, rows3, rows2, crossed)
    up3, down3, dx_late, swapped = late_group(end_flag, late_rows, handed, far, outer)
    up2_in = send(up3, inward)
    down3, swapped, up3 = send(down3, cross), send(swapped, swap), send(up3, cross)

    swapped, down3 = lax.optimization_barrier((swapped, down3))
    dx_own, dx_beside, *dx_across, up1, down1, up0, down0 = near_groups(
        end_flag, stage10, pair, down, up, dx_late, dx_early, swapped, capacity,
        (2 * capacity, 2 * capacity, 0, 0),
    )

    def add(a, b):
        return (a.astype(F32) + b.astype(F32)).astype(BF16)

    down2, down1 = add(down2, swapped), add(down1, down3)
    dx_across[0] = send(dx_across[0], beside(2))
    dx_across[1] = send(after(dx_across[1], dx_across[0]), beside(2))
    up2_in, up3 = after((up2_in, up3), down2, down1, dx_across[0])
    down2, down1 = send(down2, cross), send(down1, swap)
    up2, up1 = send(add(up2, up2_in), cross), send(add(up1, up3), swap)

    back = [dx_own, send(dx_beside, beside(1)), dx_across[0], send(dx_across[1], beside(1))]
    half_acts = unpack(place_back.T, back, tokens, 0)
    grad_acts = unpack(place_back.T, back, tokens, 1, half_acts)
    raw_down, down_squares = final_sum(down0, down2, down1)
    raw_up, up_squares = final_sum(up0, up2, up1)
    part = down_squares + up_squares
    part = part + sum(after([send(part, beside(m)) for m in range(1, plane)], half_acts))
    along = [[(i, (i // plane ^ m) * plane + i % plane) for i in range(ndevices)] for m in range(1, 4)]
    parts = after([send(part, pairs) for pairs in along], grad_acts)
    return (grad_acts, *scaled((raw_down, raw_up), (part, *parts), ndevices))


def solution(mesh):
    plane = 4
    by_planes = mesh.shape["dp"] == 4 * plane

    def per_device(*arrays):
        if by_planes:
            return move_adapters(plane, *arrays)
        return move_tokens(*arrays)

    rows, pools = P(("parts", "dp"), None), P(("parts", "dp"), None, None)
    return jax.shard_map(
        per_device,
        mesh=mesh,
        in_specs=(rows, rows, rows, P("parts"), pools, pools),
        out_specs=(rows, pools, pools),
        check_vma=False,
    )
```

```python
import jax
import jax.numpy as jnp
from jax import lax
from jax.experimental import pallas as pl
from jax.experimental.pallas import tpu as pltpu
from jax.sharding import PartitionSpec as P

BF16, F32 = jnp.bfloat16, jnp.float32
ROWS_OF = (((1,), (1,)), ((), ()))
OUTER = (((0,), (0,)), ((), ()))
INNER = (((1,), (0,)), ((), ()))
HBM = pl.BlockSpec(memory_space=pltpu.HBM)
WHOLE = pl.BlockSpec(memory_space=pltpu.VMEM)
VMEM_BYTES = 16 * 2**20


def dot32(a, b, dims=INNER):
    return lax.dot_general(a, b, dims, preferred_element_type=F32)


def route(token_task_index, task_slot_lookup, ndevices):
    pool = task_slot_lookup.shape[0]
    task_hot = (token_task_index == jnp.arange(pool, dtype=jnp.int32)[None, :]).astype(jnp.int32)
    owner = jnp.sum(task_hot * task_slot_lookup[None, :], axis=1)
    owner_hot = (owner[:, None] == jnp.arange(ndevices, dtype=jnp.int32)[None, :]).astype(jnp.int32)
    before = jnp.cumsum(owner_hot, axis=0) - owner_hot
    position = jnp.sum(before * owner_hot, axis=1)
    return owner, position


def clipped(raw_down, raw_up, ndevices):
    local_sq = jnp.sum(raw_down * raw_down) + jnp.sum(raw_up * raw_up)
    total = lax.psum(local_sq, "dp")
    norm = jnp.sqrt(total + 1e-06)
    limit = jnp.sqrt(jnp.float32(2 * raw_down.shape[0] * raw_down.shape[1] * ndevices))
    factor = jnp.minimum(jnp.float32(1.0), limit / norm)
    return (raw_down * factor)[None], (raw_up * factor)[None]


def move_tokens(acts, cotan, token_task_index, task_slot_lookup, pool_down_factors, pool_up_factors):
    ndevices = lax.axis_size("dp")
    tokens, width = acts.shape
    capacity = 2 * ((tokens + ndevices - 1) // ndevices)
    slots = ndevices * capacity
    owner, position = route(token_task_index, task_slot_lookup, ndevices)
    dest = owner * capacity + position
    placed = (jnp.arange(slots, dtype=jnp.int32)[:, None] == dest[None, :]).astype(BF16)

    def exchange(rows):
        rows = rows.reshape(ndevices, capacity, width)
        return lax.all_to_all(rows, "dp", split_axis=0, concat_axis=0, tiled=True).reshape(slots, width)

    down, up = pool_down_factors[0], pool_up_factors[0]
    rows_x = exchange(dot32(placed, acts).astype(BF16))
    rows_g = exchange(dot32(placed, cotan).astype(BF16))
    hidden = dot32(rows_x, down, ROWS_OF).astype(BF16)
    inner = dot32(rows_g, up, ROWS_OF).astype(BF16)
    returned = exchange(dot32(inner, down).astype(BF16))
    grad_acts = dot32(placed, returned, OUTER).astype(BF16)
    raw_up = dot32(hidden, rows_g, OUTER)
    raw_down = dot32(inner, rows_x, OUTER)
    return (grad_acts,) + clipped(raw_down, raw_up, ndevices)


def in_hbm(*arrays):
    return [pltpu.with_memory_space_constraint(a, pltpu.HBM) for a in arrays]


def in_vmem(*arrays):
    return [pltpu.with_memory_space_constraint(a, pltpu.VMEM) for a in arrays]


def kernel_params(semantics=("arbitrary",)):
    return pltpu.CompilerParams(dimension_semantics=semantics, vmem_limit_bytes=VMEM_BYTES)


def pack(place, acts, cotan, shapes):
    tokens, width = acts.shape
    tile = min(width, 1024)
    tiles = width // tile

    def body(place_ref, x_in, g_in, *refs):
        out_refs, (rows, sems) = refs[:-2], refs[-2:]
        step = pl.program_id(0)

        def copies(i):
            cut = pl.ds(pl.multiple_of(i * tile, tile), tile)
            return [pltpu.make_async_copy(r.at[:, cut], rows.at[k, :, cut], sems.at[k, i]) for k, r in enumerate((x_in, g_in))]

        @pl.when(step == 0)
        def _():
            for i in range(tiles):
                for c in copies(i):
                    c.start()

        for c in copies(step):
            c.wait()
        cut = pl.ds(pl.multiple_of(step * tile, tile), tile)
        for k in range(2):
            moved = dot32(place_ref[...], rows[k, :, cut]).astype(BF16)
            first = 0
            for out_ref, (columns, size) in zip(out_refs, shapes):
                for c in range(columns):
                    out_ref[c, k] = moved[first:first + size]
                    first += size

    return pl.pallas_call(
        body,
        grid=(tiles,),
        in_specs=[pl.BlockSpec(place.shape, lambda i: (0, 0)), HBM, HBM],
        out_specs=[pl.BlockSpec((c, 2, size, tile), lambda i: (0, 0, 0, i)) for c, size in shapes],
        out_shape=[jax.ShapeDtypeStruct((c, 2, size, width), BF16) for c, size in shapes],
        scratch_shapes=[pltpu.VMEM((2, tokens, width), BF16), pltpu.SemaphoreType.DMA((2, tiles))],
        compiler_params=kernel_params(),
    )(place, *in_hbm(acts, cotan))


def unpack(place, blocks, tokens, half, into=None):
    width = blocks[0].shape[1]
    tile = min(width // 2, 2048)
    first = half * (width // 2 // tile)
    rest = () if into is None else (into,)

    def body(place_ref, *refs):
        rows = jnp.concatenate([ref[...] for ref in refs[:len(blocks)]], axis=0)
        refs[-1][...] = dot32(place_ref[...], rows).astype(BF16)

    return pl.pallas_call(
        body,
        grid=(width // 2 // tile,),
        in_specs=[pl.BlockSpec(place.shape, lambda i: (0, 0))]
        + [pl.BlockSpec((b.shape[0], tile), lambda i: (0, i + first)) for b in blocks]
        + [pl.BlockSpec(memory_space=pl.ANY)] * len(rest),
        out_specs=pl.BlockSpec((tokens, tile), lambda i: (0, i + first)),
        out_shape=jax.ShapeDtypeStruct((tokens, width), BF16),
        input_output_aliases={1 + len(blocks): 0} if rest else {},
        compiler_params=kernel_params(),
    )(place, *in_hbm(blocks[0]), *blocks[1:], *rest)


def final_sum(first, *others):
    rank, width = first.shape
    tile = min(width, 1024)

    def body(first_ref, *refs):
        other_refs, (total_ref, square_ref) = refs[:-2], refs[-2:]
        squares = jnp.zeros((8, 128), F32)
        for i in range(width // tile):
            cut = pl.ds(i * tile, tile)
            total = first_ref[:, cut]
            for ref in other_refs:
                total += ref[:, cut].astype(F32)
            total_ref[:, cut] = total
            total = total * total
            for r in range(0, rank, 8):
                for c in range(0, tile, 128):
                    squares += total[r:r + 8, c:c + 128]
        square_ref[...] = squares

    return in_place(body, [((rank, width), F32), ((8, 128), F32)], first, *others)


def scaled(raws, parts, ndevices):
    rank, width = raws[0].shape
    tile = min(width, 1024)
    limit = float(2 * rank * width * ndevices) ** 0.5

    def body(*refs):
        raw_refs, part_refs = refs[:len(raws)], refs[len(raws):len(raws) + len(parts)]
        outs, (held, sems) = refs[len(raws) + len(parts):-2], refs[-2:]
        total = jnp.sum(sum(ref[...] for ref in part_refs), axis=(0, 1), keepdims=True)
        factor = jnp.minimum(jnp.float32(1.0), jnp.float32(limit) / jnp.sqrt(total + 1e-06))
        copies = []
        for i in range(width // tile):
            cut = pl.ds(i * tile, tile)
            for n, (raw_ref, out) in enumerate(zip(raw_refs, outs)):
                held[n, :, cut] = raw_ref[:, cut] * factor
                copies.append(pltpu.make_async_copy(held.at[n, :, cut], out.at[0, :, cut], sems.at[n, i]))
                copies[-1].start()
        for c in copies:
            c.wait()

    return pl.pallas_call(
        body,
        in_specs=[WHOLE] * (len(raws) + len(parts)),
        out_specs=[HBM] * len(raws),
        out_shape=[pltpu.HBM((1, rank, width), F32)] * len(raws),
        scratch_shapes=[
            pltpu.VMEM((len(raws), rank, width), F32),
            pltpu.SemaphoreType.DMA((len(raws), width // tile)),
        ],
        compiler_params=pltpu.CompilerParams(vmem_limit_bytes=VMEM_BYTES),
    )(*in_vmem(*raws, *parts))


def corner(rows, first_rows, columns, first_columns):
    upper = lax.broadcasted_iota(jnp.int32, (rows, columns), 0) < first_rows
    return upper == (lax.broadcasted_iota(jnp.int32, (rows, columns), 1) < first_columns)


def far_sums(tokens, factor, up_ref, down_ref, dx_refs):
    rank, width = up_ref.shape
    tile = min(width, 2048)
    cuts = [pl.ds(i * tile, tile) for i in range(width // tile)]
    hidden, inner = (sum(dot32(tokens(k, cut), factor(k, cut), ROWS_OF) for cut in cuts) for k in range(2))
    hidden_t, inner_t, inner = hidden.T.astype(BF16), inner.T.astype(BF16), inner.astype(BF16)
    for cut in cuts:
        up_ref[:, cut] = dot32(hidden_t, tokens(1, cut)).astype(BF16)
        down_ref[:, cut] = dot32(inner_t, tokens(0, cut)).astype(BF16)
        dx = dot32(inner, factor(0, cut)).astype(BF16)
        for n, ref in enumerate(dx_refs):
            rows = ref.shape[0]
            ref[:, cut] = dx[n * rows:(n + 1) * rows]


def in_place(body, out_shapes, *arrays, flags=None):
    first = [] if flags is None else [flags]
    return pl.pallas_call(
        body,
        in_specs=[pl.BlockSpec(memory_space=pltpu.SMEM)] * len(first) + [WHOLE] * len(arrays),
        out_specs=[WHOLE] * len(out_shapes),
        out_shape=[pltpu.VMEM(*shape) for shape in out_shapes],
        compiler_params=pltpu.CompilerParams(vmem_limit_bytes=VMEM_BYTES),
    )(*first, *in_vmem(*arrays))


def stack(down, up):
    def body(down_ref, up_ref, out_ref):
        out_ref[0] = down_ref[...]
        out_ref[1] = up_ref[...]

    return in_place(body, [((2, *down.shape), BF16)], down, up)[0]


def early_group(flags, rows3, rows2, crossed):
    _, block, width = rows2.shape
    rank = crossed.shape[1]

    def body(flags_ref, rows3_ref, rows2_ref, crossed_ref, up_ref, down_ref, dx_ref, late_ref):
        far_sums(
            lambda k, cut: rows2_ref[k, :, cut], lambda k, cut: crossed_ref[k, :, cut], up_ref, down_ref, (dx_ref,)
        )
        late_ref[...] = jnp.where(flags_ref[0] == 1, rows2_ref[...], rows3_ref[...])

    shapes = [((rank, width), BF16)] * 2 + [((block, width), BF16), ((2, block, width), BF16)]
    return in_place(body, shapes, rows3, rows2, crossed, flags=flags)


def late_group(flags, rows, handed, far, outer):
    _, block, width = rows.shape
    rank = far.shape[1]

    def body(flags_ref, rows_ref, handed_ref, outer_ref, far_ref, up_ref, down_ref, dx_ref, swap_ref):
        at_end = flags_ref[0] == 1
        far_sums(
            lambda k, cut: jnp.concatenate([rows_ref[k, :, cut], handed_ref[k, :, cut]], axis=0),
            lambda k, cut: jnp.where(at_end, outer_ref[k, :, cut], far_ref[k, :, cut]),
            up_ref,
            down_ref,
            (dx_ref, swap_ref),
        )

        @pl.when(at_end)
        def _():
            swap_ref[...] = down_ref[...]

    shapes = [((rank, width), BF16)] * 2 + [((block, width), BF16)] * 2
    return in_place(body, shapes, rows, handed, outer, far, flags=flags)


def near_groups(flags, stage, pair, down, up, dx_late, dx_early, swapped, capacity, first1):
    plane = len(stage)
    rank, width = down.shape
    block = plane * capacity
    tile = min(width, 2048)
    cuts = [pl.ds(i * tile, tile) for i in range(width // tile)]

    def body(flags_ref, *refs):
        stage_in, refs = refs[:plane], refs[plane:]
        pair_in, down_in, up_in, late_ref, early_ref, swapped_ref = refs[:6]
        dx_refs, sum_refs = refs[6:6 + plane], refs[6 + plane:]
        own_in = (down_in, up_in)
        at_end = flags_ref[0] == 1

        def rows(k, cut):
            return jnp.concatenate(
                [
                    r[0, k, pl.ds(first + n * capacity, capacity), cut]
                    for n in range(2)
                    for r, first in zip(stage_in, first1)
                ],
                axis=0,
            )

        def factors(k, cut):
            return jnp.concatenate([pair_in[k, :, cut], own_in[k][:, cut]], axis=0)

        is_mine = corner(2 * block, block, 2 * rank, rank)
        sums = [sum(dot32(rows(k, cut), factors(k, cut), ROWS_OF) for cut in cuts) for k in range(2)]
        sums = [jnp.where(is_mine, total, 0.0) for total in sums]
        left, inner = [total.T.astype(BF16) for total in sums], sums[1].astype(BF16)
        for cut in cuts:
            for k in range(2):
                both = dot32(left[k], rows(1 - k, cut))
                sum_refs[k][:, cut] = both[:rank]
                sum_refs[2 + k][:, cut] = both[rank:]
            dx = dot32(inner, factors(0, cut)).astype(BF16)
            late = late_ref[:, cut]
            moved = [jnp.where(at_end, swapped_ref[:, cut], late), jnp.where(at_end, late, early_ref[:, cut])]
            for n, dx in enumerate(moved + [dx[:block], dx[block:]]):
                for m in range(plane):
                    dx_refs[m][n * capacity:(n + 1) * capacity, cut] = dx[m * capacity:(m + 1) * capacity]

    shapes = [((4 * capacity, width), BF16)] * plane + [((rank, width), F32)] * 4
    return in_place(body, shapes, *stage, pair, down, up, dx_late, dx_early, swapped, flags=flags)


def move_adapters(plane, acts, cotan, token_task_index, task_slot_lookup, pool_down_factors, pool_up_factors):
    ndevices = lax.axis_size("dp")
    tokens, width = acts.shape
    capacity = 2 * ((tokens + ndevices - 1) // ndevices)
    me = lax.axis_index("dp")
    z, column = me // plane, me % plane
    is_end = (z == 0) | (z == 3)
    end_flag = is_end.astype(jnp.int32).reshape(1)

    def planes(pairs):
        return [(a * plane + c, b * plane + c) for a, b in pairs for c in range(plane)]

    swap = planes([(0, 1), (1, 0), (2, 3), (3, 2)])
    cross = planes([(1, 2), (2, 1)])
    outward = planes([(1, 0), (2, 3)])
    inward = planes([(0, 1), (3, 2)])

    def send(array, pairs):
        return lax.ppermute(array, "dp", pairs)

    def after(arrays, *others):
        return lax.optimization_barrier((arrays, others))[0]

    def beside(m):
        return [(i, (i // plane) * plane + ((i % plane) ^ m)) for i in range(ndevices)]

    down, up = pool_down_factors[0], pool_up_factors[0]
    own = stack(down, up)
    pair = send(own, swap)
    crossed = send(own, cross)

    owner, position = route(token_task_index, task_slot_lookup, ndevices)
    owner_z, turn = owner // plane, (owner % plane) ^ column
    other_mid = jnp.where(z < 2, 2, 1)
    kind = jnp.where(owner_z == z, 0, jnp.where(owner_z == (z ^ 1), 1, jnp.where(owner_z == other_mid, 2, 3)))

    def places(wanted, row, rows):
        hot = jnp.arange(rows, dtype=jnp.int32)[:, None] == row[None, :]
        return (hot & wanted[None, :]).astype(BF16)

    def after(arrays, *others):
        return lax.optimization_barrier((arrays, others))[0]

    block = plane * capacity
    mine = (3 - kind) * capacity + position
    row = jnp.where(kind == 2, 10 * capacity, 12 * capacity) + (turn - 2) * jnp.where(kind == 2, capacity, 2 * capacity)
    row += jnp.where(kind == 2, 0, (1 - kind) * capacity) + position
    row = jnp.where(kind == 3, (6 + turn) * capacity + position, row)
    row = jnp.where(turn < 2, turn * block + mine, row)
    place = places(kind >= 0, row, 4 * block)
    place_back = places(kind >= 0, turn * block + mine, 4 * block)
    own_rows, beside_rows, across3, across2, across10 = pack(
        place, acts, cotan, [(1, 4 * capacity)] * 2 + [(2, capacity)] * 2 + [(2, 2 * capacity)]
    )

    def over_x(blocks):
        moved = send(blocks, beside(2))
        return moved, send(moved[1:], beside(1))

    beside_rows = send(beside_rows, beside(1))
    across3 = over_x(across3)
    stage3 = (own_rows, beside_rows) + across3
    rows3 = jnp.concatenate([r[0, :, :capacity] for r in stage3], axis=1)
    handed = send(rows3, inward)
    across2 = over_x(after(across2, across3[0]))
    across10 = over_x(after(across10, across2[1]))
    rows2 = [r[0, :, capacity:2 * capacity] for r in (own_rows, beside_rows)] + [r[0] for r in across2]
    rows2 = jnp.concatenate(rows2, axis=1)
    stage10 = (own_rows, beside_rows) + across10
    outer = send(crossed, outward)
    far = send(pair, cross)

    up2, down2, dx_early, late_rows = early_group(end_flag, rows3, rows2, crossed)
    up3, down3, dx_late, swapped = late_group(end_flag, late_rows, handed, far, outer)
    up2_in = send(up3, inward)
    down3, swapped, up3 = send(down3, cross), send(swapped, swap), send(up3, cross)

    swapped, down3 = lax.optimization_barrier((swapped, down3))
    dx_own, dx_beside, *dx_across, up1, down1, up0, down0 = near_groups(
        end_flag, stage10, pair, down, up, dx_late, dx_early, swapped, capacity,
        (2 * capacity, 2 * capacity, 0, 0),
    )

    def add(a, b):
        return (a.astype(F32) + b.astype(F32)).astype(BF16)

    down2, down1 = add(down2, swapped), add(down1, down3)
    dx_across[0] = send(dx_across[0], beside(2))
    dx_across[1] = send(after(dx_across[1], dx_across[0]), beside(2))
    up2_in, up3 = after((up2_in, up3), down2, down1, dx_across[0])
    down2, down1 = send(down2, cross), send(down1, swap)
    up2, up1 = send(add(up2, up2_in), cross), send(add(up1, up3), swap)

    back = [dx_own, send(dx_beside, beside(1)), dx_across[0], send(dx_across[1], beside(1))]
    half_acts = unpack(place_back.T, back, tokens, 0)
    grad_acts = unpack(place_back.T, back, tokens, 1, half_acts)
    raw_down, down_squares = final_sum(down0, down2, down1)
    raw_up, up_squares = final_sum(up0, up2, up1)
    part = down_squares + up_squares
    part = part + sum(after([send(part, beside(m)) for m in range(1, plane)], half_acts))
    along = [[(i, (i // plane ^ m) * plane + i % plane) for i in range(ndevices)] for m in range(1, 4)]
    parts = after([send(part, pairs) for pairs in along], grad_acts)
    return (grad_acts, *scaled((raw_down, raw_up), (part, *parts), ndevices))


def solution(mesh):
    plane = 4
    by_planes = mesh.shape["dp"] == 4 * plane

    def per_device(*arrays):
        if by_planes:
            return move_adapters(plane, *arrays)
        return move_tokens(*arrays)

    rows, pools = P(("parts", "dp"), None), P(("parts", "dp"), None, None)
    return jax.shard_map(
        per_device,
        mesh=mesh,
        in_specs=(rows, rows, rows, P("parts"), pools, pools),
        out_specs=(rows, pools, pools),
        check_vma=False,
    )
```

```python
import jax
import jax.numpy as jnp
from jax import lax
from jax.experimental import pallas as pl
from jax.experimental.pallas import tpu as pltpu
from jax.sharding import PartitionSpec as P

BF16, F32 = jnp.bfloat16, jnp.float32
ROWS_OF = (((1,), (1,)), ((), ()))
OUTER = (((0,), (0,)), ((), ()))
INNER = (((1,), (0,)), ((), ()))
HBM = pl.BlockSpec(memory_space=pltpu.HBM)
WHOLE = pl.BlockSpec(memory_space=pltpu.VMEM)
VMEM_BYTES = 12 * 2**20


def dot32(a, b, dims=INNER):
    return lax.dot_general(a, b, dims, preferred_element_type=F32)


def route(token_task_index, task_slot_lookup, ndevices):
    pool = task_slot_lookup.shape[0]
    task_hot = (token_task_index == jnp.arange(pool, dtype=jnp.int32)[None, :]).astype(jnp.int32)
    owner = jnp.sum(task_hot * task_slot_lookup[None, :], axis=1)
    owner_hot = (owner[:, None] == jnp.arange(ndevices, dtype=jnp.int32)[None, :]).astype(jnp.int32)
    before = jnp.cumsum(owner_hot, axis=0) - owner_hot
    position = jnp.sum(before * owner_hot, axis=1)
    return owner, position


def clipped(raw_down, raw_up, ndevices):
    local_sq = jnp.sum(raw_down * raw_down) + jnp.sum(raw_up * raw_up)
    total = lax.psum(local_sq, "dp")
    norm = jnp.sqrt(total + 1e-06)
    limit = jnp.sqrt(jnp.float32(2 * raw_down.shape[0] * raw_down.shape[1] * ndevices))
    factor = jnp.minimum(jnp.float32(1.0), limit / norm)
    return (raw_down * factor)[None], (raw_up * factor)[None]


def move_tokens(acts, cotan, token_task_index, task_slot_lookup, pool_down_factors, pool_up_factors):
    ndevices = lax.axis_size("dp")
    tokens, width = acts.shape
    capacity = 2 * ((tokens + ndevices - 1) // ndevices)
    slots = ndevices * capacity
    owner, position = route(token_task_index, task_slot_lookup, ndevices)
    dest = owner * capacity + position
    placed = (jnp.arange(slots, dtype=jnp.int32)[:, None] == dest[None, :]).astype(BF16)

    def exchange(rows):
        rows = rows.reshape(ndevices, capacity, width)
        return lax.all_to_all(rows, "dp", split_axis=0, concat_axis=0, tiled=True).reshape(slots, width)

    down, up = pool_down_factors[0], pool_up_factors[0]
    rows_x = exchange(dot32(placed, acts).astype(BF16))
    rows_g = exchange(dot32(placed, cotan).astype(BF16))
    hidden = dot32(rows_x, down, ROWS_OF).astype(BF16)
    inner = dot32(rows_g, up, ROWS_OF).astype(BF16)
    returned = exchange(dot32(inner, down).astype(BF16))
    grad_acts = dot32(placed, returned, OUTER).astype(BF16)
    raw_up = dot32(hidden, rows_g, OUTER)
    raw_down = dot32(inner, rows_x, OUTER)
    return (grad_acts,) + clipped(raw_down, raw_up, ndevices)


def in_hbm(*arrays):
    return [pltpu.with_memory_space_constraint(a, pltpu.HBM) for a in arrays]


def in_vmem(*arrays):
    return [pltpu.with_memory_space_constraint(a, pltpu.VMEM) for a in arrays]


def kernel_params(semantics=("arbitrary",)):
    return pltpu.CompilerParams(dimension_semantics=semantics, vmem_limit_bytes=VMEM_BYTES)


def pack(place, acts, cotan, shapes):
    tokens, width = acts.shape
    tile = min(width, 1024)
    tiles = width // tile

    def body(place_ref, x_in, g_in, *refs):
        out_refs, (rows, sems) = refs[:-2], refs[-2:]
        step = pl.program_id(0)

        def copies(i):
            cut = pl.ds(pl.multiple_of(i * tile, tile), tile)
            return [pltpu.make_async_copy(r.at[:, cut], rows.at[k, :, cut], sems.at[k, i]) for k, r in enumerate((x_in, g_in))]

        @pl.when(step == 0)
        def _():
            for i in range(tiles):
                for c in copies(i):
                    c.start()

        for c in copies(step):
            c.wait()
        cut = pl.ds(pl.multiple_of(step * tile, tile), tile)
        for k in range(2):
            moved = dot32(place_ref[...], rows[k, :, cut]).astype(BF16)
            first = 0
            for out_ref, (columns, size) in zip(out_refs, shapes):
                for c in range(columns):
                    out_ref[c, k] = moved[first:first + size]
                    first += size

    return pl.pallas_call(
        body,
        grid=(tiles,),
        in_specs=[pl.BlockSpec(place.shape, lambda i: (0, 0)), HBM, HBM],
        out_specs=[pl.BlockSpec((c, 2, size, tile), lambda i: (0, 0, 0, i)) for c, size in shapes],
        out_shape=[jax.ShapeDtypeStruct((c, 2, size, width), BF16) for c, size in shapes],
        scratch_shapes=[pltpu.VMEM((2, tokens, width), BF16), pltpu.SemaphoreType.DMA((2, tiles))],
        compiler_params=kernel_params(),
    )(place, *in_hbm(acts, cotan))


def unpack(place, blocks, tokens, half, into=None):
    width = blocks[0].shape[1]
    tile = min(width // 2, 2048)
    first = half * (width // 2 // tile)
    rest = () if into is None else (into,)

    def body(place_ref, *refs):
        rows = jnp.concatenate([ref[...] for ref in refs[:len(blocks)]], axis=0)
        refs[-1][...] = dot32(place_ref[...], rows).astype(BF16)

    return pl.pallas_call(
        body,
        grid=(width // 2 // tile,),
        in_specs=[pl.BlockSpec(place.shape, lambda i: (0, 0))]
        + [pl.BlockSpec((b.shape[0], tile), lambda i: (0, i + first)) for b in blocks]
        + [pl.BlockSpec(memory_space=pl.ANY)] * len(rest),
        out_specs=pl.BlockSpec((tokens, tile), lambda i: (0, i + first)),
        out_shape=jax.ShapeDtypeStruct((tokens, width), BF16),
        input_output_aliases={1 + len(blocks): 0} if rest else {},
        compiler_params=kernel_params(),
    )(place, *in_hbm(blocks[0]), *blocks[1:], *rest)


def final_sum(first, *others):
    rank, width = first.shape
    tile = min(width, 1024)

    def body(first_ref, *refs):
        other_refs, (total_ref, square_ref) = refs[:-2], refs[-2:]
        squares = jnp.zeros((8, 128), F32)
        for i in range(width // tile):
            cut = pl.ds(i * tile, tile)
            total = first_ref[:, cut]
            for ref in other_refs:
                total += ref[:, cut].astype(F32)
            total_ref[:, cut] = total
            total = total * total
            for r in range(0, rank, 8):
                for c in range(0, tile, 128):
                    squares += total[r:r + 8, c:c + 128]
        square_ref[...] = squares

    return in_place(body, [((rank, width), F32), ((8, 128), F32)], first, *others)


def scaled(raws, parts, ndevices):
    rank, width = raws[0].shape
    tile = min(width, 1024)
    limit = float(2 * rank * width * ndevices) ** 0.5

    def body(*refs):
        raw_refs, part_refs = refs[:len(raws)], refs[len(raws):len(raws) + len(parts)]
        outs, (held, sems) = refs[len(raws) + len(parts):-2], refs[-2:]
        total = jnp.sum(sum(ref[...] for ref in part_refs), axis=(0, 1), keepdims=True)
        factor = jnp.minimum(jnp.float32(1.0), jnp.float32(limit) / jnp.sqrt(total + 1e-06))
        copies = []
        for i in range(width // tile):
            cut = pl.ds(i * tile, tile)
            for n, (raw_ref, out) in enumerate(zip(raw_refs, outs)):
                held[n, :, cut] = raw_ref[:, cut] * factor
                copies.append(pltpu.make_async_copy(held.at[n, :, cut], out.at[0, :, cut], sems.at[n, i]))
                copies[-1].start()
        for c in copies:
            c.wait()

    return pl.pallas_call(
        body,
        in_specs=[WHOLE] * (len(raws) + len(parts)),
        out_specs=[HBM] * len(raws),
        out_shape=[pltpu.HBM((1, rank, width), F32)] * len(raws),
        scratch_shapes=[
            pltpu.VMEM((len(raws), rank, width), F32),
            pltpu.SemaphoreType.DMA((len(raws), width // tile)),
        ],
        compiler_params=pltpu.CompilerParams(vmem_limit_bytes=VMEM_BYTES),
    )(*in_vmem(*raws, *parts))


def corner(rows, first_rows, columns, first_columns):
    upper = lax.broadcasted_iota(jnp.int32, (rows, columns), 0) < first_rows
    return upper == (lax.broadcasted_iota(jnp.int32, (rows, columns), 1) < first_columns)


def far_sums(tokens, factor, up_ref, down_ref, dx_ref, inner_ref=None):
    rank, width = up_ref.shape
    tile = min(width, 2048)
    cuts = [pl.ds(i * tile, tile) for i in range(width // tile)]
    hidden, inner = (sum(dot32(tokens(k, cut), factor(k, cut), ROWS_OF) for cut in cuts) for k in range(2))
    hidden_t, inner_t, inner = hidden.T.astype(BF16), inner.T.astype(BF16), inner.astype(BF16)
    rows = inner.shape[0] - dx_ref.shape[0]
    if inner_ref is not None:
        inner_ref[...] = inner[:rows]
    for cut in cuts:
        up_ref[:, cut] = dot32(hidden_t, tokens(1, cut)).astype(BF16)
        down_ref[:, cut] = dot32(inner_t, tokens(0, cut)).astype(BF16)
        dx_ref[:, cut] = dot32(inner[rows:], factor(0, cut)).astype(BF16)


def in_place(body, out_shapes, *arrays, flags=None):
    first = [] if flags is None else [flags]
    return pl.pallas_call(
        body,
        in_specs=[pl.BlockSpec(memory_space=pltpu.SMEM)] * len(first) + [WHOLE] * len(arrays),
        out_specs=[WHOLE] * len(out_shapes),
        out_shape=[pltpu.VMEM(*shape) for shape in out_shapes],
        compiler_params=pltpu.CompilerParams(vmem_limit_bytes=VMEM_BYTES),
    )(*first, *in_vmem(*arrays))


def early_group(flags, rows3, rows2, crossed):
    _, block, width = rows2.shape
    rank = crossed.shape[1]

    def body(flags_ref, rows3_ref, rows2_ref, crossed_ref, up_ref, down_ref, dx_ref, late_ref):
        far_sums(
            lambda k, cut: rows2_ref[k, :, cut], lambda k, cut: crossed_ref[k, :, cut], up_ref, down_ref, dx_ref
        )
        late_ref[...] = jnp.where(flags_ref[0] == 1, rows2_ref[...], rows3_ref[...])

    shapes = [((rank, width), BF16)] * 2 + [((block, width), BF16), ((2, block, width), BF16)]
    return in_place(body, shapes, rows3, rows2, crossed, flags=flags)


def late_group(flags, rows, handed, far, outer):
    _, block, width = rows.shape
    rank = far.shape[1]

    def body(flags_ref, rows_ref, handed_ref, outer_ref, far_ref, up_ref, down_ref, inner_ref, swap_ref):
        at_end = flags_ref[0] == 1
        far_sums(
            lambda k, cut: jnp.concatenate([rows_ref[k, :, cut], handed_ref[k, :, cut]], axis=0),
            lambda k, cut: jnp.where(at_end, outer_ref[k, :, cut], far_ref[k, :, cut]),
            up_ref,
            down_ref,
            swap_ref,
            inner_ref,
        )

        @pl.when(at_end)
        def _():
            swap_ref[...] = down_ref[...]

    shapes = [((rank, width), BF16)] * 2 + [((block, rank), BF16), ((block, width), BF16)]
    return in_place(body, shapes, rows, handed, outer, far, flags=flags)


def near_groups(flags, stage, pair, down, up, outer, far, inner_late, dx_early, swapped, capacity, first1):
    plane = len(stage)
    rank, width = down.shape
    block = plane * capacity
    tile = min(width, 2048)
    cuts = [pl.ds(i * tile, tile) for i in range(width // tile)]

    def body(flags_ref, *refs):
        stage_in, refs = refs[:plane], refs[plane:]
        pair_in, down_in, up_in, outer_in, far_in, late_ref, early_ref, swapped_ref = refs[:8]
        dx_refs, sum_refs = refs[8:8 + plane], refs[8 + plane:]
        own_in = (down_in, up_in)
        at_end = flags_ref[0] == 1

        def rows(k, cut):
            return jnp.concatenate(
                [
                    r[0, k, pl.ds(first + n * capacity, capacity), cut]
                    for n in range(2)
                    for r, first in zip(stage_in, first1)
                ],
                axis=0,
            )

        def factors(k, cut):
            return jnp.concatenate([pair_in[k, :, cut], own_in[k][:, cut]], axis=0)

        is_mine = corner(2 * block, block, 2 * rank, rank)
        sums = [sum(dot32(rows(k, cut), factors(k, cut), ROWS_OF) for cut in cuts) for k in range(2)]
        sums = [jnp.where(is_mine, total, 0.0) for total in sums]
        left, inner = [total.T.astype(BF16) for total in sums], sums[1].astype(BF16)
        for cut in cuts:
            for k in range(2):
                both = dot32(left[k], rows(1 - k, cut))
                sum_refs[k][:, cut] = both[:rank]
                sum_refs[2 + k][:, cut] = both[rank:]
            dx = dot32(inner, factors(0, cut)).astype(BF16)
            late = dot32(late_ref[...], jnp.where(at_end, outer_in[0, :, cut], far_in[0, :, cut])).astype(BF16)
            moved = [jnp.where(at_end, swapped_ref[:, cut], late), jnp.where(at_end, late, early_ref[:, cut])]
            for n, dx in enumerate(moved + [dx[:block], dx[block:]]):
                for m in range(plane):
                    dx_refs[m][n * capacity:(n + 1) * capacity, cut] = dx[m * capacity:(m + 1) * capacity]

    shapes = [((4 * capacity, width), BF16)] * plane + [((rank, width), F32)] * 4
    return in_place(body, shapes, *stage, pair, down, up, outer, far, inner_late, dx_early, swapped, flags=flags)


def move_adapters(plane, acts, cotan, token_task_index, task_slot_lookup, pool_down_factors, pool_up_factors):
    ndevices = lax.axis_size("dp")
    tokens, width = acts.shape
    capacity = 2 * ((tokens + ndevices - 1) // ndevices)
    me = lax.axis_index("dp")
    z, column = me // plane, me % plane
    is_end = (z == 0) | (z == 3)
    end_flag = is_end.astype(jnp.int32).reshape(1)

    def planes(pairs):
        return [(a * plane + c, b * plane + c) for a, b in pairs for c in range(plane)]

    swap = planes([(0, 1), (1, 0), (2, 3), (3, 2)])
    cross = planes([(1, 2), (2, 1)])
    outward = planes([(1, 0), (2, 3)])
    inward = planes([(0, 1), (3, 2)])

    def send(array, pairs):
        return lax.ppermute(array, "dp", pairs)

    def after(arrays, *others):
        return lax.optimization_barrier((arrays, others))[0]

    def beside(m):
        return [(i, (i // plane) * plane + ((i % plane) ^ m)) for i in range(ndevices)]

    down, up = pool_down_factors[0], pool_up_factors[0]
    own = jnp.concatenate([pool_down_factors, pool_up_factors])
    pair = send(own, swap)
    crossed = send(own, cross)

    owner, position = route(token_task_index, task_slot_lookup, ndevices)
    owner_z, turn = owner // plane, (owner % plane) ^ column
    other_mid = jnp.where(z < 2, 2, 1)
    kind = jnp.where(owner_z == z, 0, jnp.where(owner_z == (z ^ 1), 1, jnp.where(owner_z == other_mid, 2, 3)))

    def places(wanted, row, rows):
        hot = jnp.arange(rows, dtype=jnp.int32)[:, None] == row[None, :]
        return (hot & wanted[None, :]).astype(BF16)

    def after(arrays, *others):
        return lax.optimization_barrier((arrays, others))[0]

    block = plane * capacity
    mine = (3 - kind) * capacity + position
    row = jnp.where(kind == 2, 10 * capacity, 12 * capacity) + (turn - 2) * jnp.where(kind == 2, capacity, 2 * capacity)
    row += jnp.where(kind == 2, 0, (1 - kind) * capacity) + position
    row = jnp.where(kind == 3, (6 + turn) * capacity + position, row)
    row = jnp.where(turn < 2, turn * block + mine, row)
    place = places(kind >= 0, row, 4 * block)
    place_back = places(kind >= 0, turn * block + mine, 4 * block)
    own_rows, beside_rows, across3, across2, across10 = pack(
        place, acts, cotan, [(1, 4 * capacity)] * 2 + [(2, capacity)] * 2 + [(2, 2 * capacity)]
    )

    def over_x(blocks):
        moved = send(blocks, beside(2))
        return moved, send(moved[1:], beside(1))

    beside_rows = send(beside_rows, beside(1))
    across3 = over_x(across3)
    stage3 = (own_rows, beside_rows) + across3
    rows3 = jnp.concatenate([r[0, :, :capacity] for r in stage3], axis=1)
    handed = send(rows3, inward)
    across2 = over_x(after(across2, across3[0]))
    across10 = over_x(after(across10, across2[1]))
    rows2 = [r[0, :, capacity:2 * capacity] for r in (own_rows, beside_rows)] + [r[0] for r in across2]
    rows2 = jnp.concatenate(rows2, axis=1)
    stage10 = (own_rows, beside_rows) + across10
    outer = send(crossed, outward)
    far = send(pair, cross)

    up2, down2, dx_early, late_rows = early_group(end_flag, rows3, rows2, crossed)
    up3, down3, inner_late, swapped = late_group(end_flag, late_rows, handed, far, outer)
    up2_in = send(up3, inward)
    down3, swapped, up3 = send(down3, cross), send(swapped, swap), send(up3, cross)

    swapped, down3 = lax.optimization_barrier((swapped, down3))
    dx_own, dx_beside, *dx_across, up1, down1, up0, down0 = near_groups(
        end_flag, stage10, pair, down, up, outer, far, inner_late, dx_early, swapped, capacity,
        (2 * capacity, 2 * capacity, 0, 0),
    )

    def add(a, b):
        return (a.astype(F32) + b.astype(F32)).astype(BF16)

    down2, down1 = add(down2, swapped), add(down1, down3)
    dx_across[0] = send(dx_across[0], beside(2))
    dx_across[1] = send(after(dx_across[1], dx_across[0]), beside(2))
    up2_in, up3 = after((up2_in, up3), down2, down1, dx_across[0])
    down2, down1 = send(down2, cross), send(down1, swap)
    up2, up1 = send(add(up2, up2_in), cross), send(add(up1, up3), swap)

    back = [dx_own, send(dx_beside, beside(1)), dx_across[0], send(dx_across[1], beside(1))]
    half_acts = unpack(place_back.T, back, tokens, 0)
    grad_acts = unpack(place_back.T, back, tokens, 1, half_acts)
    raw_down, down_squares = final_sum(down0, down2, down1)
    raw_up, up_squares = final_sum(up0, up2, up1)
    part = down_squares + up_squares
    part = part + sum(after([send(part, beside(m)) for m in range(1, plane)], half_acts))
    along = [[(i, (i // plane ^ m) * plane + i % plane) for i in range(ndevices)] for m in range(1, 4)]
    parts = after([send(part, pairs) for pairs in along], grad_acts)
    return (grad_acts, *scaled((raw_down, raw_up), (part, *parts), ndevices))


def solution(mesh):
    plane = 4
    by_planes = mesh.shape["dp"] == 4 * plane

    def per_device(*arrays):
        if by_planes:
            return move_adapters(plane, *arrays)
        return move_tokens(*arrays)

    rows, pools = P(("parts", "dp"), None), P(("parts", "dp"), None, None)
    return jax.shard_map(
        per_device,
        mesh=mesh,
        in_specs=(rows, rows, rows, P("parts"), pools, pools),
        out_specs=(rows, pools, pools),
        check_vma=False,
    )
```

```python
import jax
import jax.numpy as jnp
from jax import lax
from jax.experimental import pallas as pl
from jax.experimental.pallas import tpu as pltpu
from jax.sharding import PartitionSpec as P

BF16, F32 = jnp.bfloat16, jnp.float32
ROWS_OF = (((1,), (1,)), ((), ()))
OUTER = (((0,), (0,)), ((), ()))
INNER = (((1,), (0,)), ((), ()))
HBM = pl.BlockSpec(memory_space=pltpu.HBM)
WHOLE = pl.BlockSpec(memory_space=pltpu.VMEM)
VMEM_BYTES = 12 * 2**20


def dot32(a, b, dims=INNER):
    return lax.dot_general(a, b, dims, preferred_element_type=F32)


def route(token_task_index, task_slot_lookup, ndevices):
    pool = task_slot_lookup.shape[0]
    task_hot = (token_task_index == jnp.arange(pool, dtype=jnp.int32)[None, :]).astype(jnp.int32)
    owner = jnp.sum(task_hot * task_slot_lookup[None, :], axis=1)
    owner_hot = (owner[:, None] == jnp.arange(ndevices, dtype=jnp.int32)[None, :]).astype(jnp.int32)
    before = jnp.cumsum(owner_hot, axis=0) - owner_hot
    position = jnp.sum(before * owner_hot, axis=1)
    return owner, position


def clipped(raw_down, raw_up, ndevices):
    local_sq = jnp.sum(raw_down * raw_down) + jnp.sum(raw_up * raw_up)
    total = lax.psum(local_sq, "dp")
    norm = jnp.sqrt(total + 1e-06)
    limit = jnp.sqrt(jnp.float32(2 * raw_down.shape[0] * raw_down.shape[1] * ndevices))
    factor = jnp.minimum(jnp.float32(1.0), limit / norm)
    return (raw_down * factor)[None], (raw_up * factor)[None]


def move_tokens(acts, cotan, token_task_index, task_slot_lookup, pool_down_factors, pool_up_factors):
    ndevices = lax.axis_size("dp")
    tokens, width = acts.shape
    capacity = 2 * ((tokens + ndevices - 1) // ndevices)
    slots = ndevices * capacity
    owner, position = route(token_task_index, task_slot_lookup, ndevices)
    dest = owner * capacity + position
    placed = (jnp.arange(slots, dtype=jnp.int32)[:, None] == dest[None, :]).astype(BF16)

    def exchange(rows):
        rows = rows.reshape(ndevices, capacity, width)
        return lax.all_to_all(rows, "dp", split_axis=0, concat_axis=0, tiled=True).reshape(slots, width)

    down, up = pool_down_factors[0], pool_up_factors[0]
    rows_x = exchange(dot32(placed, acts).astype(BF16))
    rows_g = exchange(dot32(placed, cotan).astype(BF16))
    hidden = dot32(rows_x, down, ROWS_OF).astype(BF16)
    inner = dot32(rows_g, up, ROWS_OF).astype(BF16)
    returned = exchange(dot32(inner, down).astype(BF16))
    grad_acts = dot32(placed, returned, OUTER).astype(BF16)
    raw_up = dot32(hidden, rows_g, OUTER)
    raw_down = dot32(inner, rows_x, OUTER)
    return (grad_acts,) + clipped(raw_down, raw_up, ndevices)


def in_hbm(*arrays):
    return [pltpu.with_memory_space_constraint(a, pltpu.HBM) for a in arrays]


def in_vmem(*arrays):
    return [pltpu.with_memory_space_constraint(a, pltpu.VMEM) for a in arrays]


def kernel_params(semantics=("arbitrary",)):
    return pltpu.CompilerParams(dimension_semantics=semantics, vmem_limit_bytes=VMEM_BYTES)


def pack(place, acts, cotan, shapes):
    tokens, width = acts.shape
    tile = min(width, 1024)
    tiles = width // tile

    def body(place_ref, x_in, g_in, *refs):
        out_refs, (rows, sems) = refs[:-2], refs[-2:]
        step = pl.program_id(0)

        def copies(i):
            cut = pl.ds(pl.multiple_of(i * tile, tile), tile)
            return [pltpu.make_async_copy(r.at[:, cut], rows.at[k, :, cut], sems.at[k, i]) for k, r in enumerate((x_in, g_in))]

        @pl.when(step == 0)
        def _():
            for i in range(tiles):
                for c in copies(i):
                    c.start()

        for c in copies(step):
            c.wait()
        cut = pl.ds(pl.multiple_of(step * tile, tile), tile)
        for k in range(2):
            moved = dot32(place_ref[...], rows[k, :, cut]).astype(BF16)
            first = 0
            for out_ref, (columns, size) in zip(out_refs, shapes):
                for c in range(columns):
                    out_ref[c, k] = moved[first:first + size]
                    first += size

    return pl.pallas_call(
        body,
        grid=(tiles,),
        in_specs=[pl.BlockSpec(place.shape, lambda i: (0, 0)), HBM, HBM],
        out_specs=[pl.BlockSpec((c, 2, size, tile), lambda i: (0, 0, 0, i)) for c, size in shapes],
        out_shape=[jax.ShapeDtypeStruct((c, 2, size, width), BF16) for c, size in shapes],
        scratch_shapes=[pltpu.VMEM((2, tokens, width), BF16), pltpu.SemaphoreType.DMA((2, tiles))],
        compiler_params=kernel_params(),
    )(place, *in_hbm(acts, cotan))


def unpack(place, blocks, tokens, half, into=None):
    width = blocks[0].shape[1]
    tile = min(width // 2, 2048)
    first = half * (width // 2 // tile)
    rest = () if into is None else (into,)

    def body(place_ref, *refs):
        rows = jnp.concatenate([ref[...] for ref in refs[:len(blocks)]], axis=0)
        refs[-1][...] = dot32(place_ref[...], rows).astype(BF16)

    return pl.pallas_call(
        body,
        grid=(width // 2 // tile,),
        in_specs=[pl.BlockSpec(place.shape, lambda i: (0, 0))]
        + [pl.BlockSpec((b.shape[0], tile), lambda i: (0, i + first)) for b in blocks]
        + [pl.BlockSpec(memory_space=pl.ANY)] * len(rest),
        out_specs=pl.BlockSpec((tokens, tile), lambda i: (0, i + first)),
        out_shape=jax.ShapeDtypeStruct((tokens, width), BF16),
        input_output_aliases={1 + len(blocks): 0} if rest else {},
        compiler_params=kernel_params(),
    )(place, *in_hbm(blocks[0]), *blocks[1:], *rest)


def final_sum(first, *others):
    rank, width = first.shape
    tile = min(width, 1024)

    def body(first_ref, *refs):
        other_refs, (total_ref, square_ref) = refs[:-2], refs[-2:]
        squares = jnp.zeros((8, 128), F32)
        for i in range(width // tile):
            cut = pl.ds(i * tile, tile)
            total = first_ref[:, cut]
            for ref in other_refs:
                total += ref[:, cut].astype(F32)
            total_ref[:, cut] = total
            total = total * total
            for r in range(0, rank, 8):
                for c in range(0, tile, 128):
                    squares += total[r:r + 8, c:c + 128]
        square_ref[...] = squares

    return in_place(body, [((rank, width), F32), ((8, 128), F32)], first, *others)


def scaled(raws, parts, ndevices):
    rank, width = raws[0].shape
    tile = min(width, 1024)
    limit = float(2 * rank * width * ndevices) ** 0.5

    def body(*refs):
        raw_refs, part_refs = refs[:len(raws)], refs[len(raws):len(raws) + len(parts)]
        outs, (held, sems) = refs[len(raws) + len(parts):-2], refs[-2:]
        total = jnp.sum(sum(ref[...] for ref in part_refs), axis=(0, 1), keepdims=True)
        factor = jnp.minimum(jnp.float32(1.0), jnp.float32(limit) / jnp.sqrt(total + 1e-06))
        copies = []
        for i in range(width // tile):
            cut = pl.ds(i * tile, tile)
            for n, (raw_ref, out) in enumerate(zip(raw_refs, outs)):
                held[n, :, cut] = raw_ref[:, cut] * factor
                copies.append(pltpu.make_async_copy(held.at[n, :, cut], out.at[0, :, cut], sems.at[n, i]))
                copies[-1].start()
        for c in copies:
            c.wait()

    return pl.pallas_call(
        body,
        in_specs=[WHOLE] * (len(raws) + len(parts)),
        out_specs=[HBM] * len(raws),
        out_shape=[pltpu.HBM((1, rank, width), F32)] * len(raws),
        scratch_shapes=[
            pltpu.VMEM((len(raws), rank, width), F32),
            pltpu.SemaphoreType.DMA((len(raws), width // tile)),
        ],
        compiler_params=pltpu.CompilerParams(vmem_limit_bytes=VMEM_BYTES),
    )(*in_vmem(*raws, *parts))


def corner(rows, first_rows, columns, first_columns):
    upper = lax.broadcasted_iota(jnp.int32, (rows, columns), 0) < first_rows
    return upper == (lax.broadcasted_iota(jnp.int32, (rows, columns), 1) < first_columns)


def far_sums(tokens, factor, up_ref, down_ref, dx_ref, inner_ref=None):
    rank, width = up_ref.shape
    tile = min(width, 2048)
    cuts = [pl.ds(i * tile, tile) for i in range(width // tile)]
    hidden, inner = (sum(dot32(tokens(k, cut), factor(k, cut), ROWS_OF) for cut in cuts) for k in range(2))
    hidden_t, inner_t, inner = hidden.T.astype(BF16), inner.T.astype(BF16), inner.astype(BF16)
    rows = inner.shape[0] - dx_ref.shape[0]
    if inner_ref is not None:
        inner_ref[...] = inner[:rows]
    for cut in cuts:
        up_ref[:, cut] = dot32(hidden_t, tokens(1, cut)).astype(BF16)
        down_ref[:, cut] = dot32(inner_t, tokens(0, cut)).astype(BF16)
        dx_ref[:, cut] = dot32(inner[rows:], factor(0, cut)).astype(BF16)


def in_place(body, out_shapes, *arrays, flags=None):
    first = [] if flags is None else [flags]
    return pl.pallas_call(
        body,
        in_specs=[pl.BlockSpec(memory_space=pltpu.SMEM)] * len(first) + [WHOLE] * len(arrays),
        out_specs=[WHOLE] * len(out_shapes),
        out_shape=[pltpu.VMEM(*shape) for shape in out_shapes],
        compiler_params=pltpu.CompilerParams(vmem_limit_bytes=VMEM_BYTES),
    )(*first, *in_vmem(*arrays))


def early_group(flags, rows3, rows2, crossed):
    _, block, width = rows2.shape
    rank = crossed.shape[1]

    def body(flags_ref, rows3_ref, rows2_ref, crossed_ref, up_ref, down_ref, dx_ref, late_ref):
        far_sums(
            lambda k, cut: rows2_ref[k, :, cut], lambda k, cut: crossed_ref[k, :, cut], up_ref, down_ref, dx_ref
        )
        late_ref[...] = jnp.where(flags_ref[0] == 1, rows2_ref[...], rows3_ref[...])

    shapes = [((rank, width), BF16)] * 2 + [((block, width), BF16), ((2, block, width), BF16)]
    return in_place(body, shapes, rows3, rows2, crossed, flags=flags)


def late_group(flags, rows, handed, far, outer):
    _, block, width = rows.shape
    rank = far.shape[1]

    def body(flags_ref, rows_ref, handed_ref, outer_ref, far_ref, up_ref, down_ref, inner_ref, swap_ref):
        at_end = flags_ref[0] == 1
        far_sums(
            lambda k, cut: jnp.concatenate([rows_ref[k, :, cut], handed_ref[k, :, cut]], axis=0),
            lambda k, cut: jnp.where(at_end, outer_ref[k, :, cut], far_ref[k, :, cut]),
            up_ref,
            down_ref,
            swap_ref,
            inner_ref,
        )

        @pl.when(at_end)
        def _():
            swap_ref[...] = down_ref[...]

    shapes = [((rank, width), BF16)] * 2 + [((block, rank), BF16), ((block, width), BF16)]
    return in_place(body, shapes, rows, handed, outer, far, flags=flags)


def near_groups(flags, stage, pair, down, up, outer, far, inner_late, dx_early, swapped, capacity, first1):
    plane = len(stage)
    rank, width = down.shape
    block = plane * capacity
    tile = min(width, 2048)
    cuts = [pl.ds(i * tile, tile) for i in range(width // tile)]

    def body(flags_ref, *refs):
        stage_in, refs = refs[:plane], refs[plane:]
        pair_in, down_in, up_in, outer_in, far_in, late_ref, early_ref, swapped_ref = refs[:8]
        dx_refs, sum_refs = refs[8:8 + plane], refs[8 + plane:]
        own_in = (down_in, up_in)
        at_end = flags_ref[0] == 1

        def rows(k, cut):
            return jnp.concatenate(
                [
                    r[0, k, pl.ds(first + n * capacity, capacity), cut]
                    for n in range(2)
                    for r, first in zip(stage_in, first1)
                ],
                axis=0,
            )

        def factors(k, cut):
            return jnp.concatenate([pair_in[k, :, cut], own_in[k][:, cut]], axis=0)

        is_mine = corner(2 * block, block, 2 * rank, rank)
        sums = [sum(dot32(rows(k, cut), factors(k, cut), ROWS_OF) for cut in cuts) for k in range(2)]
        sums = [jnp.where(is_mine, total, 0.0) for total in sums]
        left, inner = [total.T.astype(BF16) for total in sums], sums[1].astype(BF16)
        for cut in cuts:
            for k in range(2):
                both = dot32(left[k], rows(1 - k, cut))
                sum_refs[k][:, cut] = both[:rank]
                sum_refs[2 + k][:, cut] = both[rank:]
            dx = dot32(inner, factors(0, cut)).astype(BF16)
            late = dot32(late_ref[...], jnp.where(at_end, outer_in[0, :, cut], far_in[0, :, cut])).astype(BF16)
            moved = [jnp.where(at_end, swapped_ref[:, cut], late), jnp.where(at_end, late, early_ref[:, cut])]
            for n, dx in enumerate(moved + [dx[:block], dx[block:]]):
                for m in range(plane):
                    dx_refs[m][n * capacity:(n + 1) * capacity, cut] = dx[m * capacity:(m + 1) * capacity]

    shapes = [((4 * capacity, width), BF16)] * plane + [((rank, width), F32)] * 4
    return in_place(body, shapes, *stage, pair, down, up, outer, far, inner_late, dx_early, swapped, flags=flags)


def move_adapters(plane, acts, cotan, token_task_index, task_slot_lookup, pool_down_factors, pool_up_factors):
    ndevices = lax.axis_size("dp")
    tokens, width = acts.shape
    capacity = 2 * ((tokens + ndevices - 1) // ndevices)
    me = lax.axis_index("dp")
    z, column = me // plane, me % plane
    is_end = (z == 0) | (z == 3)
    end_flag = is_end.astype(jnp.int32).reshape(1)

    def planes(pairs):
        return [(a * plane + c, b * plane + c) for a, b in pairs for c in range(plane)]

    swap = planes([(0, 1), (1, 0), (2, 3), (3, 2)])
    cross = planes([(1, 2), (2, 1)])
    outward = planes([(1, 0), (2, 3)])
    inward = planes([(0, 1), (3, 2)])

    def send(array, pairs):
        return lax.ppermute(array, "dp", pairs)

    def after(arrays, *others):
        return lax.optimization_barrier((arrays, others))[0]

    def beside(m):
        return [(i, (i // plane) * plane + ((i % plane) ^ m)) for i in range(ndevices)]

    down, up = pool_down_factors[0], pool_up_factors[0]
    lowest, none = jnp.array(-jnp.inf, BF16), (0, 0, 0)
    own = jnp.maximum(
        lax.pad(pool_down_factors, lowest, ((0, 1, 0), none, none)),
        lax.pad(pool_up_factors, lowest, ((1, 0, 0), none, none)),
    )
    pair = send(own, swap)
    crossed = send(own, cross)

    owner, position = route(token_task_index, task_slot_lookup, ndevices)
    owner_z, turn = owner // plane, (owner % plane) ^ column
    other_mid = jnp.where(z < 2, 2, 1)
    kind = jnp.where(owner_z == z, 0, jnp.where(owner_z == (z ^ 1), 1, jnp.where(owner_z == other_mid, 2, 3)))

    def places(wanted, row, rows):
        hot = jnp.arange(rows, dtype=jnp.int32)[:, None] == row[None, :]
        return (hot & wanted[None, :]).astype(BF16)

    def after(arrays, *others):
        return lax.optimization_barrier((arrays, others))[0]

    block = plane * capacity
    mine = (3 - kind) * capacity + position
    row = jnp.where(kind == 2, 10 * capacity, 12 * capacity) + (turn - 2) * jnp.where(kind == 2, capacity, 2 * capacity)
    row += jnp.where(kind == 2, 0, (1 - kind) * capacity) + position
    row = jnp.where(kind == 3, (6 + turn) * capacity + position, row)
    row = jnp.where(turn < 2, turn * block + mine, row)
    place = places(kind >= 0, row, 4 * block)
    place_back = places(kind >= 0, turn * block + mine, 4 * block)
    own_rows, beside_rows, across3, across2, across10 = pack(
        place, acts, cotan, [(1, 4 * capacity)] * 2 + [(2, capacity)] * 2 + [(2, 2 * capacity)]
    )

    def over_x(blocks):
        moved = send(blocks, beside(2))
        return moved, send(moved[1:], beside(1))

    beside_rows = send(beside_rows, beside(1))
    across3 = over_x(across3)
    stage3 = (own_rows, beside_rows) + across3
    rows3 = jnp.concatenate([r[0, :, :capacity] for r in stage3], axis=1)
    handed = send(rows3, inward)
    across2 = over_x(after(across2, across3[0]))
    across10 = over_x(after(across10, across2[1]))
    rows2 = [r[0, :, capacity:2 * capacity] for r in (own_rows, beside_rows)] + [r[0] for r in across2]
    rows2 = jnp.concatenate(rows2, axis=1)
    stage10 = (own_rows, beside_rows) + across10
    outer = send(crossed, outward)
    far = send(pair, cross)

    up2, down2, dx_early, late_rows = early_group(end_flag, rows3, rows2, crossed)
    up3, down3, inner_late, swapped = late_group(end_flag, late_rows, handed, far, outer)
    up2_in = send(up3, inward)
    down3, swapped, up3 = send(down3, cross), send(swapped, swap), send(up3, cross)

    swapped, down3 = lax.optimization_barrier((swapped, down3))
    dx_own, dx_beside, *dx_across, up1, down1, up0, down0 = near_groups(
        end_flag, stage10, pair, down, up, outer, far, inner_late, dx_early, swapped, capacity,
        (2 * capacity, 2 * capacity, 0, 0),
    )

    def add(a, b):
        return (a.astype(F32) + b.astype(F32)).astype(BF16)

    down2, down1 = add(down2, swapped), add(down1, down3)
    dx_across[0] = send(dx_across[0], beside(2))
    dx_across[1] = send(after(dx_across[1], dx_across[0]), beside(2))
    up2_in, up3 = after((up2_in, up3), down2, down1, dx_across[0])
    down2, down1 = send(down2, cross), send(down1, swap)
    up2, up1 = send(add(up2, up2_in), cross), send(add(up1, up3), swap)

    back = [dx_own, send(dx_beside, beside(1)), dx_across[0], send(dx_across[1], beside(1))]
    half_acts = unpack(place_back.T, back, tokens, 0)
    grad_acts = unpack(place_back.T, back, tokens, 1, half_acts)
    raw_down, down_squares = final_sum(down0, down2, down1)
    raw_up, up_squares = final_sum(up0, up2, up1)
    part = down_squares + up_squares
    part = part + sum(after([send(part, beside(m)) for m in range(1, plane)], half_acts))
    along = [[(i, (i // plane ^ m) * plane + i % plane) for i in range(ndevices)] for m in range(1, 4)]
    parts = after([send(part, pairs) for pairs in along], grad_acts)
    return (grad_acts, *scaled((raw_down, raw_up), (part, *parts), ndevices))


def solution(mesh):
    plane = 4
    by_planes = mesh.shape["dp"] == 4 * plane

    def per_device(*arrays):
        if by_planes:
            return move_adapters(plane, *arrays)
        return move_tokens(*arrays)

    rows, pools = P(("parts", "dp"), None), P(("parts", "dp"), None, None)
    return jax.shard_map(
        per_device,
        mesh=mesh,
        in_specs=(rows, rows, rows, P("parts"), pools, pools),
        out_specs=(rows, pools, pools),
        check_vma=False,
    )
```

```python
import jax
import jax.numpy as jnp
from jax import lax
from jax.experimental import pallas as pl
from jax.experimental.pallas import tpu as pltpu
from jax.sharding import PartitionSpec as P

BF16, F32 = jnp.bfloat16, jnp.float32
ROWS_OF = (((1,), (1,)), ((), ()))
OUTER = (((0,), (0,)), ((), ()))
INNER = (((1,), (0,)), ((), ()))
HBM = pl.BlockSpec(memory_space=pltpu.HBM)
WHOLE = pl.BlockSpec(memory_space=pltpu.VMEM)
VMEM_BYTES = 12 * 2**20


def dot32(a, b, dims=INNER):
    return lax.dot_general(a, b, dims, preferred_element_type=F32)


def route(token_task_index, task_slot_lookup, ndevices):
    pool = task_slot_lookup.shape[0]
    task_hot = (token_task_index == jnp.arange(pool, dtype=jnp.int32)[None, :]).astype(jnp.int32)
    owner = jnp.sum(task_hot * task_slot_lookup[None, :], axis=1)
    owner_hot = (owner[:, None] == jnp.arange(ndevices, dtype=jnp.int32)[None, :]).astype(jnp.int32)
    before = jnp.cumsum(owner_hot, axis=0) - owner_hot
    position = jnp.sum(before * owner_hot, axis=1)
    return owner, position


def clipped(raw_down, raw_up, ndevices):
    local_sq = jnp.sum(raw_down * raw_down) + jnp.sum(raw_up * raw_up)
    total = lax.psum(local_sq, "dp")
    norm = jnp.sqrt(total + 1e-06)
    limit = jnp.sqrt(jnp.float32(2 * raw_down.shape[0] * raw_down.shape[1] * ndevices))
    factor = jnp.minimum(jnp.float32(1.0), limit / norm)
    return (raw_down * factor)[None], (raw_up * factor)[None]


def move_tokens(acts, cotan, token_task_index, task_slot_lookup, pool_down_factors, pool_up_factors):
    ndevices = lax.axis_size("dp")
    tokens, width = acts.shape
    capacity = 2 * ((tokens + ndevices - 1) // ndevices)
    slots = ndevices * capacity
    owner, position = route(token_task_index, task_slot_lookup, ndevices)
    dest = owner * capacity + position
    placed = (jnp.arange(slots, dtype=jnp.int32)[:, None] == dest[None, :]).astype(BF16)

    def exchange(rows):
        rows = rows.reshape(ndevices, capacity, width)
        return lax.all_to_all(rows, "dp", split_axis=0, concat_axis=0, tiled=True).reshape(slots, width)

    down, up = pool_down_factors[0], pool_up_factors[0]
    rows_x = exchange(dot32(placed, acts).astype(BF16))
    rows_g = exchange(dot32(placed, cotan).astype(BF16))
    hidden = dot32(rows_x, down, ROWS_OF).astype(BF16)
    inner = dot32(rows_g, up, ROWS_OF).astype(BF16)
    returned = exchange(dot32(inner, down).astype(BF16))
    grad_acts = dot32(placed, returned, OUTER).astype(BF16)
    raw_up = dot32(hidden, rows_g, OUTER)
    raw_down = dot32(inner, rows_x, OUTER)
    return (grad_acts,) + clipped(raw_down, raw_up, ndevices)


def in_hbm(*arrays):
    return [pltpu.with_memory_space_constraint(a, pltpu.HBM) for a in arrays]


def in_vmem(*arrays):
    return [pltpu.with_memory_space_constraint(a, pltpu.VMEM) for a in arrays]


def kernel_params(semantics=("arbitrary",)):
    return pltpu.CompilerParams(dimension_semantics=semantics, vmem_limit_bytes=VMEM_BYTES)


def pack(place, acts, cotan, shapes):
    tokens, width = acts.shape
    tile = min(width, 1024)
    tiles = width // tile

    def body(place_ref, x_in, g_in, *refs):
        out_refs, (rows, sems) = refs[:-2], refs[-2:]
        step = pl.program_id(0)

        def copies(i):
            cut = pl.ds(pl.multiple_of(i * tile, tile), tile)
            return [pltpu.make_async_copy(r.at[:, cut], rows.at[k, :, cut], sems.at[k, i]) for k, r in enumerate((x_in, g_in))]

        @pl.when(step == 0)
        def _():
            for i in range(tiles):
                for c in copies(i):
                    c.start()

        for c in copies(step):
            c.wait()
        cut = pl.ds(pl.multiple_of(step * tile, tile), tile)
        for k in range(2):
            moved = dot32(place_ref[...], rows[k, :, cut]).astype(BF16)
            first = 0
            for out_ref, (columns, size) in zip(out_refs, shapes):
                for c in range(columns):
                    out_ref[c, k] = moved[first:first + size]
                    first += size

    return pl.pallas_call(
        body,
        grid=(tiles,),
        in_specs=[pl.BlockSpec(place.shape, lambda i: (0, 0)), HBM, HBM],
        out_specs=[pl.BlockSpec((c, 2, size, tile), lambda i: (0, 0, 0, i)) for c, size in shapes],
        out_shape=[jax.ShapeDtypeStruct((c, 2, size, width), BF16) for c, size in shapes],
        scratch_shapes=[pltpu.VMEM((2, tokens, width), BF16), pltpu.SemaphoreType.DMA((2, tiles))],
        compiler_params=kernel_params(),
    )(place, *in_hbm(acts, cotan))


def unpack(place, blocks, tokens, half, into=None):
    width = blocks[0].shape[1]
    tile = min(width // 2, 2048)
    first = half * (width // 2 // tile)
    rest = () if into is None else (into,)

    def body(place_ref, *refs):
        rows = jnp.concatenate([ref[...] for ref in refs[:len(blocks)]], axis=0)
        refs[-1][...] = dot32(place_ref[...], rows).astype(BF16)

    return pl.pallas_call(
        body,
        grid=(width // 2 // tile,),
        in_specs=[pl.BlockSpec(place.shape, lambda i: (0, 0))]
        + [pl.BlockSpec((b.shape[0], tile), lambda i: (0, i + first)) for b in blocks]
        + [pl.BlockSpec(memory_space=pl.ANY)] * len(rest),
        out_specs=pl.BlockSpec((tokens, tile), lambda i: (0, i + first)),
        out_shape=jax.ShapeDtypeStruct((tokens, width), BF16),
        input_output_aliases={1 + len(blocks): 0} if rest else {},
        compiler_params=kernel_params(),
    )(place, *in_hbm(blocks[0]), *blocks[1:], *rest)


def final_sum(first, *others):
    rank, width = first.shape
    tile = min(width, 1024)

    def body(first_ref, *refs):
        other_refs, (total_ref, square_ref) = refs[:-2], refs[-2:]
        squares = jnp.zeros((8, 128), F32)
        for i in range(width // tile):
            cut = pl.ds(i * tile, tile)
            total = first_ref[:, cut]
            for ref in other_refs:
                total += ref[:, cut].astype(F32)
            total_ref[:, cut] = total
            total = total * total
            for r in range(0, rank, 8):
                for c in range(0, tile, 128):
                    squares += total[r:r + 8, c:c + 128]
        square_ref[...] = squares

    return in_place(body, [((rank, width), F32), ((8, 128), F32)], first, *others)


def scaled(raws, parts, ndevices):
    rank, width = raws[0].shape
    tile = min(width, 1024)
    limit = float(2 * rank * width * ndevices) ** 0.5

    def body(*refs):
        raw_refs, part_refs = refs[:len(raws)], refs[len(raws):len(raws) + len(parts)]
        outs, (held, sems) = refs[len(raws) + len(parts):-2], refs[-2:]
        total = jnp.sum(sum(ref[...] for ref in part_refs), axis=(0, 1), keepdims=True)
        factor = jnp.minimum(jnp.float32(1.0), jnp.float32(limit) / jnp.sqrt(total + 1e-06))
        copies = []
        for i in range(width // tile):
            cut = pl.ds(i * tile, tile)
            for n, (raw_ref, out) in enumerate(zip(raw_refs, outs)):
                held[n, :, cut] = raw_ref[:, cut] * factor
                copies.append(pltpu.make_async_copy(held.at[n, :, cut], out.at[0, :, cut], sems.at[n, i]))
                copies[-1].start()
        for c in copies:
            c.wait()

    return pl.pallas_call(
        body,
        in_specs=[WHOLE] * (len(raws) + len(parts)),
        out_specs=[HBM] * len(raws),
        out_shape=[pltpu.HBM((1, rank, width), F32)] * len(raws),
        scratch_shapes=[
            pltpu.VMEM((len(raws), rank, width), F32),
            pltpu.SemaphoreType.DMA((len(raws), width // tile)),
        ],
        compiler_params=pltpu.CompilerParams(vmem_limit_bytes=VMEM_BYTES),
    )(*in_vmem(*raws, *parts))


def corner(rows, first_rows, columns, first_columns):
    upper = lax.broadcasted_iota(jnp.int32, (rows, columns), 0) < first_rows
    return upper == (lax.broadcasted_iota(jnp.int32, (rows, columns), 1) < first_columns)


def far_sums(tokens, factor, up_ref, down_ref, dx_ref, inner_ref=None):
    rank, width = up_ref.shape
    tile = min(width, 2048)
    cuts = [pl.ds(i * tile, tile) for i in range(width // tile)]
    hidden, inner = (sum(dot32(tokens(k, cut), factor(k, cut), ROWS_OF) for cut in cuts) for k in range(2))
    hidden_t, inner_t, inner = hidden.T.astype(BF16), inner.T.astype(BF16), inner.astype(BF16)
    rows = inner.shape[0] - dx_ref.shape[0]
    if inner_ref is not None:
        inner_ref[...] = inner[:rows]
    for cut in cuts:
        up_ref[:, cut] = dot32(hidden_t, tokens(1, cut)).astype(BF16)
        down_ref[:, cut] = dot32(inner_t, tokens(0, cut)).astype(BF16)
        dx_ref[:, cut] = dot32(inner[rows:], factor(0, cut)).astype(BF16)


def in_place(body, out_shapes, *arrays, flags=None):
    first = [] if flags is None else [flags]
    return pl.pallas_call(
        body,
        in_specs=[pl.BlockSpec(memory_space=pltpu.SMEM)] * len(first) + [WHOLE] * len(arrays),
        out_specs=[WHOLE] * len(out_shapes),
        out_shape=[pltpu.VMEM(*shape) for shape in out_shapes],
        compiler_params=pltpu.CompilerParams(vmem_limit_bytes=VMEM_BYTES),
    )(*first, *in_vmem(*arrays))


def early_group(flags, rows3, rows2, crossed):
    _, block, width = rows2.shape
    rank = crossed.shape[1]

    def body(flags_ref, rows3_ref, rows2_ref, crossed_ref, up_ref, down_ref, dx_ref, late_ref):
        far_sums(
            lambda k, cut: rows2_ref[k, :, cut], lambda k, cut: crossed_ref[k, :, cut], up_ref, down_ref, dx_ref
        )
        late_ref[...] = jnp.where(flags_ref[0] == 1, rows2_ref[...], rows3_ref[...])

    shapes = [((rank, width), BF16)] * 2 + [((block, width), BF16), ((2, block, width), BF16)]
    return in_place(body, shapes, rows3, rows2, crossed, flags=flags)


def late_group(flags, rows, handed, far, outer):
    _, block, width = rows.shape
    rank = far.shape[1]

    def body(flags_ref, rows_ref, handed_ref, outer_ref, far_ref, up_ref, down_ref, inner_ref, swap_ref):
        at_end = flags_ref[0] == 1
        far_sums(
            lambda k, cut: jnp.concatenate([rows_ref[k, :, cut], handed_ref[k, :, cut]], axis=0),
            lambda k, cut: jnp.where(at_end, outer_ref[k, :, cut], far_ref[k, :, cut]),
            up_ref,
            down_ref,
            swap_ref,
            inner_ref,
        )

        @pl.when(at_end)
        def _():
            swap_ref[...] = down_ref[...]

    shapes = [((rank, width), BF16)] * 2 + [((block, rank), BF16), ((block, width), BF16)]
    return in_place(body, shapes, rows, handed, outer, far, flags=flags)


def near_groups(flags, stage, pair, own, outer, far, inner_late, dx_early, swapped, capacity, first1):
    plane = len(stage)
    _, rank, width = own.shape
    block = plane * capacity
    tile = min(width, 2048)
    cuts = [pl.ds(i * tile, tile) for i in range(width // tile)]

    def body(flags_ref, *refs):
        stage_in, refs = refs[:plane], refs[plane:]
        pair_in, own_in, outer_in, far_in, late_ref, early_ref, swapped_ref = refs[:7]
        dx_refs, sum_refs = refs[7:7 + plane], refs[7 + plane:]
        at_end = flags_ref[0] == 1

        def rows(k, cut):
            return jnp.concatenate(
                [
                    r[0, k, pl.ds(first + n * capacity, capacity), cut]
                    for n in range(2)
                    for r, first in zip(stage_in, first1)
                ],
                axis=0,
            )

        def factors(k, cut):
            return jnp.concatenate([pair_in[k, :, cut], own_in[k, :, cut]], axis=0)

        is_mine = corner(2 * block, block, 2 * rank, rank)
        sums = [sum(dot32(rows(k, cut), factors(k, cut), ROWS_OF) for cut in cuts) for k in range(2)]
        sums = [jnp.where(is_mine, total, 0.0) for total in sums]
        left, inner = [total.T.astype(BF16) for total in sums], sums[1].astype(BF16)
        for cut in cuts:
            for k in range(2):
                both = dot32(left[k], rows(1 - k, cut))
                sum_refs[k][:, cut] = both[:rank]
                sum_refs[2 + k][:, cut] = both[rank:]
            dx = dot32(inner, factors(0, cut)).astype(BF16)
            late = dot32(late_ref[...], jnp.where(at_end, outer_in[0, :, cut], far_in[0, :, cut])).astype(BF16)
            moved = [jnp.where(at_end, swapped_ref[:, cut], late), jnp.where(at_end, late, early_ref[:, cut])]
            for n, dx in enumerate(moved + [dx[:block], dx[block:]]):
                for m in range(plane):
                    dx_refs[m][n * capacity:(n + 1) * capacity, cut] = dx[m * capacity:(m + 1) * capacity]

    shapes = [((4 * capacity, width), BF16)] * plane + [((rank, width), F32)] * 4
    return in_place(body, shapes, *stage, pair, own, outer, far, inner_late, dx_early, swapped, flags=flags)


def move_adapters(plane, acts, cotan, token_task_index, task_slot_lookup, pool_down_factors, pool_up_factors):
    ndevices = lax.axis_size("dp")
    tokens, width = acts.shape
    capacity = 2 * ((tokens + ndevices - 1) // ndevices)
    me = lax.axis_index("dp")
    z, column = me // plane, me % plane
    is_end = (z == 0) | (z == 3)
    end_flag = is_end.astype(jnp.int32).reshape(1)

    def planes(pairs):
        return [(a * plane + c, b * plane + c) for a, b in pairs for c in range(plane)]

    swap = planes([(0, 1), (1, 0), (2, 3), (3, 2)])
    cross = planes([(1, 2), (2, 1)])
    outward = planes([(1, 0), (2, 3)])
    inward = planes([(0, 1), (3, 2)])

    def send(array, pairs):
        return lax.ppermute(array, "dp", pairs)

    def after(arrays, *others):
        return lax.optimization_barrier((arrays, others))[0]

    def beside(m):
        return [(i, (i // plane) * plane + ((i % plane) ^ m)) for i in range(ndevices)]

    lowest, none = jnp.array(-jnp.inf, BF16), (0, 0, 0)
    own = jnp.maximum(
        lax.pad(pool_down_factors, lowest, ((0, 1, 0), none, none)),
        lax.pad(pool_up_factors, lowest, ((1, 0, 0), none, none)),
    )
    pair = send(own, swap)
    crossed = send(own, cross)

    owner, position = route(token_task_index, task_slot_lookup, ndevices)
    owner_z, turn = owner // plane, (owner % plane) ^ column
    other_mid = jnp.where(z < 2, 2, 1)
    kind = jnp.where(owner_z == z, 0, jnp.where(owner_z == (z ^ 1), 1, jnp.where(owner_z == other_mid, 2, 3)))

    def places(wanted, row, rows):
        hot = jnp.arange(rows, dtype=jnp.int32)[:, None] == row[None, :]
        return (hot & wanted[None, :]).astype(BF16)

    def after(arrays, *others):
        return lax.optimization_barrier((arrays, others))[0]

    block = plane * capacity
    mine = (3 - kind) * capacity + position
    row = jnp.where(kind == 2, 10 * capacity, 12 * capacity) + (turn - 2) * jnp.where(kind == 2, capacity, 2 * capacity)
    row += jnp.where(kind == 2, 0, (1 - kind) * capacity) + position
    row = jnp.where(kind == 3, (6 + turn) * capacity + position, row)
    row = jnp.where(turn < 2, turn * block + mine, row)
    place = places(kind >= 0, row, 4 * block)
    place_back = places(kind >= 0, turn * block + mine, 4 * block)
    own_rows, beside_rows, across3, across2, across10 = pack(
        place, acts, cotan, [(1, 4 * capacity)] * 2 + [(2, capacity)] * 2 + [(2, 2 * capacity)]
    )

    def over_x(blocks):
        moved = send(blocks, beside(2))
        return moved, send(moved[1:], beside(1))

    beside_rows = send(beside_rows, beside(1))
    across3 = over_x(across3)
    stage3 = (own_rows, beside_rows) + across3
    rows3 = jnp.concatenate([r[0, :, :capacity] for r in stage3], axis=1)
    handed = send(rows3, inward)
    across2 = over_x(after(across2, across3[0]))
    across10 = over_x(after(across10, across2[1]))
    rows2 = [r[0, :, capacity:2 * capacity] for r in (own_rows, beside_rows)] + [r[0] for r in across2]
    rows2 = jnp.concatenate(rows2, axis=1)
    stage10 = (own_rows, beside_rows) + across10
    outer = send(crossed, outward)
    far = send(pair, cross)

    up2, down2, dx_early, late_rows = early_group(end_flag, rows3, rows2, crossed)
    up3, down3, inner_late, swapped = late_group(end_flag, late_rows, handed, far, outer)
    up2_in = send(up3, inward)
    down3, swapped, up3 = send(down3, cross), send(swapped, swap), send(up3, cross)

    swapped, down3 = lax.optimization_barrier((swapped, down3))
    dx_own, dx_beside, *dx_across, up1, down1, up0, down0 = near_groups(
        end_flag, stage10, pair, own, outer, far, inner_late, dx_early, swapped, capacity,
        (2 * capacity, 2 * capacity, 0, 0),
    )

    def add(a, b):
        return (a.astype(F32) + b.astype(F32)).astype(BF16)

    down2, down1 = add(down2, swapped), add(down1, down3)
    dx_across[0] = send(dx_across[0], beside(2))
    dx_across[1] = send(after(dx_across[1], dx_across[0]), beside(2))
    up2_in, up3 = after((up2_in, up3), down2, down1, dx_across[0])
    down2, down1 = send(down2, cross), send(down1, swap)
    up2, up1 = send(add(up2, up2_in), cross), send(add(up1, up3), swap)

    back = [dx_own, send(dx_beside, beside(1)), dx_across[0], send(dx_across[1], beside(1))]
    half_acts = unpack(place_back.T, back, tokens, 0)
    grad_acts = unpack(place_back.T, back, tokens, 1, half_acts)
    raw_down, down_squares = final_sum(down0, down2, down1)
    raw_up, up_squares = final_sum(up0, up2, up1)
    part = down_squares + up_squares
    part = part + sum(after([send(part, beside(m)) for m in range(1, plane)], half_acts))
    along = [[(i, (i // plane ^ m) * plane + i % plane) for i in range(ndevices)] for m in range(1, 4)]
    parts = after([send(part, pairs) for pairs in along], grad_acts)
    return (grad_acts, *scaled((raw_down, raw_up), (part, *parts), ndevices))


def solution(mesh):
    plane = 4
    by_planes = mesh.shape["dp"] == 4 * plane

    def per_device(*arrays):
        if by_planes:
            return move_adapters(plane, *arrays)
        return move_tokens(*arrays)

    rows, pools = P(("parts", "dp"), None), P(("parts", "dp"), None, None)
    return jax.shard_map(
        per_device,
        mesh=mesh,
        in_specs=(rows, rows, rows, P("parts"), pools, pools),
        out_specs=(rows, pools, pools),
        check_vma=False,
    )
```

```python
import jax
import jax.numpy as jnp
from jax import lax
from jax.experimental import pallas as pl
from jax.experimental.pallas import tpu as pltpu
from jax.sharding import PartitionSpec as P

BF16, F32 = jnp.bfloat16, jnp.float32
ROWS_OF = (((1,), (1,)), ((), ()))
OUTER = (((0,), (0,)), ((), ()))
INNER = (((1,), (0,)), ((), ()))
HBM = pl.BlockSpec(memory_space=pltpu.HBM)
WHOLE = pl.BlockSpec(memory_space=pltpu.VMEM)
VMEM_BYTES = 12 * 2**20


def dot32(a, b, dims=INNER):
    return lax.dot_general(a, b, dims, preferred_element_type=F32)


def route(token_task_index, task_slot_lookup, ndevices):
    pool = task_slot_lookup.shape[0]
    task_hot = (token_task_index == jnp.arange(pool, dtype=jnp.int32)[None, :]).astype(jnp.int32)
    owner = jnp.sum(task_hot * task_slot_lookup[None, :], axis=1)
    owner_hot = (owner[:, None] == jnp.arange(ndevices, dtype=jnp.int32)[None, :]).astype(jnp.int32)
    before = jnp.cumsum(owner_hot, axis=0) - owner_hot
    position = jnp.sum(before * owner_hot, axis=1)
    return owner, position


def clipped(raw_down, raw_up, ndevices):
    local_sq = jnp.sum(raw_down * raw_down) + jnp.sum(raw_up * raw_up)
    total = lax.psum(local_sq, "dp")
    norm = jnp.sqrt(total + 1e-06)
    limit = jnp.sqrt(jnp.float32(2 * raw_down.shape[0] * raw_down.shape[1] * ndevices))
    factor = jnp.minimum(jnp.float32(1.0), limit / norm)
    return (raw_down * factor)[None], (raw_up * factor)[None]


def move_tokens(acts, cotan, token_task_index, task_slot_lookup, pool_down_factors, pool_up_factors):
    ndevices = lax.axis_size("dp")
    tokens, width = acts.shape
    capacity = 2 * ((tokens + ndevices - 1) // ndevices)
    slots = ndevices * capacity
    owner, position = route(token_task_index, task_slot_lookup, ndevices)
    dest = owner * capacity + position
    placed = (jnp.arange(slots, dtype=jnp.int32)[:, None] == dest[None, :]).astype(BF16)

    def exchange(rows):
        rows = rows.reshape(ndevices, capacity, width)
        return lax.all_to_all(rows, "dp", split_axis=0, concat_axis=0, tiled=True).reshape(slots, width)

    down, up = pool_down_factors[0], pool_up_factors[0]
    rows_x = exchange(dot32(placed, acts).astype(BF16))
    rows_g = exchange(dot32(placed, cotan).astype(BF16))
    hidden = dot32(rows_x, down, ROWS_OF).astype(BF16)
    inner = dot32(rows_g, up, ROWS_OF).astype(BF16)
    returned = exchange(dot32(inner, down).astype(BF16))
    grad_acts = dot32(placed, returned, OUTER).astype(BF16)
    raw_up = dot32(hidden, rows_g, OUTER)
    raw_down = dot32(inner, rows_x, OUTER)
    return (grad_acts,) + clipped(raw_down, raw_up, ndevices)


def in_hbm(*arrays):
    return [pltpu.with_memory_space_constraint(a, pltpu.HBM) for a in arrays]


def in_vmem(*arrays):
    return [pltpu.with_memory_space_constraint(a, pltpu.VMEM) for a in arrays]


def kernel_params(semantics=("arbitrary",)):
    return pltpu.CompilerParams(dimension_semantics=semantics, vmem_limit_bytes=VMEM_BYTES)


def pack(place, acts, cotan, shapes):
    tokens, width = acts.shape
    tile = min(width, 1024)
    tiles = width // tile

    def body(place_ref, x_in, g_in, *refs):
        out_refs, (rows, sems) = refs[:-2], refs[-2:]
        step = pl.program_id(0)

        def copies(i):
            cut = pl.ds(pl.multiple_of(i * tile, tile), tile)
            return [pltpu.make_async_copy(r.at[:, cut], rows.at[k, :, cut], sems.at[k, i]) for k, r in enumerate((x_in, g_in))]

        @pl.when(step == 0)
        def _():
            for i in range(tiles):
                for c in copies(i):
                    c.start()

        for c in copies(step):
            c.wait()
        cut = pl.ds(pl.multiple_of(step * tile, tile), tile)
        for k in range(2):
            moved = dot32(place_ref[...], rows[k, :, cut]).astype(BF16)
            first = 0
            for out_ref, (columns, size) in zip(out_refs, shapes):
                for c in range(columns):
                    out_ref[c, k] = moved[first:first + size]
                    first += size

    return pl.pallas_call(
        body,
        grid=(tiles,),
        in_specs=[pl.BlockSpec(place.shape, lambda i: (0, 0)), HBM, HBM],
        out_specs=[pl.BlockSpec((c, 2, size, tile), lambda i: (0, 0, 0, i)) for c, size in shapes],
        out_shape=[jax.ShapeDtypeStruct((c, 2, size, width), BF16) for c, size in shapes],
        scratch_shapes=[pltpu.VMEM((2, tokens, width), BF16), pltpu.SemaphoreType.DMA((2, tiles))],
        compiler_params=kernel_params(),
    )(place, *in_hbm(acts, cotan))


def unpack(place, blocks, tokens, half, into=None):
    width = blocks[0].shape[1]
    tile = min(width // 2, 2048)
    first = half * (width // 2 // tile)
    rest = () if into is None else (into,)

    def body(place_ref, *refs):
        rows = jnp.concatenate([ref[...] for ref in refs[:len(blocks)]], axis=0)
        refs[-1][...] = dot32(place_ref[...], rows).astype(BF16)

    return pl.pallas_call(
        body,
        grid=(width // 2 // tile,),
        in_specs=[pl.BlockSpec(place.shape, lambda i: (0, 0))]
        + [pl.BlockSpec((b.shape[0], tile), lambda i: (0, i + first)) for b in blocks]
        + [pl.BlockSpec(memory_space=pl.ANY)] * len(rest),
        out_specs=pl.BlockSpec((tokens, tile), lambda i: (0, i + first)),
        out_shape=jax.ShapeDtypeStruct((tokens, width), BF16),
        input_output_aliases={1 + len(blocks): 0} if rest else {},
        compiler_params=kernel_params(),
    )(place, *in_hbm(blocks[0]), *blocks[1:], *rest)


def final_sum(first, *others):
    rank, width = first.shape
    tile = min(width, 1024)

    def body(first_ref, *refs):
        other_refs, (total_ref, square_ref) = refs[:-2], refs[-2:]
        squares = jnp.zeros((8, 128), F32)
        for i in range(width // tile):
            cut = pl.ds(i * tile, tile)
            total = first_ref[:, cut]
            for ref in other_refs:
                total += ref[:, cut].astype(F32)
            total_ref[:, cut] = total
            total = total * total
            for r in range(0, rank, 8):
                for c in range(0, tile, 128):
                    squares += total[r:r + 8, c:c + 128]
        square_ref[...] = squares

    return in_place(body, [((rank, width), F32), ((8, 128), F32)], first, *others)


def scaled(raws, parts, ndevices):
    rank, width = raws[0].shape
    tile = min(width, 1024)
    limit = float(2 * rank * width * ndevices) ** 0.5

    def body(*refs):
        raw_refs, part_refs = refs[:len(raws)], refs[len(raws):len(raws) + len(parts)]
        outs, (held, sems) = refs[len(raws) + len(parts):-2], refs[-2:]
        total = jnp.sum(sum(ref[...] for ref in part_refs), axis=(0, 1), keepdims=True)
        factor = jnp.minimum(jnp.float32(1.0), jnp.float32(limit) / jnp.sqrt(total + 1e-06))
        copies = []
        for i in range(width // tile):
            cut = pl.ds(i * tile, tile)
            for n, (raw_ref, out) in enumerate(zip(raw_refs, outs)):
                held[n, :, cut] = raw_ref[:, cut] * factor
                copies.append(pltpu.make_async_copy(held.at[n, :, cut], out.at[0, :, cut], sems.at[n, i]))
                copies[-1].start()
        for c in copies:
            c.wait()

    return pl.pallas_call(
        body,
        in_specs=[WHOLE] * (len(raws) + len(parts)),
        out_specs=[HBM] * len(raws),
        out_shape=[pltpu.HBM((1, rank, width), F32)] * len(raws),
        scratch_shapes=[
            pltpu.VMEM((len(raws), rank, width), F32),
            pltpu.SemaphoreType.DMA((len(raws), width // tile)),
        ],
        compiler_params=pltpu.CompilerParams(vmem_limit_bytes=VMEM_BYTES),
    )(*in_vmem(*raws, *parts))


def corner(rows, first_rows, columns, first_columns):
    upper = lax.broadcasted_iota(jnp.int32, (rows, columns), 0) < first_rows
    return upper == (lax.broadcasted_iota(jnp.int32, (rows, columns), 1) < first_columns)


def far_sums(tokens, factor, up_ref, down_ref, dx_ref, inner_ref=None):
    rank, width = up_ref.shape
    tile = min(width, 2048)
    cuts = [pl.ds(i * tile, tile) for i in range(width // tile)]
    hidden, inner = (sum(dot32(tokens(k, cut), factor(k, cut), ROWS_OF) for cut in cuts) for k in range(2))
    hidden_t, inner_t, inner = hidden.T.astype(BF16), inner.T.astype(BF16), inner.astype(BF16)
    rows = inner.shape[0] - dx_ref.shape[0]
    if inner_ref is not None:
        inner_ref[...] = inner[:rows]
    for cut in cuts:
        up_ref[:, cut] = dot32(hidden_t, tokens(1, cut)).astype(BF16)
        down_ref[:, cut] = dot32(inner_t, tokens(0, cut)).astype(BF16)
        dx_ref[:, cut] = dot32(inner[rows:], factor(0, cut)).astype(BF16)


def in_place(body, out_shapes, *arrays, flags=None):
    first = [] if flags is None else [flags]
    return pl.pallas_call(
        body,
        in_specs=[pl.BlockSpec(memory_space=pltpu.SMEM)] * len(first) + [WHOLE] * len(arrays),
        out_specs=[WHOLE] * len(out_shapes),
        out_shape=[pltpu.VMEM(*shape) for shape in out_shapes],
        compiler_params=pltpu.CompilerParams(vmem_limit_bytes=VMEM_BYTES),
    )(*first, *in_vmem(*arrays))


def early_group(flags, rows3, rows2, crossed):
    _, block, width = rows2.shape
    rank = crossed.shape[1]

    def body(flags_ref, rows3_ref, rows2_ref, crossed_ref, up_ref, down_ref, dx_ref, late_ref):
        far_sums(
            lambda k, cut: rows2_ref[k, :, cut], lambda k, cut: crossed_ref[k, :, cut], up_ref, down_ref, dx_ref
        )
        late_ref[...] = jnp.where(flags_ref[0] == 1, rows2_ref[...], rows3_ref[...])

    shapes = [((rank, width), BF16)] * 2 + [((block, width), BF16), ((2, block, width), BF16)]
    return in_place(body, shapes, rows3, rows2, crossed, flags=flags)


def late_group(flags, rows, handed, far, outer):
    _, block, width = rows.shape
    rank = far.shape[1]

    def body(flags_ref, rows_ref, handed_ref, outer_ref, far_ref, up_ref, down_ref, inner_ref, swap_ref):
        at_end = flags_ref[0] == 1
        far_sums(
            lambda k, cut: jnp.concatenate([rows_ref[k, :, cut], handed_ref[k, :, cut]], axis=0),
            lambda k, cut: jnp.where(at_end, outer_ref[k, :, cut], far_ref[k, :, cut]),
            up_ref,
            down_ref,
            swap_ref,
            inner_ref,
        )

        @pl.when(at_end)
        def _():
            swap_ref[...] = down_ref[...]

    shapes = [((rank, width), BF16)] * 2 + [((block, rank), BF16), ((block, width), BF16)]
    return in_place(body, shapes, rows, handed, outer, far, flags=flags)


def near_groups(flags, stage, pair, own, outer, far, inner_late, dx_early, swapped, capacity, first1):
    plane = len(stage)
    _, rank, width = own.shape
    block = plane * capacity
    tile = min(width, 2048)
    cuts = [pl.ds(i * tile, tile) for i in range(width // tile)]

    def body(flags_ref, *refs):
        stage_in, refs = refs[:plane], refs[plane:]
        pair_in, own_in, outer_in, far_in, late_ref, early_ref, swapped_ref = refs[:7]
        dx_refs, sum_refs = refs[7:7 + plane], refs[7 + plane:]
        at_end = flags_ref[0] == 1

        def rows(k, cut):
            return jnp.concatenate(
                [
                    r[0, k, pl.ds(first + n * capacity, capacity), cut]
                    for n in range(2)
                    for r, first in zip(stage_in, first1)
                ],
                axis=0,
            )

        def factors(k, cut):
            return jnp.concatenate([pair_in[k, :, cut], own_in[k, :, cut]], axis=0)

        is_mine = corner(2 * block, block, 2 * rank, rank)
        sums = [sum(dot32(rows(k, cut), factors(k, cut), ROWS_OF) for cut in cuts) for k in range(2)]
        sums = [jnp.where(is_mine, total, 0.0) for total in sums]
        left, inner = [total.T.astype(BF16) for total in sums], sums[1].astype(BF16)
        for cut in cuts:
            for k in range(2):
                both = dot32(left[k], rows(1 - k, cut))
                sum_refs[k][:, cut] = both[:rank]
                sum_refs[2 + k][:, cut] = both[rank:]
            dx = dot32(inner, factors(0, cut)).astype(BF16)
            late = dot32(late_ref[...], jnp.where(at_end, outer_in[0, :, cut], far_in[0, :, cut])).astype(BF16)
            moved = [jnp.where(at_end, swapped_ref[:, cut], late), jnp.where(at_end, late, early_ref[:, cut])]
            for n, dx in enumerate(moved + [dx[:block], dx[block:]]):
                for m in range(plane):
                    dx_refs[m][n * capacity:(n + 1) * capacity, cut] = dx[m * capacity:(m + 1) * capacity]

    shapes = [((4 * capacity, width), BF16)] * plane + [((rank, width), F32)] * 4
    return in_place(body, shapes, *stage, pair, own, outer, far, inner_late, dx_early, swapped, flags=flags)


def move_adapters(plane, acts, cotan, token_task_index, task_slot_lookup, pool_down_factors, pool_up_factors):
    ndevices = lax.axis_size("dp")
    tokens, width = acts.shape
    capacity = 2 * ((tokens + ndevices - 1) // ndevices)
    me = lax.axis_index("dp")
    z, column = me // plane, me % plane
    is_end = (z == 0) | (z == 3)
    end_flag = is_end.astype(jnp.int32).reshape(1)

    def planes(pairs):
        return [(a * plane + c, b * plane + c) for a, b in pairs for c in range(plane)]

    swap = planes([(0, 1), (1, 0), (2, 3), (3, 2)])
    cross = planes([(1, 2), (2, 1)])
    outward = planes([(1, 0), (2, 3)])
    inward = planes([(0, 1), (3, 2)])

    def send(array, pairs):
        return lax.ppermute(array, "dp", pairs)

    def after(arrays, *others):
        return lax.optimization_barrier((arrays, others))[0]

    def beside(m):
        return [(i, (i // plane) * plane + ((i % plane) ^ m)) for i in range(ndevices)]

    def stacked(first, second):
        lowest, none = jnp.array(-jnp.inf, BF16), (0, 0, 0)
        padded = lax.pad(first, lowest, ((0, 1, 0), none, none)), lax.pad(second, lowest, ((1, 0, 0), none, none))
        return jnp.maximum(*padded)

    own = stacked(pool_down_factors, pool_up_factors)
    pair = send(own, swap)
    own = after(own, own[0, 0, 0] * 2)
    crossed = send(own, cross)

    owner, position = route(after(token_task_index, own), task_slot_lookup, ndevices)
    owner_z, turn = owner // plane, (owner % plane) ^ column
    other_mid = jnp.where(z < 2, 2, 1)
    kind = jnp.where(owner_z == z, 0, jnp.where(owner_z == (z ^ 1), 1, jnp.where(owner_z == other_mid, 2, 3)))

    def places(wanted, row, rows):
        hot = jnp.arange(rows, dtype=jnp.int32)[:, None] == row[None, :]
        return (hot & wanted[None, :]).astype(BF16)

    def after(arrays, *others):
        return lax.optimization_barrier((arrays, others))[0]

    block = plane * capacity
    mine = (3 - kind) * capacity + position
    row = jnp.where(kind == 2, 10 * capacity, 12 * capacity) + (turn - 2) * jnp.where(kind == 2, capacity, 2 * capacity)
    row += jnp.where(kind == 2, 0, (1 - kind) * capacity) + position
    row = jnp.where(kind == 3, (6 + turn) * capacity + position, row)
    row = jnp.where(turn < 2, turn * block + mine, row)
    place = places(kind >= 0, row, 4 * block)
    place_back = places(kind >= 0, turn * block + mine, 4 * block)
    own_rows, beside_rows, across3, across2, across10 = pack(
        place, acts, cotan, [(1, 4 * capacity)] * 2 + [(2, capacity)] * 2 + [(2, 2 * capacity)]
    )

    def over_x(blocks):
        moved = send(blocks, beside(2))
        return moved, send(moved[1:], beside(1))

    beside_rows = send(beside_rows, beside(1))
    across3 = over_x(across3)
    stage3 = (own_rows, beside_rows) + across3
    rows3 = jnp.concatenate([r[0, :, :capacity] for r in stage3], axis=1)
    handed = send(rows3, inward)
    across2 = over_x(after(across2, across3[0]))
    across10 = over_x(after(across10, across2[1]))
    rows2 = [r[0, :, capacity:2 * capacity] for r in (own_rows, beside_rows)] + [r[0] for r in across2]
    rows2 = jnp.concatenate(rows2, axis=1)
    stage10 = (own_rows, beside_rows) + across10
    outer = send(crossed, outward)
    far = send(pair, cross)

    up2, down2, dx_early, late_rows = early_group(end_flag, rows3, rows2, crossed)
    up3, down3, inner_late, swapped = late_group(end_flag, late_rows, handed, far, outer)
    up2_in = send(up3, inward)
    down3, swapped, up3 = send(down3, cross), send(swapped, swap), send(up3, cross)

    swapped, down3 = lax.optimization_barrier((swapped, down3))
    dx_own, dx_beside, *dx_across, up1, down1, up0, down0 = near_groups(
        end_flag, stage10, pair, own, outer, far, inner_late, dx_early, swapped, capacity,
        (2 * capacity, 2 * capacity, 0, 0),
    )

    def add(a, b):
        return (a.astype(F32) + b.astype(F32)).astype(BF16)

    down2, down1 = add(down2, swapped), add(down1, down3)
    dx_across[0] = send(dx_across[0], beside(2))
    dx_across[1] = send(after(dx_across[1], dx_across[0]), beside(2))
    up2_in, up3 = after((up2_in, up3), down2, down1, dx_across[0])
    down2, down1 = send(down2, cross), send(down1, swap)
    up2, up1 = send(add(up2, up2_in), cross), send(add(up1, up3), swap)

    back = [dx_own, send(dx_beside, beside(1)), dx_across[0], send(dx_across[1], beside(1))]
    half_acts = unpack(place_back.T, back, tokens, 0)
    grad_acts = unpack(place_back.T, back, tokens, 1, half_acts)
    raw_down, down_squares = final_sum(down0, down2, down1)
    raw_up, up_squares = final_sum(up0, up2, up1)
    part = down_squares + up_squares
    part = part + sum(after([send(part, beside(m)) for m in range(1, plane)], half_acts))
    along = [[(i, (i // plane ^ m) * plane + i % plane) for i in range(ndevices)] for m in range(1, 4)]
    parts = after([send(part, pairs) for pairs in along], grad_acts)
    return (grad_acts, *scaled((raw_down, raw_up), (part, *parts), ndevices))


def solution(mesh):
    plane = 4
    by_planes = mesh.shape["dp"] == 4 * plane

    def per_device(*arrays):
        if by_planes:
            return move_adapters(plane, *arrays)
        return move_tokens(*arrays)

    rows, pools = P(("parts", "dp"), None), P(("parts", "dp"), None, None)
    return jax.shard_map(
        per_device,
        mesh=mesh,
        in_specs=(rows, rows, rows, P("parts"), pools, pools),
        out_specs=(rows, pools, pools),
        check_vma=False,
    )
```

```python
import jax
import jax.numpy as jnp
from jax import lax
from jax.experimental import pallas as pl
from jax.experimental.pallas import tpu as pltpu
from jax.sharding import PartitionSpec as P

BF16, F32 = jnp.bfloat16, jnp.float32
ROWS_OF = (((1,), (1,)), ((), ()))
OUTER = (((0,), (0,)), ((), ()))
INNER = (((1,), (0,)), ((), ()))
HBM = pl.BlockSpec(memory_space=pltpu.HBM)
WHOLE = pl.BlockSpec(memory_space=pltpu.VMEM)
VMEM_BYTES = 12 * 2**20


def dot32(a, b, dims=INNER):
    return lax.dot_general(a, b, dims, preferred_element_type=F32)


def route(token_task_index, task_slot_lookup, ndevices):
    pool = task_slot_lookup.shape[0]
    task_hot = (token_task_index == jnp.arange(pool, dtype=jnp.int32)[None, :]).astype(jnp.int32)
    owner = jnp.sum(task_hot * task_slot_lookup[None, :], axis=1)
    owner_hot = (owner[:, None] == jnp.arange(ndevices, dtype=jnp.int32)[None, :]).astype(jnp.int32)
    before = jnp.cumsum(owner_hot, axis=0) - owner_hot
    position = jnp.sum(before * owner_hot, axis=1)
    return owner, position


def clipped(raw_down, raw_up, ndevices):
    local_sq = jnp.sum(raw_down * raw_down) + jnp.sum(raw_up * raw_up)
    total = lax.psum(local_sq, "dp")
    norm = jnp.sqrt(total + 1e-06)
    limit = jnp.sqrt(jnp.float32(2 * raw_down.shape[0] * raw_down.shape[1] * ndevices))
    factor = jnp.minimum(jnp.float32(1.0), limit / norm)
    return (raw_down * factor)[None], (raw_up * factor)[None]


def move_tokens(acts, cotan, token_task_index, task_slot_lookup, pool_down_factors, pool_up_factors):
    ndevices = lax.axis_size("dp")
    tokens, width = acts.shape
    capacity = 2 * ((tokens + ndevices - 1) // ndevices)
    slots = ndevices * capacity
    owner, position = route(token_task_index, task_slot_lookup, ndevices)
    dest = owner * capacity + position
    placed = (jnp.arange(slots, dtype=jnp.int32)[:, None] == dest[None, :]).astype(BF16)

    def exchange(rows):
        rows = rows.reshape(ndevices, capacity, width)
        return lax.all_to_all(rows, "dp", split_axis=0, concat_axis=0, tiled=True).reshape(slots, width)

    down, up = pool_down_factors[0], pool_up_factors[0]
    rows_x = exchange(dot32(placed, acts).astype(BF16))
    rows_g = exchange(dot32(placed, cotan).astype(BF16))
    hidden = dot32(rows_x, down, ROWS_OF).astype(BF16)
    inner = dot32(rows_g, up, ROWS_OF).astype(BF16)
    returned = exchange(dot32(inner, down).astype(BF16))
    grad_acts = dot32(placed, returned, OUTER).astype(BF16)
    raw_up = dot32(hidden, rows_g, OUTER)
    raw_down = dot32(inner, rows_x, OUTER)
    return (grad_acts,) + clipped(raw_down, raw_up, ndevices)


def in_hbm(*arrays):
    return [pltpu.with_memory_space_constraint(a, pltpu.HBM) for a in arrays]


def in_vmem(*arrays):
    return [pltpu.with_memory_space_constraint(a, pltpu.VMEM) for a in arrays]


def kernel_params(semantics=("arbitrary",)):
    return pltpu.CompilerParams(dimension_semantics=semantics, vmem_limit_bytes=VMEM_BYTES)


def pack(place, acts, cotan, shapes):
    tokens, width = acts.shape
    tile = min(width, 1024)
    tiles = width // tile

    def body(place_ref, x_in, g_in, *refs):
        out_refs, (rows, sems) = refs[:-2], refs[-2:]
        step = pl.program_id(0)

        def copies(i):
            cut = pl.ds(pl.multiple_of(i * tile, tile), tile)
            return [pltpu.make_async_copy(r.at[:, cut], rows.at[k, :, cut], sems.at[k, i]) for k, r in enumerate((x_in, g_in))]

        @pl.when(step == 0)
        def _():
            for i in range(tiles):
                for c in copies(i):
                    c.start()

        for c in copies(step):
            c.wait()
        cut = pl.ds(pl.multiple_of(step * tile, tile), tile)
        for k in range(2):
            moved = dot32(place_ref[...], rows[k, :, cut]).astype(BF16)
            first = 0
            for out_ref, (columns, size) in zip(out_refs, shapes):
                for c in range(columns):
                    out_ref[c, k] = moved[first:first + size]
                    first += size

    return pl.pallas_call(
        body,
        grid=(tiles,),
        in_specs=[pl.BlockSpec(place.shape, lambda i: (0, 0)), HBM, HBM],
        out_specs=[pl.BlockSpec((c, 2, size, tile), lambda i: (0, 0, 0, i)) for c, size in shapes],
        out_shape=[jax.ShapeDtypeStruct((c, 2, size, width), BF16) for c, size in shapes],
        scratch_shapes=[pltpu.VMEM((2, tokens, width), BF16), pltpu.SemaphoreType.DMA((2, tiles))],
        compiler_params=kernel_params(),
    )(place, *in_hbm(acts, cotan))


def unpack(place, blocks, tokens, half, into=None):
    width = blocks[0].shape[1]
    tile = min(width // 2, 2048)
    first = half * (width // 2 // tile)
    rest = () if into is None else (into,)

    def body(place_ref, *refs):
        rows = jnp.concatenate([ref[...] for ref in refs[:len(blocks)]], axis=0)
        refs[-1][...] = dot32(place_ref[...], rows).astype(BF16)

    return pl.pallas_call(
        body,
        grid=(width // 2 // tile,),
        in_specs=[pl.BlockSpec(place.shape, lambda i: (0, 0))]
        + [pl.BlockSpec((b.shape[0], tile), lambda i: (0, i + first)) for b in blocks]
        + [pl.BlockSpec(memory_space=pl.ANY)] * len(rest),
        out_specs=pl.BlockSpec((tokens, tile), lambda i: (0, i + first)),
        out_shape=jax.ShapeDtypeStruct((tokens, width), BF16),
        input_output_aliases={1 + len(blocks): 0} if rest else {},
        compiler_params=kernel_params(),
    )(place, *in_hbm(blocks[0]), *blocks[1:], *rest)


def final_sum(first, *others):
    rank, width = first.shape
    tile = min(width, 1024)

    def body(first_ref, *refs):
        other_refs, (total_ref, square_ref) = refs[:-2], refs[-2:]
        squares = jnp.zeros((8, 128), F32)
        for i in range(width // tile):
            cut = pl.ds(i * tile, tile)
            total = first_ref[:, cut]
            for ref in other_refs:
                total += ref[:, cut].astype(F32)
            total_ref[:, cut] = total
            total = total * total
            for r in range(0, rank, 8):
                for c in range(0, tile, 128):
                    squares += total[r:r + 8, c:c + 128]
        square_ref[...] = squares

    return in_place(body, [((rank, width), F32), ((8, 128), F32)], first, *others)


def scaled(raws, parts, ndevices):
    rank, width = raws[0].shape
    tile = min(width, 1024)
    limit = float(2 * rank * width * ndevices) ** 0.5

    def body(*refs):
        raw_refs, part_refs = refs[:len(raws)], refs[len(raws):len(raws) + len(parts)]
        outs, (held, sems) = refs[len(raws) + len(parts):-2], refs[-2:]
        total = jnp.sum(sum(ref[...] for ref in part_refs), axis=(0, 1), keepdims=True)
        factor = jnp.minimum(jnp.float32(1.0), jnp.float32(limit) / jnp.sqrt(total + 1e-06))
        copies = []
        for i in range(width // tile):
            cut = pl.ds(i * tile, tile)
            for n, (raw_ref, out) in enumerate(zip(raw_refs, outs)):
                held[n, :, cut] = raw_ref[:, cut] * factor
                copies.append(pltpu.make_async_copy(held.at[n, :, cut], out.at[0, :, cut], sems.at[n, i]))
                copies[-1].start()
        for c in copies:
            c.wait()

    return pl.pallas_call(
        body,
        in_specs=[WHOLE] * (len(raws) + len(parts)),
        out_specs=[HBM] * len(raws),
        out_shape=[pltpu.HBM((1, rank, width), F32)] * len(raws),
        scratch_shapes=[
            pltpu.VMEM((len(raws), rank, width), F32),
            pltpu.SemaphoreType.DMA((len(raws), width // tile)),
        ],
        compiler_params=pltpu.CompilerParams(vmem_limit_bytes=VMEM_BYTES),
    )(*in_vmem(*raws, *parts))


def corner(rows, first_rows, columns, first_columns):
    upper = lax.broadcasted_iota(jnp.int32, (rows, columns), 0) < first_rows
    return upper == (lax.broadcasted_iota(jnp.int32, (rows, columns), 1) < first_columns)


def far_sums(tokens, factor, up_ref, down_ref, dx_ref, inner_ref=None):
    rank, width = up_ref.shape
    tile = min(width, 4096)
    cuts = [pl.ds(i * tile, tile) for i in range(width // tile)]
    hidden, inner = (sum(dot32(tokens(k, cut), factor(k, cut), ROWS_OF) for cut in cuts) for k in range(2))
    hidden_t, inner_t, inner = hidden.T.astype(BF16), inner.T.astype(BF16), inner.astype(BF16)
    rows = inner.shape[0] - dx_ref.shape[0]
    if inner_ref is not None:
        inner_ref[...] = inner[:rows]
    for cut in cuts:
        up_ref[:, cut] = dot32(hidden_t, tokens(1, cut)).astype(BF16)
        down_ref[:, cut] = dot32(inner_t, tokens(0, cut)).astype(BF16)
        dx_ref[:, cut] = dot32(inner[rows:], factor(0, cut)).astype(BF16)


def in_place(body, out_shapes, *arrays, flags=None):
    first = [] if flags is None else [flags]
    return pl.pallas_call(
        body,
        in_specs=[pl.BlockSpec(memory_space=pltpu.SMEM)] * len(first) + [WHOLE] * len(arrays),
        out_specs=[WHOLE] * len(out_shapes),
        out_shape=[pltpu.VMEM(*shape) for shape in out_shapes],
        compiler_params=pltpu.CompilerParams(vmem_limit_bytes=VMEM_BYTES),
    )(*first, *in_vmem(*arrays))


def early_group(flags, rows3, rows2, crossed):
    _, block, width = rows2.shape
    rank = crossed.shape[1]

    def body(flags_ref, rows3_ref, rows2_ref, crossed_ref, up_ref, down_ref, dx_ref, late_ref):
        far_sums(
            lambda k, cut: rows2_ref[k, :, cut], lambda k, cut: crossed_ref[k, :, cut], up_ref, down_ref, dx_ref
        )
        late_ref[...] = jnp.where(flags_ref[0] == 1, rows2_ref[...], rows3_ref[...])

    shapes = [((rank, width), BF16)] * 2 + [((block, width), BF16), ((2, block, width), BF16)]
    return in_place(body, shapes, rows3, rows2, crossed, flags=flags)


def late_group(flags, rows, handed, far, outer):
    _, block, width = rows.shape
    rank = far.shape[1]

    def body(flags_ref, rows_ref, handed_ref, outer_ref, far_ref, up_ref, down_ref, inner_ref, swap_ref):
        at_end = flags_ref[0] == 1
        far_sums(
            lambda k, cut: jnp.concatenate([rows_ref[k, :, cut], handed_ref[k, :, cut]], axis=0),
            lambda k, cut: jnp.where(at_end, outer_ref[k, :, cut], far_ref[k, :, cut]),
            up_ref,
            down_ref,
            swap_ref,
            inner_ref,
        )

        @pl.when(at_end)
        def _():
            swap_ref[...] = down_ref[...]

    shapes = [((rank, width), BF16)] * 2 + [((block, rank), BF16), ((block, width), BF16)]
    return in_place(body, shapes, rows, handed, outer, far, flags=flags)


def near_groups(flags, stage, pair, own, outer, far, inner_late, dx_early, swapped, capacity, first1):
    plane = len(stage)
    _, rank, width = own.shape
    block = plane * capacity
    tile = min(width, 2048)
    cuts = [pl.ds(i * tile, tile) for i in range(width // tile)]

    def body(flags_ref, *refs):
        stage_in, refs = refs[:plane], refs[plane:]
        pair_in, own_in, outer_in, far_in, late_ref, early_ref, swapped_ref = refs[:7]
        dx_refs, sum_refs = refs[7:7 + plane], refs[7 + plane:]
        at_end = flags_ref[0] == 1

        def rows(k, cut):
            return jnp.concatenate(
                [
                    r[0, k, pl.ds(first + n * capacity, capacity), cut]
                    for n in range(2)
                    for r, first in zip(stage_in, first1)
                ],
                axis=0,
            )

        def factors(k, cut):
            return jnp.concatenate([pair_in[k, :, cut], own_in[k, :, cut]], axis=0)

        is_mine = corner(2 * block, block, 2 * rank, rank)
        sums = [sum(dot32(rows(k, cut), factors(k, cut), ROWS_OF) for cut in cuts) for k in range(2)]
        sums = [jnp.where(is_mine, total, 0.0) for total in sums]
        left, inner = [total.T.astype(BF16) for total in sums], sums[1].astype(BF16)
        for cut in cuts:
            for k in range(2):
                both = dot32(left[k], rows(1 - k, cut))
                sum_refs[k][:, cut] = both[:rank]
                sum_refs[2 + k][:, cut] = both[rank:]
            dx = dot32(inner, factors(0, cut)).astype(BF16)
            late = dot32(late_ref[...], jnp.where(at_end, outer_in[0, :, cut], far_in[0, :, cut])).astype(BF16)
            moved = [jnp.where(at_end, swapped_ref[:, cut], late), jnp.where(at_end, late, early_ref[:, cut])]
            for n, dx in enumerate(moved + [dx[:block], dx[block:]]):
                for m in range(plane):
                    dx_refs[m][n * capacity:(n + 1) * capacity, cut] = dx[m * capacity:(m + 1) * capacity]

    shapes = [((4 * capacity, width), BF16)] * plane + [((rank, width), F32)] * 4
    return in_place(body, shapes, *stage, pair, own, outer, far, inner_late, dx_early, swapped, flags=flags)


def move_adapters(plane, acts, cotan, token_task_index, task_slot_lookup, pool_down_factors, pool_up_factors):
    ndevices = lax.axis_size("dp")
    tokens, width = acts.shape
    capacity = 2 * ((tokens + ndevices - 1) // ndevices)
    me = lax.axis_index("dp")
    z, column = me // plane, me % plane
    is_end = (z == 0) | (z == 3)
    end_flag = is_end.astype(jnp.int32).reshape(1)

    def planes(pairs):
        return [(a * plane + c, b * plane + c) for a, b in pairs for c in range(plane)]

    swap = planes([(0, 1), (1, 0), (2, 3), (3, 2)])
    cross = planes([(1, 2), (2, 1)])
    outward = planes([(1, 0), (2, 3)])
    inward = planes([(0, 1), (3, 2)])

    def send(array, pairs):
        return lax.ppermute(array, "dp", pairs)

    def after(arrays, *others):
        return lax.optimization_barrier((arrays, others))[0]

    def beside(m):
        return [(i, (i // plane) * plane + ((i % plane) ^ m)) for i in range(ndevices)]

    lowest, none = jnp.array(-jnp.inf, BF16), (0, 0, 0)
    own = jnp.maximum(
        lax.pad(pool_down_factors, lowest, ((0, 1, 0), none, none)),
        lax.pad(pool_up_factors, lowest, ((1, 0, 0), none, none)),
    )
    pair = send(own, swap)
    crossed = send(own, cross)

    owner, position = route(token_task_index, task_slot_lookup, ndevices)
    owner_z, turn = owner // plane, (owner % plane) ^ column
    other_mid = jnp.where(z < 2, 2, 1)
    kind = jnp.where(owner_z == z, 0, jnp.where(owner_z == (z ^ 1), 1, jnp.where(owner_z == other_mid, 2, 3)))

    def places(wanted, row, rows):
        hot = jnp.arange(rows, dtype=jnp.int32)[:, None] == row[None, :]
        return (hot & wanted[None, :]).astype(BF16)

    def after(arrays, *others):
        return lax.optimization_barrier((arrays, others))[0]

    block = plane * capacity
    mine = (3 - kind) * capacity + position
    row = jnp.where(kind == 2, 10 * capacity, 12 * capacity) + (turn - 2) * jnp.where(kind == 2, capacity, 2 * capacity)
    row += jnp.where(kind == 2, 0, (1 - kind) * capacity) + position
    row = jnp.where(kind == 3, (6 + turn) * capacity + position, row)
    row = jnp.where(turn < 2, turn * block + mine, row)
    place = places(kind >= 0, row, 4 * block)
    place_back = places(kind >= 0, turn * block + mine, 4 * block)
    own_rows, beside_rows, across3, across2, across10 = pack(
        place, acts, cotan, [(1, 4 * capacity)] * 2 + [(2, capacity)] * 2 + [(2, 2 * capacity)]
    )

    def over_x(blocks):
        moved = send(blocks, beside(2))
        return moved, send(moved[1:], beside(1))

    beside_rows = send(beside_rows, beside(1))
    across3 = over_x(across3)
    stage3 = (own_rows, beside_rows) + across3
    rows3 = jnp.concatenate([r[0, :, :capacity] for r in stage3], axis=1)
    handed = send(rows3, inward)
    across2 = over_x(after(across2, across3[0]))
    across10 = over_x(after(across10, across2[1]))
    rows2 = [r[0, :, capacity:2 * capacity] for r in (own_rows, beside_rows)] + [r[0] for r in across2]
    rows2 = jnp.concatenate(rows2, axis=1)
    stage10 = (own_rows, beside_rows) + across10
    outer = send(crossed, outward)
    far = send(pair, cross)

    up2, down2, dx_early, late_rows = early_group(end_flag, rows3, rows2, crossed)
    up3, down3, inner_late, swapped = late_group(end_flag, late_rows, handed, far, outer)
    up2_in = send(up3, inward)
    down3, swapped, up3 = send(down3, cross), send(swapped, swap), send(up3, cross)

    swapped, down3 = lax.optimization_barrier((swapped, down3))
    dx_own, dx_beside, *dx_across, up1, down1, up0, down0 = near_groups(
        end_flag, stage10, pair, own, outer, far, inner_late, dx_early, swapped, capacity,
        (2 * capacity, 2 * capacity, 0, 0),
    )

    def add(a, b):
        return (a.astype(F32) + b.astype(F32)).astype(BF16)

    down2, down1 = add(down2, swapped), add(down1, down3)
    dx_across[0] = send(dx_across[0], beside(2))
    dx_across[1] = send(after(dx_across[1], dx_across[0]), beside(2))
    up2_in, up3 = after((up2_in, up3), down2, down1, dx_across[0])
    down2, down1 = send(down2, cross), send(down1, swap)
    up2, up1 = send(add(up2, up2_in), cross), send(add(up1, up3), swap)

    back = [dx_own, send(dx_beside, beside(1)), dx_across[0], send(dx_across[1], beside(1))]
    half_acts = unpack(place_back.T, back, tokens, 0)
    grad_acts = unpack(place_back.T, back, tokens, 1, half_acts)
    raw_down, down_squares = final_sum(down0, down2, down1)
    raw_up, up_squares = final_sum(up0, up2, up1)
    part = down_squares + up_squares
    part = part + sum(after([send(part, beside(m)) for m in range(1, plane)], half_acts))
    along = [[(i, (i // plane ^ m) * plane + i % plane) for i in range(ndevices)] for m in (3, 2, 1)]
    parts = after([send(part, pairs) for pairs in along], grad_acts)
    return (grad_acts, *scaled((raw_down, raw_up), (part, *parts), ndevices))


def solution(mesh):
    plane = 4
    by_planes = mesh.shape["dp"] == 4 * plane

    def per_device(*arrays):
        if by_planes:
            return move_adapters(plane, *arrays)
        return move_tokens(*arrays)

    rows, pools = P(("parts", "dp"), None), P(("parts", "dp"), None, None)
    return jax.shard_map(
        per_device,
        mesh=mesh,
        in_specs=(rows, rows, rows, P("parts"), pools, pools),
        out_specs=(rows, pools, pools),
        check_vma=False,
    )
```

```python
import jax
import jax.numpy as jnp
from jax import lax
from jax.experimental import pallas as pl
from jax.experimental.pallas import tpu as pltpu
from jax.sharding import PartitionSpec as P

BF16, F32 = jnp.bfloat16, jnp.float32
ROWS_OF = (((1,), (1,)), ((), ()))
OUTER = (((0,), (0,)), ((), ()))
INNER = (((1,), (0,)), ((), ()))
HBM = pl.BlockSpec(memory_space=pltpu.HBM)
WHOLE = pl.BlockSpec(memory_space=pltpu.VMEM)
VMEM_BYTES = 12 * 2**20


def dot32(a, b, dims=INNER):
    return lax.dot_general(a, b, dims, preferred_element_type=F32)


def route(token_task_index, task_slot_lookup, ndevices):
    pool = task_slot_lookup.shape[0]
    task_hot = (token_task_index == jnp.arange(pool, dtype=jnp.int32)[None, :]).astype(jnp.int32)
    owner = jnp.sum(task_hot * task_slot_lookup[None, :], axis=1)
    owner_hot = (owner[:, None] == jnp.arange(ndevices, dtype=jnp.int32)[None, :]).astype(jnp.int32)
    before = jnp.cumsum(owner_hot, axis=0) - owner_hot
    position = jnp.sum(before * owner_hot, axis=1)
    return owner, position


def clipped(raw_down, raw_up, ndevices):
    local_sq = jnp.sum(raw_down * raw_down) + jnp.sum(raw_up * raw_up)
    total = lax.psum(local_sq, "dp")
    norm = jnp.sqrt(total + 1e-06)
    limit = jnp.sqrt(jnp.float32(2 * raw_down.shape[0] * raw_down.shape[1] * ndevices))
    factor = jnp.minimum(jnp.float32(1.0), limit / norm)
    return (raw_down * factor)[None], (raw_up * factor)[None]


def move_tokens(acts, cotan, token_task_index, task_slot_lookup, pool_down_factors, pool_up_factors):
    ndevices = lax.axis_size("dp")
    tokens, width = acts.shape
    capacity = 2 * ((tokens + ndevices - 1) // ndevices)
    slots = ndevices * capacity
    owner, position = route(token_task_index, task_slot_lookup, ndevices)
    dest = owner * capacity + position
    placed = (jnp.arange(slots, dtype=jnp.int32)[:, None] == dest[None, :]).astype(BF16)

    def exchange(rows):
        rows = rows.reshape(ndevices, capacity, width)
        return lax.all_to_all(rows, "dp", split_axis=0, concat_axis=0, tiled=True).reshape(slots, width)

    down, up = pool_down_factors[0], pool_up_factors[0]
    rows_x = exchange(dot32(placed, acts).astype(BF16))
    rows_g = exchange(dot32(placed, cotan).astype(BF16))
    hidden = dot32(rows_x, down, ROWS_OF).astype(BF16)
    inner = dot32(rows_g, up, ROWS_OF).astype(BF16)
    returned = exchange(dot32(inner, down).astype(BF16))
    grad_acts = dot32(placed, returned, OUTER).astype(BF16)
    raw_up = dot32(hidden, rows_g, OUTER)
    raw_down = dot32(inner, rows_x, OUTER)
    return (grad_acts,) + clipped(raw_down, raw_up, ndevices)


def in_hbm(*arrays):
    return [pltpu.with_memory_space_constraint(a, pltpu.HBM) for a in arrays]


def in_vmem(*arrays):
    return [pltpu.with_memory_space_constraint(a, pltpu.VMEM) for a in arrays]


def kernel_params(semantics=("arbitrary",)):
    return pltpu.CompilerParams(dimension_semantics=semantics, vmem_limit_bytes=VMEM_BYTES)


def pack(place, acts, cotan, shapes):
    tokens, width = acts.shape
    tile = min(width, 1024)
    tiles = width // tile

    def body(place_ref, x_in, g_in, *refs):
        out_refs, (rows, sems) = refs[:-2], refs[-2:]
        step = pl.program_id(0)

        def copies(i):
            cut = pl.ds(pl.multiple_of(i * tile, tile), tile)
            return [pltpu.make_async_copy(r.at[:, cut], rows.at[k, :, cut], sems.at[k, i]) for k, r in enumerate((x_in, g_in))]

        @pl.when(step == 0)
        def _():
            for i in range(tiles):
                for c in copies(i):
                    c.start()

        for c in copies(step):
            c.wait()
        cut = pl.ds(pl.multiple_of(step * tile, tile), tile)
        for k in range(2):
            moved = dot32(place_ref[...], rows[k, :, cut]).astype(BF16)
            first = 0
            for out_ref, (columns, size) in zip(out_refs, shapes):
                for c in range(columns):
                    out_ref[c, k] = moved[first:first + size]
                    first += size

    return pl.pallas_call(
        body,
        grid=(tiles,),
        in_specs=[pl.BlockSpec(place.shape, lambda i: (0, 0)), HBM, HBM],
        out_specs=[pl.BlockSpec((c, 2, size, tile), lambda i: (0, 0, 0, i)) for c, size in shapes],
        out_shape=[jax.ShapeDtypeStruct((c, 2, size, width), BF16) for c, size in shapes],
        scratch_shapes=[pltpu.VMEM((2, tokens, width), BF16), pltpu.SemaphoreType.DMA((2, tiles))],
        compiler_params=kernel_params(),
    )(place, *in_hbm(acts, cotan))


def unpack(place, blocks, tokens, half, into=None):
    width = blocks[0].shape[1]
    tile = min(width // 2, 2048)
    first = half * (width // 2 // tile)
    rest = () if into is None else (into,)

    def body(place_ref, *refs):
        rows = jnp.concatenate([ref[...] for ref in refs[:len(blocks)]], axis=0)
        refs[-1][...] = dot32(place_ref[...], rows).astype(BF16)

    return pl.pallas_call(
        body,
        grid=(width // 2 // tile,),
        in_specs=[pl.BlockSpec(place.shape, lambda i: (0, 0))]
        + [pl.BlockSpec((b.shape[0], tile), lambda i: (0, i + first)) for b in blocks]
        + [pl.BlockSpec(memory_space=pl.ANY)] * len(rest),
        out_specs=pl.BlockSpec((tokens, tile), lambda i: (0, i + first)),
        out_shape=jax.ShapeDtypeStruct((tokens, width), BF16),
        input_output_aliases={1 + len(blocks): 0} if rest else {},
        compiler_params=kernel_params(),
    )(place, *in_hbm(blocks[0]), *blocks[1:], *rest)


def final_sum(first, *others):
    rank, width = first.shape
    tile = min(width, 1024)

    def body(first_ref, *refs):
        other_refs, (total_ref, square_ref) = refs[:-2], refs[-2:]
        squares = jnp.zeros((8, 128), F32)
        for i in range(width // tile):
            cut = pl.ds(i * tile, tile)
            total = first_ref[:, cut]
            for ref in other_refs:
                total += ref[:, cut].astype(F32)
            total_ref[:, cut] = total
            total = total * total
            for r in range(0, rank, 8):
                for c in range(0, tile, 128):
                    squares += total[r:r + 8, c:c + 128]
        square_ref[...] = squares

    return in_place(body, [((rank, width), F32), ((8, 128), F32)], first, *others)


def scaled(raws, parts, ndevices):
    rank, width = raws[0].shape
    tile = min(width, 512)
    limit = float(2 * rank * width * ndevices) ** 0.5

    def body(*refs):
        raw_refs, part_refs = refs[:len(raws)], refs[len(raws):len(raws) + len(parts)]
        outs, (held, sems) = refs[len(raws) + len(parts):-2], refs[-2:]
        total = jnp.sum(sum(ref[...] for ref in part_refs), axis=(0, 1), keepdims=True)
        factor = jnp.minimum(jnp.float32(1.0), jnp.float32(limit) / jnp.sqrt(total + 1e-06))
        copies = []
        for i in range(width // tile):
            cut = pl.ds(i * tile, tile)
            for n, (raw_ref, out) in enumerate(zip(raw_refs, outs)):
                held[n, :, cut] = raw_ref[:, cut] * factor
                copies.append(pltpu.make_async_copy(held.at[n, :, cut], out.at[0, :, cut], sems.at[n, i]))
                copies[-1].start()
        for c in copies:
            c.wait()

    return pl.pallas_call(
        body,
        in_specs=[WHOLE] * (len(raws) + len(parts)),
        out_specs=[HBM] * len(raws),
        out_shape=[pltpu.HBM((1, rank, width), F32)] * len(raws),
        scratch_shapes=[
            pltpu.VMEM((len(raws), rank, width), F32),
            pltpu.SemaphoreType.DMA((len(raws), width // tile)),
        ],
        compiler_params=pltpu.CompilerParams(vmem_limit_bytes=VMEM_BYTES),
    )(*in_vmem(*raws, *parts))


def corner(rows, first_rows, columns, first_columns):
    upper = lax.broadcasted_iota(jnp.int32, (rows, columns), 0) < first_rows
    return upper == (lax.broadcasted_iota(jnp.int32, (rows, columns), 1) < first_columns)


def far_sums(tokens, factor, up_ref, down_ref, dx_ref, inner_ref=None):
    rank, width = up_ref.shape
    tile = min(width, 4096)
    cuts = [pl.ds(i * tile, tile) for i in range(width // tile)]
    hidden, inner = (sum(dot32(tokens(k, cut), factor(k, cut), ROWS_OF) for cut in cuts) for k in range(2))
    hidden_t, inner_t, inner = hidden.T.astype(BF16), inner.T.astype(BF16), inner.astype(BF16)
    rows = inner.shape[0] - dx_ref.shape[0]
    if inner_ref is not None:
        inner_ref[...] = inner[:rows]
    for cut in cuts:
        up_ref[:, cut] = dot32(hidden_t, tokens(1, cut)).astype(BF16)
        down_ref[:, cut] = dot32(inner_t, tokens(0, cut)).astype(BF16)
        dx_ref[:, cut] = dot32(inner[rows:], factor(0, cut)).astype(BF16)


def in_place(body, out_shapes, *arrays, flags=None):
    first = [] if flags is None else [flags]
    return pl.pallas_call(
        body,
        in_specs=[pl.BlockSpec(memory_space=pltpu.SMEM)] * len(first) + [WHOLE] * len(arrays),
        out_specs=[WHOLE] * len(out_shapes),
        out_shape=[pltpu.VMEM(*shape) for shape in out_shapes],
        compiler_params=pltpu.CompilerParams(vmem_limit_bytes=VMEM_BYTES),
    )(*first, *in_vmem(*arrays))


def early_group(flags, rows3, rows2, crossed):
    _, block, width = rows2.shape
    rank = crossed.shape[1]

    def body(flags_ref, rows3_ref, rows2_ref, crossed_ref, up_ref, down_ref, dx_ref, late_ref):
        far_sums(
            lambda k, cut: rows2_ref[k, :, cut], lambda k, cut: crossed_ref[k, :, cut], up_ref, down_ref, dx_ref
        )
        late_ref[...] = jnp.where(flags_ref[0] == 1, rows2_ref[...], rows3_ref[...])

    shapes = [((rank, width), BF16)] * 2 + [((block, width), BF16), ((2, block, width), BF16)]
    return in_place(body, shapes, rows3, rows2, crossed, flags=flags)


def late_group(flags, rows, handed, far, outer):
    _, block, width = rows.shape
    rank = far.shape[1]

    def body(flags_ref, rows_ref, handed_ref, outer_ref, far_ref, up_ref, down_ref, inner_ref, swap_ref):
        at_end = flags_ref[0] == 1
        far_sums(
            lambda k, cut: jnp.concatenate([rows_ref[k, :, cut], handed_ref[k, :, cut]], axis=0),
            lambda k, cut: jnp.where(at_end, outer_ref[k, :, cut], far_ref[k, :, cut]),
            up_ref,
            down_ref,
            swap_ref,
            inner_ref,
        )

        @pl.when(at_end)
        def _():
            swap_ref[...] = down_ref[...]

    shapes = [((rank, width), BF16)] * 2 + [((block, rank), BF16), ((block, width), BF16)]
    return in_place(body, shapes, rows, handed, outer, far, flags=flags)


def near_groups(flags, stage, pair, own, outer, far, inner_late, dx_early, swapped, capacity, first1):
    plane = len(stage)
    _, rank, width = own.shape
    block = plane * capacity
    tile = min(width, 2048)
    cuts = [pl.ds(i * tile, tile) for i in range(width // tile)]

    def body(flags_ref, *refs):
        stage_in, refs = refs[:plane], refs[plane:]
        pair_in, own_in, outer_in, far_in, late_ref, early_ref, swapped_ref = refs[:7]
        dx_refs, sum_refs = refs[7:7 + plane], refs[7 + plane:]
        at_end = flags_ref[0] == 1

        def rows(k, cut):
            return jnp.concatenate(
                [
                    r[0, k, pl.ds(first + n * capacity, capacity), cut]
                    for n in range(2)
                    for r, first in zip(stage_in, first1)
                ],
                axis=0,
            )

        def factors(k, cut):
            return jnp.concatenate([pair_in[k, :, cut], own_in[k, :, cut]], axis=0)

        is_mine = corner(2 * block, block, 2 * rank, rank)
        sums = [sum(dot32(rows(k, cut), factors(k, cut), ROWS_OF) for cut in cuts) for k in range(2)]
        sums = [jnp.where(is_mine, total, 0.0) for total in sums]
        left, inner = [total.T.astype(BF16) for total in sums], sums[1].astype(BF16)
        for cut in cuts:
            for k in range(2):
                both = dot32(left[k], rows(1 - k, cut))
                sum_refs[k][:, cut] = both[:rank]
                sum_refs[2 + k][:, cut] = both[rank:]
            dx = dot32(inner, factors(0, cut)).astype(BF16)
            late = dot32(late_ref[...], jnp.where(at_end, outer_in[0, :, cut], far_in[0, :, cut])).astype(BF16)
            moved = [jnp.where(at_end, swapped_ref[:, cut], late), jnp.where(at_end, late, early_ref[:, cut])]
            for n, dx in enumerate(moved + [dx[:block], dx[block:]]):
                for m in range(plane):
                    dx_refs[m][n * capacity:(n + 1) * capacity, cut] = dx[m * capacity:(m + 1) * capacity]

    shapes = [((4 * capacity, width), BF16)] * plane + [((rank, width), F32)] * 4
    return in_place(body, shapes, *stage, pair, own, outer, far, inner_late, dx_early, swapped, flags=flags)


def move_adapters(plane, acts, cotan, token_task_index, task_slot_lookup, pool_down_factors, pool_up_factors):
    ndevices = lax.axis_size("dp")
    tokens, width = acts.shape
    capacity = 2 * ((tokens + ndevices - 1) // ndevices)
    me = lax.axis_index("dp")
    z, column = me // plane, me % plane
    is_end = (z == 0) | (z == 3)
    end_flag = is_end.astype(jnp.int32).reshape(1)

    def planes(pairs):
        return [(a * plane + c, b * plane + c) for a, b in pairs for c in range(plane)]

    swap = planes([(0, 1), (1, 0), (2, 3), (3, 2)])
    cross = planes([(1, 2), (2, 1)])
    outward = planes([(1, 0), (2, 3)])
    inward = planes([(0, 1), (3, 2)])

    def send(array, pairs):
        return lax.ppermute(array, "dp", pairs)

    def after(arrays, *others):
        return lax.optimization_barrier((arrays, others))[0]

    def beside(m):
        return [(i, (i // plane) * plane + ((i % plane) ^ m)) for i in range(ndevices)]

    lowest, none = jnp.array(-jnp.inf, BF16), (0, 0, 0)
    own = jnp.maximum(
        lax.pad(pool_down_factors, lowest, ((0, 1, 0), none, none)),
        lax.pad(pool_up_factors, lowest, ((1, 0, 0), none, none)),
    )
    pair = send(own, swap)
    crossed = send(own, cross)

    owner, position = route(token_task_index, task_slot_lookup, ndevices)
    owner_z, turn = owner // plane, (owner % plane) ^ column
    other_mid = jnp.where(z < 2, 2, 1)
    kind = jnp.where(owner_z == z, 0, jnp.where(owner_z == (z ^ 1), 1, jnp.where(owner_z == other_mid, 2, 3)))

    def places(wanted, row, rows):
        hot = jnp.arange(rows, dtype=jnp.int32)[:, None] == row[None, :]
        return (hot & wanted[None, :]).astype(BF16)

    def after(arrays, *others):
        return lax.optimization_barrier((arrays, others))[0]

    block = plane * capacity
    mine = (3 - kind) * capacity + position
    row = jnp.where(kind == 2, 10 * capacity, 12 * capacity) + (turn - 2) * jnp.where(kind == 2, capacity, 2 * capacity)
    row += jnp.where(kind == 2, 0, (1 - kind) * capacity) + position
    row = jnp.where(kind == 3, (6 + turn) * capacity + position, row)
    row = jnp.where(turn < 2, turn * block + mine, row)
    place = places(kind >= 0, row, 4 * block)
    place_back = places(kind >= 0, turn * block + mine, 4 * block)
    own_rows, beside_rows, across3, across2, across10 = pack(
        place, acts, cotan, [(1, 4 * capacity)] * 2 + [(2, capacity)] * 2 + [(2, 2 * capacity)]
    )

    def over_x(blocks):
        moved = send(blocks, beside(2))
        return moved, send(moved[1:], beside(1))

    beside_rows = send(beside_rows, beside(1))
    across3 = over_x(across3)
    stage3 = (own_rows, beside_rows) + across3
    rows3 = jnp.concatenate([r[0, :, :capacity] for r in stage3], axis=1)
    handed = send(rows3, inward)
    across2 = over_x(after(across2, across3[0]))
    across10 = over_x(after(across10, across2[1]))
    rows2 = [r[0, :, capacity:2 * capacity] for r in (own_rows, beside_rows)] + [r[0] for r in across2]
    rows2 = jnp.concatenate(rows2, axis=1)
    stage10 = (own_rows, beside_rows) + across10
    outer = send(crossed, outward)
    far = send(pair, cross)

    up2, down2, dx_early, late_rows = early_group(end_flag, rows3, rows2, crossed)
    up3, down3, inner_late, swapped = late_group(end_flag, late_rows, handed, far, outer)
    up2_in = send(up3, inward)
    down3, swapped, up3 = send(down3, cross), send(swapped, swap), send(up3, cross)

    swapped, down3 = lax.optimization_barrier((swapped, down3))
    dx_own, dx_beside, *dx_across, up1, down1, up0, down0 = near_groups(
        end_flag, stage10, pair, own, outer, far, inner_late, dx_early, swapped, capacity,
        (2 * capacity, 2 * capacity, 0, 0),
    )

    def add(a, b):
        return (a.astype(F32) + b.astype(F32)).astype(BF16)

    down2, down1 = add(down2, swapped), add(down1, down3)
    dx_across[0] = send(dx_across[0], beside(2))
    dx_across[1] = send(after(dx_across[1], dx_across[0]), beside(2))
    up2_in, up3 = after((up2_in, up3), down2, down1, dx_across[0])
    down2, down1 = send(down2, cross), send(down1, swap)
    up2, up1 = send(add(up2, up2_in), cross), send(add(up1, up3), swap)

    back = [dx_own, send(dx_beside, beside(1)), dx_across[0], send(dx_across[1], beside(1))]
    half_acts = unpack(place_back.T, back, tokens, 0)
    grad_acts = unpack(place_back.T, back, tokens, 1, half_acts)
    raw_down, down_squares = final_sum(down0, down2, down1)
    raw_up, up_squares = final_sum(up0, up2, up1)
    part = down_squares + up_squares
    part = part + sum(after([send(part, beside(m)) for m in range(plane - 1, 0, -1)], half_acts))
    along = [[(i, (i // plane ^ m) * plane + i % plane) for i in range(ndevices)] for m in (3, 2, 1)]
    parts = after([send(part, pairs) for pairs in along], grad_acts)
    return (grad_acts, *scaled((raw_down, raw_up), (part, *parts), ndevices))


def solution(mesh):
    plane = 4
    by_planes = mesh.shape["dp"] == 4 * plane

    def per_device(*arrays):
        if by_planes:
            return move_adapters(plane, *arrays)
        return move_tokens(*arrays)

    rows, pools = P(("parts", "dp"), None), P(("parts", "dp"), None, None)
    return jax.shard_map(
        per_device,
        mesh=mesh,
        in_specs=(rows, rows, rows, P("parts"), pools, pools),
        out_specs=(rows, pools, pools),
        check_vma=False,
    )
```
